32 devices in a mesh: bank: 4 (over z), freq: 8 (over y, x, core).
Axes of the slice: x: 2, y: 2, z: 4, core: 2. Of those that a mesh axis runs over, the one named last changes fastest.
Arguments:
- strain: float32 [3, 2, 512, 2048], P(None, None, 'freq', 'bank'), may hold values from -6 to 6
- templates: float32 [8, 2, 512, 2048], P('bank', None, 'freq'), may hold values from -6 to 6
- coinc_tmpl: int32 [4], P('bank'), may hold values from 0 to 1
- coinc_det: int32 [4], P('bank'), may hold values from 0 to 2
- bin_edges: int32 [8, 15], P('bank'), may hold values from 1 to 31, as said below
Outputs:
- snr: float32 [8, 3, 2, 2048, 512], P('bank', None, None, 'freq')
- chi_sq: float32 [4, 2048, 512], P('bank', 'freq')
The draws below stay inside these ranges and needn't reach their ends.
Inputs may be any that keep to these rules, and one draw needn't show every extreme that they name: `coinc_tmpl`: the entries of shard j // 1 of bank name templates of that shard. `bin_edges`: each row is strictly increasing.
All inputs are finite; a program needn't handle non-finite values.
Results may differ from the reference program's by a relative error of at most 0.0003.
Values sent between devices are 32-bit elements; how exact they have to be, the bound alone decides.
No kernel may reach another device: no remote copies, remote signals or barrier semaphores. Data moves between devices by JAX's collectives and lax.ppermute only.
A program may use at most 192 MiB of HBM per device.

```python
import jax
import jax.numpy as jnp
from jax import lax

N1 = 2048
N2 = 512
DET = 3
NBLK = 32
BINS = 16
TPL_DEV = 2
CO_DEV = 1
TEMPL = 8
CO_ALL = 4


def draw_bin_edges(key, part):
    row_keys = jax.random.split(key, TEMPL)

    def one_row(row_key):
        shuffled = jax.random.permutation(row_key, NBLK - 1) + 1
        return jnp.sort(shuffled[:BINS - 1])
    return jax.vmap(one_row)(row_keys).astype(jnp.int32)


def with_ends(entries, key, smallest, high):
    extent = entries.shape
    place = [jax.random.randint(jax.random.fold_in(key, axis), (), 0, extent[axis]) for axis in range(len(extent))]
    entries = entries.at[tuple(place)].set(smallest)
    longest = extent.index(max(extent))
    place[longest] = (place[longest] + 1) % extent[longest]
    return entries.at[tuple(place)].set(high)


def block_levels(rng, dims, cuts, low, largest):
    def one(axis_at, blocks):
        heights = jax.random.uniform(jax.random.fold_in(jax.random.fold_in(rng, 6), axis_at), (blocks,), jnp.float32, low / len(cuts), largest / len(cuts))
        return jnp.repeat(jnp.exp(heights), dims[axis_at] // blocks).reshape((-1,) + (1,) * (len(dims) - axis_at - 1))

    gain = one(*cuts[0])
    for cut in cuts[1:]:
        gain = gain * one(*cut)
    return gain


def gaussian(key, extent, scale, reach, pieces=(), held_as=jnp.bfloat16):
    values = jax.random.normal(key, extent, jnp.float32) * scale
    if len(pieces) > 0:
        values = block_levels(key, extent, pieces, -0.22, 0.18) * values
    return jnp.clip(values, min=-reach, max=reach).astype(held_as)


def setup_inputs(seed: int = 0) -> dict:
    streams_of = jax.random.split(jax.random.key(seed), 6)
    strain = gaussian(streams_of[0], (DET, 2, N2, N1), 1.0, 6.0, ((2, 8), (3, 4)), jnp.float32)
    templates = gaussian(streams_of[1], (TEMPL, 2, N2, N1), 1.0, 6.0, ((0, 4), (2, 8)), jnp.float32)
    coinc_tmpl = with_ends(jax.random.randint(streams_of[2], (CO_ALL,), 0, TPL_DEV), jax.random.fold_in(streams_of[2], 1), 0, TPL_DEV - 1).astype(jnp.int32)
    coinc_det = with_ends(jax.random.randint(streams_of[3], (CO_ALL,), 0, DET), jax.random.fold_in(streams_of[3], 1), 0, DET - 1).astype(jnp.int32)
    bin_edges = draw_bin_edges(jax.random.fold_in(streams_of[5], 71), 0)
    return dict(strain=strain, templates=templates, coinc_tmpl=coinc_tmpl, coinc_det=coinc_det, bin_edges=bin_edges)


def series(part_re, part_im):
    flattened = lax.complex(part_re.T.reshape(-1), part_im.T.reshape(-1))
    signal = jnp.fft.ifft(flattened) * (N1 * N2)
    signal = signal.reshape(N2, N1).T
    return jnp.stack([jnp.real(signal), jnp.imag(signal)])

def reference(strain, templates, coinc_tmpl, coinc_det, bin_edges):
    tmpl_re = templates[:, 0]
    tmpl_im = templates[:, 1]
    strain_re = strain[:, 0]
    strain_im = strain[:, 1]
    block_rows = N1 // NBLK
    block_power = (tmpl_re * tmpl_re + tmpl_im * tmpl_im).reshape(TEMPL, N2, NBLK, block_rows).sum(axis=(1, 3))
    sigma_sq = block_power.sum(axis=1)
    inv_sigma = 1.0 / jnp.sqrt(sigma_sq)
    bin_of = lax.optimization_barrier(jnp.sum(jnp.arange(NBLK, dtype=jnp.int32)[None, :, None] >= bin_edges[:, None, :], axis=2))
    weights = jnp.stack([lax.optimization_barrier(jnp.sum(jnp.where(bin_of == level, block_power, 0.0), axis=1)) for level in range(BINS)], axis=1) / sigma_sq[:, None]

    def per_template(which):
        prod_re = tmpl_re[which][None] * strain_re + tmpl_im[which][None] * strain_im
        prod_im = tmpl_re[which][None] * strain_im - tmpl_im[which][None] * strain_re
        return jax.vmap(series)(prod_re, prod_im) * inv_sigma[which]
    snr = lax.map(per_template, jnp.arange(TEMPL, dtype=jnp.int32))
    slot_tmpl = jnp.arange(CO_ALL, dtype=jnp.int32) // CO_DEV * TPL_DEV + coinc_tmpl
    row_block = jnp.arange(N1, dtype=jnp.int32) // block_rows

    def per_slot(slot_index):
        which = slot_tmpl[slot_index]
        detector = coinc_det[slot_index]
        prod_re = tmpl_re[which] * strain_re[detector] + tmpl_im[which] * strain_im[detector]
        prod_im = tmpl_re[which] * strain_im[detector] - tmpl_im[which] * strain_re[detector]
        row_bin = bin_of[which][row_block]

        def per_bin(level):
            inside = (row_bin == level)[None, :]
            return series(jnp.where(inside, prod_re, 0.0), jnp.where(inside, prod_im, 0.0)) * inv_sigma[which]
        levels = lax.map(per_bin, jnp.arange(BINS, dtype=jnp.int32))
        total = levels.sum(axis=0)
        spread = weights[which][:, None, None, None]
        deviation = levels - spread * total[None]
        return lax.optimization_barrier(jnp.sum((deviation[:, 0] ** 2 + deviation[:, 1] ** 2) / spread[:, 0], axis=0))
    chi_sq = lax.map(per_slot, jnp.arange(CO_ALL, dtype=jnp.int32))
    return (snr, chi_sq)
```

```python
import functools

import jax
import jax.numpy as jnp
import ml_dtypes
import numpy as np
from jax import lax
from jax.experimental import pallas as pl
from jax.experimental.pallas import tpu as pltpu
from jax.sharding import PartitionSpec as P

N1 = 2048
N2 = 512
NBLK = 32
BLOCK = N1 // NBLK
BINS = 16
LANES = 128
COARSE = N1 // LANES
FOUR = N2 // LANES
F32 = jnp.float32
BF16 = jnp.bfloat16
MIB = 1 << 20


def split_table(table):
    high = table.astype(ml_dtypes.bfloat16)
    low = (table - high.astype(np.float64)).astype(ml_dtypes.bfloat16)
    return high, low


def first_table():
    angle = 2 * np.pi * (np.outer(np.arange(LANES), np.arange(LANES)) % LANES) / LANES
    cos, sin = np.cos(angle), np.sin(angle)
    return split_table(np.block([[cos, sin], [-sin, cos]]))


def stage_table():
    angle = 2 * np.pi * np.outer(np.arange(COARSE), np.arange(LANES)) / N1
    return np.concatenate([np.cos(angle), np.sin(angle)]).astype(np.float32)


def second_table():
    blocks = []
    for a in range(FOUR):
        n2 = a + FOUR * np.arange(LANES)
        angle = 2 * np.pi * (np.outer(n2, np.arange(LANES)) % N2) / N2
        cos, sin = np.cos(angle), np.sin(angle)
        blocks.append(np.block([[cos, -sin], [sin, cos]]))
    return split_table(np.concatenate(blocks))


def split(x):
    high = x.astype(BF16)
    return high, (x - high.astype(F32)).astype(BF16)


def phase(index, length):
    angle = (index % length).astype(F32) * (2.0 * np.pi / length)
    return jnp.cos(angle), jnp.sin(angle)


def times_i(z):
    return (-z[1], z[0])


def plus(x, y):
    return (x[0] + y[0], x[1] + y[1])


def minus(x, y):
    return (x[0] - y[0], x[1] - y[1])


def dft4(x):
    s0, s1 = plus(x[0], x[2]), minus(x[0], x[2])
    s2, s3 = plus(x[1], x[3]), times_i(minus(x[1], x[3]))
    return [plus(s0, s2), plus(s1, s3), minus(s0, s2), minus(s1, s3)]


def turn(z, step):
    step %= 16
    if step == 0:
        return z
    if step == 4:
        return times_i(z)
    if step == 8:
        return (-z[0], -z[1])
    half = float(np.sqrt(0.5))
    if step == 2:
        return ((z[0] - z[1]) * half, (z[0] + z[1]) * half)
    if step == 6:
        return ((z[0] + z[1]) * -half, (z[0] - z[1]) * half)
    cos, sin = float(np.cos(np.pi * step / 8)), float(np.sin(np.pi * step / 8))
    return (z[0] * cos - z[1] * sin, z[0] * sin + z[1] * cos)


def dft16(x):
    columns = [dft4([x[4 * u1 + u0] for u1 in range(4)]) for u0 in range(4)]
    out = [None] * 16
    for a0 in range(4):
        ys = dft4([turn(columns[u0][a0], u0 * a0) for u0 in range(4)])
        for a1 in range(4):
            out[a0 + 4 * a1] = ys[a1]
    return out


def dot3(left, right):
    (lh, ll), (rh, rl) = left, right
    d = functools.partial(jnp.dot, preferred_element_type=F32)
    return d(lh, rh) + (d(lh, rl) + d(ll, rh))


def first_kernel(
    freq, tmpl_ref, strain_ref, wh_ref, wl_ref, stage_ref, tw_ref, out_ref, gh, gl
):
    tmpls, _, rows, _ = tmpl_ref.shape
    per_piece = COARSE // strain_ref.shape[0]
    for t in range(tmpls):
        x = []
        for u in range(COARSE):
            at = slice(u * LANES, (u + 1) * LANES)
            off = u % per_piece
            there = slice(off * LANES, (off + 1) * LANES)
            hr, hi = tmpl_ref[t, 0, :, at], tmpl_ref[t, 1, :, at]
            sr = strain_ref[u // per_piece, 0, :, there]
            si = strain_ref[u // per_piece, 1, :, there]
            x.append((hr * sr + hi * si, hr * si - hi * sr))
        y = dft16(x)
        for a in range(COARSE):
            cos, sin = stage_ref[a : a + 1, :], stage_ref[COARSE + a : COARSE + a + 1, :]
            yr, yi = y[a]
            at = pl.ds((a * tmpls + t) * rows, rows)
            gh[at, :LANES], gl[at, :LANES] = split(yr * cos - yi * sin)
            gh[at, LANES:], gl[at, LANES:] = split(yr * sin + yi * cos)
    z = dot3((gh[...], gl[...]), (wh_ref[...], wl_ref[...]))
    width = LANES // freq
    slot = lax.broadcasted_iota(jnp.int32, (rows, LANES), 1) // width
    for t in range(tmpls):
        for group in range(COARSE // freq):
            turned = []
            for i in range(freq):
                a = group * freq + i
                at = slice((a * tmpls + t) * rows, (a * tmpls + t + 1) * rows)
                zr, zi = z[at, :LANES], z[at, LANES:]
                lane = slice(a * LANES, (a + 1) * LANES)
                cos, sin = tw_ref[0, :, lane], tw_ref[1, :, lane]
                pair = (zr * cos - zi * sin, zr * sin + zi * cos)
                if i:
                    pair = tuple(pltpu.roll(v, i * width, 1) for v in pair)
                turned.append(pair)
            for q in range(freq):
                for p in range(2):
                    value = turned[(0 - q) % freq][p]
                    for s in range(1, freq):
                        value = jnp.where(slot == s, turned[(s - q) % freq][p], value)
                    out_ref[q, t, p, group] = value


def first_section(freq, templates, strain, first, stage, twist):
    tmpls, _, cols, _ = templates.shape
    pieces, _, _, piece_len = strain.shape
    groups = COARSE // freq
    rows = 16
    whole = lambda shape: pl.BlockSpec(shape, lambda c: (0,) * len(shape))
    return pl.pallas_call(
        functools.partial(first_kernel, freq),
        grid=(cols // rows,),
        in_specs=[
            pl.BlockSpec((tmpls, 2, rows, N1), lambda c: (0, 0, c, 0)),
            pl.BlockSpec((pieces, 2, rows, piece_len), lambda c: (0, 0, c, 0)),
            whole((2 * LANES, 2 * LANES)),
            whole((2 * LANES, 2 * LANES)),
            whole((2 * COARSE, LANES)),
            pl.BlockSpec((2, rows, N1), lambda c: (0, c, 0)),
        ],
        out_specs=pl.BlockSpec(
            (freq, tmpls, 2, groups, rows, LANES), lambda c: (0, 0, 0, 0, c, 0)
        ),
        out_shape=jax.ShapeDtypeStruct((freq, tmpls, 2, groups, cols, LANES), F32),
        scratch_shapes=[pltpu.VMEM((COARSE * tmpls * rows, 2 * LANES), BF16)] * 2,
        compiler_params=pltpu.CompilerParams(vmem_limit_bytes=32 * MIB),
        cost_estimate=pl.CostEstimate(
            flops=6 * tmpls * cols * N1 * 4 * LANES,
            bytes_accessed=4 * MIB,
            transcendentals=0,
        ),
        name="first_section",
    )(templates, strain, first[0], first[1], stage, twist)


def entry_kernel(which_ref, tmpl_ref, *refs):
    strain_refs, out_ref = refs[:-1], refs[-1]
    rows = out_ref.shape[0]
    lane = lax.broadcasted_iota(jnp.int32, (rows, LANES), 1)
    first_half = lane < BLOCK
    t = which_ref[0]
    for d, strain_ref in enumerate(strain_refs):

        @pl.when(which_ref[1] == d)
        def _():
            per_piece = COARSE // strain_ref.shape[0]
            for u in range(COARSE):
                at = slice(u * LANES, (u + 1) * LANES)
                off = u % per_piece
                there = slice(off * LANES, (off + 1) * LANES)
                hr, hi = tmpl_ref[t, 0, :, at], tmpl_ref[t, 1, :, at]
                sr = strain_ref[u // per_piece, 0, :, there]
                si = strain_ref[u // per_piece, 1, :, there]
                re, im = hr * sr + hi * si, hr * si - hi * sr
                lane0 = slice(2 * u * LANES, (2 * u + 1) * LANES)
                lane1 = slice((2 * u + 1) * LANES, (2 * u + 2) * LANES)
                out_ref[:, lane0] = jnp.where(first_half, re, pltpu.roll(im, BLOCK, 1))
                out_ref[:, lane1] = jnp.where(first_half, pltpu.roll(re, BLOCK, 1), im)


def entry_product(which, templates, strains):
    tmpls, _, cols, _ = templates.shape
    pieces, _, _, piece_len = strains[0].shape
    rows = 16
    return pl.pallas_call(
        entry_kernel,
        grid_spec=pltpu.PrefetchScalarGridSpec(
            num_scalar_prefetch=1,
            grid=(cols // rows,),
            in_specs=[pl.BlockSpec((tmpls, 2, rows, N1), lambda c, w: (0, 0, c, 0))]
            + [pl.BlockSpec((pieces, 2, rows, piece_len), lambda c, w: (0, 0, c, 0))]
            * len(strains),
            out_specs=pl.BlockSpec((rows, 2 * N1), lambda c, w: (c, 0)),
        ),
        out_shape=jax.ShapeDtypeStruct((cols, 2 * N1), F32),
        compiler_params=pltpu.CompilerParams(vmem_limit_bytes=32 * MIB),
        cost_estimate=pl.CostEstimate(
            flops=8 * cols * N1, bytes_accessed=6 * MIB, transcendentals=0
        ),
        name="entry_product",
    )(which, templates, *strains)


def second_points(x, w2h_ref, w2l_ref, use):
    for a, (yr, yi) in enumerate(dft4(x)):
        y = jnp.concatenate([yr, yi], axis=0)
        at = slice(a * 2 * LANES, (a + 1) * 2 * LANES)
        z = dot3((w2h_ref[at, :], w2l_ref[at, :]), split(y))
        use(a, z[:LANES], z[LANES:])


def second_kernel(freq, place_ref, scale_ref, part_ref, w2h_ref, w2l_ref, *refs):
    out_ref, hold, order = refs[-3:]
    groups, cols = part_ref.shape[3], part_ref.shape[4]
    per = LANES // cols
    width = LANES // freq
    scale = scale_ref[pl.program_id(0)]

    def rows_of(p, u):
        tiles = [
            jnp.concatenate(
                [part_ref[u * per + f, 0, p, g] for f in range(per)], axis=0
            )
            for g in range(groups)
        ]
        return jnp.concatenate(tiles, axis=1)

    x = [(rows_of(0, u), rows_of(1, u)) for u in range(FOUR)]

    def keep(a, re, im):
        for p, value in enumerate((re, im)):
            for g in range(groups):
                hold[p, g, pl.ds(a, LANES, stride=FOUR), :] = (
                    value[:, g * LANES : (g + 1) * LANES] * scale
                )

    second_points(x, w2h_ref, w2l_ref, keep)
    for p in range(2):
        for g in range(groups):
            turned = hold[p, g].T
            for s in range(freq):
                a = g * freq + lax.rem(s - place_ref[0] + freq, freq)
                for j in range(FOUR):
                    order[p, j, pl.ds(a, width, stride=COARSE), :] = turned[
                        s * width : (s + 1) * width, j * LANES : (j + 1) * LANES
                    ]
        for j in range(FOUR):
            out_ref[0, 0, p, :, j * LANES : (j + 1) * LANES] = order[p, j]


def second_section(freq, det, place, scale, parts, second, dets, earlier):
    _, tmpls, _, groups, cols, _ = parts.shape
    times = groups * LANES
    smem = pl.BlockSpec(memory_space=pltpu.SMEM)
    table = pl.BlockSpec((FOUR * 2 * LANES, 2 * LANES), lambda t: (0, 0))
    operands = [place, scale, parts, second[0], second[1]]
    in_specs = [
        smem,
        smem,
        pl.BlockSpec(
            (freq, 1, 2, groups, cols, LANES), lambda t: (0, t, 0, 0, 0, 0)
        ),
        table,
        table,
    ]
    aliases = {}
    if earlier is not None:
        operands.append(earlier)
        in_specs.append(pl.BlockSpec(memory_space=pl.ANY))
        aliases = {5: 0}
    return pl.pallas_call(
        functools.partial(second_kernel, freq),
        grid=(tmpls,),
        in_specs=in_specs,
        out_specs=pl.BlockSpec((1, 1, 2, times, N2), lambda t: (t, det, 0, 0, 0)),
        out_shape=jax.ShapeDtypeStruct((tmpls, dets, 2, times, N2), F32),
        scratch_shapes=[
            pltpu.VMEM((2, groups, N2, LANES), F32),
            pltpu.VMEM((2, FOUR, times, LANES), F32),
        ],
        input_output_aliases=aliases,
        compiler_params=pltpu.CompilerParams(vmem_limit_bytes=32 * MIB),
        cost_estimate=pl.CostEstimate(
            flops=6 * tmpls * times * FOUR * 4 * LANES * LANES,
            bytes_accessed=8 * MIB,
            transcendentals=0,
        ),
        name="second_section",
    )(*operands)


def bins_kernel(
    edge_ref, gain_ref, share_ref, entry_ref, wh_ref, wl_ref, tw_ref, w2h_ref, w2l_ref,
    out_ref, xh, xl, acc, levels, total, chi, hold,
):
    times = out_ref.shape[0]

    def cut(i, carry):
        at = pl.ds(pl.multiple_of(i * 2 * LANES, 2 * LANES), 2 * LANES)
        xh[:, at], xl[:, at] = split(entry_ref[:, at])
        return carry

    lax.fori_loop(0, 2 * N1 // (2 * LANES), cut, 0)
    total[...] = jnp.zeros_like(total)

    def add(block, blocks):
        at = pl.ds(pl.multiple_of(block * LANES, LANES), blocks * LANES)
        acc[...] += dot3((xh[:, at], xl[:, at]), (wh_ref[at, :], wl_ref[at, :]))

    def first(level, carry):
        start, end = edge_ref[level], edge_ref[level + 1]
        acc[...] = jnp.zeros_like(acc)

        def two(i, inner):
            add(start + 2 * i, 2)
            return inner

        lax.fori_loop(0, (end - start) // 2, two, 0)

        @pl.when((end - start) % 2 == 1)
        def _():
            add(end - 1, 1)

        for u in range(FOUR):
            at = slice(u * LANES, (u + 1) * LANES)
            re, im = acc[at, :times], acc[at, times:]
            cos, sin = tw_ref[0, at, :], tw_ref[1, at, :]
            vr, vi = re * cos - im * sin, re * sin + im * cos
            levels[level, 0, at, :] = vr
            levels[level, 1, at, :] = vi
            total[0, at, :] += vr
            total[1, at, :] += vi
        return carry

    lax.fori_loop(0, BINS, first, 0)
    chi[...] = jnp.zeros_like(chi)

    def second(level, carry):
        gain, share = gain_ref[level], share_ref[level]

        def rows_of(p, u):
            at = slice(u * LANES, (u + 1) * LANES)
            return levels[level, p, at, :] * gain - total[p, at, :] * share

        def keep(a, re, im):
            chi[a] += re * re + im * im

        x = [(rows_of(0, u), rows_of(1, u)) for u in range(FOUR)]
        second_points(x, w2h_ref, w2l_ref, keep)
        return carry

    lax.fori_loop(0, BINS, second, 0)
    for g in range(times // LANES):
        lane = slice(g * LANES, (g + 1) * LANES)
        for a in range(FOUR):
            hold[pl.ds(a, LANES, stride=FOUR), :] = chi[a, :, lane]
        out_ref[lane, :] = hold[...].T


def bins_section(edges, gain, share, entry, bank_table, twist, second):
    times = twist.shape[2]
    smem = pl.BlockSpec(memory_space=pltpu.SMEM)
    vmem = pl.BlockSpec(memory_space=pltpu.VMEM)
    return pl.pallas_call(
        bins_kernel,
        in_specs=[smem] * 3 + [vmem] * 6,
        out_specs=vmem,
        out_shape=jax.ShapeDtypeStruct((times, N2), F32),
        scratch_shapes=[
            pltpu.VMEM((N2, 2 * N1), BF16),
            pltpu.VMEM((N2, 2 * N1), BF16),
            pltpu.VMEM((N2, 2 * times), F32),
            pltpu.VMEM((BINS, 2, N2, times), F32),
            pltpu.VMEM((2, N2, times), F32),
            pltpu.VMEM((FOUR, LANES, times), F32),
            pltpu.VMEM((N2, LANES), F32),
        ],
        compiler_params=pltpu.CompilerParams(vmem_limit_bytes=58 * MIB),
        cost_estimate=pl.CostEstimate(
            flops=6 * 24 * N2 * 4 * LANES * times + 6 * BINS * FOUR * 4 * LANES**2 * times,
            bytes_accessed=20 * MIB,
            transcendentals=0,
        ),
        name="bins",
    )(edges, gain, share, entry, bank_table[0], bank_table[1], twist, *second)


def time_table(place, times):
    block = jnp.arange(NBLK, dtype=jnp.int32)[:, None, None]
    inner = jnp.arange(BLOCK, dtype=jnp.int32)[None, :, None]
    time = place * times + jnp.arange(times, dtype=jnp.int32)[None, None, :]
    cos, sin = phase((block * BLOCK + inner) * time, N1)
    real = jnp.concatenate([cos, sin], axis=2)
    imag = jnp.concatenate([-sin, cos], axis=2)
    table = jnp.concatenate([real, imag], axis=1).reshape(2 * N1, 2 * times)
    high = lax.reduce_precision(table, 8, 7)
    low = lax.reduce_precision(table - high, 8, 7)
    return high.astype(BF16), low.astype(BF16)


def per_device(strain, templates, coinc_tmpl, coinc_det, bin_edges):
    freq = lax.axis_size("freq")
    place = lax.axis_index("freq").astype(jnp.int32)
    tmpls, _, cols, _ = templates.shape
    dets = strain.shape[0]
    times = N1 // freq

    strains = [lax.all_gather(strain[d], "bank", axis=0, tiled=False) for d in range(dets)]

    first = tuple(jnp.asarray(t) for t in first_table())
    second = tuple(jnp.asarray(t) for t in second_table())
    stage = jnp.asarray(stage_table())

    power = (templates[:, 0] ** 2 + templates[:, 1] ** 2).sum(axis=1)
    local_power = power.reshape(tmpls, NBLK, BLOCK).sum(axis=2)
    block_power = lax.psum(local_power, "freq")
    sigma_sq = block_power.sum(axis=1)
    inv_sigma = lax.rsqrt(sigma_sq)
    bin_of = jnp.sum(
        jnp.arange(NBLK, dtype=jnp.int32)[None, :, None] >= bin_edges[:, None, :], axis=2
    )
    inside = bin_of[:, None, :] == jnp.arange(BINS, dtype=jnp.int32)[None, :, None]
    weights = jnp.where(inside, block_power[:, None, :], 0.0).sum(axis=2) / sigma_sq[:, None]

    column = place * cols + jnp.arange(cols, dtype=jnp.int32)
    lane = jnp.arange(N1, dtype=jnp.int32)
    time_of_lane = lane // LANES + COARSE * (lane % LANES)
    twist = jnp.stack(phase(column[:, None] * time_of_lane[None, :], N1 * N2))
    own_time = place * times + jnp.arange(times, dtype=jnp.int32)
    all_columns = jnp.arange(N2, dtype=jnp.int32)
    own_twist = jnp.stack(phase(all_columns[:, None] * own_time[None, :], N1 * N2))
    bank_table = time_table(place, times)

    parts = []
    for d in range(dets):
        sent = first_section(freq, templates, strains[d], first, stage, twist)
        shape = sent.shape
        got = lax.all_to_all(
            sent.reshape(freq, -1, LANES), "freq", split_axis=0, concat_axis=0, tiled=True
        )
        parts.append(got.reshape(shape))

    chi = []
    for j in range(coinc_tmpl.shape[0]):
        which = jnp.stack([coinc_tmpl[j], coinc_det[j]])
        product = entry_product(which, templates, strains)
        entry = lax.all_gather(product, "freq", axis=0, tiled=True)
        t = coinc_tmpl[j]
        edges = jnp.concatenate(
            [jnp.zeros((1,), jnp.int32), bin_edges[t], jnp.full((1,), NBLK, jnp.int32)]
        )
        gain = inv_sigma[t] * lax.rsqrt(weights[t])
        chi.append(
            bins_section(edges, gain, gain * weights[t], entry, bank_table, own_twist, second)
        )

    snr = None
    for d in range(dets):
        snr = second_section(
            freq, d, place.reshape(1), inv_sigma, parts[d], second, dets, snr
        )
    return (snr, jnp.stack(chi))


def solution(mesh):
    placed = (
        P(None, None, "freq", "bank"),
        P("bank", None, "freq", None),
        P("bank"),
        P("bank"),
        P("bank", None),
    )
    return jax.shard_map(
        per_device,
        mesh=mesh,
        in_specs=placed,
        out_specs=(P("bank", None, None, "freq", None), P("bank", "freq", None)),
        check_vma=False,
    )
```

```python
import functools

import jax
import jax.numpy as jnp
import ml_dtypes
import numpy as np
from jax import lax
from jax.experimental import pallas as pl
from jax.experimental.pallas import tpu as pltpu
from jax.sharding import PartitionSpec as P

N1 = 2048
N2 = 512
NBLK = 32
BLOCK = N1 // NBLK
BINS = 16
LANES = 128
COARSE = N1 // LANES
FOUR = N2 // LANES
F32 = jnp.float32
BF16 = jnp.bfloat16
MIB = 1 << 20
VMEM_LIMIT = 56 * MIB
ANY = pl.BlockSpec(memory_space=pl.ANY)


def split_table(table):
    high = table.astype(ml_dtypes.bfloat16)
    low = (table - high.astype(np.float64)).astype(ml_dtypes.bfloat16)
    return high, low


def first_table():
    angle = 2 * np.pi * (np.outer(np.arange(LANES), np.arange(LANES)) % LANES) / LANES
    cos, sin = np.cos(angle), np.sin(angle)
    return split_table(np.block([[cos, sin], [-sin, cos]]))


def stage_table():
    angle = 2 * np.pi * np.outer(np.arange(COARSE), np.arange(LANES)) / N1
    return np.concatenate([np.cos(angle), np.sin(angle)]).astype(np.float32)


def second_table(cols, halves):
    order = np.arange(LANES).reshape(LANES // cols, halves, cols // halves)
    order = order.transpose(1, 0, 2).reshape(-1)
    blocks = []
    for a in range(FOUR):
        n2 = a + FOUR * np.arange(LANES)
        angle = 2 * np.pi * (np.outer(n2, order) % N2) / N2
        cos, sin = np.cos(angle), np.sin(angle)
        blocks.append(np.block([[cos, -sin], [sin, cos]]))
    return split_table(np.concatenate(blocks))


def split(x):
    high = x.astype(BF16)
    return high, (x - high.astype(F32)).astype(BF16)


def phase(index, length):
    angle = (index % length).astype(F32) * (2.0 * np.pi / length)
    return jnp.cos(angle), jnp.sin(angle)


def times_i(z):
    return (-z[1], z[0])


def plus(x, y):
    return (x[0] + y[0], x[1] + y[1])


def minus(x, y):
    return (x[0] - y[0], x[1] - y[1])


def dft4(x):
    s0, s1 = plus(x[0], x[2]), minus(x[0], x[2])
    s2, s3 = plus(x[1], x[3]), times_i(minus(x[1], x[3]))
    return [plus(s0, s2), plus(s1, s3), minus(s0, s2), minus(s1, s3)]


def turn(z, step):
    step %= 16
    if step == 0:
        return z
    if step == 4:
        return times_i(z)
    if step == 8:
        return (-z[0], -z[1])
    half = float(np.sqrt(0.5))
    if step == 2:
        return ((z[0] - z[1]) * half, (z[0] + z[1]) * half)
    if step == 6:
        return ((z[0] + z[1]) * -half, (z[0] - z[1]) * half)
    cos, sin = float(np.cos(np.pi * step / 8)), float(np.sin(np.pi * step / 8))
    return (z[0] * cos - z[1] * sin, z[0] * sin + z[1] * cos)


def dft16(x):
    columns = [dft4([x[4 * u1 + u0] for u1 in range(4)]) for u0 in range(4)]
    out = [None] * 16
    for a0 in range(4):
        ys = dft4([turn(columns[u0][a0], u0 * a0) for u0 in range(4)])
        for a1 in range(4):
            out[a0 + 4 * a1] = ys[a1]
    return out


def dot3(left, right):
    (lh, ll), (rh, rl) = left, right
    d = functools.partial(jnp.dot, preferred_element_type=F32)
    return d(lh, rh) + (d(lh, rl) + d(ll, rh))


def products(tmpl, strain_ref, where):
    per_piece = COARSE // strain_ref.shape[0]
    for u in range(COARSE):
        off = u % per_piece
        there = slice(off * LANES, (off + 1) * LANES)
        hr, hi = tmpl(0, u), tmpl(1, u)
        sr = strain_ref[(u // per_piece,) + where + (0, slice(None), there)]
        si = strain_ref[(u // per_piece,) + where + (1, slice(None), there)]
        yield u, hr * sr + hi * si, hr * si - hi * sr


def tile(u):
    return slice(u * LANES, (u + 1) * LANES)


def first_kernel(
    freq, tmpl_ref, strain_ref, wh_ref, wl_ref, stage_ref, tw_ref, *refs
):
    out_ref, gh, gl = refs[-3:]
    tmpls, _, rows, _ = tmpl_ref.shape
    for t in range(tmpls):
        got = products(lambda p, u: tmpl_ref[t, p, :, tile(u)], strain_ref, (0,))
        y = dft16([(re, im) for _, re, im in got])
        for a in range(COARSE):
            cos, sin = stage_ref[a : a + 1, :], stage_ref[COARSE + a : COARSE + a + 1, :]
            yr, yi = y[a]
            at = pl.ds((a * tmpls + t) * rows, rows)
            gh[at, :LANES], gl[at, :LANES] = split(yr * cos - yi * sin)
            gh[at, LANES:], gl[at, LANES:] = split(yr * sin + yi * cos)
    z = dot3((gh[...], gl[...]), (wh_ref[...], wl_ref[...]))
    width = LANES // freq
    slot = lax.broadcasted_iota(jnp.int32, (rows, LANES), 1) // width
    for t in range(tmpls):
        for group in range(COARSE // freq):
            turned = []
            for i in range(freq):
                a = group * freq + i
                at = slice((a * tmpls + t) * rows, (a * tmpls + t + 1) * rows)
                zr, zi = z[at, :LANES], z[at, LANES:]
                cos, sin = tw_ref[0, :, tile(a)], tw_ref[1, :, tile(a)]
                pair = (zr * cos - zi * sin, zr * sin + zi * cos)
                if i:
                    pair = tuple(pltpu.roll(v, i * width, 1) for v in pair)
                turned.append(pair)
            for q in range(freq):
                for p in range(2):
                    value = turned[(0 - q) % freq][p]
                    for s in range(1, freq):
                        value = jnp.where(slot == s, turned[(s - q) % freq][p], value)
                    out_ref[q, 0, t, p, group] = value


ROWS = 16


def first_section(freq, half, templates, strain, first, stage, twist, after):
    tmpls = templates.shape[0]
    pieces, dets, _, cols, piece_len = strain.shape
    groups = COARSE // freq
    steps = cols // ROWS
    table = pl.BlockSpec((2 * LANES, 2 * LANES), lambda c, d: (0, 0))
    return pl.pallas_call(
        functools.partial(first_kernel, freq),
        grid=(steps, dets),
        in_specs=[
            pl.BlockSpec((tmpls, 2, ROWS, N1), lambda c, d: (0, 0, half * steps + c, 0)),
            pl.BlockSpec((pieces, 1, 2, ROWS, piece_len), lambda c, d: (0, d, 0, c, 0)),
            table,
            table,
            pl.BlockSpec((2 * COARSE, LANES), lambda c, d: (0, 0)),
            pl.BlockSpec((2, ROWS, N1), lambda c, d: (0, half * steps + c, 0)),
        ]
        + [ANY] * len(after),
        out_specs=pl.BlockSpec(
            (freq, 1, tmpls, 2, groups, ROWS, LANES), lambda c, d: (0, d, 0, 0, 0, c, 0)
        ),
        out_shape=jax.ShapeDtypeStruct((freq, dets, tmpls, 2, groups, cols, LANES), F32),
        scratch_shapes=[pltpu.VMEM((COARSE * tmpls * ROWS, 2 * LANES), BF16)] * 2,
        compiler_params=pltpu.CompilerParams(vmem_limit_bytes=VMEM_LIMIT),
        cost_estimate=pl.CostEstimate(
            flops=60 * dets * tmpls * cols * N1 * LANES,
            bytes_accessed=12 * MIB,
            transcendentals=0,
        ),
        name="first_section",
    )(templates, strain, first[0], first[1], stage, twist, *after)


def entry_kernel(which_ref, tmpl_ref, strain_ref, *refs):
    out_ref = refs[-1]
    first_half = lax.broadcasted_iota(jnp.int32, (ROWS, LANES), 1) < BLOCK
    got = products(lambda p, u: tmpl_ref[0, p, :, tile(u)], strain_ref, (0,))
    for u, re, im in got:
        out_ref[:, tile(2 * u)] = jnp.where(first_half, re, pltpu.roll(im, BLOCK, 1))
        out_ref[:, tile(2 * u + 1)] = jnp.where(first_half, pltpu.roll(re, BLOCK, 1), im)


def entry_product(which, half, templates, strain, after):
    pieces, _, _, cols, piece_len = strain.shape
    steps = cols // ROWS
    return pl.pallas_call(
        entry_kernel,
        grid_spec=pltpu.PrefetchScalarGridSpec(
            num_scalar_prefetch=1,
            grid=(steps,),
            in_specs=[
                pl.BlockSpec((1, 2, ROWS, N1), lambda c, w: (w[0], 0, half * steps + c, 0)),
                pl.BlockSpec((pieces, 1, 2, ROWS, piece_len), lambda c, w: (0, w[1], 0, c, 0)),
            ]
            + [ANY] * len(after),
            out_specs=pl.BlockSpec((ROWS, 2 * N1), lambda c, w: (c, 0)),
        ),
        out_shape=jax.ShapeDtypeStruct((cols, 2 * N1), F32),
        compiler_params=pltpu.CompilerParams(vmem_limit_bytes=VMEM_LIMIT),
        cost_estimate=pl.CostEstimate(
            flops=8 * cols * N1, bytes_accessed=2 * MIB, transcendentals=0
        ),
        name="entry_product",
    )(which, templates, strain, *after)


def second_points(x, w2h_ref, w2l_ref, use):
    for a, (yr, yi) in enumerate(dft4(x)):
        y = jnp.concatenate([yr, yi], axis=0)
        at = slice(a * 2 * LANES, (a + 1) * 2 * LANES)
        z = dot3((w2h_ref[at, :], w2l_ref[at, :]), split(y))
        use(a, z[:LANES], z[LANES:])


def second_kernel(freq, halves, place_ref, scale_ref, *refs):
    part_refs, (w2h_ref, w2l_ref), rest = refs[:halves], refs[halves : halves + 2], refs[-3:]
    out_ref, hold, order = rest
    groups, cols = part_refs[0].shape[4:6]
    per = LANES // (halves * cols)
    width = LANES // freq
    scale = scale_ref[pl.program_id(0)]

    def rows_of(p, u):
        tiles = [
            jnp.concatenate(
                [ref[u * per + f, 0, 0, p, g] for ref in part_refs for f in range(per)],
                axis=0,
            )
            for g in range(groups)
        ]
        return jnp.concatenate(tiles, axis=1)

    x = [(rows_of(0, u), rows_of(1, u)) for u in range(FOUR)]

    def keep(a, re, im):
        for p, value in enumerate((re, im)):
            for g in range(groups):
                hold[p, g, pl.ds(a, LANES, stride=FOUR), :] = value[:, tile(g)] * scale

    second_points(x, w2h_ref, w2l_ref, keep)
    for p in range(2):
        for g in range(groups):
            turned = hold[p, g].T
            for s in range(freq):
                a = g * freq + lax.rem(s - place_ref[0] + freq, freq)
                for j in range(FOUR):
                    order[p, j, pl.ds(a, width, stride=COARSE), :] = turned[
                        s * width : (s + 1) * width, tile(j)
                    ]
        for j in range(FOUR):
            out_ref[0, 0, p, :, tile(j)] = order[p, j]


def second_section(place, scale, parts, second, after):
    freq, dets, tmpls, _, groups, cols, _ = parts[0].shape
    halves = len(parts)
    times = groups * LANES
    smem = pl.BlockSpec(memory_space=pltpu.SMEM)
    table = pl.BlockSpec((FOUR * 2 * LANES, 2 * LANES), lambda t, d: (0, 0))
    part = pl.BlockSpec(
        (freq, 1, 1, 2, groups, cols, LANES), lambda t, d: (0, d, t, 0, 0, 0, 0)
    )
    return pl.pallas_call(
        functools.partial(second_kernel, freq, halves),
        grid=(tmpls, dets),
        in_specs=[smem, smem] + [part] * halves + [table, table] + [ANY] * len(after),
        out_specs=pl.BlockSpec((1, 1, 2, times, N2), lambda t, d: (t, d, 0, 0, 0)),
        out_shape=jax.ShapeDtypeStruct((tmpls, dets, 2, times, N2), F32),
        scratch_shapes=[
            pltpu.VMEM((2, groups, N2, LANES), F32),
            pltpu.VMEM((2, FOUR, times, LANES), F32),
        ],
        compiler_params=pltpu.CompilerParams(vmem_limit_bytes=VMEM_LIMIT),
        cost_estimate=pl.CostEstimate(
            flops=60 * dets * tmpls * times * FOUR * LANES * LANES,
            bytes_accessed=24 * MIB,
            transcendentals=0,
        ),
        name="second_section",
    )(place, scale, *parts, *second, *after)


def bank_kernel(block_ref, inner_ref, high_ref, low_ref):
    times = block_ref.shape[-1]
    bc, bs = block_ref[0, 0:1, :], block_ref[0, 1:2, :]
    rc, rs = inner_ref[0], inner_ref[1]
    cos, sin = bc * rc - bs * rs, bc * rs + bs * rc
    cos, sin = split(cos), split(sin)
    for ref, c, s in zip((high_ref, low_ref), cos, sin):
        ref[:BLOCK, :times] = c
        ref[:BLOCK, times:] = s
        ref[BLOCK:, :times] = -s
        ref[BLOCK:, times:] = c


def bank_table(own_time):
    times = own_time.shape[0]
    block = jnp.arange(NBLK, dtype=jnp.int32)[:, None] * own_time[None, :]
    block = jnp.stack(phase(block, NBLK), axis=1)
    inner = jnp.arange(BLOCK, dtype=jnp.int32)[:, None] * own_time[None, :]
    inner = jnp.stack(phase(inner, N1))
    return pl.pallas_call(
        bank_kernel,
        grid=(NBLK,),
        in_specs=[
            pl.BlockSpec((1, 2, times), lambda b: (b, 0, 0)),
            pl.BlockSpec((2, BLOCK, times), lambda b: (0, 0, 0)),
        ],
        out_specs=[pl.BlockSpec((2 * BLOCK, 2 * times), lambda b: (b, 0))] * 2,
        out_shape=[jax.ShapeDtypeStruct((2 * N1, 2 * times), BF16)] * 2,
        compiler_params=pltpu.CompilerParams(vmem_limit_bytes=VMEM_LIMIT),
        cost_estimate=pl.CostEstimate(
            flops=8 * N1 * times, bytes_accessed=8 * MIB, transcendentals=0
        ),
        name="bank_table",
    )(block, inner)


def bins_first_kernel(pieces, place_ref, edge_ref, *refs):
    piece_refs = refs[:pieces]
    wh_ref, wl_ref, tw_ref = refs[pieces : pieces + 3]
    level_ref, total_ref, xh, xl, acc = refs[-5:]
    times = total_ref.shape[-1]
    cols = piece_refs[0].shape[0]
    level = pl.program_id(0)

    @pl.when(level == 0)
    def _():
        for k, ref in enumerate(piece_refs):
            row = pl.multiple_of((place_ref[0] ^ k) * cols, cols)

            def cut(i, carry):
                at = pl.ds(pl.multiple_of(i * FOUR * LANES, FOUR * LANES), FOUR * LANES)
                xh[pl.ds(row, cols), at], xl[pl.ds(row, cols), at] = split(ref[:, at])
                return carry

            lax.fori_loop(0, 2 * N1 // (FOUR * LANES), cut, 0)
        total_ref[...] = jnp.zeros_like(total_ref)

    def add(block, blocks):
        at = pl.ds(pl.multiple_of(block * LANES, LANES), blocks * LANES)
        acc[...] += dot3((xh[:, at], xl[:, at]), (wh_ref[at, :], wl_ref[at, :]))

    start, end = edge_ref[level], edge_ref[level + 1]
    acc[...] = jnp.zeros_like(acc)

    def two(i, carry):
        add(start + 2 * i, 2)
        return carry

    lax.fori_loop(0, (end - start) // 2, two, 0)

    @pl.when((end - start) % 2 == 1)
    def _():
        add(end - 1, 1)

    for u in range(pieces * cols // LANES):
        at = tile(u)
        re, im = acc[at, :times], acc[at, times:]
        cos, sin = tw_ref[0, at, :], tw_ref[1, at, :]
        vr, vi = re * cos - im * sin, re * sin + im * cos
        level_ref[0, 0, at, :] = vr
        level_ref[0, 1, at, :] = vi
        total_ref[0, at, :] += vr
        total_ref[1, at, :] += vi


def bins_first(place, edges, pieces, table, twist, after):
    cols = pieces[0].shape[0]
    rows, times = twist.shape[1:]
    smem = pl.BlockSpec(memory_space=pltpu.SMEM)
    fixed = lambda shape: pl.BlockSpec(shape, lambda i: (0,) * len(shape))
    return pl.pallas_call(
        functools.partial(bins_first_kernel, len(pieces)),
        grid=(BINS,),
        in_specs=[smem, smem]
        + [fixed((cols, 2 * N1))] * len(pieces)
        + [fixed((2 * N1, 2 * times))] * 2
        + [fixed((2, rows, times))]
        + [ANY] * len(after),
        out_specs=[
            pl.BlockSpec((1, 2, rows, times), lambda i: (i, 0, 0, 0)),
            fixed((2, rows, times)),
        ],
        out_shape=[
            jax.ShapeDtypeStruct((BINS, 2, rows, times), F32),
            jax.ShapeDtypeStruct((2, rows, times), F32),
        ],
        scratch_shapes=[
            pltpu.VMEM((rows, 2 * N1), BF16),
            pltpu.VMEM((rows, 2 * N1), BF16),
            pltpu.VMEM((rows, 2 * times), F32),
        ],
        compiler_params=pltpu.CompilerParams(vmem_limit_bytes=VMEM_LIMIT),
        cost_estimate=pl.CostEstimate(
            flops=600 * rows * LANES * times * BINS,
            bytes_accessed=20 * MIB,
            transcendentals=0,
        ),
        name="bins_first",
    )(place, edges, *pieces, *table, twist, *after)


def bins_second_kernel(halves, gain_ref, share_ref, *refs):
    level_refs, total_refs = refs[:halves], refs[halves : 2 * halves]
    w2h_ref, w2l_ref, out_ref, chi, hold = refs[2 * halves :]
    times = out_ref.shape[0]
    part_rows = LANES // halves
    level = pl.program_id(0)
    gain, share = gain_ref[level], share_ref[level]

    @pl.when(level == 0)
    def _():
        chi[...] = jnp.zeros_like(chi)

    def rows_of(p, u):
        at = slice(u * part_rows, (u + 1) * part_rows)
        return jnp.concatenate(
            [
                one[0, p, at, :] * gain - whole[p, at, :] * share
                for one, whole in zip(level_refs, total_refs)
            ],
            axis=0,
        )

    def keep(a, re, im):
        chi[a] += re * re + im * im

    x = [(rows_of(0, u), rows_of(1, u)) for u in range(FOUR)]
    second_points(x, w2h_ref, w2l_ref, keep)

    @pl.when(level == BINS - 1)
    def _():
        for g in range(times // LANES):
            for a in range(FOUR):
                hold[pl.ds(a, LANES, stride=FOUR), :] = chi[a, :, tile(g)]
            out_ref[tile(g), :] = hold[...].T


def bins_second(gain, share, levels, totals, second):
    _, _, rows, times = levels[0].shape
    halves = len(levels)
    smem = pl.BlockSpec(memory_space=pltpu.SMEM)
    fixed = lambda shape: pl.BlockSpec(shape, lambda i: (0,) * len(shape))
    return pl.pallas_call(
        functools.partial(bins_second_kernel, halves),
        grid=(BINS,),
        in_specs=[smem, smem]
        + [pl.BlockSpec((1, 2, rows, times), lambda i: (i, 0, 0, 0))] * halves
        + [fixed((2, rows, times))] * halves
        + [fixed((FOUR * 2 * LANES, 2 * LANES))] * 2,
        out_specs=fixed((times, N2)),
        out_shape=jax.ShapeDtypeStruct((times, N2), F32),
        scratch_shapes=[
            pltpu.VMEM((FOUR, LANES, times), F32),
            pltpu.VMEM((N2, LANES), F32),
        ],
        compiler_params=pltpu.CompilerParams(vmem_limit_bytes=VMEM_LIMIT),
        cost_estimate=pl.CostEstimate(
            flops=60 * BINS * FOUR * LANES**2 * times,
            bytes_accessed=20 * MIB,
            transcendentals=0,
        ),
        name="bins_second",
    )(gain, share, *levels, *totals, *second)


def spread_pieces(own, freq):
    def swap(x, k):
        return lax.ppermute(x, "freq", [(i, i ^ k) for i in range(freq)])

    pieces = [own] + [None] * (freq - 1)
    for k in range(2, freq, 2):
        pieces[k] = swap(own, k)
    for k in range(1, freq, 2):
        pieces[k] = swap(pieces[k - 1], 1)
    return pieces


HALVES = 2


def per_device(strain, templates, coinc_tmpl, coinc_det, bin_edges):
    freq = lax.axis_size("freq")
    place = lax.axis_index("freq").astype(jnp.int32)
    tmpls, _, cols, _ = templates.shape
    slots = coinc_tmpl.shape[0]
    times = N1 // freq
    part = cols // HALVES

    strains = [
        lax.all_gather(strain[:, :, h * part : (h + 1) * part], "bank", axis=0, tiled=False)
        for h in range(HALVES)
    ]
    first = tuple(jnp.asarray(t) for t in first_table())
    second = tuple(jnp.asarray(t) for t in second_table(cols, HALVES))
    stage = jnp.asarray(stage_table())

    power = (templates[:, 0] ** 2 + templates[:, 1] ** 2).sum(axis=1)
    local_power = power.reshape(tmpls, NBLK, BLOCK).sum(axis=2)
    block_power = lax.psum(local_power, "freq")
    sigma_sq = block_power.sum(axis=1)
    inv_sigma = lax.rsqrt(sigma_sq)
    bin_of = jnp.sum(
        jnp.arange(NBLK, dtype=jnp.int32)[None, :, None] >= bin_edges[:, None, :], axis=2
    )
    inside = bin_of[:, None, :] == jnp.arange(BINS, dtype=jnp.int32)[None, :, None]
    weights = jnp.where(inside, block_power[:, None, :], 0.0).sum(axis=2) / sigma_sq[:, None]

    column = place * cols + jnp.arange(cols, dtype=jnp.int32)
    lane = jnp.arange(N1, dtype=jnp.int32)
    time_of_lane = lane // LANES + COARSE * (lane % LANES)
    twist = jnp.stack(phase(column[:, None] * time_of_lane[None, :], N1 * N2))
    own_time = place * times + jnp.arange(times, dtype=jnp.int32)
    table = bank_table(own_time)
    own_twist = []
    for h in range(HALVES):
        rows = jnp.arange(freq * part, dtype=jnp.int32)
        rows = rows // part * cols + h * part + rows % part
        own_twist.append(jnp.stack(phase(rows[:, None] * own_time[None, :], N1 * N2)))

    which = [jnp.stack([coinc_tmpl[j], coinc_det[j]]) for j in range(slots)]
    which, inv_sigma, weights, twist, table, own_twist = lax.optimization_barrier(
        (which, inv_sigma, weights, twist, table, own_twist)
    )
    here = place.reshape(1)
    pieces, sent, parts = [], [], []
    for h in range(HALVES):
        after = [x for entry in pieces for x in entry[2::2]] + sent
        half = [entry_product(w, h, templates, strains[h], after) for w in which]
        pieces = [spread_pieces(x, freq) for x in half]
        if h == 0:
            early = pieces
        sent = [first_section(freq, h, templates, strains[h], first, stage, twist, half)]
        got = lax.all_to_all(
            sent[0].reshape(freq, -1, LANES), "freq", split_axis=0, concat_axis=0, tiled=True
        )
        parts.append(got.reshape(sent[0].shape))

    chi = []
    for j in range(slots):
        t = coinc_tmpl[j]
        ends = jnp.zeros((1,), jnp.int32), jnp.full((1,), NBLK, jnp.int32)
        edges = jnp.concatenate([ends[0], bin_edges[t], ends[1]])
        halves = [
            bins_first(here, edges, entry[j], table, own_twist[h], sent)
            for h, entry in enumerate((early, pieces))
        ]
        levels, totals = zip(*halves)
        gain = inv_sigma[t] * lax.rsqrt(weights[t])
        chi.append(bins_second(gain, gain * weights[t], levels, totals, second))
    snr = second_section(here, inv_sigma, parts, second, chi)
    return (snr, jnp.stack(chi))


def solution(mesh):
    placed = (
        P(None, None, "freq", "bank"),
        P("bank", None, "freq", None),
        P("bank"),
        P("bank"),
        P("bank", None),
    )
    return jax.shard_map(
        per_device,
        mesh=mesh,
        in_specs=placed,
        out_specs=(P("bank", None, None, "freq", None), P("bank", "freq", None)),
        check_vma=False,
    )
```

```python
import functools

import jax
import jax.numpy as jnp
import ml_dtypes
import numpy as np
from jax import lax
from jax.experimental import pallas as pl
from jax.experimental.pallas import tpu as pltpu
from jax.sharding import PartitionSpec as P

N1 = 2048
N2 = 512
NBLK = 32
BLOCK = N1 // NBLK
BINS = 16
LANES = 128
COARSE = N1 // LANES
FOUR = N2 // LANES
F32 = jnp.float32
BF16 = jnp.bfloat16
MIB = 1 << 20
VMEM_LIMIT = 56 * MIB
ANY = pl.BlockSpec(memory_space=pl.ANY)
COST = pl.CostEstimate(flops=MIB, bytes_accessed=MIB, transcendentals=0)


def split_table(table):
    high = table.astype(ml_dtypes.bfloat16)
    low = (table - high.astype(np.float64)).astype(ml_dtypes.bfloat16)
    return high, low


def first_table():
    angle = 2 * np.pi * (np.outer(np.arange(LANES), np.arange(LANES)) % LANES) / LANES
    cos, sin = np.cos(angle), np.sin(angle)
    return split_table(np.block([[cos, sin], [-sin, cos]]))


def stage_table():
    angle = 2 * np.pi * np.outer(np.arange(COARSE), np.arange(LANES)) / N1
    return np.concatenate([np.cos(angle), np.sin(angle)]).astype(np.float32)


def second_table(cols, halves):
    order = np.arange(LANES).reshape(LANES // cols, halves, cols // halves)
    order = order.transpose(1, 0, 2).reshape(-1)
    blocks = []
    for a in range(FOUR):
        n2 = a + FOUR * np.arange(LANES)
        angle = 2 * np.pi * (np.outer(n2, order) % N2) / N2
        cos, sin = np.cos(angle), np.sin(angle)
        blocks.append(np.block([[cos, -sin], [sin, cos]]))
    return split_table(np.concatenate(blocks))


def split(x):
    high = x.astype(BF16)
    return high, (x - high.astype(F32)).astype(BF16)


def phase(index, length):
    angle = (index % length).astype(F32) * (2.0 * np.pi / length)
    return jnp.cos(angle), jnp.sin(angle)


def times_i(z):
    return (-z[1], z[0])


def plus(x, y):
    return (x[0] + y[0], x[1] + y[1])


def minus(x, y):
    return (x[0] - y[0], x[1] - y[1])


def dft4(x):
    s0, s1 = plus(x[0], x[2]), minus(x[0], x[2])
    s2, s3 = plus(x[1], x[3]), times_i(minus(x[1], x[3]))
    return [plus(s0, s2), plus(s1, s3), minus(s0, s2), minus(s1, s3)]


def turn(z, step):
    step %= 16
    if step == 0:
        return z
    if step == 4:
        return times_i(z)
    if step == 8:
        return (-z[0], -z[1])
    half = float(np.sqrt(0.5))
    if step == 2:
        return ((z[0] - z[1]) * half, (z[0] + z[1]) * half)
    if step == 6:
        return ((z[0] + z[1]) * -half, (z[0] - z[1]) * half)
    cos, sin = float(np.cos(np.pi * step / 8)), float(np.sin(np.pi * step / 8))
    return (z[0] * cos - z[1] * sin, z[0] * sin + z[1] * cos)


def dft16(x):
    columns = [dft4([x[4 * u1 + u0] for u1 in range(4)]) for u0 in range(4)]
    out = [None] * 16
    for a0 in range(4):
        ys = dft4([turn(columns[u0][a0], u0 * a0) for u0 in range(4)])
        for a1 in range(4):
            out[a0 + 4 * a1] = ys[a1]
    return out


def dot3(left, right):
    (lh, ll), (rh, rl) = left, right
    d = functools.partial(jnp.dot, preferred_element_type=F32)
    return d(lh, rh) + (d(lh, rl) + d(ll, rh))


def products(tmpl, strain_ref, where):
    per_piece = COARSE // strain_ref.shape[0]
    for u in range(COARSE):
        off = u % per_piece
        there = slice(off * LANES, (off + 1) * LANES)
        hr, hi = tmpl(0, u), tmpl(1, u)
        sr = strain_ref[(u // per_piece,) + where + (0, slice(None), there)]
        si = strain_ref[(u // per_piece,) + where + (1, slice(None), there)]
        yield u, hr * sr + hi * si, hr * si - hi * sr


def tile(u):
    return slice(u * LANES, (u + 1) * LANES)


def first_kernel(
    freq, info_ref, tmpl_ref, strain_ref, wh_ref, wl_ref, stage_ref, tw_ref, *refs
):
    out_ref, gh, gl = refs[-3:]
    rows = tmpl_ref.shape[2]
    got = products(lambda p, u: tmpl_ref[0, p, :, tile(u)], strain_ref, (0,))
    y = dft16([(re, im) for _, re, im in got])
    for a in range(COARSE):
        cos, sin = stage_ref[a : a + 1, :], stage_ref[COARSE + a : COARSE + a + 1, :]
        yr, yi = y[a]
        at = pl.ds(a * rows, rows)
        gh[at, :LANES], gl[at, :LANES] = split(yr * cos - yi * sin)
        gh[at, LANES:], gl[at, LANES:] = split(yr * sin + yi * cos)
    z = dot3((gh[...], gl[...]), (wh_ref[...], wl_ref[...]))
    width = LANES // freq
    slot = lax.broadcasted_iota(jnp.int32, (rows, LANES), 1) // width
    for group in range(COARSE // freq):
        turned = []
        for i in range(freq):
            a = group * freq + i
            at = slice(a * rows, (a + 1) * rows)
            zr, zi = z[at, :LANES], z[at, LANES:]
            cos, sin = tw_ref[0, :, tile(a)], tw_ref[1, :, tile(a)]
            pair = (zr * cos - zi * sin, zr * sin + zi * cos)
            if i:
                pair = tuple(pltpu.roll(v, i * width, 1) for v in pair)
            turned.append(pair)
        for q in range(freq):
            for p in range(2):
                value = turned[(0 - q) % freq][p]
                for s in range(1, freq):
                    value = jnp.where(slot == s, turned[(s - q) % freq][p], value)
                out_ref[q, 0, p, group] = value


ROWS = 16


def first_section(freq, half, info, templates, strain, first, stage, twist, after):
    tmpls = templates.shape[0]
    pieces, dets, _, cols, piece_len = strain.shape
    series = tmpls * dets - 1
    groups = COARSE // freq
    steps = cols // ROWS
    table = pl.BlockSpec((2 * LANES, 2 * LANES), lambda c, i, n: (0, 0))
    out = (freq, series, 2, groups, cols, LANES)
    return pl.pallas_call(
        functools.partial(first_kernel, freq),
        grid_spec=pltpu.PrefetchScalarGridSpec(
            num_scalar_prefetch=1,
            grid=(steps, series),
            in_specs=[
                pl.BlockSpec(
                    (1, 2, ROWS, N1), lambda c, i, n: (n[1 + 2 * i], 0, half * steps + c, 0)
                ),
                pl.BlockSpec(
                    (pieces, 1, 2, ROWS, piece_len), lambda c, i, n: (0, n[2 + 2 * i], 0, c, 0)
                ),
                table,
                table,
                pl.BlockSpec((2 * COARSE, LANES), lambda c, i, n: (0, 0)),
                pl.BlockSpec((2, ROWS, N1), lambda c, i, n: (0, half * steps + c, 0)),
            ]
            + [ANY] * len(after),
            out_specs=pl.BlockSpec(
                (freq, 1, 2, groups, ROWS, LANES), lambda c, i, n: (0, i, 0, 0, c, 0)
            ),
            scratch_shapes=[
                pltpu.VMEM((COARSE * ROWS, 2 * LANES), BF16),
                pltpu.VMEM((COARSE * ROWS, 2 * LANES), BF16),
            ],
        ),
        out_shape=jax.ShapeDtypeStruct(out, F32),
        compiler_params=pltpu.CompilerParams(vmem_limit_bytes=VMEM_LIMIT),
        cost_estimate=COST,
        name="first_section",
    )(info, templates, strain, first[0], first[1], stage, twist, *after)


def entry_kernel(which_ref, tmpl_ref, strain_ref, *refs):
    out_ref = refs[-1]
    first_half = lax.broadcasted_iota(jnp.int32, (ROWS, LANES), 1) < BLOCK
    got = products(lambda p, u: tmpl_ref[0, p, :, tile(u)], strain_ref, (0,))
    for u, re, im in got:
        out_ref[:, tile(2 * u)] = jnp.where(first_half, re, pltpu.roll(im, BLOCK, 1))
        out_ref[:, tile(2 * u + 1)] = jnp.where(first_half, pltpu.roll(re, BLOCK, 1), im)


def entry_product(which, half, templates, strain, after):
    pieces, _, _, cols, piece_len = strain.shape
    steps = cols // ROWS
    return pl.pallas_call(
        entry_kernel,
        grid_spec=pltpu.PrefetchScalarGridSpec(
            num_scalar_prefetch=1,
            grid=(steps,),
            in_specs=[
                pl.BlockSpec((1, 2, ROWS, N1), lambda c, w: (w[0], 0, half * steps + c, 0)),
                pl.BlockSpec((pieces, 1, 2, ROWS, piece_len), lambda c, w: (0, w[1], 0, c, 0)),
            ]
            + [ANY] * len(after),
            out_specs=pl.BlockSpec((ROWS, 2 * N1), lambda c, w: (c, 0)),
        ),
        out_shape=jax.ShapeDtypeStruct((cols, 2 * N1), F32),
        compiler_params=pltpu.CompilerParams(vmem_limit_bytes=VMEM_LIMIT),
        cost_estimate=COST,
        name="entry_product",
    )(which, templates, strain, *after)


def second_points(x, w2h_ref, w2l_ref, use):
    for a, (yr, yi) in enumerate(dft4(x)):
        y = jnp.concatenate([yr, yi], axis=0)
        at = slice(a * 2 * LANES, (a + 1) * 2 * LANES)
        z = dot3((w2h_ref[at, :], w2l_ref[at, :]), split(y))
        use(a, z[:LANES], z[LANES:])


def second_kernel(freq, halves, info_ref, scale_ref, *refs):
    part_refs, (w2h_ref, w2l_ref) = refs[:halves], refs[halves : halves + 2]
    out_ref, hold, order = refs[-3:]
    place = info_ref[0]
    groups, cols = part_refs[0].shape[3:5]
    per = LANES // (halves * cols)
    width = LANES // freq
    scale = scale_ref[info_ref[1 + 2 * pl.program_id(0)]]

    def rows_of(p, u):
        tiles = [
            jnp.concatenate(
                [ref[u * per + f, 0, p, g] for ref in part_refs for f in range(per)],
                axis=0,
            )
            for g in range(groups)
        ]
        return jnp.concatenate(tiles, axis=1)

    x = [(rows_of(0, u), rows_of(1, u)) for u in range(FOUR)]

    def keep(a, re, im):
        for p, value in enumerate((re, im)):
            for g in range(groups):
                hold[p, g, pl.ds(a, LANES, stride=FOUR), :] = value[:, tile(g)] * scale

    second_points(x, w2h_ref, w2l_ref, keep)
    for p in range(2):
        for g in range(groups):
            turned = hold[p, g].T
            for s in range(freq):
                a = g * freq + lax.rem(s - place + freq, freq)
                for j in range(FOUR):
                    order[p, j, pl.ds(a, width, stride=COARSE), :] = turned[
                        s * width : (s + 1) * width, tile(j)
                    ]
        for j in range(FOUR):
            out_ref[0, 0, p, :, tile(j)] = order[p, j]


def second_section(freq, info, scale, parts, second, snr, after):
    _, series, _, groups, cols, _ = parts[0].shape
    halves = len(parts)
    times = groups * LANES
    smem = pl.BlockSpec(memory_space=pltpu.SMEM)
    table = pl.BlockSpec((FOUR * 2 * LANES, 2 * LANES), lambda i, n: (0, 0))
    part = pl.BlockSpec(
        (freq, 1, 2, groups, cols, LANES), lambda i, n: (0, i, 0, 0, 0, 0)
    )
    return pl.pallas_call(
        functools.partial(second_kernel, freq, halves),
        grid_spec=pltpu.PrefetchScalarGridSpec(
            num_scalar_prefetch=1,
            grid=(series,),
            in_specs=[smem] + [part] * halves + [table, table, ANY] + [ANY] * len(after),
            out_specs=pl.BlockSpec(
                (1, 1, 2, times, N2), lambda i, n: (n[1 + 2 * i], n[2 + 2 * i], 0, 0, 0)
            ),
            scratch_shapes=[
                pltpu.VMEM((2, groups, N2, LANES), F32),
                pltpu.VMEM((2, FOUR, times, LANES), F32),
            ],
        ),
        out_shape=jax.ShapeDtypeStruct(snr.shape, F32),
        input_output_aliases={4 + halves: 0},
        compiler_params=pltpu.CompilerParams(vmem_limit_bytes=VMEM_LIMIT),
        cost_estimate=COST,
        name="second_section",
    )(info, scale, *parts, *second, snr, *after)


def sum_kernel(halves, which_ref, scale_ref, *refs):
    total_refs, (w2h_ref, w2l_ref, out_ref, hold) = refs[:halves], refs[halves:]
    times = out_ref.shape[3]
    part_rows = LANES // halves
    scale = scale_ref[which_ref[0]]

    def rows_of(p, u):
        at = slice(u * part_rows, (u + 1) * part_rows)
        return jnp.concatenate([ref[p, at, :] for ref in total_refs], axis=0)

    def keep(a, re, im):
        for p, value in enumerate((re, im)):
            for g in range(times // LANES):
                hold[p, g, pl.ds(a, LANES, stride=FOUR), :] = value[:, tile(g)] * scale

    x = [(rows_of(0, u), rows_of(1, u)) for u in range(FOUR)]
    second_points(x, w2h_ref, w2l_ref, keep)
    for p in range(2):
        for g in range(times // LANES):
            out_ref[0, 0, p, tile(g), :] = hold[p, g].T


def entry_series(which, scale, totals, second, tmpls, dets):
    _, rows, times = totals[0].shape
    halves = len(totals)
    smem = pl.BlockSpec(memory_space=pltpu.SMEM)
    return pl.pallas_call(
        functools.partial(sum_kernel, halves),
        grid_spec=pltpu.PrefetchScalarGridSpec(
            num_scalar_prefetch=1,
            grid=(1,),
            in_specs=[smem]
            + [pl.BlockSpec((2, rows, times), lambda i, w: (0, 0, 0))] * halves
            + [pl.BlockSpec((FOUR * 2 * LANES, 2 * LANES), lambda i, w: (0, 0))] * 2,
            out_specs=pl.BlockSpec((1, 1, 2, times, N2), lambda i, w: (w[0], w[1], 0, 0, 0)),
            scratch_shapes=[pltpu.VMEM((2, times // LANES, N2, LANES), F32)],
        ),
        out_shape=jax.ShapeDtypeStruct((tmpls, dets, 2, times, N2), F32),
        compiler_params=pltpu.CompilerParams(vmem_limit_bytes=VMEM_LIMIT),
        cost_estimate=COST,
        name="entry_series",
    )(which, scale, *totals, *second)


BLOCKS = 4


def bank_kernel(block_ref, inner_ref, high_ref, low_ref):
    times = block_ref.shape[-1]
    rc, rs = inner_ref[0], inner_ref[1]
    for b in range(BLOCKS):
        bc, bs = block_ref[b, 0:1, :], block_ref[b, 1:2, :]
        cos, sin = split(bc * rc - bs * rs), split(bc * rs + bs * rc)
        top = slice(2 * b * BLOCK, (2 * b + 1) * BLOCK)
        low = slice((2 * b + 1) * BLOCK, (2 * b + 2) * BLOCK)
        for ref, c, s in zip((high_ref, low_ref), cos, sin):
            ref[top, :times] = c
            ref[top, times:] = s
            ref[low, :times] = -s
            ref[low, times:] = c


def bank_table(own_time):
    times = own_time.shape[0]
    block = jnp.arange(NBLK, dtype=jnp.int32)[:, None] * own_time[None, :]
    block = jnp.stack(phase(block, NBLK), axis=1)
    inner = jnp.arange(BLOCK, dtype=jnp.int32)[:, None] * own_time[None, :]
    inner = jnp.stack(phase(inner, N1))
    return pl.pallas_call(
        bank_kernel,
        grid=(NBLK // BLOCKS,),
        in_specs=[
            pl.BlockSpec((BLOCKS, 2, times), lambda b: (b, 0, 0)),
            pl.BlockSpec((2, BLOCK, times), lambda b: (0, 0, 0)),
        ],
        out_specs=[pl.BlockSpec((BLOCKS * 2 * BLOCK, 2 * times), lambda b: (b, 0))] * 2,
        out_shape=[jax.ShapeDtypeStruct((2 * N1, 2 * times), BF16)] * 2,
        compiler_params=pltpu.CompilerParams(vmem_limit_bytes=VMEM_LIMIT),
        cost_estimate=COST,
        name="bank_table",
    )(block, inner)


def bins_first_kernel(pieces, place_ref, edge_ref, *refs):
    piece_refs = refs[:pieces]
    wh_ref, wl_ref, tw_ref = refs[pieces : pieces + 3]
    level_ref, total_ref, xh, xl, acc = refs[-5:]
    times = total_ref.shape[-1]
    cols = piece_refs[0].shape[0]
    level = pl.program_id(0)

    @pl.when(level == 0)
    def _():
        for k, ref in enumerate(piece_refs):
            row = pl.multiple_of((place_ref[0] ^ k) * cols, cols)

            def cut(i, carry):
                at = pl.ds(pl.multiple_of(i * FOUR * LANES, FOUR * LANES), FOUR * LANES)
                xh[pl.ds(row, cols), at], xl[pl.ds(row, cols), at] = split(ref[:, at])
                return carry

            lax.fori_loop(0, 2 * N1 // (FOUR * LANES), cut, 0)
        total_ref[...] = jnp.zeros_like(total_ref)

    def add(block, blocks):
        at = pl.ds(pl.multiple_of(block * LANES, LANES), blocks * LANES)
        acc[...] += dot3((xh[:, at], xl[:, at]), (wh_ref[at, :], wl_ref[at, :]))

    start, end = edge_ref[level], edge_ref[level + 1]
    acc[...] = jnp.zeros_like(acc)

    def two(i, carry):
        add(start + 2 * i, 2)
        return carry

    lax.fori_loop(0, (end - start) // 2, two, 0)

    @pl.when((end - start) % 2 == 1)
    def _():
        add(end - 1, 1)

    for u in range(pieces * cols // LANES):
        at = tile(u)
        re, im = acc[at, :times], acc[at, times:]
        cos, sin = tw_ref[0, at, :], tw_ref[1, at, :]
        vr, vi = re * cos - im * sin, re * sin + im * cos
        level_ref[0, 0, at, :] = vr
        level_ref[0, 1, at, :] = vi
        total_ref[0, at, :] += vr
        total_ref[1, at, :] += vi


def bins_first(place, edges, pieces, table, twist, after):
    cols = pieces[0].shape[0]
    rows, times = twist.shape[1:]
    smem = pl.BlockSpec(memory_space=pltpu.SMEM)
    fixed = lambda shape: pl.BlockSpec(shape, lambda i: (0,) * len(shape))
    return pl.pallas_call(
        functools.partial(bins_first_kernel, len(pieces)),
        grid=(BINS,),
        in_specs=[smem, smem]
        + [fixed((cols, 2 * N1))] * len(pieces)
        + [fixed((2 * N1, 2 * times))] * 2
        + [fixed((2, rows, times))]
        + [ANY] * len(after),
        out_specs=[
            pl.BlockSpec((1, 2, rows, times), lambda i: (i, 0, 0, 0)),
            fixed((2, rows, times)),
        ],
        out_shape=[
            jax.ShapeDtypeStruct((BINS, 2, rows, times), F32),
            jax.ShapeDtypeStruct((2, rows, times), F32),
        ],
        scratch_shapes=[
            pltpu.VMEM((rows, 2 * N1), BF16),
            pltpu.VMEM((rows, 2 * N1), BF16),
            pltpu.VMEM((rows, 2 * times), F32),
        ],
        compiler_params=pltpu.CompilerParams(vmem_limit_bytes=VMEM_LIMIT),
        cost_estimate=COST,
        name="bins_first",
    )(place, edges, *pieces, *table, twist, *after)


def bins_second_kernel(halves, gain_ref, share_ref, *refs):
    level_refs, total_refs = refs[:halves], refs[halves : 2 * halves]
    w2h_ref, w2l_ref, out_ref, chi, hold = refs[2 * halves :]
    times = out_ref.shape[0]
    part_rows = LANES // halves
    level = pl.program_id(0)
    gain, share = gain_ref[level], share_ref[level]

    @pl.when(level == 0)
    def _():
        chi[...] = jnp.zeros_like(chi)

    def rows_of(p, u):
        at = slice(u * part_rows, (u + 1) * part_rows)
        return jnp.concatenate(
            [
                one[0, p, at, :] * gain - whole[p, at, :] * share
                for one, whole in zip(level_refs, total_refs)
            ],
            axis=0,
        )

    def keep(a, re, im):
        chi[a] += re * re + im * im

    x = [(rows_of(0, u), rows_of(1, u)) for u in range(FOUR)]
    second_points(x, w2h_ref, w2l_ref, keep)

    @pl.when(level == BINS - 1)
    def _():
        for g in range(times // LANES):
            for a in range(FOUR):
                hold[pl.ds(a, LANES, stride=FOUR), :] = chi[a, :, tile(g)]
            out_ref[tile(g), :] = hold[...].T


def bins_second(gain, share, levels, totals, second):
    _, _, rows, times = levels[0].shape
    halves = len(levels)
    smem = pl.BlockSpec(memory_space=pltpu.SMEM)
    fixed = lambda shape: pl.BlockSpec(shape, lambda i: (0,) * len(shape))
    return pl.pallas_call(
        functools.partial(bins_second_kernel, halves),
        grid=(BINS,),
        in_specs=[smem, smem]
        + [pl.BlockSpec((1, 2, rows, times), lambda i: (i, 0, 0, 0))] * halves
        + [fixed((2, rows, times))] * halves
        + [fixed((FOUR * 2 * LANES, 2 * LANES))] * 2,
        out_specs=fixed((times, N2)),
        out_shape=jax.ShapeDtypeStruct((times, N2), F32),
        scratch_shapes=[
            pltpu.VMEM((FOUR, LANES, times), F32),
            pltpu.VMEM((N2, LANES), F32),
        ],
        compiler_params=pltpu.CompilerParams(vmem_limit_bytes=VMEM_LIMIT),
        cost_estimate=COST,
        name="bins_second",
    )(gain, share, *levels, *totals, *second)


def swap(x, freq, k):
    return lax.ppermute(x, "freq", [(i, i ^ k) for i in range(freq)])


def spread_pieces(own, freq):
    pieces = [own] + [None] * (freq - 1)
    for k in range(2, freq, 2):
        pieces[k] = swap(own, freq, k)
    for k in range(1, freq, 2):
        pieces[k] = swap(pieces[k - 1], freq, 1)
    return pieces


HALVES = 2


def per_device(strain, templates, coinc_tmpl, coinc_det, bin_edges):
    freq = lax.axis_size("freq")
    place = lax.axis_index("freq").astype(jnp.int32)
    tmpls, _, cols, _ = templates.shape
    slots, dets = coinc_tmpl.shape[0], strain.shape[0]
    times = N1 // freq
    part = cols // HALVES

    strains = [
        lax.all_gather(strain[:, :, h * part : (h + 1) * part], "bank", axis=0, tiled=False)
        for h in range(HALVES)
    ]
    first = tuple(jnp.asarray(t) for t in first_table())
    second = tuple(jnp.asarray(t) for t in second_table(cols, HALVES))
    stage = jnp.asarray(stage_table())

    power = (templates[:, 0] ** 2 + templates[:, 1] ** 2).sum(axis=1)
    local_power = power.reshape(tmpls, NBLK, BLOCK).sum(axis=2)
    block_power = lax.psum(local_power, "freq")
    sigma_sq = block_power.sum(axis=1)
    inv_sigma = lax.rsqrt(sigma_sq)
    bin_of = jnp.sum(
        jnp.arange(NBLK, dtype=jnp.int32)[None, :, None] >= bin_edges[:, None, :], axis=2
    )
    inside = bin_of[:, None, :] == jnp.arange(BINS, dtype=jnp.int32)[None, :, None]
    weights = jnp.where(inside, block_power[:, None, :], 0.0).sum(axis=2) / sigma_sq[:, None]

    column = place * cols + jnp.arange(cols, dtype=jnp.int32)
    lane = jnp.arange(N1, dtype=jnp.int32)
    time_of_lane = lane // LANES + COARSE * (lane % LANES)
    twist = jnp.stack(phase(column[:, None] * time_of_lane[None, :], N1 * N2))
    own_time = place * times + jnp.arange(times, dtype=jnp.int32)
    table = bank_table(own_time)
    own_twist = []
    for h in range(HALVES):
        rows = jnp.arange(freq * part, dtype=jnp.int32)
        rows = rows // part * cols + h * part + rows % part
        own_twist.append(jnp.stack(phase(rows[:, None] * own_time[None, :], N1 * N2)))

    which = [jnp.stack([coinc_tmpl[j], coinc_det[j]]) for j in range(slots)]
    series = jnp.arange(tmpls * dets - 1, dtype=jnp.int32)
    series = series + (series >= which[0][0] * dets + which[0][1])
    info = jnp.stack([series // dets, series % dets], axis=1).reshape(-1)
    info = jnp.concatenate([place.reshape(1), info])
    which, inv_sigma, weights, table, twist, own_twist, info = lax.optimization_barrier(
        (which, inv_sigma, weights, table, twist, own_twist, info)
    )
    here = place.reshape(1)
    pieces, sent, parts, after = [], [], [], []
    for h in range(HALVES):
        half = [entry_product(w, h, templates, strains[h], after) for w in which]
        early, pieces = pieces, [spread_pieces(x, freq) for x in half]
        sent = first_section(freq, h, info, templates, strains[h], first, stage, twist, half)
        got = lax.all_to_all(
            sent.reshape(freq, -1, LANES), "freq", split_axis=0, concat_axis=0, tiled=True
        )
        parts.append(got.reshape(sent.shape))
        after = [x for entry in pieces for x in entry[2::2]] + [sent]

    chi, totals = [], []
    for j in range(slots):
        t = coinc_tmpl[j]
        ends = jnp.zeros((1,), jnp.int32), jnp.full((1,), NBLK, jnp.int32)
        edges = jnp.concatenate([ends[0], bin_edges[t], ends[1]])
        halves = [
            bins_first(here, edges, entry[j], table, own_twist[h], [sent, parts[0]])
            for h, entry in enumerate((early, pieces))
        ]
        levels, total = zip(*halves)
        totals.append(total)
        gain = inv_sigma[t] * lax.rsqrt(weights[t])
        chi.append(bins_second(gain, gain * weights[t], levels, total, second))
    snr = entry_series(which[0], inv_sigma, totals[0], second, tmpls, dets)
    snr = second_section(freq, info, inv_sigma, parts, second, snr, chi)
    return (snr, jnp.stack(chi))


def solution(mesh):
    placed = (
        P(None, None, "freq", "bank"),
        P("bank", None, "freq", None),
        P("bank"),
        P("bank"),
        P("bank", None),
    )
    return jax.shard_map(
        per_device,
        mesh=mesh,
        in_specs=placed,
        out_specs=(P("bank", None, None, "freq", None), P("bank", "freq", None)),
        check_vma=False,
    )
```

```python
import functools

import jax
import jax.numpy as jnp
import ml_dtypes
import numpy as np
from jax import lax
from jax.experimental import pallas as pl
from jax.experimental.pallas import tpu as pltpu
from jax.sharding import PartitionSpec as P

N1 = 2048
N2 = 512
NBLK = 32
BLOCK = N1 // NBLK
BINS = 16
LANES = 128
COARSE = N1 // LANES
FOUR = N2 // LANES
F32 = jnp.float32
BF16 = jnp.bfloat16
MIB = 1 << 20
VMEM_LIMIT = 56 * MIB
ANY = pl.BlockSpec(memory_space=pl.ANY)
COST = pl.CostEstimate(flops=MIB, bytes_accessed=MIB, transcendentals=0)


def split_table(table):
    high = table.astype(ml_dtypes.bfloat16)
    low = (table - high.astype(np.float64)).astype(ml_dtypes.bfloat16)
    return high, low


def first_table():
    angle = 2 * np.pi * (np.outer(np.arange(LANES), np.arange(LANES)) % LANES) / LANES
    cos, sin = np.cos(angle), np.sin(angle)
    return split_table(np.block([[cos, sin], [-sin, cos]]))


def stage_table():
    angle = 2 * np.pi * np.outer(np.arange(COARSE), np.arange(LANES)) / N1
    return np.concatenate([np.cos(angle), np.sin(angle)]).astype(np.float32)


def second_table(cols, halves):
    order = np.arange(LANES).reshape(LANES // cols, halves, cols // halves)
    order = order.transpose(1, 0, 2).reshape(-1)
    blocks = []
    for a in range(FOUR):
        n2 = a + FOUR * np.arange(LANES)
        angle = 2 * np.pi * (np.outer(n2, order) % N2) / N2
        cos, sin = np.cos(angle), np.sin(angle)
        blocks.append(np.block([[cos, -sin], [sin, cos]]))
    return split_table(np.concatenate(blocks))


def split(x):
    high = x.astype(BF16)
    return high, (x - high.astype(F32)).astype(BF16)


def phase(index, length):
    angle = (index % length).astype(F32) * (2.0 * np.pi / length)
    return jnp.cos(angle), jnp.sin(angle)


def times_i(z):
    return (-z[1], z[0])


def plus(x, y):
    return (x[0] + y[0], x[1] + y[1])


def minus(x, y):
    return (x[0] - y[0], x[1] - y[1])


def dft4(x):
    s0, s1 = plus(x[0], x[2]), minus(x[0], x[2])
    s2, s3 = plus(x[1], x[3]), times_i(minus(x[1], x[3]))
    return [plus(s0, s2), plus(s1, s3), minus(s0, s2), minus(s1, s3)]


def turn(z, step):
    step %= 16
    if step == 0:
        return z
    if step == 4:
        return times_i(z)
    if step == 8:
        return (-z[0], -z[1])
    half = float(np.sqrt(0.5))
    if step == 2:
        return ((z[0] - z[1]) * half, (z[0] + z[1]) * half)
    if step == 6:
        return ((z[0] + z[1]) * -half, (z[0] - z[1]) * half)
    cos, sin = float(np.cos(np.pi * step / 8)), float(np.sin(np.pi * step / 8))
    return (z[0] * cos - z[1] * sin, z[0] * sin + z[1] * cos)


def dft16(x):
    columns = [dft4([x[4 * u1 + u0] for u1 in range(4)]) for u0 in range(4)]
    out = [None] * 16
    for a0 in range(4):
        ys = dft4([turn(columns[u0][a0], u0 * a0) for u0 in range(4)])
        for a1 in range(4):
            out[a0 + 4 * a1] = ys[a1]
    return out


def dot3(left, right):
    (lh, ll), (rh, rl) = left, right
    return jnp.dot(
        jnp.concatenate([lh, lh, ll], axis=1),
        jnp.concatenate([rh, rl, rh], axis=0),
        preferred_element_type=F32,
    )


def products(tmpl, strain_ref, where, rows=slice(None)):
    per_piece = COARSE // strain_ref.shape[0]
    for u in range(COARSE):
        off = u % per_piece
        there = slice(off * LANES, (off + 1) * LANES)
        hr, hi = tmpl(0, u), tmpl(1, u)
        sr = strain_ref[(u // per_piece,) + where + (0, rows, there)]
        si = strain_ref[(u // per_piece,) + where + (1, rows, there)]
        yield u, hr * sr + hi * si, hr * si - hi * sr


def tile(u):
    return slice(u * LANES, (u + 1) * LANES)


def first_kernel(
    freq, info_ref, tmpl_ref, strain_ref, wh_ref, wl_ref, stage_ref, tw_ref, *refs
):
    out_ref, gh, gl, z = refs[-4:]
    rows = tmpl_ref.shape[2]
    for r in range(0, rows, ROWS):
        at = slice(r, r + ROWS)
        got = products(lambda p, u: tmpl_ref[0, p, at, tile(u)], strain_ref, (0,), at)
        y = dft16([(re, im) for _, re, im in got])
        for a in range(COARSE):
            cos, sin = stage_ref[a : a + 1, :], stage_ref[COARSE + a : COARSE + a + 1, :]
            yr, yi = y[a]
            to = slice(a * rows + r, a * rows + r + ROWS)
            gh[to, :LANES], gl[to, :LANES] = split(yr * cos - yi * sin)
            gh[to, LANES:], gl[to, LANES:] = split(yr * sin + yi * cos)
    z[...] = dot3((gh[...], gl[...]), (wh_ref[...], wl_ref[...]))
    width = LANES // freq
    slot = lax.broadcasted_iota(jnp.int32, (ROWS, LANES), 1) // width
    for group in range(COARSE // freq):
        for r in range(0, rows, ROWS):
            at = slice(r, r + ROWS)
            turned = []
            for i in range(freq):
                a = group * freq + i
                to = slice(a * rows + r, a * rows + r + ROWS)
                zr, zi = z[to, :LANES], z[to, LANES:]
                cos, sin = tw_ref[0, at, tile(a)], tw_ref[1, at, tile(a)]
                pair = (zr * cos - zi * sin, zr * sin + zi * cos)
                if i:
                    pair = tuple(pltpu.roll(v, i * width, 1) for v in pair)
                turned.append(pair)
            for q in range(freq):
                for p in range(2):
                    value = turned[(0 - q) % freq][p]
                    for s in range(1, freq):
                        value = jnp.where(slot == s, turned[(s - q) % freq][p], value)
                    out_ref[q, 0, p, group, at] = value


ROWS = 16


def first_section(freq, half, info, templates, strain, first, stage, twist, after):
    tmpls = templates.shape[0]
    pieces, dets, _, cols, piece_len = strain.shape
    series = tmpls * dets - 1
    groups = COARSE // freq
    rows = 2 * ROWS if cols % (2 * ROWS) == 0 else ROWS
    steps = cols // rows
    table = pl.BlockSpec((2 * LANES, 2 * LANES), lambda c, i, n: (0, 0))
    out = (freq, series, 2, groups, cols, LANES)
    return pl.pallas_call(
        functools.partial(first_kernel, freq),
        grid_spec=pltpu.PrefetchScalarGridSpec(
            num_scalar_prefetch=1,
            grid=(steps, series),
            in_specs=[
                pl.BlockSpec(
                    (1, 2, rows, N1), lambda c, i, n: (n[1 + 2 * i], 0, half * steps + c, 0)
                ),
                pl.BlockSpec(
                    (pieces, 1, 2, rows, piece_len), lambda c, i, n: (0, n[2 + 2 * i], 0, c, 0)
                ),
                table,
                table,
                pl.BlockSpec((2 * COARSE, LANES), lambda c, i, n: (0, 0)),
                pl.BlockSpec((2, rows, N1), lambda c, i, n: (0, half * steps + c, 0)),
            ]
            + [ANY] * len(after),
            out_specs=pl.BlockSpec(
                (freq, 1, 2, groups, rows, LANES), lambda c, i, n: (0, i, 0, 0, c, 0)
            ),
            scratch_shapes=[
                pltpu.VMEM((COARSE * rows, 2 * LANES), BF16),
                pltpu.VMEM((COARSE * rows, 2 * LANES), BF16),
                pltpu.VMEM((COARSE * rows, 2 * LANES), F32),
            ],
        ),
        out_shape=jax.ShapeDtypeStruct(out, F32),
        compiler_params=pltpu.CompilerParams(vmem_limit_bytes=VMEM_LIMIT),
        cost_estimate=pl.CostEstimate(
            flops=60 * series * cols * N1 * LANES, bytes_accessed=16 * MIB, transcendentals=0
        ),
        name="first_section",
    )(info, templates, strain, first[0], first[1], stage, twist, *after)


def entry_kernel(which_ref, tmpl_ref, strain_ref, *refs):
    out_ref = refs[-1]
    first_half = lax.broadcasted_iota(jnp.int32, (ROWS, LANES), 1) < BLOCK
    got = products(lambda p, u: tmpl_ref[0, p, :, tile(u)], strain_ref, (0,))
    for u, re, im in got:
        out_ref[:, tile(2 * u)] = jnp.where(first_half, re, pltpu.roll(im, BLOCK, 1))
        out_ref[:, tile(2 * u + 1)] = jnp.where(first_half, pltpu.roll(re, BLOCK, 1), im)


def entry_product(which, half, templates, strain, after):
    pieces, _, _, cols, piece_len = strain.shape
    steps = cols // ROWS
    return pl.pallas_call(
        entry_kernel,
        grid_spec=pltpu.PrefetchScalarGridSpec(
            num_scalar_prefetch=1,
            grid=(steps,),
            in_specs=[
                pl.BlockSpec((1, 2, ROWS, N1), lambda c, w: (w[0], 0, half * steps + c, 0)),
                pl.BlockSpec((pieces, 1, 2, ROWS, piece_len), lambda c, w: (0, w[1], 0, c, 0)),
            ]
            + [ANY] * len(after),
            out_specs=pl.BlockSpec((ROWS, 2 * N1), lambda c, w: (c, 0)),
        ),
        out_shape=jax.ShapeDtypeStruct((cols, 2 * N1), F32),
        compiler_params=pltpu.CompilerParams(vmem_limit_bytes=VMEM_LIMIT),
        cost_estimate=COST,
        name="entry_product",
    )(which, templates, strain, *after)


def second_points(x, w2h_ref, w2l_ref, use):
    for a, (yr, yi) in enumerate(dft4(x)):
        y = jnp.concatenate([yr, yi], axis=0)
        at = slice(a * 2 * LANES, (a + 1) * 2 * LANES)
        z = dot3((w2h_ref[at, :], w2l_ref[at, :]), split(y))
        use(a, z[:LANES], z[LANES:])


def second_kernel(freq, halves, info_ref, scale_ref, *refs):
    part_refs, (w2h_ref, w2l_ref) = refs[:halves], refs[halves : halves + 2]
    out_ref, hold, order = refs[-3:]
    place = info_ref[0]
    groups, cols = part_refs[0].shape[3:5]
    per = LANES // (halves * cols)
    width = LANES // freq
    scale = scale_ref[info_ref[1 + 2 * pl.program_id(0)]]

    def rows_of(p, u):
        tiles = [
            jnp.concatenate(
                [ref[u * per + f, 0, p, g] for ref in part_refs for f in range(per)],
                axis=0,
            )
            for g in range(groups)
        ]
        return jnp.concatenate(tiles, axis=1)

    x = [(rows_of(0, u), rows_of(1, u)) for u in range(FOUR)]

    def keep(a, re, im):
        for p, value in enumerate((re, im)):
            for g in range(groups):
                hold[p, g, pl.ds(a, LANES, stride=FOUR), :] = value[:, tile(g)] * scale

    second_points(x, w2h_ref, w2l_ref, keep)
    for p in range(2):
        for g in range(groups):
            turned = hold[p, g].T
            for s in range(freq):
                a = g * freq + lax.rem(s - place + freq, freq)
                for j in range(FOUR):
                    order[p, j, pl.ds(a, width, stride=COARSE), :] = turned[
                        s * width : (s + 1) * width, tile(j)
                    ]
        for j in range(FOUR):
            out_ref[0, 0, p, :, tile(j)] = order[p, j]


def second_section(freq, info, scale, parts, second, snr, after):
    _, series, _, groups, cols, _ = parts[0].shape
    halves = len(parts)
    times = groups * LANES
    smem = pl.BlockSpec(memory_space=pltpu.SMEM)
    table = pl.BlockSpec((FOUR * 2 * LANES, 2 * LANES), lambda i, n: (0, 0))
    part = pl.BlockSpec(
        (freq, 1, 2, groups, cols, LANES), lambda i, n: (0, i, 0, 0, 0, 0)
    )
    return pl.pallas_call(
        functools.partial(second_kernel, freq, halves),
        grid_spec=pltpu.PrefetchScalarGridSpec(
            num_scalar_prefetch=1,
            grid=(series,),
            in_specs=[smem] + [part] * halves + [table, table, ANY] + [ANY] * len(after),
            out_specs=pl.BlockSpec(
                (1, 1, 2, times, N2), lambda i, n: (n[1 + 2 * i], n[2 + 2 * i], 0, 0, 0)
            ),
            scratch_shapes=[
                pltpu.VMEM((2, groups, N2, LANES), F32),
                pltpu.VMEM((2, FOUR, times, LANES), F32),
            ],
        ),
        out_shape=jax.ShapeDtypeStruct(snr.shape, F32),
        input_output_aliases={4 + halves: 0},
        compiler_params=pltpu.CompilerParams(vmem_limit_bytes=VMEM_LIMIT),
        cost_estimate=COST,
        name="second_section",
    )(info, scale, *parts, *second, snr, *after)


BLOCKS = 4


def bank_kernel(block_ref, inner_ref, high_ref, low_ref):
    times = block_ref.shape[-1]
    rc, rs = inner_ref[0], inner_ref[1]
    for b in range(BLOCKS):
        bc, bs = block_ref[b, 0:1, :], block_ref[b, 1:2, :]
        cos, sin = split(bc * rc - bs * rs), split(bc * rs + bs * rc)
        top = slice(2 * b * BLOCK, (2 * b + 1) * BLOCK)
        low = slice((2 * b + 1) * BLOCK, (2 * b + 2) * BLOCK)
        for ref, c, s in zip((high_ref, low_ref), cos, sin):
            ref[top, :times] = c
            ref[top, times:] = s
            ref[low, :times] = -s
            ref[low, times:] = c


def bank_table(own_time):
    times = own_time.shape[0]
    block = jnp.arange(NBLK, dtype=jnp.int32)[:, None] * own_time[None, :]
    block = jnp.stack(phase(block, NBLK), axis=1)
    inner = jnp.arange(BLOCK, dtype=jnp.int32)[:, None] * own_time[None, :]
    inner = jnp.stack(phase(inner, N1))
    return pl.pallas_call(
        bank_kernel,
        grid=(NBLK // BLOCKS,),
        in_specs=[
            pl.BlockSpec((BLOCKS, 2, times), lambda b: (b, 0, 0)),
            pl.BlockSpec((2, BLOCK, times), lambda b: (0, 0, 0)),
        ],
        out_specs=[pl.BlockSpec((BLOCKS * 2 * BLOCK, 2 * times), lambda b: (b, 0))] * 2,
        out_shape=[jax.ShapeDtypeStruct((2 * N1, 2 * times), BF16)] * 2,
        compiler_params=pltpu.CompilerParams(vmem_limit_bytes=VMEM_LIMIT),
        cost_estimate=COST,
        name="bank_table",
    )(block, inner)


def bins_first_kernel(pieces, place_ref, edge_ref, *refs):
    piece_refs = refs[:pieces]
    wh_ref, wl_ref, tw_ref = refs[pieces : pieces + 3]
    level_ref, total_ref, xh, xl, acc = refs[-5:]
    times = total_ref.shape[-1]
    cols = piece_refs[0].shape[0]
    level = pl.program_id(0)

    @pl.when(level == 0)
    def _():
        for k, ref in enumerate(piece_refs):
            row = pl.multiple_of((place_ref[0] ^ k) * cols, cols)

            def cut(i, carry):
                at = pl.ds(pl.multiple_of(i * FOUR * LANES, FOUR * LANES), FOUR * LANES)
                xh[pl.ds(row, cols), at], xl[pl.ds(row, cols), at] = split(ref[:, at])
                return carry

            lax.fori_loop(0, 2 * N1 // (FOUR * LANES), cut, 0)
        total_ref[...] = jnp.zeros_like(total_ref)

    def blocks_at(block, blocks):
        at = pl.ds(pl.multiple_of(block * LANES, LANES), blocks * LANES)
        return dot3((xh[:, at], xl[:, at]), (wh_ref[at, :], wl_ref[at, :]))

    start, end = edge_ref[level], edge_ref[level + 1]
    odd = (end - start) % 2

    @pl.when(odd == 1)
    def _():
        acc[...] = blocks_at(end - 1, 1)

    @pl.when(odd == 0)
    def _():
        acc[...] = blocks_at(end - 2, 2)

    def two(i, carry):
        acc[...] += blocks_at(start + 2 * i, 2)
        return carry

    lax.fori_loop(0, (end - start - 1) // 2, two, 0)

    for u in range(pieces * cols // LANES):
        at = tile(u)
        re, im = acc[at, :times], acc[at, times:]
        cos, sin = tw_ref[0, at, :], tw_ref[1, at, :]
        vr, vi = re * cos - im * sin, re * sin + im * cos
        level_ref[0, 0, at, :] = vr
        level_ref[0, 1, at, :] = vi
        total_ref[0, at, :] += vr
        total_ref[1, at, :] += vi


def bins_first(place, edges, pieces, table, twist, after):
    cols = pieces[0].shape[0]
    rows, times = twist.shape[1:]
    smem = pl.BlockSpec(memory_space=pltpu.SMEM)
    fixed = lambda shape: pl.BlockSpec(shape, lambda i: (0,) * len(shape))
    return pl.pallas_call(
        functools.partial(bins_first_kernel, len(pieces)),
        grid=(BINS,),
        in_specs=[smem, smem]
        + [fixed((cols, 2 * N1))] * len(pieces)
        + [fixed((2 * N1, 2 * times))] * 2
        + [fixed((2, rows, times))]
        + [ANY] * len(after),
        out_specs=[
            pl.BlockSpec((1, 2, rows, times), lambda i: (i, 0, 0, 0)),
            fixed((2, rows, times)),
        ],
        out_shape=[
            jax.ShapeDtypeStruct((BINS, 2, rows, times), F32),
            jax.ShapeDtypeStruct((2, rows, times), F32),
        ],
        scratch_shapes=[
            pltpu.VMEM((rows, 2 * N1), BF16),
            pltpu.VMEM((rows, 2 * N1), BF16),
            pltpu.VMEM((rows, 2 * times), F32),
        ],
        compiler_params=pltpu.CompilerParams(vmem_limit_bytes=VMEM_LIMIT),
        cost_estimate=COST,
        name="bins_first",
    )(place, edges, *pieces, *table, twist, *after)


def bins_second_kernel(halves, which_ref, scale_ref, gain_ref, share_ref, *refs):
    level_refs, total_refs = refs[:halves], refs[halves : 2 * halves]
    w2h_ref, w2l_ref, out_ref, snr_ref, chi, hold = refs[2 * halves :]
    times = out_ref.shape[0]
    part_rows = LANES // halves
    level = pl.program_id(0)
    gain, share = gain_ref[level], share_ref[level]

    @pl.when(level == 0)
    def _():
        chi[...] = jnp.zeros_like(chi)

    def rows_of(get, u):
        at = slice(u * part_rows, (u + 1) * part_rows)
        return jnp.concatenate([get(h, at) for h in range(halves)], axis=0)

    def keep(a, re, im):
        chi[a] += re * re + im * im

    def deviation(p):
        return lambda h, at: level_refs[h][0, p, at, :] * gain - total_refs[h][p, at, :] * share

    x = [tuple(rows_of(deviation(p), u) for p in range(2)) for u in range(FOUR)]
    second_points(x, w2h_ref, w2l_ref, keep)

    @pl.when(level == BINS - 1)
    def _():
        scale = scale_ref[which_ref[0]]

        def whole(p):
            return lambda h, at: total_refs[h][p, at, :] * scale

        def put(a, re, im):
            for p, value in enumerate((re, im)):
                for g in range(times // LANES):
                    hold[p, g, pl.ds(a, LANES, stride=FOUR), :] = value[:, tile(g)]

        y = [tuple(rows_of(whole(p), u) for p in range(2)) for u in range(FOUR)]
        second_points(y, w2h_ref, w2l_ref, put)
        for g in range(times // LANES):
            for a in range(FOUR):
                hold[2, g, pl.ds(a, LANES, stride=FOUR), :] = chi[a, :, tile(g)]
            for p in range(2):
                snr_ref[0, 0, p, tile(g), :] = hold[p, g].T
            out_ref[tile(g), :] = hold[2, g].T


def bins_second(which, scale, gain, share, levels, totals, second, tmpls, dets):
    _, _, rows, times = levels[0].shape
    halves = len(levels)
    smem = pl.BlockSpec(memory_space=pltpu.SMEM)
    fixed = lambda shape: pl.BlockSpec(shape, lambda i, w: (0,) * len(shape))
    return pl.pallas_call(
        functools.partial(bins_second_kernel, halves),
        grid_spec=pltpu.PrefetchScalarGridSpec(
            num_scalar_prefetch=1,
            grid=(BINS,),
            in_specs=[smem, smem, smem]
            + [pl.BlockSpec((1, 2, rows, times), lambda i, w: (i, 0, 0, 0))] * halves
            + [fixed((2, rows, times))] * halves
            + [fixed((FOUR * 2 * LANES, 2 * LANES))] * 2,
            out_specs=[
                fixed((times, N2)),
                pl.BlockSpec((1, 1, 2, times, N2), lambda i, w: (w[0], w[1], 0, 0, 0)),
            ],
            scratch_shapes=[
                pltpu.VMEM((FOUR, LANES, times), F32),
                pltpu.VMEM((3, times // LANES, N2, LANES), F32),
            ],
        ),
        out_shape=[
            jax.ShapeDtypeStruct((times, N2), F32),
            jax.ShapeDtypeStruct((tmpls, dets, 2, times, N2), F32),
        ],
        compiler_params=pltpu.CompilerParams(vmem_limit_bytes=VMEM_LIMIT),
        cost_estimate=COST,
        name="bins_second",
    )(which, scale, gain, share, *levels, *totals, *second)


def handed_on(arrays, after):
    count = len(arrays)
    return pl.pallas_call(
        lambda *refs: None,
        in_specs=[ANY] * (count + len(after)),
        out_specs=[ANY] * count,
        out_shape=[jax.ShapeDtypeStruct(x.shape, x.dtype) for x in arrays],
        input_output_aliases={i: i for i in range(count)},
        compiler_params=pltpu.CompilerParams(vmem_limit_bytes=VMEM_LIMIT),
        cost_estimate=COST,
        name="handed_on",
    )(*arrays, *after)


def swap(x, freq, k):
    return lax.ppermute(x, "freq", [(i, i ^ k) for i in range(freq)])


def far_pieces(own, freq):
    return [own] + [swap(own, freq, k) for k in range(2, freq, 2)]


def near_pieces(far, freq):
    return [x for even in far for x in (even, swap(even, freq, 1))]


HALVES = 2


def per_device(strain, templates, coinc_tmpl, coinc_det, bin_edges):
    freq = lax.axis_size("freq")
    place = lax.axis_index("freq").astype(jnp.int32)
    tmpls, _, cols, _ = templates.shape
    slots, dets = coinc_tmpl.shape[0], strain.shape[0]
    times = N1 // freq
    part = cols // HALVES

    strains = [
        lax.all_gather(strain[:, :, h * part : (h + 1) * part], "bank", axis=0, tiled=False)
        for h in range(HALVES)
    ]
    first = tuple(jnp.asarray(t) for t in first_table())
    second = tuple(jnp.asarray(t) for t in second_table(cols, HALVES))
    stage = jnp.asarray(stage_table())

    power = (templates[:, 0] ** 2 + templates[:, 1] ** 2).sum(axis=1)
    local_power = power.reshape(tmpls, NBLK, BLOCK).sum(axis=2)
    block_power = lax.psum(local_power, "freq")
    sigma_sq = block_power.sum(axis=1)
    inv_sigma = lax.rsqrt(sigma_sq)
    bin_of = jnp.sum(
        jnp.arange(NBLK, dtype=jnp.int32)[None, :, None] >= bin_edges[:, None, :], axis=2
    )
    inside = bin_of[:, None, :] == jnp.arange(BINS, dtype=jnp.int32)[None, :, None]
    weights = jnp.where(inside, block_power[:, None, :], 0.0).sum(axis=2) / sigma_sq[:, None]

    column = place * cols + jnp.arange(cols, dtype=jnp.int32)
    lane = jnp.arange(N1, dtype=jnp.int32)
    time_of_lane = lane // LANES + COARSE * (lane % LANES)
    twist = jnp.stack(phase(column[:, None] * time_of_lane[None, :], N1 * N2))
    own_time = place * times + jnp.arange(times, dtype=jnp.int32)
    table = bank_table(own_time)
    own_twist = []
    for h in range(HALVES):
        rows = jnp.arange(freq * part, dtype=jnp.int32)
        rows = rows // part * cols + h * part + rows % part
        own_twist.append(jnp.stack(phase(rows[:, None] * own_time[None, :], N1 * N2)))

    which = [jnp.stack([coinc_tmpl[j], coinc_det[j]]) for j in range(slots)]
    series = jnp.arange(tmpls * dets - 1, dtype=jnp.int32)
    series = series + (series >= which[0][0] * dets + which[0][1])
    info = jnp.stack([series // dets, series % dets], axis=1).reshape(-1)
    info = jnp.concatenate([place.reshape(1), info])
    which, inv_sigma, weights, table, twist, own_twist, info = lax.optimization_barrier(
        (which, inv_sigma, weights, table, twist, own_twist, info)
    )
    here = place.reshape(1)
    pieces, sent, parts, after = [], [], [], []
    for h in range(HALVES):
        half = [entry_product(w, h, templates, strains[h], after) for w in which]
        far = [far_pieces(x, freq) for x in half]
        sent = first_section(freq, h, info, templates, strains[h], first, stage, twist, half)
        far = [x[:1] + list(handed_on(x[1:], [sent])) for x in far]
        early, pieces = pieces, [near_pieces(x, freq) for x in far]
        (ready,) = handed_on([sent], [x for entry in pieces for x in entry[1:]])
        got = lax.all_to_all(
            ready.reshape(freq, -1, LANES), "freq", split_axis=0, concat_axis=0, tiled=True
        )
        parts.append(got.reshape(sent.shape))
        after = [ready]

    chi, snr = [], None
    for j in range(slots):
        t = coinc_tmpl[j]
        ends = jnp.zeros((1,), jnp.int32), jnp.full((1,), NBLK, jnp.int32)
        edges = jnp.concatenate([ends[0], bin_edges[t], ends[1]])
        halves = [
            bins_first(here, edges, early[j], table, own_twist[0], [sent]),
            bins_first(here, edges, pieces[j], table, own_twist[1], [ready]),
        ]
        levels, totals = zip(*halves)
        gain = inv_sigma[t] * lax.rsqrt(weights[t])
        one, series_of = bins_second(
            which[j], inv_sigma, gain, gain * weights[t], levels, totals, second, tmpls, dets
        )
        chi.append(one)
        snr = series_of if snr is None else snr
    snr = second_section(freq, info, inv_sigma, parts, second, snr, chi)
    return (snr, jnp.stack(chi))


def solution(mesh):
    placed = (
        P(None, None, "freq", "bank"),
        P("bank", None, "freq", None),
        P("bank"),
        P("bank"),
        P("bank", None),
    )
    return jax.shard_map(
        per_device,
        mesh=mesh,
        in_specs=placed,
        out_specs=(P("bank", None, None, "freq", None), P("bank", "freq", None)),
        check_vma=False,
    )
```

```python
import functools

import jax
import jax.numpy as jnp
import ml_dtypes
import numpy as np
from jax import lax
from jax.experimental import pallas as pl
from jax.experimental.pallas import tpu as pltpu
from jax.sharding import PartitionSpec as P

N1 = 2048
N2 = 512
NBLK = 32
BLOCK = N1 // NBLK
BINS = 16
LANES = 128
COARSE = N1 // LANES
FOUR = N2 // LANES
F32 = jnp.float32
BF16 = jnp.bfloat16
MIB = 1 << 20
VMEM_LIMIT = 56 * MIB
ANY = pl.BlockSpec(memory_space=pl.ANY)
COST = pl.CostEstimate(flops=MIB, bytes_accessed=MIB, transcendentals=0)


def split_table(table):
    high = table.astype(ml_dtypes.bfloat16)
    low = (table - high.astype(np.float64)).astype(ml_dtypes.bfloat16)
    return high, low


def first_table():
    angle = 2 * np.pi * (np.outer(np.arange(LANES), np.arange(LANES)) % LANES) / LANES
    cos, sin = np.cos(angle), np.sin(angle)
    return split_table(np.block([[cos, sin], [-sin, cos]]))


def stage_table():
    angle = 2 * np.pi * np.outer(np.arange(COARSE), np.arange(LANES)) / N1
    return np.concatenate([np.cos(angle), np.sin(angle)]).astype(np.float32)


def second_table(cols, halves):
    order = np.arange(LANES).reshape(LANES // cols, halves, cols // halves)
    order = order.transpose(1, 0, 2).reshape(-1)
    blocks = []
    for a in range(FOUR):
        n2 = a + FOUR * np.arange(LANES)
        angle = 2 * np.pi * (np.outer(n2, order) % N2) / N2
        cos, sin = np.cos(angle), np.sin(angle)
        blocks.append(np.block([[cos, -sin], [sin, cos]]))
    return split_table(np.concatenate(blocks))


def split(x):
    high = x.astype(BF16)
    return high, (x - high.astype(F32)).astype(BF16)


def phase(index, length):
    angle = (index % length).astype(F32) * (2.0 * np.pi / length)
    return jnp.cos(angle), jnp.sin(angle)


def times_i(z):
    return (-z[1], z[0])


def plus(x, y):
    return (x[0] + y[0], x[1] + y[1])


def minus(x, y):
    return (x[0] - y[0], x[1] - y[1])


def dft4(x):
    s0, s1 = plus(x[0], x[2]), minus(x[0], x[2])
    s2, s3 = plus(x[1], x[3]), times_i(minus(x[1], x[3]))
    return [plus(s0, s2), plus(s1, s3), minus(s0, s2), minus(s1, s3)]


def turn(z, step):
    step %= 16
    if step == 0:
        return z
    if step == 4:
        return times_i(z)
    if step == 8:
        return (-z[0], -z[1])
    half = float(np.sqrt(0.5))
    if step == 2:
        return ((z[0] - z[1]) * half, (z[0] + z[1]) * half)
    if step == 6:
        return ((z[0] + z[1]) * -half, (z[0] - z[1]) * half)
    cos, sin = float(np.cos(np.pi * step / 8)), float(np.sin(np.pi * step / 8))
    return (z[0] * cos - z[1] * sin, z[0] * sin + z[1] * cos)


def dft16(x):
    columns = [dft4([x[4 * u1 + u0] for u1 in range(4)]) for u0 in range(4)]
    out = [None] * 16
    for a0 in range(4):
        ys = dft4([turn(columns[u0][a0], u0 * a0) for u0 in range(4)])
        for a1 in range(4):
            out[a0 + 4 * a1] = ys[a1]
    return out


def dot3(left, right):
    (lh, ll), (rh, rl) = left, right
    return jnp.dot(
        jnp.concatenate([lh, lh, ll], axis=1),
        jnp.concatenate([rh, rl, rh], axis=0),
        preferred_element_type=F32,
    )


def products(tmpl, strain_ref, where, rows=slice(None)):
    per_piece = COARSE // strain_ref.shape[0]
    for u in range(COARSE):
        off = u % per_piece
        there = slice(off * LANES, (off + 1) * LANES)
        hr, hi = tmpl(0, u), tmpl(1, u)
        sr = strain_ref[(u // per_piece,) + where + (0, rows, there)]
        si = strain_ref[(u // per_piece,) + where + (1, rows, there)]
        yield u, hr * sr + hi * si, hr * si - hi * sr


def tile(u):
    return slice(u * LANES, (u + 1) * LANES)


def first_kernel(
    freq, info_ref, tmpl_ref, strain_ref, wh_ref, wl_ref, stage_ref, tw_ref, *refs
):
    out_ref, gh, gl, z = refs[-4:]
    rows = tmpl_ref.shape[2]
    for r in range(0, rows, ROWS):
        at = slice(r, r + ROWS)
        got = products(lambda p, u: tmpl_ref[0, p, at, tile(u)], strain_ref, (0,), at)
        y = dft16([(re, im) for _, re, im in got])
        for a in range(COARSE):
            cos, sin = stage_ref[a : a + 1, :], stage_ref[COARSE + a : COARSE + a + 1, :]
            yr, yi = y[a]
            to = slice(a * rows + r, a * rows + r + ROWS)
            gh[to, :LANES], gl[to, :LANES] = split(yr * cos - yi * sin)
            gh[to, LANES:], gl[to, LANES:] = split(yr * sin + yi * cos)
    z[...] = dot3((gh[...], gl[...]), (wh_ref[...], wl_ref[...]))
    width = LANES // freq
    slot = lax.broadcasted_iota(jnp.int32, (ROWS, LANES), 1) // width
    for group in range(COARSE // freq):
        for r in range(0, rows, ROWS):
            at = slice(r, r + ROWS)
            turned = []
            for i in range(freq):
                a = group * freq + i
                to = slice(a * rows + r, a * rows + r + ROWS)
                zr, zi = z[to, :LANES], z[to, LANES:]
                cos, sin = tw_ref[0, at, tile(a)], tw_ref[1, at, tile(a)]
                pair = (zr * cos - zi * sin, zr * sin + zi * cos)
                if i:
                    pair = tuple(pltpu.roll(v, i * width, 1) for v in pair)
                turned.append(pair)
            for q in range(freq):
                for p in range(2):
                    value = turned[(0 - q) % freq][p]
                    for s in range(1, freq):
                        value = jnp.where(slot == s, turned[(s - q) % freq][p], value)
                    out_ref[q, 0, p, group, at] = value


ROWS = 16
TOGETHER = 2


def first_section(freq, half, info, templates, strain, first, stage, twist, after):
    tmpls = templates.shape[0]
    pieces, dets, _, cols, piece_len = strain.shape
    series = tmpls * dets - 1
    groups = COARSE // freq
    rows = 2 * ROWS if cols % (2 * ROWS) == 0 else ROWS
    steps = cols // rows
    table = pl.BlockSpec((2 * LANES, 2 * LANES), lambda c, i, n: (0, 0))
    out = (freq, series, 2, groups, cols, LANES)
    return pl.pallas_call(
        functools.partial(first_kernel, freq),
        grid_spec=pltpu.PrefetchScalarGridSpec(
            num_scalar_prefetch=1,
            grid=(steps, series),
            in_specs=[
                pl.BlockSpec(
                    (1, 2, rows, N1), lambda c, i, n: (n[1 + 2 * i], 0, half * steps + c, 0)
                ),
                pl.BlockSpec(
                    (pieces, 1, 2, rows, piece_len), lambda c, i, n: (0, n[2 + 2 * i], 0, c, 0)
                ),
                table,
                table,
                pl.BlockSpec((2 * COARSE, LANES), lambda c, i, n: (0, 0)),
                pl.BlockSpec((2, rows, N1), lambda c, i, n: (0, half * steps + c, 0)),
            ]
            + [ANY] * len(after),
            out_specs=pl.BlockSpec(
                (freq, 1, 2, groups, rows, LANES), lambda c, i, n: (0, i, 0, 0, c, 0)
            ),
            scratch_shapes=[
                pltpu.VMEM((COARSE * rows, 2 * LANES), BF16),
                pltpu.VMEM((COARSE * rows, 2 * LANES), BF16),
                pltpu.VMEM((COARSE * rows, 2 * LANES), F32),
            ],
        ),
        out_shape=jax.ShapeDtypeStruct(out, F32),
        compiler_params=pltpu.CompilerParams(vmem_limit_bytes=VMEM_LIMIT),
        cost_estimate=pl.CostEstimate(
            flops=60 * series * cols * N1 * LANES, bytes_accessed=16 * MIB, transcendentals=0
        ),
        name="first_section",
    )(info, templates, strain, first[0], first[1], stage, twist, *after)


def entry_kernel(which_ref, tmpl_ref, strain_ref, *refs):
    out_ref = refs[-1]
    first_half = lax.broadcasted_iota(jnp.int32, (ROWS, LANES), 1) < BLOCK
    got = products(lambda p, u: tmpl_ref[0, p, :, tile(u)], strain_ref, (0,))
    for u, re, im in got:
        out_ref[:, tile(2 * u)] = jnp.where(first_half, re, pltpu.roll(im, BLOCK, 1))
        out_ref[:, tile(2 * u + 1)] = jnp.where(first_half, pltpu.roll(re, BLOCK, 1), im)


def entry_product(which, half, templates, strain, after):
    pieces, _, _, cols, piece_len = strain.shape
    steps = cols // ROWS
    return pl.pallas_call(
        entry_kernel,
        grid_spec=pltpu.PrefetchScalarGridSpec(
            num_scalar_prefetch=1,
            grid=(steps,),
            in_specs=[
                pl.BlockSpec((1, 2, ROWS, N1), lambda c, w: (w[0], 0, half * steps + c, 0)),
                pl.BlockSpec((pieces, 1, 2, ROWS, piece_len), lambda c, w: (0, w[1], 0, c, 0)),
            ]
            + [ANY] * len(after),
            out_specs=pl.BlockSpec((ROWS, 2 * N1), lambda c, w: (c, 0)),
        ),
        out_shape=jax.ShapeDtypeStruct((cols, 2 * N1), F32),
        compiler_params=pltpu.CompilerParams(vmem_limit_bytes=VMEM_LIMIT),
        cost_estimate=COST,
        name="entry_product",
    )(which, templates, strain, *after)


def second_points(x, w2h_ref, w2l_ref, use):
    for a, (yr, yi) in enumerate(dft4(x)):
        y = jnp.concatenate([yr, yi], axis=0)
        at = slice(a * 2 * LANES, (a + 1) * 2 * LANES)
        z = dot3((w2h_ref[at, :], w2l_ref[at, :]), split(y))
        use(a, z[:LANES], z[LANES:])


def second_kernel(freq, halves, info_ref, scale_ref, *refs):
    part_refs, (w2h_ref, w2l_ref) = refs[:halves], refs[halves : halves + 2]
    out_ref, hold, order = refs[-3:]
    place = info_ref[0]
    groups, cols = part_refs[0].shape[3:5]
    per = LANES // (halves * cols)
    width = LANES // freq
    scale = scale_ref[info_ref[1 + 2 * pl.program_id(0)]]

    def rows_of(p, u):
        tiles = [
            jnp.concatenate(
                [ref[u * per + f, 0, p, g] for ref in part_refs for f in range(per)],
                axis=0,
            )
            for g in range(groups)
        ]
        return jnp.concatenate(tiles, axis=1)

    x = [(rows_of(0, u), rows_of(1, u)) for u in range(FOUR)]

    def keep(a, re, im):
        for p, value in enumerate((re, im)):
            for g in range(groups):
                hold[p, g, pl.ds(a, LANES, stride=FOUR), :] = value[:, tile(g)] * scale

    second_points(x, w2h_ref, w2l_ref, keep)
    for p in range(2):
        for g in range(groups):
            turned = hold[p, g].T
            for s in range(freq):
                a = g * freq + lax.rem(s - place + freq, freq)
                for j in range(FOUR):
                    order[p, j, pl.ds(a, width, stride=COARSE), :] = turned[
                        s * width : (s + 1) * width, tile(j)
                    ]
        for j in range(FOUR):
            out_ref[0, 0, p, :, tile(j)] = order[p, j]


def second_section(freq, info, scale, parts, second, snr, after):
    _, series, _, groups, cols, _ = parts[0].shape
    halves = len(parts)
    times = groups * LANES
    smem = pl.BlockSpec(memory_space=pltpu.SMEM)
    table = pl.BlockSpec((FOUR * 2 * LANES, 2 * LANES), lambda i, n: (0, 0))
    part = pl.BlockSpec(
        (freq, 1, 2, groups, cols, LANES), lambda i, n: (0, i, 0, 0, 0, 0)
    )
    return pl.pallas_call(
        functools.partial(second_kernel, freq, halves),
        grid_spec=pltpu.PrefetchScalarGridSpec(
            num_scalar_prefetch=1,
            grid=(series,),
            in_specs=[smem] + [part] * halves + [table, table, ANY] + [ANY] * len(after),
            out_specs=pl.BlockSpec(
                (1, 1, 2, times, N2), lambda i, n: (n[1 + 2 * i], n[2 + 2 * i], 0, 0, 0)
            ),
            scratch_shapes=[
                pltpu.VMEM((2, groups, N2, LANES), F32),
                pltpu.VMEM((2, FOUR, times, LANES), F32),
            ],
        ),
        out_shape=jax.ShapeDtypeStruct(snr.shape, F32),
        input_output_aliases={4 + halves: 0},
        compiler_params=pltpu.CompilerParams(vmem_limit_bytes=VMEM_LIMIT),
        cost_estimate=COST,
        name="second_section",
    )(info, scale, *parts, *second, snr, *after)


BLOCKS = 4


def bank_kernel(block_ref, inner_ref, high_ref, low_ref):
    times = block_ref.shape[-1]
    rc, rs = inner_ref[0], inner_ref[1]
    for b in range(BLOCKS):
        bc, bs = block_ref[b, 0:1, :], block_ref[b, 1:2, :]
        cos, sin = split(bc * rc - bs * rs), split(bc * rs + bs * rc)
        top = slice(2 * b * BLOCK, (2 * b + 1) * BLOCK)
        low = slice((2 * b + 1) * BLOCK, (2 * b + 2) * BLOCK)
        for ref, c, s in zip((high_ref, low_ref), cos, sin):
            ref[top, :times] = c
            ref[top, times:] = s
            ref[low, :times] = -s
            ref[low, times:] = c


def bank_table(own_time):
    times = own_time.shape[0]
    block = jnp.arange(NBLK, dtype=jnp.int32)[:, None] * own_time[None, :]
    block = jnp.stack(phase(block, NBLK), axis=1)
    inner = jnp.arange(BLOCK, dtype=jnp.int32)[:, None] * own_time[None, :]
    inner = jnp.stack(phase(inner, N1))
    return pl.pallas_call(
        bank_kernel,
        grid=(NBLK // BLOCKS,),
        in_specs=[
            pl.BlockSpec((BLOCKS, 2, times), lambda b: (b, 0, 0)),
            pl.BlockSpec((2, BLOCK, times), lambda b: (0, 0, 0)),
        ],
        out_specs=[pl.BlockSpec((BLOCKS * 2 * BLOCK, 2 * times), lambda b: (b, 0))] * 2,
        out_shape=[jax.ShapeDtypeStruct((2 * N1, 2 * times), BF16)] * 2,
        compiler_params=pltpu.CompilerParams(vmem_limit_bytes=VMEM_LIMIT),
        cost_estimate=COST,
        name="bank_table",
    )(block, inner)


def bins_first_kernel(pieces, place_ref, edge_ref, *refs):
    piece_refs = refs[:pieces]
    wh_ref, wl_ref, tw_ref = refs[pieces : pieces + 3]
    level_ref, total_ref, xh, xl, acc = refs[-5:]
    times = total_ref.shape[-1]
    cols = piece_refs[0].shape[0]
    step = pl.program_id(0)

    @pl.when(step == 0)
    def _():
        for k, ref in enumerate(piece_refs):
            row = pl.multiple_of((place_ref[0] ^ k) * cols, cols)

            def cut(i, carry):
                at = pl.ds(pl.multiple_of(i * FOUR * LANES, FOUR * LANES), FOUR * LANES)
                xh[pl.ds(row, cols), at], xl[pl.ds(row, cols), at] = split(ref[:, at])
                return carry

            lax.fori_loop(0, 2 * N1 // (FOUR * LANES), cut, 0)
        total_ref[...] = jnp.zeros_like(total_ref)

    def blocks_at(block, blocks):
        at = pl.ds(pl.multiple_of(block * LANES, LANES), blocks * LANES)
        return dot3((xh[:, at], xl[:, at]), (wh_ref[at, :], wl_ref[at, :]))

    for i in range(TOGETHER):
        start, end = edge_ref[step * TOGETHER + i], edge_ref[step * TOGETHER + i + 1]
        odd = (end - start) % 2

        @pl.when(odd == 1)
        def _():
            acc[i] = blocks_at(end - 1, 1)

        @pl.when(odd == 0)
        def _():
            acc[i] = blocks_at(end - 2, 2)

        def two(n, carry):
            acc[i] += blocks_at(start + 2 * n, 2)
            return carry

        lax.fori_loop(0, (end - start - 1) // 2, two, 0)

    for u in range(pieces * cols // LANES):
        at = tile(u)
        cos, sin = tw_ref[0, at, :], tw_ref[1, at, :]
        sum_r, sum_i = total_ref[0, at, :], total_ref[1, at, :]
        for i in range(TOGETHER):
            re, im = acc[i, at, :times], acc[i, at, times:]
            vr, vi = re * cos - im * sin, re * sin + im * cos
            level_ref[i, 0, at, :] = vr
            level_ref[i, 1, at, :] = vi
            sum_r, sum_i = sum_r + vr, sum_i + vi
        total_ref[0, at, :] = sum_r
        total_ref[1, at, :] = sum_i


def bins_first(place, edges, pieces, table, twist, after):
    cols = pieces[0].shape[0]
    rows, times = twist.shape[1:]
    smem = pl.BlockSpec(memory_space=pltpu.SMEM)
    fixed = lambda shape: pl.BlockSpec(shape, lambda i: (0,) * len(shape))
    return pl.pallas_call(
        functools.partial(bins_first_kernel, len(pieces)),
        grid=(BINS // TOGETHER,),
        in_specs=[smem, smem]
        + [fixed((cols, 2 * N1))] * len(pieces)
        + [fixed((2 * N1, 2 * times))] * 2
        + [fixed((2, rows, times))]
        + [ANY] * len(after),
        out_specs=[
            pl.BlockSpec((TOGETHER, 2, rows, times), lambda i: (i, 0, 0, 0)),
            fixed((2, rows, times)),
        ],
        out_shape=[
            jax.ShapeDtypeStruct((BINS, 2, rows, times), F32),
            jax.ShapeDtypeStruct((2, rows, times), F32),
        ],
        scratch_shapes=[
            pltpu.VMEM((rows, 2 * N1), BF16),
            pltpu.VMEM((rows, 2 * N1), BF16),
            pltpu.VMEM((TOGETHER, rows, 2 * times), F32),
        ],
        compiler_params=pltpu.CompilerParams(vmem_limit_bytes=VMEM_LIMIT),
        cost_estimate=COST,
        name="bins_first",
    )(place, edges, *pieces, *table, twist, *after)


def bins_second_kernel(halves, which_ref, scale_ref, gain_ref, share_ref, *refs):
    level_refs, total_refs = refs[:halves], refs[halves : 2 * halves]
    w2h_ref, w2l_ref, out_ref, snr_ref, chi, hold = refs[2 * halves :]
    times = out_ref.shape[0]
    part_rows = LANES // halves
    step = pl.program_id(0)

    @pl.when(step == 0)
    def _():
        chi[...] = jnp.zeros_like(chi)

    def rows_of(get, u):
        at = slice(u * part_rows, (u + 1) * part_rows)
        return jnp.concatenate([get(h, at) for h in range(halves)], axis=0)

    def keep(a, re, im):
        chi[a] += re * re + im * im

    for i in range(TOGETHER):
        gain, share = gain_ref[step * TOGETHER + i], share_ref[step * TOGETHER + i]

        def deviation(p):
            return lambda h, at: (
                level_refs[h][i, p, at, :] * gain - total_refs[h][p, at, :] * share
            )

        x = [tuple(rows_of(deviation(p), u) for p in range(2)) for u in range(FOUR)]
        second_points(x, w2h_ref, w2l_ref, keep)

    @pl.when(step == BINS // TOGETHER - 1)
    def _():
        scale = scale_ref[which_ref[0]]

        def whole(p):
            return lambda h, at: total_refs[h][p, at, :] * scale

        def put(a, re, im):
            for p, value in enumerate((re, im)):
                for g in range(times // LANES):
                    hold[p, g, pl.ds(a, LANES, stride=FOUR), :] = value[:, tile(g)]

        y = [tuple(rows_of(whole(p), u) for p in range(2)) for u in range(FOUR)]
        second_points(y, w2h_ref, w2l_ref, put)
        for g in range(times // LANES):
            for a in range(FOUR):
                hold[2, g, pl.ds(a, LANES, stride=FOUR), :] = chi[a, :, tile(g)]
            for p in range(2):
                snr_ref[0, 0, p, tile(g), :] = hold[p, g].T
            out_ref[tile(g), :] = hold[2, g].T


def bins_second(which, scale, gain, share, levels, totals, second, tmpls, dets):
    _, _, rows, times = levels[0].shape
    halves = len(levels)
    smem = pl.BlockSpec(memory_space=pltpu.SMEM)
    fixed = lambda shape: pl.BlockSpec(shape, lambda i, w: (0,) * len(shape))
    return pl.pallas_call(
        functools.partial(bins_second_kernel, halves),
        grid_spec=pltpu.PrefetchScalarGridSpec(
            num_scalar_prefetch=1,
            grid=(BINS // TOGETHER,),
            in_specs=[smem, smem, smem]
            + [pl.BlockSpec((TOGETHER, 2, rows, times), lambda i, w: (i, 0, 0, 0))] * halves
            + [fixed((2, rows, times))] * halves
            + [fixed((FOUR * 2 * LANES, 2 * LANES))] * 2,
            out_specs=[
                fixed((times, N2)),
                pl.BlockSpec((1, 1, 2, times, N2), lambda i, w: (w[0], w[1], 0, 0, 0)),
            ],
            scratch_shapes=[
                pltpu.VMEM((FOUR, LANES, times), F32),
                pltpu.VMEM((3, times // LANES, N2, LANES), F32),
            ],
        ),
        out_shape=[
            jax.ShapeDtypeStruct((times, N2), F32),
            jax.ShapeDtypeStruct((tmpls, dets, 2, times, N2), F32),
        ],
        compiler_params=pltpu.CompilerParams(vmem_limit_bytes=VMEM_LIMIT),
        cost_estimate=COST,
        name="bins_second",
    )(which, scale, gain, share, *levels, *totals, *second)


def handed_on(arrays, after):
    count = len(arrays)
    return pl.pallas_call(
        lambda *refs: None,
        in_specs=[ANY] * (count + len(after)),
        out_specs=[ANY] * count,
        out_shape=[jax.ShapeDtypeStruct(x.shape, x.dtype) for x in arrays],
        input_output_aliases={i: i for i in range(count)},
        compiler_params=pltpu.CompilerParams(vmem_limit_bytes=VMEM_LIMIT),
        cost_estimate=COST,
        name="handed_on",
    )(*arrays, *after)


def swap(x, freq, k):
    return lax.ppermute(x, "freq", [(i, i ^ k) for i in range(freq)])


def far_pieces(own, freq):
    return [own] + [swap(own, freq, k) for k in range(2, freq, 2)]


def near_pieces(far, freq):
    return [x for even in far for x in (even, swap(even, freq, 1))]


HALVES = 2


def per_device(strain, templates, coinc_tmpl, coinc_det, bin_edges):
    freq = lax.axis_size("freq")
    place = lax.axis_index("freq").astype(jnp.int32)
    tmpls, _, cols, _ = templates.shape
    slots, dets = coinc_tmpl.shape[0], strain.shape[0]
    times = N1 // freq
    part = cols // HALVES

    strains = [
        lax.all_gather(strain[:, :, h * part : (h + 1) * part], "bank", axis=0, tiled=False)
        for h in range(HALVES)
    ]
    first = tuple(jnp.asarray(t) for t in first_table())
    second = tuple(jnp.asarray(t) for t in second_table(cols, HALVES))
    stage = jnp.asarray(stage_table())

    power = (templates[:, 0] ** 2 + templates[:, 1] ** 2).sum(axis=1)
    local_power = power.reshape(tmpls, NBLK, BLOCK).sum(axis=2)
    block_power = lax.psum(local_power, "freq")
    sigma_sq = block_power.sum(axis=1)
    inv_sigma = lax.rsqrt(sigma_sq)
    bin_of = jnp.sum(
        jnp.arange(NBLK, dtype=jnp.int32)[None, :, None] >= bin_edges[:, None, :], axis=2
    )
    inside = bin_of[:, None, :] == jnp.arange(BINS, dtype=jnp.int32)[None, :, None]
    weights = jnp.where(inside, block_power[:, None, :], 0.0).sum(axis=2) / sigma_sq[:, None]

    column = place * cols + jnp.arange(cols, dtype=jnp.int32)
    lane = jnp.arange(N1, dtype=jnp.int32)
    time_of_lane = lane // LANES + COARSE * (lane % LANES)
    twist = jnp.stack(phase(column[:, None] * time_of_lane[None, :], N1 * N2))
    own_time = place * times + jnp.arange(times, dtype=jnp.int32)
    table = bank_table(own_time)
    own_twist = []
    for h in range(HALVES):
        rows = jnp.arange(freq * part, dtype=jnp.int32)
        rows = rows // part * cols + h * part + rows % part
        own_twist.append(jnp.stack(phase(rows[:, None] * own_time[None, :], N1 * N2)))

    which = [jnp.stack([coinc_tmpl[j], coinc_det[j]]) for j in range(slots)]
    series = jnp.arange(tmpls * dets - 1, dtype=jnp.int32)
    series = series + (series >= which[0][0] * dets + which[0][1])
    info = jnp.stack([series // dets, series % dets], axis=1).reshape(-1)
    info = jnp.concatenate([place.reshape(1), info])
    which, inv_sigma, weights, table, twist, own_twist, info = lax.optimization_barrier(
        (which, inv_sigma, weights, table, twist, own_twist, info)
    )
    here = place.reshape(1)
    ends = jnp.zeros((1,), jnp.int32), jnp.full((1,), NBLK, jnp.int32)
    edges = [
        jnp.concatenate([ends[0], bin_edges[coinc_tmpl[j]], ends[1]]) for j in range(slots)
    ]
    parts, halves, after, bins = [], [], [], []
    for h in range(HALVES):
        half = [entry_product(w, h, templates, strains[h], after) for w in which]
        far = [far_pieces(x, freq) for x in half]
        sent = first_section(freq, h, info, templates, strains[h], first, stage, twist, half)
        if bins:
            halves.append([bins_first(here, *x, table, own_twist[h - 1], [sent]) for x in bins])
        done = [sent] + [x[0] for x in halves[-1]] if halves else [sent]
        far = [x[:1] + list(handed_on(x[1:], done)) for x in far]
        bins = [(edges[j], near_pieces(x, freq)) for j, x in enumerate(far)]
        (ready,) = handed_on([sent], [x for _, entry in bins for x in entry[1:]])
        got = lax.all_to_all(
            ready.reshape(freq, -1, LANES), "freq", split_axis=0, concat_axis=0, tiled=True
        )
        parts.append(got.reshape(sent.shape))
        after = [ready]
    halves.append([bins_first(here, *x, table, own_twist[-1], after) for x in bins])

    chi, snr = [], None
    for j in range(slots):
        t = coinc_tmpl[j]
        levels, totals = zip(*[x[j] for x in halves])
        gain = inv_sigma[t] * lax.rsqrt(weights[t])
        one, series_of = bins_second(
            which[j], inv_sigma, gain, gain * weights[t], levels, totals, second, tmpls, dets
        )
        chi.append(one)
        snr = series_of if snr is None else snr
    snr = second_section(freq, info, inv_sigma, parts, second, snr, chi)
    return (snr, jnp.stack(chi))


def solution(mesh):
    placed = (
        P(None, None, "freq", "bank"),
        P("bank", None, "freq", None),
        P("bank"),
        P("bank"),
        P("bank", None),
    )
    return jax.shard_map(
        per_device,
        mesh=mesh,
        in_specs=placed,
        out_specs=(P("bank", None, None, "freq", None), P("bank", "freq", None)),
        check_vma=False,
    )
```

```python
import functools

import jax
import jax.numpy as jnp
import ml_dtypes
import numpy as np
from jax import lax
from jax.experimental import pallas as pl
from jax.experimental.pallas import tpu as pltpu
from jax.sharding import PartitionSpec as P

N1 = 2048
N2 = 512
NBLK = 32
BLOCK = N1 // NBLK
BINS = 16
LANES = 128
COARSE = N1 // LANES
FOUR = N2 // LANES
F32 = jnp.float32
BF16 = jnp.bfloat16
MIB = 1 << 20
VMEM_LIMIT = 56 * MIB
ANY = pl.BlockSpec(memory_space=pl.ANY)
COST = pl.CostEstimate(flops=MIB, bytes_accessed=MIB, transcendentals=0)


def split_table(table):
    high = table.astype(ml_dtypes.bfloat16)
    low = (table - high.astype(np.float64)).astype(ml_dtypes.bfloat16)
    return high, low


def first_table():
    angle = 2 * np.pi * (np.outer(np.arange(LANES), np.arange(LANES)) % LANES) / LANES
    cos, sin = np.cos(angle), np.sin(angle)
    return split_table(np.block([[cos, sin], [-sin, cos]]))


def stage_table():
    angle = 2 * np.pi * np.outer(np.arange(COARSE), np.arange(LANES)) / N1
    return np.concatenate([np.cos(angle), np.sin(angle)]).astype(np.float32)


def second_table(cols, halves):
    order = np.arange(LANES).reshape(LANES // cols, halves, cols // halves)
    order = order.transpose(1, 0, 2).reshape(-1)
    blocks = []
    for a in range(FOUR):
        n2 = a + FOUR * np.arange(LANES)
        angle = 2 * np.pi * (np.outer(n2, order) % N2) / N2
        cos, sin = np.cos(angle), np.sin(angle)
        blocks.append(np.block([[cos, -sin], [sin, cos]]))
    return split_table(np.concatenate(blocks))


def split(x):
    high = x.astype(BF16)
    return high, (x - high.astype(F32)).astype(BF16)


def phase(index, length):
    angle = (index % length).astype(F32) * (2.0 * np.pi / length)
    return jnp.cos(angle), jnp.sin(angle)


def times_i(z):
    return (-z[1], z[0])


def plus(x, y):
    return (x[0] + y[0], x[1] + y[1])


def minus(x, y):
    return (x[0] - y[0], x[1] - y[1])


def dft4(x):
    s0, s1 = plus(x[0], x[2]), minus(x[0], x[2])
    s2, s3 = plus(x[1], x[3]), times_i(minus(x[1], x[3]))
    return [plus(s0, s2), plus(s1, s3), minus(s0, s2), minus(s1, s3)]


def turn(z, step):
    step %= 16
    if step == 0:
        return z
    if step == 4:
        return times_i(z)
    if step == 8:
        return (-z[0], -z[1])
    half = float(np.sqrt(0.5))
    if step == 2:
        return ((z[0] - z[1]) * half, (z[0] + z[1]) * half)
    if step == 6:
        return ((z[0] + z[1]) * -half, (z[0] - z[1]) * half)
    cos, sin = float(np.cos(np.pi * step / 8)), float(np.sin(np.pi * step / 8))
    return (z[0] * cos - z[1] * sin, z[0] * sin + z[1] * cos)


def dft16(x):
    columns = [dft4([x[4 * u1 + u0] for u1 in range(4)]) for u0 in range(4)]
    out = [None] * 16
    for a0 in range(4):
        ys = dft4([turn(columns[u0][a0], u0 * a0) for u0 in range(4)])
        for a1 in range(4):
            out[a0 + 4 * a1] = ys[a1]
    return out


def dot3(left, right):
    (lh, ll), (rh, rl) = left, right
    return jnp.dot(
        jnp.concatenate([lh, lh, ll], axis=1),
        jnp.concatenate([rh, rl, rh], axis=0),
        preferred_element_type=F32,
    )


def products(tmpl, strain_ref, where, rows=slice(None)):
    per_piece = COARSE // strain_ref.shape[0]
    for u in range(COARSE):
        off = u % per_piece
        there = slice(off * LANES, (off + 1) * LANES)
        hr, hi = tmpl(0, u), tmpl(1, u)
        sr = strain_ref[(u // per_piece,) + where + (0, rows, there)]
        si = strain_ref[(u // per_piece,) + where + (1, rows, there)]
        yield u, hr * sr + hi * si, hr * si - hi * sr


def tile(u):
    return slice(u * LANES, (u + 1) * LANES)


def first_kernel(
    freq, info_ref, tmpl_ref, strain_ref, wh_ref, wl_ref, stage_ref, tw_ref, *refs
):
    out_ref, token_ref, gh, gl, z = refs[-5:]
    token_ref[...] = jnp.zeros_like(token_ref)
    rows = tmpl_ref.shape[2]
    for r in range(0, rows, ROWS):
        at = slice(r, r + ROWS)
        got = products(lambda p, u: tmpl_ref[0, p, at, tile(u)], strain_ref, (0,), at)
        y = dft16([(re, im) for _, re, im in got])
        for a in range(COARSE):
            cos, sin = stage_ref[a : a + 1, :], stage_ref[COARSE + a : COARSE + a + 1, :]
            yr, yi = y[a]
            to = slice(a * rows + r, a * rows + r + ROWS)
            gh[to, :LANES], gl[to, :LANES] = split(yr * cos - yi * sin)
            gh[to, LANES:], gl[to, LANES:] = split(yr * sin + yi * cos)
    z[...] = dot3((gh[...], gl[...]), (wh_ref[...], wl_ref[...]))
    width = LANES // freq
    slot = lax.broadcasted_iota(jnp.int32, (ROWS, LANES), 1) // width
    for group in range(COARSE // freq):
        for r in range(0, rows, ROWS):
            at = slice(r, r + ROWS)
            turned = []
            for i in range(freq):
                a = group * freq + i
                to = slice(a * rows + r, a * rows + r + ROWS)
                zr, zi = z[to, :LANES], z[to, LANES:]
                cos, sin = tw_ref[0, at, tile(a)], tw_ref[1, at, tile(a)]
                pair = (zr * cos - zi * sin, zr * sin + zi * cos)
                if i:
                    pair = tuple(pltpu.roll(v, i * width, 1) for v in pair)
                turned.append(pair)
            for q in range(freq):
                for p in range(2):
                    value = turned[(0 - q) % freq][p]
                    for s in range(1, freq):
                        value = jnp.where(slot == s, turned[(s - q) % freq][p], value)
                    out_ref[q, 0, p, group, at] = value


ROWS = 16
HALVES = 2
TOGETHER = 2


def first_section(freq, half, info, templates, strain, first, stage, twist, earlier):
    tmpls = templates.shape[0]
    pieces, dets, _, cols, piece_len = strain.shape
    series = tmpls * dets - 1
    groups = COARSE // freq
    rows = cols // HALVES
    table = pl.BlockSpec((2 * LANES, 2 * LANES), lambda i, n: (0, 0))
    out = (freq, series, 2, groups, cols, LANES)
    return pl.pallas_call(
        functools.partial(first_kernel, freq),
        grid_spec=pltpu.PrefetchScalarGridSpec(
            num_scalar_prefetch=1,
            grid=(series,),
            in_specs=[
                pl.BlockSpec(
                    (1, 2, rows, N1), lambda i, n: (n[1 + 2 * i], 0, half, 0)
                ),
                pl.BlockSpec(
                    (pieces, 1, 2, rows, piece_len), lambda i, n: (0, n[2 + 2 * i], 0, half, 0)
                ),
                table,
                table,
                pl.BlockSpec((2 * COARSE, LANES), lambda i, n: (0, 0)),
                pl.BlockSpec((2, rows, N1), lambda i, n: (0, half, 0)),
            ]
            + [ANY] * len(earlier),
            out_specs=[
                pl.BlockSpec(
                    (freq, 1, 2, groups, rows, LANES), lambda i, n: (0, i, 0, 0, half, 0)
                ),
                pl.BlockSpec((8, LANES), lambda i, n: (0, 0)),
            ],
            scratch_shapes=[
                pltpu.VMEM((COARSE * rows, 2 * LANES), BF16),
                pltpu.VMEM((COARSE * rows, 2 * LANES), BF16),
                pltpu.VMEM((COARSE * rows, 2 * LANES), F32),
            ],
        ),
        out_shape=[
            jax.ShapeDtypeStruct(out, F32),
            jax.ShapeDtypeStruct((8, LANES), F32),
        ],
        input_output_aliases={7: 0} if earlier else {},
        compiler_params=pltpu.CompilerParams(vmem_limit_bytes=VMEM_LIMIT),
        cost_estimate=pl.CostEstimate(
            flops=60 * series * cols * N1 * LANES, bytes_accessed=16 * MIB, transcendentals=0
        ),
        name="first_section",
    )(info, templates, strain, first[0], first[1], stage, twist, *earlier)


def entry_kernel(which_ref, tmpl_ref, *refs):
    quarter_refs, out_ref = refs[:-1], refs[-1]
    banks = len(quarter_refs)
    length = N1 // banks
    first_half = lax.broadcasted_iota(jnp.int32, (ROWS, LANES), 1) < BLOCK
    for k, ref in enumerate(quarter_refs):
        start = lax.rem(which_ref[1] - k + banks, banks) * length
        for u in range(length // LANES):
            lane = pl.ds(pl.multiple_of(start + u * LANES, LANES), LANES)
            hr, hi = tmpl_ref[0, 0, :, lane], tmpl_ref[0, 1, :, lane]
            sr, si = ref[0, :, tile(u)], ref[1, :, tile(u)]
            re, im = hr * sr + hi * si, hr * si - hi * sr
            to = pl.multiple_of(2 * start + 2 * u * LANES, 2 * LANES)
            out_ref[:, pl.ds(to, LANES)] = jnp.where(first_half, re, pltpu.roll(im, BLOCK, 1))
            to = pl.multiple_of(to + LANES, LANES)
            out_ref[:, pl.ds(to, LANES)] = jnp.where(first_half, pltpu.roll(re, BLOCK, 1), im)


def entry_product(which, templates, quarters):
    _, cols, length = quarters[0].shape
    return pl.pallas_call(
        entry_kernel,
        grid_spec=pltpu.PrefetchScalarGridSpec(
            num_scalar_prefetch=1,
            grid=(cols // ROWS,),
            in_specs=[pl.BlockSpec((1, 2, ROWS, N1), lambda c, w: (w[0], 0, c, 0))]
            + [pl.BlockSpec((2, ROWS, length), lambda c, w: (0, c, 0))] * len(quarters),
            out_specs=pl.BlockSpec((ROWS, 2 * N1), lambda c, w: (c, 0)),
        ),
        out_shape=jax.ShapeDtypeStruct((cols, 2 * N1), F32),
        compiler_params=pltpu.CompilerParams(vmem_limit_bytes=VMEM_LIMIT),
        cost_estimate=COST,
        name="entry_product",
    )(which, templates, *quarters)


def second_points(x, w2h_ref, w2l_ref, use):
    for a, (yr, yi) in enumerate(dft4(x)):
        y = jnp.concatenate([yr, yi], axis=0)
        at = slice(a * 2 * LANES, (a + 1) * 2 * LANES)
        z = dot3((w2h_ref[at, :], w2l_ref[at, :]), split(y))
        use(a, z[:LANES], z[LANES:])


def second_kernel(freq, halves, info_ref, scale_ref, *refs):
    part_refs, (w2h_ref, w2l_ref) = refs[:halves], refs[halves : halves + 2]
    out_ref, hold, order = refs[-3:]
    place = info_ref[0]
    groups, cols = part_refs[0].shape[3:5]
    per = LANES // (halves * cols)
    width = LANES // freq
    scale = scale_ref[info_ref[1 + 2 * pl.program_id(0)]]

    def rows_of(p, u):
        tiles = [
            jnp.concatenate(
                [ref[u * per + f, 0, p, g] for ref in part_refs for f in range(per)],
                axis=0,
            )
            for g in range(groups)
        ]
        return jnp.concatenate(tiles, axis=1)

    x = [(rows_of(0, u), rows_of(1, u)) for u in range(FOUR)]

    def keep(a, re, im):
        for p, value in enumerate((re, im)):
            for g in range(groups):
                hold[p, g, pl.ds(a, LANES, stride=FOUR), :] = value[:, tile(g)] * scale

    second_points(x, w2h_ref, w2l_ref, keep)
    for p in range(2):
        for g in range(groups):
            turned = hold[p, g].T
            for s in range(freq):
                a = g * freq + lax.rem(s - place + freq, freq)
                for j in range(FOUR):
                    order[p, j, pl.ds(a, width, stride=COARSE), :] = turned[
                        s * width : (s + 1) * width, tile(j)
                    ]
        for j in range(FOUR):
            out_ref[0, 0, p, :, tile(j)] = order[p, j]


def second_section(freq, info, scale, parts, second, snr, after):
    _, series, _, groups, cols, _ = parts[0].shape
    halves = len(parts)
    times = groups * LANES
    smem = pl.BlockSpec(memory_space=pltpu.SMEM)
    table = pl.BlockSpec((FOUR * 2 * LANES, 2 * LANES), lambda i, n: (0, 0))
    part = pl.BlockSpec(
        (freq, 1, 2, groups, cols, LANES), lambda i, n: (0, i, 0, 0, 0, 0)
    )
    return pl.pallas_call(
        functools.partial(second_kernel, freq, halves),
        grid_spec=pltpu.PrefetchScalarGridSpec(
            num_scalar_prefetch=1,
            grid=(series,),
            in_specs=[smem] + [part] * halves + [table, table, ANY] + [ANY] * len(after),
            out_specs=pl.BlockSpec(
                (1, 1, 2, times, N2), lambda i, n: (n[1 + 2 * i], n[2 + 2 * i], 0, 0, 0)
            ),
            scratch_shapes=[
                pltpu.VMEM((2, groups, N2, LANES), F32),
                pltpu.VMEM((2, FOUR, times, LANES), F32),
            ],
        ),
        out_shape=jax.ShapeDtypeStruct(snr.shape, F32),
        input_output_aliases={4 + halves: 0},
        compiler_params=pltpu.CompilerParams(vmem_limit_bytes=VMEM_LIMIT),
        cost_estimate=COST,
        name="second_section",
    )(info, scale, *parts, *second, snr, *after)


BLOCKS = 4


def bank_kernel(block_ref, inner_ref, high_ref, low_ref):
    times = block_ref.shape[-1]
    rc, rs = inner_ref[0], inner_ref[1]
    for b in range(BLOCKS):
        bc, bs = block_ref[b, 0:1, :], block_ref[b, 1:2, :]
        cos, sin = split(bc * rc - bs * rs), split(bc * rs + bs * rc)
        top = slice(2 * b * BLOCK, (2 * b + 1) * BLOCK)
        low = slice((2 * b + 1) * BLOCK, (2 * b + 2) * BLOCK)
        for ref, c, s in zip((high_ref, low_ref), cos, sin):
            ref[top, :times] = c
            ref[top, times:] = s
            ref[low, :times] = -s
            ref[low, times:] = c


def bank_table(own_time):
    times = own_time.shape[0]
    block = jnp.arange(NBLK, dtype=jnp.int32)[:, None] * own_time[None, :]
    block = jnp.stack(phase(block, NBLK), axis=1)
    inner = jnp.arange(BLOCK, dtype=jnp.int32)[:, None] * own_time[None, :]
    inner = jnp.stack(phase(inner, N1))
    return pl.pallas_call(
        bank_kernel,
        grid=(NBLK // BLOCKS,),
        in_specs=[
            pl.BlockSpec((BLOCKS, 2, times), lambda b: (b, 0, 0)),
            pl.BlockSpec((2, BLOCK, times), lambda b: (0, 0, 0)),
        ],
        out_specs=[pl.BlockSpec((BLOCKS * 2 * BLOCK, 2 * times), lambda b: (b, 0))] * 2,
        out_shape=[jax.ShapeDtypeStruct((2 * N1, 2 * times), BF16)] * 2,
        compiler_params=pltpu.CompilerParams(vmem_limit_bytes=VMEM_LIMIT),
        cost_estimate=COST,
        name="bank_table",
    )(block, inner)


def bins_first_kernel(pieces, place_ref, edge_ref, *refs):
    piece_refs = refs[:pieces]
    wh_ref, wl_ref, tw_ref = refs[pieces : pieces + 3]
    level_ref, total_ref, xh, xl, acc = refs[-5:]
    times = total_ref.shape[-1]
    cols = piece_refs[0].shape[0]
    step = pl.program_id(0)

    @pl.when(step == 0)
    def _():
        for k, ref in enumerate(piece_refs):
            row = pl.multiple_of((place_ref[0] ^ k) * cols, cols)

            def cut(i, carry):
                at = pl.ds(pl.multiple_of(i * FOUR * LANES, FOUR * LANES), FOUR * LANES)
                xh[pl.ds(row, cols), at], xl[pl.ds(row, cols), at] = split(ref[:, at])
                return carry

            lax.fori_loop(0, 2 * N1 // (FOUR * LANES), cut, 0)
        total_ref[...] = jnp.zeros_like(total_ref)

    def blocks_at(block, blocks):
        at = pl.ds(pl.multiple_of(block * LANES, LANES), blocks * LANES)
        return dot3((xh[:, at], xl[:, at]), (wh_ref[at, :], wl_ref[at, :]))

    for i in range(TOGETHER):
        start, end = edge_ref[step * TOGETHER + i], edge_ref[step * TOGETHER + i + 1]
        odd = (end - start) % 2

        @pl.when(odd == 1)
        def _():
            acc[i] = blocks_at(end - 1, 1)

        @pl.when(odd == 0)
        def _():
            acc[i] = blocks_at(end - 2, 2)

        def two(n, carry):
            acc[i] += blocks_at(start + 2 * n, 2)
            return carry

        lax.fori_loop(0, (end - start - 1) // 2, two, 0)

    for u in range(pieces * cols // LANES):
        at = tile(u)
        cos, sin = tw_ref[0, at, :], tw_ref[1, at, :]
        sum_r, sum_i = total_ref[0, at, :], total_ref[1, at, :]
        for i in range(TOGETHER):
            re, im = acc[i, at, :times], acc[i, at, times:]
            vr, vi = re * cos - im * sin, re * sin + im * cos
            level_ref[i, 0, at, :] = vr
            level_ref[i, 1, at, :] = vi
            sum_r, sum_i = sum_r + vr, sum_i + vi
        total_ref[0, at, :] = sum_r
        total_ref[1, at, :] = sum_i


def bins_first(half, place, edges, pieces, table, twist, after):
    cols = pieces[0].shape[0] // HALVES
    rows, times = twist.shape[1:]
    smem = pl.BlockSpec(memory_space=pltpu.SMEM)
    fixed = lambda shape: pl.BlockSpec(shape, lambda i: (0,) * len(shape))
    return pl.pallas_call(
        functools.partial(bins_first_kernel, len(pieces)),
        grid=(BINS // TOGETHER,),
        in_specs=[smem, smem]
        + [pl.BlockSpec((cols, 2 * N1), lambda i: (half, 0))] * len(pieces)
        + [fixed((2 * N1, 2 * times))] * 2
        + [fixed((2, rows, times))]
        + [ANY] * len(after),
        out_specs=[
            pl.BlockSpec((TOGETHER, 2, rows, times), lambda i: (i, 0, 0, 0)),
            fixed((2, rows, times)),
        ],
        out_shape=[
            jax.ShapeDtypeStruct((BINS, 2, rows, times), F32),
            jax.ShapeDtypeStruct((2, rows, times), F32),
        ],
        scratch_shapes=[
            pltpu.VMEM((rows, 2 * N1), BF16),
            pltpu.VMEM((rows, 2 * N1), BF16),
            pltpu.VMEM((TOGETHER, rows, 2 * times), F32),
        ],
        compiler_params=pltpu.CompilerParams(vmem_limit_bytes=VMEM_LIMIT),
        cost_estimate=COST,
        name="bins_first",
    )(place, edges, *pieces, *table, twist, *after)


def bins_second_kernel(halves, which_ref, scale_ref, gain_ref, share_ref, *refs):
    level_refs, total_refs = refs[:halves], refs[halves : 2 * halves]
    w2h_ref, w2l_ref, out_ref, snr_ref, chi, hold = refs[2 * halves :]
    times = out_ref.shape[0]
    part_rows = LANES // halves
    step = pl.program_id(0)

    @pl.when(step == 0)
    def _():
        chi[...] = jnp.zeros_like(chi)

    def rows_of(get, u):
        at = slice(u * part_rows, (u + 1) * part_rows)
        return jnp.concatenate([get(h, at) for h in range(halves)], axis=0)

    def keep(a, re, im):
        chi[a] += re * re + im * im

    for i in range(TOGETHER):
        gain, share = gain_ref[step * TOGETHER + i], share_ref[step * TOGETHER + i]

        def deviation(p):
            return lambda h, at: (
                level_refs[h][i, p, at, :] * gain - total_refs[h][p, at, :] * share
            )

        x = [tuple(rows_of(deviation(p), u) for p in range(2)) for u in range(FOUR)]
        second_points(x, w2h_ref, w2l_ref, keep)

    @pl.when(step == BINS // TOGETHER - 1)
    def _():
        scale = scale_ref[which_ref[0]]

        def whole(p):
            return lambda h, at: total_refs[h][p, at, :] * scale

        def put(a, re, im):
            for p, value in enumerate((re, im)):
                for g in range(times // LANES):
                    hold[p, g, pl.ds(a, LANES, stride=FOUR), :] = value[:, tile(g)]

        y = [tuple(rows_of(whole(p), u) for p in range(2)) for u in range(FOUR)]
        second_points(y, w2h_ref, w2l_ref, put)
        for g in range(times // LANES):
            for a in range(FOUR):
                hold[2, g, pl.ds(a, LANES, stride=FOUR), :] = chi[a, :, tile(g)]
            for p in range(2):
                snr_ref[0, 0, p, tile(g), :] = hold[p, g].T
            out_ref[tile(g), :] = hold[2, g].T


def bins_second(which, scale, gain, share, levels, totals, second, tmpls, dets):
    _, _, rows, times = levels[0].shape
    halves = len(levels)
    smem = pl.BlockSpec(memory_space=pltpu.SMEM)
    fixed = lambda shape: pl.BlockSpec(shape, lambda i, w: (0,) * len(shape))
    return pl.pallas_call(
        functools.partial(bins_second_kernel, halves),
        grid_spec=pltpu.PrefetchScalarGridSpec(
            num_scalar_prefetch=1,
            grid=(BINS // TOGETHER,),
            in_specs=[smem, smem, smem]
            + [pl.BlockSpec((TOGETHER, 2, rows, times), lambda i, w: (i, 0, 0, 0))] * halves
            + [fixed((2, rows, times))] * halves
            + [fixed((FOUR * 2 * LANES, 2 * LANES))] * 2,
            out_specs=[
                fixed((times, N2)),
                pl.BlockSpec((1, 1, 2, times, N2), lambda i, w: (w[0], w[1], 0, 0, 0)),
            ],
            scratch_shapes=[
                pltpu.VMEM((FOUR, LANES, times), F32),
                pltpu.VMEM((3, times // LANES, N2, LANES), F32),
            ],
        ),
        out_shape=[
            jax.ShapeDtypeStruct((times, N2), F32),
            jax.ShapeDtypeStruct((tmpls, dets, 2, times, N2), F32),
        ],
        compiler_params=pltpu.CompilerParams(vmem_limit_bytes=VMEM_LIMIT),
        cost_estimate=COST,
        name="bins_second",
    )(which, scale, gain, share, *levels, *totals, *second)


def handed_on(arrays, after):
    count = len(arrays)
    return pl.pallas_call(
        lambda *refs: None,
        in_specs=[ANY] * (count + len(after)),
        out_specs=[ANY] * count,
        out_shape=[jax.ShapeDtypeStruct(x.shape, x.dtype) for x in arrays],
        input_output_aliases={i: i for i in range(count)},
        compiler_params=pltpu.CompilerParams(vmem_limit_bytes=VMEM_LIMIT),
        cost_estimate=COST,
        name="handed_on",
    )(*arrays, *after)


def swap(x, freq, k):
    return lax.ppermute(x, "freq", [(i, i ^ k) for i in range(freq)])


def far_pieces(own, freq):
    return [own] + [swap(own, freq, k) for k in range(2, freq, 2)]


def near_pieces(far, freq):
    return [x for even in far for x in (even, swap(even, freq, 1))]


def per_device(strain, templates, coinc_tmpl, coinc_det, bin_edges):
    freq, banks = lax.axis_size("freq"), lax.axis_size("bank")
    place = lax.axis_index("freq").astype(jnp.int32)
    bank = lax.axis_index("bank").astype(jnp.int32)
    tmpls, _, cols, _ = templates.shape
    slots, dets = coinc_tmpl.shape[0], strain.shape[0]
    times = N1 // freq
    part = cols // HALVES

    def to_bank(x, k):
        return lax.ppermute(x, "bank", [(i, (i + k) % banks) for i in range(banks)])

    asked = [coinc_det] + [to_bank(coinc_det, -k) for k in range(1, banks)]
    quarters = []
    for j in range(slots):
        own = lax.dynamic_index_in_dim(strain, coinc_det[j], 0, keepdims=False)
        one = [own]
        for k in range(1, banks):
            picked = lax.dynamic_index_in_dim(strain, asked[k][j], 0, keepdims=False)
            one.append(to_bank(picked, k))
        quarters.append(one)
    strains = lax.all_gather(strain, "bank", axis=0, tiled=False)

    first = tuple(jnp.asarray(t) for t in first_table())
    second = tuple(jnp.asarray(t) for t in second_table(cols, 1))
    second_halves = tuple(jnp.asarray(t) for t in second_table(cols, HALVES))
    stage = jnp.asarray(stage_table())

    power = (templates[:, 0] ** 2 + templates[:, 1] ** 2).sum(axis=1)
    local_power = power.reshape(tmpls, NBLK, BLOCK).sum(axis=2)
    block_power = lax.all_gather(local_power, "freq", axis=0, tiled=False).sum(axis=0)
    sigma_sq = block_power.sum(axis=1)
    inv_sigma = lax.rsqrt(sigma_sq)
    bin_of = jnp.sum(
        jnp.arange(NBLK, dtype=jnp.int32)[None, :, None] >= bin_edges[:, None, :], axis=2
    )
    inside = bin_of[:, None, :] == jnp.arange(BINS, dtype=jnp.int32)[None, :, None]
    weights = jnp.where(inside, block_power[:, None, :], 0.0).sum(axis=2) / sigma_sq[:, None]

    column = place * cols + jnp.arange(cols, dtype=jnp.int32)
    lane = jnp.arange(N1, dtype=jnp.int32)
    time_of_lane = lane // LANES + COARSE * (lane % LANES)
    twist = jnp.stack(phase(column[:, None] * time_of_lane[None, :], N1 * N2))
    own_time = place * times + jnp.arange(times, dtype=jnp.int32)
    table = bank_table(own_time)
    own_twist = []
    for h in range(HALVES):
        rows = jnp.arange(freq * part, dtype=jnp.int32)
        rows = rows // part * cols + h * part + rows % part
        own_twist.append(jnp.stack(phase(rows[:, None] * own_time[None, :], N1 * N2)))

    which = [jnp.stack([coinc_tmpl[j], coinc_det[j]]) for j in range(slots)]
    series = jnp.arange(tmpls * dets - 1, dtype=jnp.int32)
    series = series + (series >= which[0][0] * dets + which[0][1])
    info = jnp.stack([series // dets, series % dets], axis=1).reshape(-1)
    info = jnp.concatenate([place.reshape(1), info])
    ends = jnp.zeros((1,), jnp.int32), jnp.full((1,), NBLK, jnp.int32)
    edges = [
        jnp.concatenate([ends[0], bin_edges[coinc_tmpl[j]], ends[1]]) for j in range(slots)
    ]
    info, edges, table, twist, own_twist = lax.optimization_barrier(
        (info, edges, table, twist, own_twist)
    )

    here = place.reshape(1)
    own = [
        entry_product(jnp.stack([coinc_tmpl[j], bank]), templates, quarters[j])
        for j in range(slots)
    ]
    far = [far_pieces(x, freq) for x in own]
    sent, token = first_section(freq, 0, info, templates, strains, first, stage, twist, [])
    far = [x[:1] + list(handed_on(x[1:], [token])) for x in far]
    pieces = [near_pieces(x, freq) for x in far]
    sent, _ = first_section(freq, 1, info, templates, strains, first, stage, twist, [sent])
    (ready,) = handed_on([sent], [x for entry in pieces for x in entry[1:]])
    got = lax.all_to_all(
        ready.reshape(freq, -1, LANES), "freq", split_axis=0, concat_axis=0, tiled=True
    )
    got = got.reshape(sent.shape)

    chi, snr = [], None
    for j in range(slots):
        t = coinc_tmpl[j]
        halves = [
            bins_first(h, here, edges[j], pieces[j], table, own_twist[h], [ready])
            for h in range(HALVES)
        ]
        levels, totals = zip(*halves)
        gain = inv_sigma[t] * lax.rsqrt(weights[t])
        share = gain * weights[t]
        one, series_of = bins_second(
            which[j], inv_sigma, gain, share, levels, totals, second_halves, tmpls, dets
        )
        chi.append(one)
        snr = series_of if snr is None else snr
    snr = second_section(freq, info, inv_sigma, [got], second, snr, chi)
    return (snr, jnp.stack(chi))


def solution(mesh):
    placed = (
        P(None, None, "freq", "bank"),
        P("bank", None, "freq", None),
        P("bank"),
        P("bank"),
        P("bank", None),
    )
    return jax.shard_map(
        per_device,
        mesh=mesh,
        in_specs=placed,
        out_specs=(P("bank", None, None, "freq", None), P("bank", "freq", None)),
        check_vma=False,
    )
```

```python
import functools

import jax
import jax.numpy as jnp
import ml_dtypes
import numpy as np
from jax import lax
from jax.experimental import pallas as pl
from jax.experimental.pallas import tpu as pltpu
from jax.sharding import PartitionSpec as P

N1 = 2048
N2 = 512
NBLK = 32
BLOCK = N1 // NBLK
BINS = 16
LANES = 128
COARSE = N1 // LANES
FOUR = N2 // LANES
F32 = jnp.float32
BF16 = jnp.bfloat16
MIB = 1 << 20
VMEM_LIMIT = 56 * MIB
ANY = pl.BlockSpec(memory_space=pl.ANY)
COST = pl.CostEstimate(flops=MIB, bytes_accessed=MIB, transcendentals=0)


def split_table(table):
    high = table.astype(ml_dtypes.bfloat16)
    low = (table - high.astype(np.float64)).astype(ml_dtypes.bfloat16)
    return high, low


def first_table():
    angle = 2 * np.pi * (np.outer(np.arange(LANES), np.arange(LANES)) % LANES) / LANES
    cos, sin = np.cos(angle), np.sin(angle)
    return split_table(np.block([[cos, sin], [-sin, cos]]))


def stage_table():
    angle = 2 * np.pi * np.outer(np.arange(COARSE), np.arange(LANES)) / N1
    return np.concatenate([np.cos(angle), np.sin(angle)]).astype(np.float32)


def second_table(cols, halves):
    order = np.arange(LANES).reshape(LANES // cols, halves, cols // halves)
    order = order.transpose(1, 0, 2).reshape(-1)
    blocks = []
    for a in range(FOUR):
        n2 = a + FOUR * np.arange(LANES)
        angle = 2 * np.pi * (np.outer(n2, order) % N2) / N2
        cos, sin = np.cos(angle), np.sin(angle)
        blocks.append(np.block([[cos, -sin], [sin, cos]]))
    return split_table(np.concatenate(blocks))


def split(x):
    high = x.astype(BF16)
    return high, (x - high.astype(F32)).astype(BF16)


def phase(index, length):
    angle = (index % length).astype(F32) * (2.0 * np.pi / length)
    return jnp.cos(angle), jnp.sin(angle)


def times_i(z):
    return (-z[1], z[0])


def plus(x, y):
    return (x[0] + y[0], x[1] + y[1])


def minus(x, y):
    return (x[0] - y[0], x[1] - y[1])


def dft4(x):
    s0, s1 = plus(x[0], x[2]), minus(x[0], x[2])
    s2, s3 = plus(x[1], x[3]), times_i(minus(x[1], x[3]))
    return [plus(s0, s2), plus(s1, s3), minus(s0, s2), minus(s1, s3)]


def turn(z, step):
    step %= 16
    if step == 0:
        return z
    if step == 4:
        return times_i(z)
    if step == 8:
        return (-z[0], -z[1])
    half = float(np.sqrt(0.5))
    if step == 2:
        return ((z[0] - z[1]) * half, (z[0] + z[1]) * half)
    if step == 6:
        return ((z[0] + z[1]) * -half, (z[0] - z[1]) * half)
    cos, sin = float(np.cos(np.pi * step / 8)), float(np.sin(np.pi * step / 8))
    return (z[0] * cos - z[1] * sin, z[0] * sin + z[1] * cos)


def dft16(x):
    columns = [dft4([x[4 * u1 + u0] for u1 in range(4)]) for u0 in range(4)]
    out = [None] * 16
    for a0 in range(4):
        ys = dft4([turn(columns[u0][a0], u0 * a0) for u0 in range(4)])
        for a1 in range(4):
            out[a0 + 4 * a1] = ys[a1]
    return out


def dot3(left, right):
    (lh, ll), (rh, rl) = left, right
    return jnp.dot(
        jnp.concatenate([lh, lh, ll], axis=1),
        jnp.concatenate([rh, rl, rh], axis=0),
        preferred_element_type=F32,
    )


def products(tmpl, strain_ref, where, rows=slice(None)):
    per_piece = COARSE // strain_ref.shape[0]
    for u in range(COARSE):
        off = u % per_piece
        there = slice(off * LANES, (off + 1) * LANES)
        hr, hi = tmpl(0, u), tmpl(1, u)
        sr = strain_ref[(u // per_piece,) + where + (0, rows, there)]
        si = strain_ref[(u // per_piece,) + where + (1, rows, there)]
        yield u, hr * sr + hi * si, hr * si - hi * sr


def tile(u):
    return slice(u * LANES, (u + 1) * LANES)


def first_kernel(
    freq, info_ref, tmpl_ref, strain_ref, wh_ref, wl_ref, stage_ref, tw_ref, *refs
):
    out_ref, token_ref, gh, gl, z = refs[-5:]
    token_ref[...] = jnp.zeros_like(token_ref)
    rows = tmpl_ref.shape[2]
    for r in range(0, rows, ROWS):
        at = slice(r, r + ROWS)
        got = products(lambda p, u: tmpl_ref[0, p, at, tile(u)], strain_ref, (0,), at)
        y = dft16([(re, im) for _, re, im in got])
        for a in range(COARSE):
            cos, sin = stage_ref[a : a + 1, :], stage_ref[COARSE + a : COARSE + a + 1, :]
            yr, yi = y[a]
            to = slice(a * rows + r, a * rows + r + ROWS)
            gh[to, :LANES], gl[to, :LANES] = split(yr * cos - yi * sin)
            gh[to, LANES:], gl[to, LANES:] = split(yr * sin + yi * cos)
    z[...] = dot3((gh[...], gl[...]), (wh_ref[...], wl_ref[...]))
    width = LANES // freq
    slot = lax.broadcasted_iota(jnp.int32, (ROWS, LANES), 1) // width
    for group in range(COARSE // freq):
        for r in range(0, rows, ROWS):
            at = slice(r, r + ROWS)
            turned = []
            for i in range(freq):
                a = group * freq + i
                to = slice(a * rows + r, a * rows + r + ROWS)
                zr, zi = z[to, :LANES], z[to, LANES:]
                cos, sin = tw_ref[0, at, tile(a)], tw_ref[1, at, tile(a)]
                pair = (zr * cos - zi * sin, zr * sin + zi * cos)
                if i:
                    pair = tuple(pltpu.roll(v, i * width, 1) for v in pair)
                turned.append(pair)
            for q in range(freq):
                for p in range(2):
                    value = turned[(0 - q) % freq][p]
                    for s in range(1, freq):
                        value = jnp.where(slot == s, turned[(s - q) % freq][p], value)
                    out_ref[q, 0, p, group, at] = value


ROWS = 16
HALVES = 2
TOGETHER = 2


def first_section(freq, half, info, templates, strain, first, stage, twist, earlier):
    tmpls = templates.shape[0]
    pieces, dets, _, rows, piece_len = strain.shape
    cols = templates.shape[2]
    series = tmpls * dets - 1
    groups = COARSE // freq
    table = pl.BlockSpec((2 * LANES, 2 * LANES), lambda i, n: (0, 0))
    out = (freq, series, 2, groups, cols, LANES)
    return pl.pallas_call(
        functools.partial(first_kernel, freq),
        grid_spec=pltpu.PrefetchScalarGridSpec(
            num_scalar_prefetch=1,
            grid=(series,),
            in_specs=[
                pl.BlockSpec(
                    (1, 2, rows, N1), lambda i, n: (n[1 + 2 * i], 0, half, 0)
                ),
                pl.BlockSpec(
                    (pieces, 1, 2, rows, piece_len), lambda i, n: (0, n[2 + 2 * i], 0, 0, 0)
                ),
                table,
                table,
                pl.BlockSpec((2 * COARSE, LANES), lambda i, n: (0, 0)),
                pl.BlockSpec((2, rows, N1), lambda i, n: (0, half, 0)),
            ]
            + [ANY] * len(earlier),
            out_specs=[
                pl.BlockSpec(
                    (freq, 1, 2, groups, rows, LANES), lambda i, n: (0, i, 0, 0, half, 0)
                ),
                pl.BlockSpec((8, LANES), lambda i, n: (0, 0)),
            ],
            scratch_shapes=[
                pltpu.VMEM((COARSE * rows, 2 * LANES), BF16),
                pltpu.VMEM((COARSE * rows, 2 * LANES), BF16),
                pltpu.VMEM((COARSE * rows, 2 * LANES), F32),
            ],
        ),
        out_shape=[
            jax.ShapeDtypeStruct(out, F32),
            jax.ShapeDtypeStruct((8, LANES), F32),
        ],
        input_output_aliases={7: 0} if earlier else {},
        compiler_params=pltpu.CompilerParams(vmem_limit_bytes=VMEM_LIMIT),
        cost_estimate=pl.CostEstimate(
            flops=60 * series * cols * N1 * LANES, bytes_accessed=16 * MIB, transcendentals=0
        ),
        name="first_section",
    )(info, templates, strain, first[0], first[1], stage, twist, *earlier)


def entry_kernel(steps, banks, which_ref, tmpl_ref, strain_ref, *refs):
    out_ref = refs[-1]
    length = N1 // banks
    first_half = lax.broadcasted_iota(jnp.int32, (ROWS, LANES), 1) < BLOCK
    for n, k in enumerate(steps):
        part = lax.rem(which_ref[2] + k, banks)
        for u in range(length // LANES):
            lane = pl.ds(pl.multiple_of(part * length + u * LANES, LANES), LANES)
            hr, hi = tmpl_ref[0, 0, :, lane], tmpl_ref[0, 1, :, lane]
            piece = 0 if strain_ref.shape[0] == 1 else part
            sr, si = strain_ref[piece, 0, 0, :, tile(u)], strain_ref[piece, 0, 1, :, tile(u)]
            re, im = hr * sr + hi * si, hr * si - hi * sr
            to = 2 * (n * length // LANES + u)
            out_ref[:, tile(to)] = jnp.where(first_half, re, pltpu.roll(im, BLOCK, 1))
            out_ref[:, tile(to + 1)] = jnp.where(first_half, pltpu.roll(re, BLOCK, 1), im)


def entry_product(steps, banks, half, which, templates, strain, after):
    pieces, _, _, cols, length = strain.shape
    first = half * cols // ROWS
    return pl.pallas_call(
        functools.partial(entry_kernel, steps, banks),
        grid_spec=pltpu.PrefetchScalarGridSpec(
            num_scalar_prefetch=1,
            grid=(cols // ROWS,),
            in_specs=[
                pl.BlockSpec((1, 2, ROWS, N1), lambda c, w: (w[0], 0, first + c, 0)),
                pl.BlockSpec((pieces, 1, 2, ROWS, length), lambda c, w: (0, w[1], 0, c, 0)),
            ]
            + [ANY] * len(after),
            out_specs=pl.BlockSpec((ROWS, 2 * length * len(steps)), lambda c, w: (c, 0)),
        ),
        out_shape=jax.ShapeDtypeStruct((cols, 2 * length * len(steps)), F32),
        compiler_params=pltpu.CompilerParams(vmem_limit_bytes=VMEM_LIMIT),
        cost_estimate=COST,
        name="entry_product",
    )(which, templates, strain, *after)


def second_points(x, w2h_ref, w2l_ref, use):
    for a, (yr, yi) in enumerate(dft4(x)):
        y = jnp.concatenate([yr, yi], axis=0)
        at = slice(a * 2 * LANES, (a + 1) * 2 * LANES)
        z = dot3((w2h_ref[at, :], w2l_ref[at, :]), split(y))
        use(a, z[:LANES], z[LANES:])


def second_kernel(freq, halves, info_ref, scale_ref, *refs):
    part_refs, (w2h_ref, w2l_ref) = refs[:halves], refs[halves : halves + 2]
    out_ref, hold, order = refs[-3:]
    place = info_ref[0]
    groups, cols = part_refs[0].shape[3:5]
    per = LANES // (halves * cols)
    width = LANES // freq
    scale = scale_ref[info_ref[1 + 2 * pl.program_id(0)]]

    def rows_of(p, u):
        tiles = [
            jnp.concatenate(
                [ref[u * per + f, 0, p, g] for ref in part_refs for f in range(per)],
                axis=0,
            )
            for g in range(groups)
        ]
        return jnp.concatenate(tiles, axis=1)

    x = [(rows_of(0, u), rows_of(1, u)) for u in range(FOUR)]

    def keep(a, re, im):
        for p, value in enumerate((re, im)):
            for g in range(groups):
                hold[p, g, pl.ds(a, LANES, stride=FOUR), :] = value[:, tile(g)] * scale

    second_points(x, w2h_ref, w2l_ref, keep)
    for p in range(2):
        for g in range(groups):
            turned = hold[p, g].T
            for s in range(freq):
                a = g * freq + lax.rem(s - place + freq, freq)
                for j in range(FOUR):
                    order[p, j, pl.ds(a, width, stride=COARSE), :] = turned[
                        s * width : (s + 1) * width, tile(j)
                    ]
        for j in range(FOUR):
            out_ref[0, 0, p, :, tile(j)] = order[p, j]


def second_section(freq, info, scale, parts, second, snr, after):
    _, series, _, groups, cols, _ = parts[0].shape
    halves = len(parts)
    times = groups * LANES
    smem = pl.BlockSpec(memory_space=pltpu.SMEM)
    table = pl.BlockSpec((FOUR * 2 * LANES, 2 * LANES), lambda i, n: (0, 0))
    part = pl.BlockSpec(
        (freq, 1, 2, groups, cols, LANES), lambda i, n: (0, i, 0, 0, 0, 0)
    )
    return pl.pallas_call(
        functools.partial(second_kernel, freq, halves),
        grid_spec=pltpu.PrefetchScalarGridSpec(
            num_scalar_prefetch=1,
            grid=(series,),
            in_specs=[smem] + [part] * halves + [table, table, ANY] + [ANY] * len(after),
            out_specs=pl.BlockSpec(
                (1, 1, 2, times, N2), lambda i, n: (n[1 + 2 * i], n[2 + 2 * i], 0, 0, 0)
            ),
            scratch_shapes=[
                pltpu.VMEM((2, groups, N2, LANES), F32),
                pltpu.VMEM((2, FOUR, times, LANES), F32),
            ],
        ),
        out_shape=jax.ShapeDtypeStruct(snr.shape, F32),
        input_output_aliases={4 + halves: 0},
        compiler_params=pltpu.CompilerParams(vmem_limit_bytes=VMEM_LIMIT),
        cost_estimate=COST,
        name="second_section",
    )(info, scale, *parts, *second, snr, *after)


BLOCKS = 4


def bank_kernel(block_ref, inner_ref, high_ref, low_ref):
    times = block_ref.shape[-1]
    rc, rs = inner_ref[0], inner_ref[1]
    for b in range(BLOCKS):
        bc, bs = block_ref[b, 0:1, :], block_ref[b, 1:2, :]
        cos, sin = split(bc * rc - bs * rs), split(bc * rs + bs * rc)
        top = slice(2 * b * BLOCK, (2 * b + 1) * BLOCK)
        low = slice((2 * b + 1) * BLOCK, (2 * b + 2) * BLOCK)
        for ref, c, s in zip((high_ref, low_ref), cos, sin):
            ref[top, :times] = c
            ref[top, times:] = s
            ref[low, :times] = -s
            ref[low, times:] = c


def bank_table(own_time):
    times = own_time.shape[0]
    block = jnp.arange(NBLK, dtype=jnp.int32)[:, None] * own_time[None, :]
    block = jnp.stack(phase(block, NBLK), axis=1)
    inner = jnp.arange(BLOCK, dtype=jnp.int32)[:, None] * own_time[None, :]
    inner = jnp.stack(phase(inner, N1))
    return pl.pallas_call(
        bank_kernel,
        grid=(NBLK // BLOCKS,),
        in_specs=[
            pl.BlockSpec((BLOCKS, 2, times), lambda b: (b, 0, 0)),
            pl.BlockSpec((2, BLOCK, times), lambda b: (0, 0, 0)),
        ],
        out_specs=[pl.BlockSpec((BLOCKS * 2 * BLOCK, 2 * times), lambda b: (b, 0))] * 2,
        out_shape=[jax.ShapeDtypeStruct((2 * N1, 2 * times), BF16)] * 2,
        compiler_params=pltpu.CompilerParams(vmem_limit_bytes=VMEM_LIMIT),
        cost_estimate=COST,
        name="bank_table",
    )(block, inner)


def bins_first_kernel(pieces, banks, place_ref, edge_ref, *refs):
    own_refs, rest_refs = refs[:pieces], refs[pieces : 2 * pieces]
    wh_ref, wl_ref, tw_ref = refs[2 * pieces : 2 * pieces + 3]
    level_ref, total_ref, xh, xl, acc = refs[-5:]
    times = total_ref.shape[-1]
    cols = own_refs[0].shape[0]
    length = 2 * N1 // banks
    chunk = FOUR * LANES
    step = pl.program_id(0)

    @pl.when(step == 0)
    def _():
        for k in range(pieces):
            row = pl.ds(pl.multiple_of((place_ref[0] ^ k) * cols, cols), cols)
            for n in range(banks):
                ref = rest_refs[k] if n else own_refs[k]
                start = lax.rem(place_ref[1] + n, banks) * length

                def cut(i, carry):
                    lane = max(n - 1, 0) * length + i * chunk
                    x = ref[:, pl.ds(pl.multiple_of(lane, chunk), chunk)]
                    to = pl.ds(pl.multiple_of(start + i * chunk, chunk), chunk)
                    xh[row, to], xl[row, to] = split(x)
                    return carry

                lax.fori_loop(0, length // chunk, cut, 0)
        total_ref[...] = jnp.zeros_like(total_ref)

    def blocks_at(block, blocks):
        at = pl.ds(pl.multiple_of(block * LANES, LANES), blocks * LANES)
        return dot3((xh[:, at], xl[:, at]), (wh_ref[at, :], wl_ref[at, :]))

    for i in range(TOGETHER):
        start, end = edge_ref[step * TOGETHER + i], edge_ref[step * TOGETHER + i + 1]
        odd = (end - start) % 2

        @pl.when(odd == 1)
        def _():
            acc[i] = blocks_at(end - 1, 1)

        @pl.when(odd == 0)
        def _():
            acc[i] = blocks_at(end - 2, 2)

        def two(n, carry):
            acc[i] += blocks_at(start + 2 * n, 2)
            return carry

        lax.fori_loop(0, (end - start - 1) // 2, two, 0)

    for u in range(pieces * cols // LANES):
        at = tile(u)
        cos, sin = tw_ref[0, at, :], tw_ref[1, at, :]
        sum_r, sum_i = total_ref[0, at, :], total_ref[1, at, :]
        for i in range(TOGETHER):
            re, im = acc[i, at, :times], acc[i, at, times:]
            vr, vi = re * cos - im * sin, re * sin + im * cos
            level_ref[i, 0, at, :] = vr
            level_ref[i, 1, at, :] = vi
            sum_r, sum_i = sum_r + vr, sum_i + vi
        total_ref[0, at, :] = sum_r
        total_ref[1, at, :] = sum_i


def bins_first(half, banks, place, edges, own, rest, table, twist, after):
    cols, length = rest[0].shape
    rows, times = twist.shape[1:]
    smem = pl.BlockSpec(memory_space=pltpu.SMEM)
    fixed = lambda shape: pl.BlockSpec(shape, lambda i: (0,) * len(shape))
    return pl.pallas_call(
        functools.partial(bins_first_kernel, len(own), banks),
        grid=(BINS // TOGETHER,),
        in_specs=[smem, smem]
        + [pl.BlockSpec((cols, 2 * N1 - length), lambda i: (half, 0))] * len(own)
        + [fixed((cols, length))] * len(rest)
        + [fixed((2 * N1, 2 * times))] * 2
        + [fixed((2, rows, times))]
        + [ANY] * len(after),
        out_specs=[
            pl.BlockSpec((TOGETHER, 2, rows, times), lambda i: (i, 0, 0, 0)),
            fixed((2, rows, times)),
        ],
        out_shape=[
            jax.ShapeDtypeStruct((BINS, 2, rows, times), F32),
            jax.ShapeDtypeStruct((2, rows, times), F32),
        ],
        scratch_shapes=[
            pltpu.VMEM((rows, 2 * N1), BF16),
            pltpu.VMEM((rows, 2 * N1), BF16),
            pltpu.VMEM((TOGETHER, rows, 2 * times), F32),
        ],
        compiler_params=pltpu.CompilerParams(vmem_limit_bytes=VMEM_LIMIT),
        cost_estimate=COST,
        name="bins_first",
    )(place, edges, *own, *rest, *table, twist, *after)


def bins_second_kernel(halves, which_ref, scale_ref, gain_ref, share_ref, *refs):
    level_refs, total_refs = refs[:halves], refs[halves : 2 * halves]
    w2h_ref, w2l_ref, out_ref, snr_ref, chi, hold = refs[2 * halves :]
    times = out_ref.shape[0]
    part_rows = LANES // halves
    step = pl.program_id(0)

    @pl.when(step == 0)
    def _():
        chi[...] = jnp.zeros_like(chi)

    def rows_of(get, u):
        at = slice(u * part_rows, (u + 1) * part_rows)
        return jnp.concatenate([get(h, at) for h in range(halves)], axis=0)

    def keep(a, re, im):
        chi[a] += re * re + im * im

    for i in range(TOGETHER):
        gain, share = gain_ref[step * TOGETHER + i], share_ref[step * TOGETHER + i]

        def deviation(p):
            return lambda h, at: (
                level_refs[h][i, p, at, :] * gain - total_refs[h][p, at, :] * share
            )

        x = [tuple(rows_of(deviation(p), u) for p in range(2)) for u in range(FOUR)]
        second_points(x, w2h_ref, w2l_ref, keep)

    @pl.when(step == BINS // TOGETHER - 1)
    def _():
        scale = scale_ref[which_ref[0]]

        def whole(p):
            return lambda h, at: total_refs[h][p, at, :] * scale

        def put(a, re, im):
            for p, value in enumerate((re, im)):
                for g in range(times // LANES):
                    hold[p, g, pl.ds(a, LANES, stride=FOUR), :] = value[:, tile(g)]

        y = [tuple(rows_of(whole(p), u) for p in range(2)) for u in range(FOUR)]
        second_points(y, w2h_ref, w2l_ref, put)
        for g in range(times // LANES):
            for a in range(FOUR):
                hold[2, g, pl.ds(a, LANES, stride=FOUR), :] = chi[a, :, tile(g)]
            for p in range(2):
                snr_ref[0, 0, p, tile(g), :] = hold[p, g].T
            out_ref[tile(g), :] = hold[2, g].T


def bins_second(which, scale, gain, share, levels, totals, second, tmpls, dets):
    _, _, rows, times = levels[0].shape
    halves = len(levels)
    smem = pl.BlockSpec(memory_space=pltpu.SMEM)
    fixed = lambda shape: pl.BlockSpec(shape, lambda i, w: (0,) * len(shape))
    return pl.pallas_call(
        functools.partial(bins_second_kernel, halves),
        grid_spec=pltpu.PrefetchScalarGridSpec(
            num_scalar_prefetch=1,
            grid=(BINS // TOGETHER,),
            in_specs=[smem, smem, smem]
            + [pl.BlockSpec((TOGETHER, 2, rows, times), lambda i, w: (i, 0, 0, 0))] * halves
            + [fixed((2, rows, times))] * halves
            + [fixed((FOUR * 2 * LANES, 2 * LANES))] * 2,
            out_specs=[
                fixed((times, N2)),
                pl.BlockSpec((1, 1, 2, times, N2), lambda i, w: (w[0], w[1], 0, 0, 0)),
            ],
            scratch_shapes=[
                pltpu.VMEM((FOUR, LANES, times), F32),
                pltpu.VMEM((3, times // LANES, N2, LANES), F32),
            ],
        ),
        out_shape=[
            jax.ShapeDtypeStruct((times, N2), F32),
            jax.ShapeDtypeStruct((tmpls, dets, 2, times, N2), F32),
        ],
        compiler_params=pltpu.CompilerParams(vmem_limit_bytes=VMEM_LIMIT),
        cost_estimate=COST,
        name="bins_second",
    )(which, scale, gain, share, *levels, *totals, *second)


def handed_on(arrays, after):
    count = len(arrays)
    return pl.pallas_call(
        lambda *refs: None,
        in_specs=[ANY] * (count + len(after)),
        out_specs=[ANY] * count,
        out_shape=[jax.ShapeDtypeStruct(x.shape, x.dtype) for x in arrays],
        input_output_aliases={i: i for i in range(count)},
        compiler_params=pltpu.CompilerParams(vmem_limit_bytes=VMEM_LIMIT),
        cost_estimate=COST,
        name="handed_on",
    )(*arrays, *after)


def swap(x, freq, k):
    return lax.ppermute(x, "freq", [(i, i ^ k) for i in range(freq)])


def far_pieces(own, freq):
    return [own] + [swap(own, freq, k) for k in range(2, freq, 2)]


def near_pieces(far, freq):
    return [x for even in far for x in (even, swap(even, freq, 1))]


def per_device(strain, templates, coinc_tmpl, coinc_det, bin_edges):
    freq, banks = lax.axis_size("freq"), lax.axis_size("bank")
    place = lax.axis_index("freq").astype(jnp.int32)
    bank = lax.axis_index("bank").astype(jnp.int32)
    tmpls, _, cols, _ = templates.shape
    slots, dets = coinc_tmpl.shape[0], strain.shape[0]
    times = N1 // freq
    part = cols // HALVES

    strains = [
        lax.all_gather(strain[:, :, h * part : (h + 1) * part], "bank", axis=0, tiled=False)
        for h in range(HALVES)
    ]
    first = tuple(jnp.asarray(t) for t in first_table())
    second = tuple(jnp.asarray(t) for t in second_table(cols, 1))
    second_halves = tuple(jnp.asarray(t) for t in second_table(cols, HALVES))
    stage = jnp.asarray(stage_table())

    power = (templates[:, 0] ** 2 + templates[:, 1] ** 2).sum(axis=1)
    local_power = power.reshape(tmpls, NBLK, BLOCK).sum(axis=2)
    block_power = lax.psum(local_power, "freq")
    sigma_sq = block_power.sum(axis=1)
    inv_sigma = lax.rsqrt(sigma_sq)
    bin_of = jnp.sum(
        jnp.arange(NBLK, dtype=jnp.int32)[None, :, None] >= bin_edges[:, None, :], axis=2
    )
    inside = bin_of[:, None, :] == jnp.arange(BINS, dtype=jnp.int32)[None, :, None]
    weights = jnp.where(inside, block_power[:, None, :], 0.0).sum(axis=2) / sigma_sq[:, None]

    column = place * cols + jnp.arange(cols, dtype=jnp.int32)
    lane = jnp.arange(N1, dtype=jnp.int32)
    time_of_lane = lane // LANES + COARSE * (lane % LANES)
    twist = jnp.stack(phase(column[:, None] * time_of_lane[None, :], N1 * N2))
    own_time = place * times + jnp.arange(times, dtype=jnp.int32)
    table = bank_table(own_time)
    own_twist = []
    for h in range(HALVES):
        rows = jnp.arange(freq * part, dtype=jnp.int32)
        rows = rows // part * cols + h * part + rows % part
        own_twist.append(jnp.stack(phase(rows[:, None] * own_time[None, :], N1 * N2)))

    which = [jnp.stack([coinc_tmpl[j], coinc_det[j], bank]) for j in range(slots)]
    series = jnp.arange(tmpls * dets - 1, dtype=jnp.int32)
    series = series + (series >= which[0][0] * dets + which[0][1])
    info = jnp.stack([series // dets, series % dets], axis=1).reshape(-1)
    info = jnp.concatenate([place.reshape(1), info])
    ends = jnp.zeros((1,), jnp.int32), jnp.full((1,), NBLK, jnp.int32)
    edges = [
        jnp.concatenate([ends[0], bin_edges[coinc_tmpl[j]], ends[1]]) for j in range(slots)
    ]
    here = jnp.stack([place, bank])

    own = [entry_product((0,), banks, 0, w, templates, strain[None], []) for w in which]
    own = [near_pieces(far_pieces(x, freq), freq) for x in own]
    gathered = [x for entry in own for x in entry[1:]]
    which, inv_sigma, weights, twist, info = lax.optimization_barrier(
        (which, inv_sigma, weights, twist, info)
    )

    rest, sent = [], []
    later = tuple(range(1, banks))
    for h in range(HALVES):
        after = gathered if h == 0 else gathered + [table[0], *own_twist]
        half = [entry_product(later, banks, h, w, templates, strains[h], after) for w in which]
        far = [far_pieces(x, freq) for x in half]
        *sent, token = first_section(
            freq, h, info, templates, strains[h], first, stage, twist, sent
        )
        far = [x[:1] + list(handed_on(x[1:], [token])) for x in far]
        rest.append([near_pieces(x, freq) for x in far])
        gathered = [x for entry in rest[-1] for x in entry[1:]]
    (ready,) = handed_on(sent, gathered)
    got = lax.all_to_all(
        ready.reshape(freq, -1, LANES), "freq", split_axis=0, concat_axis=0, tiled=True
    )
    got = got.reshape(ready.shape)

    chi, snr = [], None
    for j in range(slots):
        t = coinc_tmpl[j]
        halves = [
            bins_first(
                h, banks, here, edges[j], own[j], rest[h][j], table, own_twist[h], [ready]
            )
            for h in range(HALVES)
        ]
        levels, totals = zip(*halves)
        gain = inv_sigma[t] * lax.rsqrt(weights[t])
        share = gain * weights[t]
        one, series_of = bins_second(
            which[j], inv_sigma, gain, share, levels, totals, second_halves, tmpls, dets
        )
        chi.append(one)
        snr = series_of if snr is None else snr
    snr = second_section(freq, info, inv_sigma, [got], second, snr, chi)
    return (snr, jnp.stack(chi))


def solution(mesh):
    placed = (
        P(None, None, "freq", "bank"),
        P("bank", None, "freq", None),
        P("bank"),
        P("bank"),
        P("bank", None),
    )
    return jax.shard_map(
        per_device,
        mesh=mesh,
        in_specs=placed,
        out_specs=(P("bank", None, None, "freq", None), P("bank", "freq", None)),
        check_vma=False,
    )
```

```python
import functools

import jax
import jax.numpy as jnp
import ml_dtypes
import numpy as np
from jax import lax
from jax.experimental import pallas as pl
from jax.experimental.pallas import tpu as pltpu
from jax.sharding import PartitionSpec as P

N1 = 2048
N2 = 512
NBLK = 32
BLOCK = N1 // NBLK
BINS = 16
LANES = 128
COARSE = N1 // LANES
FOUR = N2 // LANES
F32 = jnp.float32
BF16 = jnp.bfloat16
MIB = 1 << 20
VMEM_LIMIT = 56 * MIB
ANY = pl.BlockSpec(memory_space=pl.ANY)
COST = pl.CostEstimate(flops=MIB, bytes_accessed=MIB, transcendentals=0)


def split_table(table):
    high = table.astype(ml_dtypes.bfloat16)
    low = (table - high.astype(np.float64)).astype(ml_dtypes.bfloat16)
    return high, low


def first_table():
    angle = 2 * np.pi * (np.outer(np.arange(LANES), np.arange(LANES)) % LANES) / LANES
    cos, sin = np.cos(angle), np.sin(angle)
    return split_table(np.block([[cos, sin], [-sin, cos]]))


def stage_table():
    angle = 2 * np.pi * np.outer(np.arange(COARSE), np.arange(LANES)) / N1
    return np.concatenate([np.cos(angle), np.sin(angle)]).astype(np.float32)


def second_table(cols, halves):
    order = np.arange(LANES).reshape(LANES // cols, halves, cols // halves)
    order = order.transpose(1, 0, 2).reshape(-1)
    blocks = []
    for a in range(FOUR):
        n2 = a + FOUR * np.arange(LANES)
        angle = 2 * np.pi * (np.outer(n2, order) % N2) / N2
        cos, sin = np.cos(angle), np.sin(angle)
        blocks.append(np.block([[cos, -sin], [sin, cos]]))
    return split_table(np.concatenate(blocks))


def split(x):
    high = x.astype(BF16)
    return high, (x - high.astype(F32)).astype(BF16)


def phase(index, length):
    angle = (index % length).astype(F32) * (2.0 * np.pi / length)
    return jnp.cos(angle), jnp.sin(angle)


def times_i(z):
    return (-z[1], z[0])


def plus(x, y):
    return (x[0] + y[0], x[1] + y[1])


def minus(x, y):
    return (x[0] - y[0], x[1] - y[1])


def dft4(x):
    s0, s1 = plus(x[0], x[2]), minus(x[0], x[2])
    s2, s3 = plus(x[1], x[3]), times_i(minus(x[1], x[3]))
    return [plus(s0, s2), plus(s1, s3), minus(s0, s2), minus(s1, s3)]


def turn(z, step):
    step %= 16
    if step == 0:
        return z
    if step == 4:
        return times_i(z)
    if step == 8:
        return (-z[0], -z[1])
    half = float(np.sqrt(0.5))
    if step == 2:
        return ((z[0] - z[1]) * half, (z[0] + z[1]) * half)
    if step == 6:
        return ((z[0] + z[1]) * -half, (z[0] - z[1]) * half)
    cos, sin = float(np.cos(np.pi * step / 8)), float(np.sin(np.pi * step / 8))
    return (z[0] * cos - z[1] * sin, z[0] * sin + z[1] * cos)


def dft16(x):
    columns = [dft4([x[4 * u1 + u0] for u1 in range(4)]) for u0 in range(4)]
    out = [None] * 16
    for a0 in range(4):
        ys = dft4([turn(columns[u0][a0], u0 * a0) for u0 in range(4)])
        for a1 in range(4):
            out[a0 + 4 * a1] = ys[a1]
    return out


def dot3(left, right):
    (lh, ll), (rh, rl) = left, right
    return jnp.dot(
        jnp.concatenate([lh, lh, ll], axis=1),
        jnp.concatenate([rh, rl, rh], axis=0),
        preferred_element_type=F32,
    )


def products(tmpl, strain_ref, where, rows=slice(None)):
    per_piece = COARSE // strain_ref.shape[0]
    for u in range(COARSE):
        off = u % per_piece
        there = slice(off * LANES, (off + 1) * LANES)
        hr, hi = tmpl(0, u), tmpl(1, u)
        sr = strain_ref[(u // per_piece,) + where + (0, rows, there)]
        si = strain_ref[(u // per_piece,) + where + (1, rows, there)]
        yield u, hr * sr + hi * si, hr * si - hi * sr


def tile(u):
    return slice(u * LANES, (u + 1) * LANES)


def first_kernel(
    freq, info_ref, tmpl_ref, strain_ref, wh_ref, wl_ref, stage_ref, tw_ref, *refs
):
    out_ref, token_ref, gh, gl, z = refs[-5:]
    token_ref[...] = jnp.zeros_like(token_ref)
    rows = tmpl_ref.shape[2]
    for r in range(0, rows, ROWS):
        at = slice(r, r + ROWS)
        got = products(lambda p, u: tmpl_ref[0, p, at, tile(u)], strain_ref, (0,), at)
        y = dft16([(re, im) for _, re, im in got])
        for a in range(COARSE):
            cos, sin = stage_ref[a : a + 1, :], stage_ref[COARSE + a : COARSE + a + 1, :]
            yr, yi = y[a]
            to = slice(a * rows + r, a * rows + r + ROWS)
            gh[to, :LANES], gl[to, :LANES] = split(yr * cos - yi * sin)
            gh[to, LANES:], gl[to, LANES:] = split(yr * sin + yi * cos)
    z[...] = dot3((gh[...], gl[...]), (wh_ref[...], wl_ref[...]))
    width = LANES // freq
    slot = lax.broadcasted_iota(jnp.int32, (ROWS, LANES), 1) // width
    for group in range(COARSE // freq):
        for r in range(0, rows, ROWS):
            at = slice(r, r + ROWS)
            turned = []
            for i in range(freq):
                a = group * freq + i
                to = slice(a * rows + r, a * rows + r + ROWS)
                zr, zi = z[to, :LANES], z[to, LANES:]
                cos, sin = tw_ref[0, at, tile(a)], tw_ref[1, at, tile(a)]
                pair = (zr * cos - zi * sin, zr * sin + zi * cos)
                if i:
                    pair = tuple(pltpu.roll(v, i * width, 1) for v in pair)
                turned.append(pair)
            for q in range(freq):
                for p in range(2):
                    value = turned[(0 - q) % freq][p]
                    for s in range(1, freq):
                        value = jnp.where(slot == s, turned[(s - q) % freq][p], value)
                    out_ref[q, 0, p, group, at] = value


ROWS = 16
HALVES = 2
TOGETHER = 4


def first_section(freq, half, info, templates, strain, first, stage, twist):
    tmpls = templates.shape[0]
    pieces, dets, _, rows, piece_len = strain.shape
    series = tmpls * dets - 1
    groups = COARSE // freq
    table = pl.BlockSpec((2 * LANES, 2 * LANES), lambda i, n: (0, 0))
    out = (freq, series, 2, groups, rows, LANES)
    return pl.pallas_call(
        functools.partial(first_kernel, freq),
        grid_spec=pltpu.PrefetchScalarGridSpec(
            num_scalar_prefetch=1,
            grid=(series,),
            in_specs=[
                pl.BlockSpec(
                    (1, 2, rows, N1), lambda i, n: (n[1 + 2 * i], 0, half, 0)
                ),
                pl.BlockSpec(
                    (pieces, 1, 2, rows, piece_len), lambda i, n: (0, n[2 + 2 * i], 0, 0, 0)
                ),
                table,
                table,
                pl.BlockSpec((2 * COARSE, LANES), lambda i, n: (0, 0)),
                pl.BlockSpec((2, rows, N1), lambda i, n: (0, half, 0)),
            ],
            out_specs=[
                pl.BlockSpec(
                    (freq, 1, 2, groups, rows, LANES), lambda i, n: (0, i, 0, 0, 0, 0)
                ),
                pl.BlockSpec((8, LANES), lambda i, n: (0, 0)),
            ],
            scratch_shapes=[
                pltpu.VMEM((COARSE * rows, 2 * LANES), BF16),
                pltpu.VMEM((COARSE * rows, 2 * LANES), BF16),
                pltpu.VMEM((COARSE * rows, 2 * LANES), F32),
            ],
        ),
        out_shape=[
            jax.ShapeDtypeStruct(out, F32),
            jax.ShapeDtypeStruct((8, LANES), F32),
        ],
        compiler_params=pltpu.CompilerParams(vmem_limit_bytes=VMEM_LIMIT),
        cost_estimate=pl.CostEstimate(
            flops=60 * series * rows * N1 * LANES, bytes_accessed=16 * MIB, transcendentals=0
        ),
        name="first_section",
    )(info, templates, strain, first[0], first[1], stage, twist)


def entry_kernel(steps, banks, which_ref, tmpl_ref, strain_ref, *refs):
    out_ref = refs[-1]
    length = N1 // banks
    first_half = lax.broadcasted_iota(jnp.int32, (ROWS, LANES), 1) < BLOCK
    for n, k in enumerate(steps):
        part = lax.rem(which_ref[2] + k, banks)
        for u in range(length // LANES):
            lane = pl.ds(pl.multiple_of(part * length + u * LANES, LANES), LANES)
            hr, hi = tmpl_ref[0, 0, :, lane], tmpl_ref[0, 1, :, lane]
            piece = 0 if strain_ref.shape[0] == 1 else part
            sr, si = strain_ref[piece, 0, 0, :, tile(u)], strain_ref[piece, 0, 1, :, tile(u)]
            re, im = hr * sr + hi * si, hr * si - hi * sr
            to = 2 * (n * length // LANES + u)
            out_ref[:, tile(to)] = jnp.where(first_half, re, pltpu.roll(im, BLOCK, 1))
            out_ref[:, tile(to + 1)] = jnp.where(first_half, pltpu.roll(re, BLOCK, 1), im)


def entry_product(steps, banks, half, which, templates, strain, after):
    pieces, _, _, cols, length = strain.shape
    first = half * cols // ROWS
    return pl.pallas_call(
        functools.partial(entry_kernel, steps, banks),
        grid_spec=pltpu.PrefetchScalarGridSpec(
            num_scalar_prefetch=1,
            grid=(cols // ROWS,),
            in_specs=[
                pl.BlockSpec((1, 2, ROWS, N1), lambda c, w: (w[0], 0, first + c, 0)),
                pl.BlockSpec((pieces, 1, 2, ROWS, length), lambda c, w: (0, w[1], 0, c, 0)),
            ]
            + [ANY] * len(after),
            out_specs=pl.BlockSpec((ROWS, 2 * length * len(steps)), lambda c, w: (c, 0)),
        ),
        out_shape=jax.ShapeDtypeStruct((cols, 2 * length * len(steps)), F32),
        compiler_params=pltpu.CompilerParams(vmem_limit_bytes=VMEM_LIMIT),
        cost_estimate=COST,
        name="entry_product",
    )(which, templates, strain, *after)


def second_points(x, w2h_ref, w2l_ref, use):
    for a, (yr, yi) in enumerate(dft4(x)):
        y = jnp.concatenate([yr, yi], axis=0)
        at = slice(a * 2 * LANES, (a + 1) * 2 * LANES)
        z = dot3((w2h_ref[at, :], w2l_ref[at, :]), split(y))
        use(a, z[:LANES], z[LANES:])


def second_kernel(freq, halves, info_ref, scale_ref, *refs):
    part_refs, (w2h_ref, w2l_ref) = refs[:halves], refs[halves : halves + 2]
    out_ref, hold, order = refs[-3:]
    place = info_ref[0]
    groups, cols = part_refs[0].shape[3:5]
    per = LANES // (halves * cols)
    width = LANES // freq
    scale = scale_ref[info_ref[1 + 2 * pl.program_id(0)]]

    def rows_of(p, u):
        tiles = [
            jnp.concatenate(
                [ref[u * per + f, 0, p, g] for ref in part_refs for f in range(per)],
                axis=0,
            )
            for g in range(groups)
        ]
        return jnp.concatenate(tiles, axis=1)

    x = [(rows_of(0, u), rows_of(1, u)) for u in range(FOUR)]

    def keep(a, re, im):
        for p, value in enumerate((re, im)):
            for g in range(groups):
                hold[p, g, pl.ds(a, LANES, stride=FOUR), :] = value[:, tile(g)] * scale

    second_points(x, w2h_ref, w2l_ref, keep)
    for p in range(2):
        for g in range(groups):
            turned = hold[p, g].T
            for s in range(freq):
                a = g * freq + lax.rem(s - place + freq, freq)
                for j in range(FOUR):
                    order[p, j, pl.ds(a, width, stride=COARSE), :] = turned[
                        s * width : (s + 1) * width, tile(j)
                    ]
        for j in range(FOUR):
            out_ref[0, 0, p, :, tile(j)] = order[p, j]


def second_section(freq, info, scale, parts, second, snr, after):
    _, series, _, groups, cols, _ = parts[0].shape
    halves = len(parts)
    times = groups * LANES
    smem = pl.BlockSpec(memory_space=pltpu.SMEM)
    table = pl.BlockSpec((FOUR * 2 * LANES, 2 * LANES), lambda i, n: (0, 0))
    part = pl.BlockSpec(
        (freq, 1, 2, groups, cols, LANES), lambda i, n: (0, i, 0, 0, 0, 0)
    )
    return pl.pallas_call(
        functools.partial(second_kernel, freq, halves),
        grid_spec=pltpu.PrefetchScalarGridSpec(
            num_scalar_prefetch=1,
            grid=(series,),
            in_specs=[smem] + [part] * halves + [table, table, ANY] + [ANY] * len(after),
            out_specs=pl.BlockSpec(
                (1, 1, 2, times, N2), lambda i, n: (n[1 + 2 * i], n[2 + 2 * i], 0, 0, 0)
            ),
            scratch_shapes=[
                pltpu.VMEM((2, groups, N2, LANES), F32),
                pltpu.VMEM((2, FOUR, times, LANES), F32),
            ],
        ),
        out_shape=jax.ShapeDtypeStruct(snr.shape, F32),
        input_output_aliases={4 + halves: 0},
        compiler_params=pltpu.CompilerParams(vmem_limit_bytes=VMEM_LIMIT),
        cost_estimate=COST,
        name="second_section",
    )(info, scale, *parts, *second, snr, *after)


BLOCKS = 4


def bank_kernel(block_ref, inner_ref, high_ref, low_ref):
    times = block_ref.shape[-1]
    rc, rs = inner_ref[0], inner_ref[1]
    for b in range(BLOCKS):
        bc, bs = block_ref[b, 0:1, :], block_ref[b, 1:2, :]
        cos, sin = split(bc * rc - bs * rs), split(bc * rs + bs * rc)
        top = slice(2 * b * BLOCK, (2 * b + 1) * BLOCK)
        low = slice((2 * b + 1) * BLOCK, (2 * b + 2) * BLOCK)
        for ref, c, s in zip((high_ref, low_ref), cos, sin):
            ref[top, :times] = c
            ref[top, times:] = s
            ref[low, :times] = -s
            ref[low, times:] = c


def bank_table(own_time):
    times = own_time.shape[0]
    block = jnp.arange(NBLK, dtype=jnp.int32)[:, None] * own_time[None, :]
    block = jnp.stack(phase(block, NBLK), axis=1)
    inner = jnp.arange(BLOCK, dtype=jnp.int32)[:, None] * own_time[None, :]
    inner = jnp.stack(phase(inner, N1))
    return pl.pallas_call(
        bank_kernel,
        grid=(NBLK // BLOCKS,),
        in_specs=[
            pl.BlockSpec((BLOCKS, 2, times), lambda b: (b, 0, 0)),
            pl.BlockSpec((2, BLOCK, times), lambda b: (0, 0, 0)),
        ],
        out_specs=[pl.BlockSpec((BLOCKS * 2 * BLOCK, 2 * times), lambda b: (b, 0))] * 2,
        out_shape=[jax.ShapeDtypeStruct((2 * N1, 2 * times), BF16)] * 2,
        compiler_params=pltpu.CompilerParams(vmem_limit_bytes=VMEM_LIMIT),
        cost_estimate=COST,
        name="bank_table",
    )(block, inner)


def bins_first_kernel(pieces, banks, place_ref, edge_ref, *refs):
    own_refs, rest_refs = refs[:pieces], refs[pieces : 2 * pieces]
    wh_ref, wl_ref, tw_ref = refs[2 * pieces : 2 * pieces + 3]
    level_ref, total_ref, xh, xl, acc = refs[-5:]
    times = total_ref.shape[-1]
    cols = own_refs[0].shape[0]
    length = 2 * N1 // banks
    chunk = FOUR * LANES
    step = pl.program_id(0)

    @pl.when(step == 0)
    def _():
        for k in range(pieces):
            row = pl.ds(pl.multiple_of((place_ref[0] ^ k) * cols, cols), cols)
            for n in range(banks):
                ref = rest_refs[k] if n else own_refs[k]
                start = lax.rem(place_ref[1] + n, banks) * length

                def cut(i, carry):
                    lane = max(n - 1, 0) * length + i * chunk
                    x = ref[:, pl.ds(pl.multiple_of(lane, chunk), chunk)]
                    to = pl.ds(pl.multiple_of(start + i * chunk, chunk), chunk)
                    xh[row, to], xl[row, to] = split(x)
                    return carry

                lax.fori_loop(0, length // chunk, cut, 0)
        total_ref[...] = jnp.zeros_like(total_ref)

    def blocks_at(block, blocks):
        at = pl.ds(pl.multiple_of(block * LANES, LANES), blocks * LANES)
        return dot3((xh[:, at], xl[:, at]), (wh_ref[at, :], wl_ref[at, :]))

    for i in range(TOGETHER):
        start, end = edge_ref[step * TOGETHER + i], edge_ref[step * TOGETHER + i + 1]
        odd = (end - start) % 2

        @pl.when(odd == 1)
        def _():
            acc[i] = blocks_at(end - 1, 1)

        @pl.when(odd == 0)
        def _():
            acc[i] = blocks_at(end - 2, 2)

        def two(n, carry):
            acc[i] += blocks_at(start + 2 * n, 2)
            return carry

        lax.fori_loop(0, (end - start - 1) // 2, two, 0)

    for u in range(pieces * cols // LANES):
        at = tile(u)
        cos, sin = tw_ref[0, at, :], tw_ref[1, at, :]
        sum_r, sum_i = total_ref[0, at, :], total_ref[1, at, :]
        for i in range(TOGETHER):
            re, im = acc[i, at, :times], acc[i, at, times:]
            vr, vi = re * cos - im * sin, re * sin + im * cos
            level_ref[i, 0, at, :] = vr
            level_ref[i, 1, at, :] = vi
            sum_r, sum_i = sum_r + vr, sum_i + vi
        total_ref[0, at, :] = sum_r
        total_ref[1, at, :] = sum_i


def bins_first(half, banks, place, edges, own, rest, table, twist, after):
    cols, length = rest[0].shape
    rows, times = twist.shape[1:]
    smem = pl.BlockSpec(memory_space=pltpu.SMEM)
    fixed = lambda shape: pl.BlockSpec(shape, lambda i: (0,) * len(shape))
    return pl.pallas_call(
        functools.partial(bins_first_kernel, len(own), banks),
        grid=(BINS // TOGETHER,),
        in_specs=[smem, smem]
        + [pl.BlockSpec((cols, 2 * N1 - length), lambda i: (half, 0))] * len(own)
        + [fixed((cols, length))] * len(rest)
        + [fixed((2 * N1, 2 * times))] * 2
        + [fixed((2, rows, times))]
        + [ANY] * len(after),
        out_specs=[
            pl.BlockSpec((TOGETHER, 2, rows, times), lambda i: (i, 0, 0, 0)),
            fixed((2, rows, times)),
        ],
        out_shape=[
            jax.ShapeDtypeStruct((BINS, 2, rows, times), F32),
            jax.ShapeDtypeStruct((2, rows, times), F32),
        ],
        scratch_shapes=[
            pltpu.VMEM((rows, 2 * N1), BF16),
            pltpu.VMEM((rows, 2 * N1), BF16),
            pltpu.VMEM((TOGETHER, rows, 2 * times), F32),
        ],
        compiler_params=pltpu.CompilerParams(vmem_limit_bytes=VMEM_LIMIT),
        cost_estimate=COST,
        name="bins_first",
    )(place, edges, *own, *rest, *table, twist, *after)


def bins_second_kernel(halves, which_ref, scale_ref, gain_ref, share_ref, *refs):
    level_refs, total_refs = refs[:halves], refs[halves : 2 * halves]
    w2h_ref, w2l_ref, out_ref, snr_ref, chi, hold = refs[2 * halves :]
    times = out_ref.shape[0]
    part_rows = LANES // halves
    step = pl.program_id(0)

    @pl.when(step == 0)
    def _():
        chi[...] = jnp.zeros_like(chi)

    def rows_of(get, u):
        at = slice(u * part_rows, (u + 1) * part_rows)
        return jnp.concatenate([get(h, at) for h in range(halves)], axis=0)

    def keep(a, re, im):
        chi[a] += re * re + im * im

    for i in range(TOGETHER):
        gain, share = gain_ref[step * TOGETHER + i], share_ref[step * TOGETHER + i]

        def deviation(p):
            return lambda h, at: (
                level_refs[h][i, p, at, :] * gain - total_refs[h][p, at, :] * share
            )

        x = [tuple(rows_of(deviation(p), u) for p in range(2)) for u in range(FOUR)]
        second_points(x, w2h_ref, w2l_ref, keep)

    @pl.when(step == BINS // TOGETHER - 1)
    def _():
        scale = scale_ref[which_ref[0]]

        def whole(p):
            return lambda h, at: total_refs[h][p, at, :] * scale

        def put(a, re, im):
            for p, value in enumerate((re, im)):
                for g in range(times // LANES):
                    hold[p, g, pl.ds(a, LANES, stride=FOUR), :] = value[:, tile(g)]

        y = [tuple(rows_of(whole(p), u) for p in range(2)) for u in range(FOUR)]
        second_points(y, w2h_ref, w2l_ref, put)
        for g in range(times // LANES):
            for a in range(FOUR):
                hold[2, g, pl.ds(a, LANES, stride=FOUR), :] = chi[a, :, tile(g)]
            for p in range(2):
                snr_ref[0, 0, p, tile(g), :] = hold[p, g].T
            out_ref[tile(g), :] = hold[2, g].T


def bins_second(which, scale, gain, share, levels, totals, second, tmpls, dets):
    _, _, rows, times = levels[0].shape
    halves = len(levels)
    smem = pl.BlockSpec(memory_space=pltpu.SMEM)
    fixed = lambda shape: pl.BlockSpec(shape, lambda i, w: (0,) * len(shape))
    return pl.pallas_call(
        functools.partial(bins_second_kernel, halves),
        grid_spec=pltpu.PrefetchScalarGridSpec(
            num_scalar_prefetch=1,
            grid=(BINS // TOGETHER,),
            in_specs=[smem, smem, smem]
            + [pl.BlockSpec((TOGETHER, 2, rows, times), lambda i, w: (i, 0, 0, 0))] * halves
            + [fixed((2, rows, times))] * halves
            + [fixed((FOUR * 2 * LANES, 2 * LANES))] * 2,
            out_specs=[
                fixed((times, N2)),
                pl.BlockSpec((1, 1, 2, times, N2), lambda i, w: (w[0], w[1], 0, 0, 0)),
            ],
            scratch_shapes=[
                pltpu.VMEM((FOUR, LANES, times), F32),
                pltpu.VMEM((3, times // LANES, N2, LANES), F32),
            ],
        ),
        out_shape=[
            jax.ShapeDtypeStruct((times, N2), F32),
            jax.ShapeDtypeStruct((tmpls, dets, 2, times, N2), F32),
        ],
        compiler_params=pltpu.CompilerParams(vmem_limit_bytes=VMEM_LIMIT),
        cost_estimate=COST,
        name="bins_second",
    )(which, scale, gain, share, *levels, *totals, *second)


def handed_on(arrays, after):
    count = len(arrays)
    return pl.pallas_call(
        lambda *refs: None,
        in_specs=[ANY] * (count + len(after)),
        out_specs=[ANY] * count,
        out_shape=[jax.ShapeDtypeStruct(x.shape, x.dtype) for x in arrays],
        input_output_aliases={i: i for i in range(count)},
        compiler_params=pltpu.CompilerParams(vmem_limit_bytes=VMEM_LIMIT),
        cost_estimate=COST,
        name="handed_on",
    )(*arrays, *after)


def swap(x, freq, k):
    return lax.ppermute(x, "freq", [(i, i ^ k) for i in range(freq)])


def far_pieces(own, freq):
    return [own] + [swap(own, freq, k) for k in range(2, freq, 2)]


def near_pieces(far, freq):
    return [x for even in far for x in (even, swap(even, freq, 1))]


def per_device(strain, templates, coinc_tmpl, coinc_det, bin_edges):
    freq, banks = lax.axis_size("freq"), lax.axis_size("bank")
    place = lax.axis_index("freq").astype(jnp.int32)
    bank = lax.axis_index("bank").astype(jnp.int32)
    tmpls, _, cols, _ = templates.shape
    slots, dets = coinc_tmpl.shape[0], strain.shape[0]
    times = N1 // freq
    part = cols // HALVES

    strains = [
        lax.all_gather(strain[:, :, h * part : (h + 1) * part], "bank", axis=0, tiled=False)
        for h in range(HALVES)
    ]
    first = tuple(jnp.asarray(t) for t in first_table())
    second = tuple(jnp.asarray(t) for t in second_table(cols, HALVES))
    stage = jnp.asarray(stage_table())

    column = place * cols + jnp.arange(cols, dtype=jnp.int32)
    lane = jnp.arange(N1, dtype=jnp.int32)
    time_of_lane = lane // LANES + COARSE * (lane % LANES)
    twist = jnp.stack(phase(column[:, None] * time_of_lane[None, :], N1 * N2))
    own_time = place * times + jnp.arange(times, dtype=jnp.int32)
    table = bank_table(own_time)
    own_twist = []
    for h in range(HALVES):
        rows = jnp.arange(freq * part, dtype=jnp.int32)
        rows = rows // part * cols + h * part + rows % part
        own_twist.append(jnp.stack(phase(rows[:, None] * own_time[None, :], N1 * N2)))

    which = [jnp.stack([coinc_tmpl[j], coinc_det[j], bank]) for j in range(slots)]
    series = jnp.arange(tmpls * dets - 1, dtype=jnp.int32)
    series = series + (series >= which[0][0] * dets + which[0][1])
    info = jnp.stack([series // dets, series % dets], axis=1).reshape(-1)
    info = jnp.concatenate([place.reshape(1), info])
    ends = jnp.zeros((1,), jnp.int32), jnp.full((1,), NBLK, jnp.int32)
    edges = [
        jnp.concatenate([ends[0], bin_edges[coinc_tmpl[j]], ends[1]]) for j in range(slots)
    ]
    here = jnp.stack([place, bank])

    power = (templates[:, 0] ** 2 + templates[:, 1] ** 2).sum(axis=1)
    power = power.reshape(tmpls, NBLK, BLOCK).sum(axis=2)
    own = [entry_product((0,), banks, 0, w, templates, strain[None], []) for w in which]
    wide = own[0].shape[1]
    power = jnp.pad(power.reshape(1, -1), ((0, 7), (0, wide - tmpls * NBLK)))
    own[0] = jnp.concatenate([own[0], power], axis=0)
    own = [near_pieces(far_pieces(x, freq), freq) for x in own]
    gathered = [x for entry in own for x in entry[1:]]

    block_power = sum(x[cols, : tmpls * NBLK] for x in own[0]).reshape(tmpls, NBLK)
    sigma_sq = block_power.sum(axis=1)
    inv_sigma = lax.rsqrt(sigma_sq)
    bin_of = jnp.sum(
        jnp.arange(NBLK, dtype=jnp.int32)[None, :, None] >= bin_edges[:, None, :], axis=2
    )
    inside = bin_of[:, None, :] == jnp.arange(BINS, dtype=jnp.int32)[None, :, None]
    weights = jnp.where(inside, block_power[:, None, :], 0.0).sum(axis=2) / sigma_sq[:, None]
    gains = [inv_sigma[coinc_tmpl[j]] * lax.rsqrt(weights[coinc_tmpl[j]]) for j in range(slots)]
    shares = [gains[j] * weights[coinc_tmpl[j]] for j in range(slots)]
    which, inv_sigma, gains, shares, twist, info, edges, here, table, own_twist = (
        lax.optimization_barrier(
            (which, inv_sigma, gains, shares, twist, info, edges, here, table, own_twist)
        )
    )

    parts, halves = [], []
    later = tuple(range(1, banks))
    for h in range(HALVES):
        after = [x[0] for x in halves[-1]] if halves else gathered
        half = [entry_product(later, banks, h, w, templates, strains[h], after) for w in which]
        far = [far_pieces(x, freq) for x in half]
        sent, token = first_section(freq, h, info, templates, strains[h], first, stage, twist)
        far = [x[:1] + list(handed_on(x[1:], [token] + parts)) for x in far]
        rest = [near_pieces(x, freq) for x in far]
        (ready,) = handed_on([sent], [x for entry in rest for x in entry[1:]])
        got = lax.all_to_all(
            ready.reshape(freq, -1, LANES), "freq", split_axis=0, concat_axis=0, tiled=True
        )
        parts.append(got.reshape(ready.shape))
        halves.append(
            [
                bins_first(
                    h, banks, here, edges[j], own[j], rest[j], table, own_twist[h], [ready]
                )
                for j in range(slots)
            ]
        )

    chi, snr = [], None
    for j in range(slots):
        levels, totals = zip(*[x[j] for x in halves])
        one, series_of = bins_second(
            which[j], inv_sigma, gains[j], shares[j], levels, totals, second, tmpls, dets
        )
        chi.append(one)
        snr = series_of if snr is None else snr
    snr = second_section(freq, info, inv_sigma, parts, second, snr, chi)
    return (snr, jnp.stack(chi))


def solution(mesh):
    placed = (
        P(None, None, "freq", "bank"),
        P("bank", None, "freq", None),
        P("bank"),
        P("bank"),
        P("bank", None),
    )
    return jax.shard_map(
        per_device,
        mesh=mesh,
        in_specs=placed,
        out_specs=(P("bank", None, None, "freq", None), P("bank", "freq", None)),
        check_vma=False,
    )
```

```python
import functools

import jax
import jax.numpy as jnp
import ml_dtypes
import numpy as np
from jax import lax
from jax.experimental import pallas as pl
from jax.experimental.pallas import tpu as pltpu
from jax.sharding import PartitionSpec as P

N1 = 2048
N2 = 512
NBLK = 32
BLOCK = N1 // NBLK
BINS = 16
LANES = 128
COARSE = N1 // LANES
FOUR = N2 // LANES
F32 = jnp.float32
BF16 = jnp.bfloat16
MIB = 1 << 20
VMEM_LIMIT = 56 * MIB
ANY = pl.BlockSpec(memory_space=pl.ANY)
COST = pl.CostEstimate(flops=MIB, bytes_accessed=MIB, transcendentals=0)


def split_table(table):
    high = table.astype(ml_dtypes.bfloat16)
    low = (table - high.astype(np.float64)).astype(ml_dtypes.bfloat16)
    return high, low


def first_table():
    angle = 2 * np.pi * (np.outer(np.arange(LANES), np.arange(LANES)) % LANES) / LANES
    cos, sin = np.cos(angle), np.sin(angle)
    return split_table(np.block([[cos, sin], [-sin, cos]]))


def stage_table():
    angle = 2 * np.pi * np.outer(np.arange(COARSE), np.arange(LANES)) / N1
    return np.concatenate([np.cos(angle), np.sin(angle)]).astype(np.float32)


def second_table(cols, halves):
    order = np.arange(LANES).reshape(LANES // cols, halves, cols // halves)
    order = order.transpose(1, 0, 2).reshape(-1)
    blocks = []
    for a in range(FOUR):
        n2 = a + FOUR * np.arange(LANES)
        angle = 2 * np.pi * (np.outer(n2, order) % N2) / N2
        cos, sin = np.cos(angle), np.sin(angle)
        blocks.append(np.block([[cos, -sin], [sin, cos]]))
    return split_table(np.concatenate(blocks))


def split(x):
    high = x.astype(BF16)
    return high, (x - high.astype(F32)).astype(BF16)


def phase(index, length):
    angle = (index % length).astype(F32) * (2.0 * np.pi / length)
    return jnp.cos(angle), jnp.sin(angle)


def times_i(z):
    return (-z[1], z[0])


def plus(x, y):
    return (x[0] + y[0], x[1] + y[1])


def minus(x, y):
    return (x[0] - y[0], x[1] - y[1])


def dft4(x):
    s0, s1 = plus(x[0], x[2]), minus(x[0], x[2])
    s2, s3 = plus(x[1], x[3]), times_i(minus(x[1], x[3]))
    return [plus(s0, s2), plus(s1, s3), minus(s0, s2), minus(s1, s3)]


def turn(z, step):
    step %= 16
    if step == 0:
        return z
    if step == 4:
        return times_i(z)
    if step == 8:
        return (-z[0], -z[1])
    half = float(np.sqrt(0.5))
    if step == 2:
        return ((z[0] - z[1]) * half, (z[0] + z[1]) * half)
    if step == 6:
        return ((z[0] + z[1]) * -half, (z[0] - z[1]) * half)
    cos, sin = float(np.cos(np.pi * step / 8)), float(np.sin(np.pi * step / 8))
    return (z[0] * cos - z[1] * sin, z[0] * sin + z[1] * cos)


def dft16(x):
    columns = [dft4([x[4 * u1 + u0] for u1 in range(4)]) for u0 in range(4)]
    out = [None] * 16
    for a0 in range(4):
        ys = dft4([turn(columns[u0][a0], u0 * a0) for u0 in range(4)])
        for a1 in range(4):
            out[a0 + 4 * a1] = ys[a1]
    return out


def dot3(left, right):
    (lh, ll), (rh, rl) = left, right
    return jnp.dot(
        jnp.concatenate([lh, lh, ll], axis=1),
        jnp.concatenate([rh, rl, rh], axis=0),
        preferred_element_type=F32,
    )


def products(tmpl, strain_ref, where, rows=slice(None)):
    per_piece = COARSE // strain_ref.shape[0]
    for u in range(COARSE):
        off = u % per_piece
        there = slice(off * LANES, (off + 1) * LANES)
        hr, hi = tmpl(0, u), tmpl(1, u)
        sr = strain_ref[(u // per_piece,) + where + (0, rows, there)]
        si = strain_ref[(u // per_piece,) + where + (1, rows, there)]
        yield u, hr * sr + hi * si, hr * si - hi * sr


def tile(u):
    return slice(u * LANES, (u + 1) * LANES)


def first_kernel(
    freq, info_ref, tmpl_ref, strain_ref, wh_ref, wl_ref, stage_ref, tw_ref, *refs
):
    out_ref, token_ref, gh, gl, z = refs[-5:]
    token_ref[...] = jnp.zeros_like(token_ref)
    rows = tmpl_ref.shape[2]
    for r in range(0, rows, ROWS):
        at = slice(r, r + ROWS)
        got = products(lambda p, u: tmpl_ref[0, p, at, tile(u)], strain_ref, (0,), at)
        y = dft16([(re, im) for _, re, im in got])
        for a in range(COARSE):
            cos, sin = stage_ref[a : a + 1, :], stage_ref[COARSE + a : COARSE + a + 1, :]
            yr, yi = y[a]
            to = slice(a * rows + r, a * rows + r + ROWS)
            gh[to, :LANES], gl[to, :LANES] = split(yr * cos - yi * sin)
            gh[to, LANES:], gl[to, LANES:] = split(yr * sin + yi * cos)
    z[...] = dot3((gh[...], gl[...]), (wh_ref[...], wl_ref[...]))
    width = LANES // freq
    slot = lax.broadcasted_iota(jnp.int32, (ROWS, LANES), 1) // width
    for group in range(COARSE // freq):
        for r in range(0, rows, ROWS):
            at = slice(r, r + ROWS)
            turned = []
            for i in range(freq):
                a = group * freq + i
                to = slice(a * rows + r, a * rows + r + ROWS)
                zr, zi = z[to, :LANES], z[to, LANES:]
                cos, sin = tw_ref[0, at, tile(a)], tw_ref[1, at, tile(a)]
                pair = (zr * cos - zi * sin, zr * sin + zi * cos)
                if i:
                    pair = tuple(pltpu.roll(v, i * width, 1) for v in pair)
                turned.append(pair)
            for q in range(freq):
                for p in range(2):
                    value = turned[(0 - q) % freq][p]
                    for s in range(1, freq):
                        value = jnp.where(slot == s, turned[(s - q) % freq][p], value)
                    out_ref[q, 0, p, group, at] = value


ROWS = 16
HALVES = 2
TOGETHER = 2


def first_section(freq, half, lot, slot, slots, info, templates, strain, first, stage, twist, earlier, after):
    pieces, _, _, rows, piece_len = strain.shape
    base, series = lot[0], len(lot)
    groups = COARSE // freq
    table = pl.BlockSpec((2 * LANES, 2 * LANES), lambda i, n: (0, 0))
    out = (freq, slots, 2, groups, rows, LANES)
    return pl.pallas_call(
        functools.partial(first_kernel, freq),
        grid_spec=pltpu.PrefetchScalarGridSpec(
            num_scalar_prefetch=1,
            grid=(series,),
            in_specs=[
                pl.BlockSpec(
                    (1, 2, rows, N1), lambda i, n: (n[1 + 2 * (base + i)], 0, half, 0)
                ),
                pl.BlockSpec(
                    (pieces, 1, 2, rows, piece_len), lambda i, n: (0, n[2 + 2 * (base + i)], 0, 0, 0)
                ),
                table,
                table,
                pl.BlockSpec((2 * COARSE, LANES), lambda i, n: (0, 0)),
                pl.BlockSpec((2, rows, N1), lambda i, n: (0, half, 0)),
            ]
            + [ANY] * (len(earlier) + len(after)),
            out_specs=[
                pl.BlockSpec(
                    (freq, 1, 2, groups, rows, LANES), lambda i, n: (0, slot + i, 0, 0, 0, 0)
                ),
                pl.BlockSpec((8, LANES), lambda i, n: (0, 0)),
            ],
            scratch_shapes=[
                pltpu.VMEM((COARSE * rows, 2 * LANES), BF16),
                pltpu.VMEM((COARSE * rows, 2 * LANES), BF16),
                pltpu.VMEM((COARSE * rows, 2 * LANES), F32),
            ],
        ),
        out_shape=[
            jax.ShapeDtypeStruct(out, F32),
            jax.ShapeDtypeStruct((8, LANES), F32),
        ],
        input_output_aliases={7: 0} if earlier else {},
        compiler_params=pltpu.CompilerParams(vmem_limit_bytes=VMEM_LIMIT),
        cost_estimate=pl.CostEstimate(
            flops=60 * series * rows * N1 * LANES, bytes_accessed=16 * MIB, transcendentals=0
        ),
        name="first_section",
    )(info, templates, strain, first[0], first[1], stage, twist, *earlier, *after)


def entry_kernel(steps, banks, which_ref, tmpl_ref, strain_ref, *refs):
    out_ref = refs[-1]
    length = N1 // banks
    first_half = lax.broadcasted_iota(jnp.int32, (ROWS, LANES), 1) < BLOCK
    for n, k in enumerate(steps):
        part = lax.rem(which_ref[2] + k, banks)
        for u in range(length // LANES):
            lane = pl.ds(pl.multiple_of(part * length + u * LANES, LANES), LANES)
            hr, hi = tmpl_ref[0, 0, :, lane], tmpl_ref[0, 1, :, lane]
            piece = 0 if strain_ref.shape[0] == 1 else part
            sr, si = strain_ref[piece, 0, 0, :, tile(u)], strain_ref[piece, 0, 1, :, tile(u)]
            re, im = hr * sr + hi * si, hr * si - hi * sr
            to = 2 * (n * length // LANES + u)
            out_ref[:, tile(to)] = jnp.where(first_half, re, pltpu.roll(im, BLOCK, 1))
            out_ref[:, tile(to + 1)] = jnp.where(first_half, pltpu.roll(re, BLOCK, 1), im)


def entry_product(steps, banks, half, which, templates, strain, after):
    pieces, _, _, cols, length = strain.shape
    first = half * cols // ROWS
    return pl.pallas_call(
        functools.partial(entry_kernel, steps, banks),
        grid_spec=pltpu.PrefetchScalarGridSpec(
            num_scalar_prefetch=1,
            grid=(cols // ROWS,),
            in_specs=[
                pl.BlockSpec((1, 2, ROWS, N1), lambda c, w: (w[0], 0, first + c, 0)),
                pl.BlockSpec((pieces, 1, 2, ROWS, length), lambda c, w: (0, w[1], 0, c, 0)),
            ]
            + [ANY] * len(after),
            out_specs=pl.BlockSpec((ROWS, 2 * length * len(steps)), lambda c, w: (c, 0)),
        ),
        out_shape=jax.ShapeDtypeStruct((cols, 2 * length * len(steps)), F32),
        compiler_params=pltpu.CompilerParams(vmem_limit_bytes=VMEM_LIMIT),
        cost_estimate=COST,
        name="entry_product",
    )(which, templates, strain, *after)


def second_points(x, w2h_ref, w2l_ref, use):
    for a, (yr, yi) in enumerate(dft4(x)):
        y = jnp.concatenate([yr, yi], axis=0)
        at = slice(a * 2 * LANES, (a + 1) * 2 * LANES)
        z = dot3((w2h_ref[at, :], w2l_ref[at, :]), split(y))
        use(a, z[:LANES], z[LANES:])


def second_kernel(freq, base, halves, info_ref, scale_ref, *refs):
    part_refs, (w2h_ref, w2l_ref) = refs[:halves], refs[halves : halves + 2]
    out_ref, hold, order = refs[-3:]
    place = info_ref[0]
    groups, cols = part_refs[0].shape[3:5]
    per = LANES // (halves * cols)
    width = LANES // freq
    scale = scale_ref[info_ref[1 + 2 * (base + pl.program_id(0))]]

    def rows_of(p, u):
        tiles = [
            jnp.concatenate(
                [ref[u * per + f, 0, p, g] for ref in part_refs for f in range(per)],
                axis=0,
            )
            for g in range(groups)
        ]
        return jnp.concatenate(tiles, axis=1)

    x = [(rows_of(0, u), rows_of(1, u)) for u in range(FOUR)]

    def keep(a, re, im):
        for p, value in enumerate((re, im)):
            for g in range(groups):
                hold[p, g, pl.ds(a, LANES, stride=FOUR), :] = value[:, tile(g)] * scale

    second_points(x, w2h_ref, w2l_ref, keep)
    for p in range(2):
        for g in range(groups):
            turned = hold[p, g].T
            for s in range(freq):
                a = g * freq + lax.rem(s - place + freq, freq)
                for j in range(FOUR):
                    order[p, j, pl.ds(a, width, stride=COARSE), :] = turned[
                        s * width : (s + 1) * width, tile(j)
                    ]
        for j in range(FOUR):
            out_ref[0, 0, p, :, tile(j)] = order[p, j]


def second_section(freq, lot, info, scale, parts, second, snr, after):
    parts, firsts = zip(*parts)
    base, series = lot[0], len(lot)
    _, _, _, groups, cols, _ = parts[0].shape
    halves = len(parts)
    times = groups * LANES
    smem = pl.BlockSpec(memory_space=pltpu.SMEM)
    table = pl.BlockSpec((FOUR * 2 * LANES, 2 * LANES), lambda i, n: (0, 0))


    def part(slot):
        return pl.BlockSpec(
            (freq, 1, 2, groups, cols, LANES), lambda i, n: (0, slot + i, 0, 0, 0, 0)
        )

    return pl.pallas_call(
        functools.partial(second_kernel, freq, base, halves),
        grid_spec=pltpu.PrefetchScalarGridSpec(
            num_scalar_prefetch=1,
            grid=(series,),
            in_specs=[smem] + [part(x) for x in firsts] + [table, table, ANY] + [ANY] * len(after),
            out_specs=pl.BlockSpec(
                (1, 1, 2, times, N2), lambda i, n: (n[1 + 2 * (base + i)], n[2 + 2 * (base + i)], 0, 0, 0)
            ),
            scratch_shapes=[
                pltpu.VMEM((2, groups, N2, LANES), F32),
                pltpu.VMEM((2, FOUR, times, LANES), F32),
            ],
        ),
        out_shape=jax.ShapeDtypeStruct(snr.shape, F32),
        input_output_aliases={4 + halves: 0},
        compiler_params=pltpu.CompilerParams(vmem_limit_bytes=VMEM_LIMIT),
        cost_estimate=COST,
        name="second_section",
    )(info, scale, *parts, *second, snr, *after)


BLOCKS = 4


def bank_kernel(block_ref, inner_ref, high_ref, low_ref):
    times = block_ref.shape[-1]
    rc, rs = inner_ref[0], inner_ref[1]
    for b in range(BLOCKS):
        bc, bs = block_ref[b, 0:1, :], block_ref[b, 1:2, :]
        cos, sin = split(bc * rc - bs * rs), split(bc * rs + bs * rc)
        top = slice(2 * b * BLOCK, (2 * b + 1) * BLOCK)
        low = slice((2 * b + 1) * BLOCK, (2 * b + 2) * BLOCK)
        for ref, c, s in zip((high_ref, low_ref), cos, sin):
            ref[top, :times] = c
            ref[top, times:] = s
            ref[low, :times] = -s
            ref[low, times:] = c


def bank_table(own_time):
    times = own_time.shape[0]
    block = jnp.arange(NBLK, dtype=jnp.int32)[:, None] * own_time[None, :]
    block = jnp.stack(phase(block, NBLK), axis=1)
    inner = jnp.arange(BLOCK, dtype=jnp.int32)[:, None] * own_time[None, :]
    inner = jnp.stack(phase(inner, N1))
    return pl.pallas_call(
        bank_kernel,
        grid=(NBLK // BLOCKS,),
        in_specs=[
            pl.BlockSpec((BLOCKS, 2, times), lambda b: (b, 0, 0)),
            pl.BlockSpec((2, BLOCK, times), lambda b: (0, 0, 0)),
        ],
        out_specs=[pl.BlockSpec((BLOCKS * 2 * BLOCK, 2 * times), lambda b: (b, 0))] * 2,
        out_shape=[jax.ShapeDtypeStruct((2 * N1, 2 * times), BF16)] * 2,
        compiler_params=pltpu.CompilerParams(vmem_limit_bytes=VMEM_LIMIT),
        cost_estimate=COST,
        name="bank_table",
    )(block, inner)


def bins_first_kernel(pieces, banks, place_ref, edge_ref, *refs):
    own_refs, rest_refs = refs[:pieces], refs[pieces : 2 * pieces]
    wh_ref, wl_ref, tw_ref = refs[2 * pieces : 2 * pieces + 3]
    level_ref, total_ref, xh, xl, acc = refs[-5:]
    times = total_ref.shape[-1]
    cols = own_refs[0].shape[0]
    length = 2 * N1 // banks
    chunk = FOUR * LANES
    step = pl.program_id(0)

    @pl.when(step == 0)
    def _():
        for k in range(pieces):
            row = pl.ds(pl.multiple_of((place_ref[0] ^ k) * cols, cols), cols)
            for n in range(banks):
                ref = rest_refs[k] if n else own_refs[k]
                start = lax.rem(place_ref[1] + n, banks) * length

                def cut(i, carry):
                    lane = max(n - 1, 0) * length + i * chunk
                    x = ref[:, pl.ds(pl.multiple_of(lane, chunk), chunk)]
                    to = pl.ds(pl.multiple_of(start + i * chunk, chunk), chunk)
                    xh[row, to], xl[row, to] = split(x)
                    return carry

                lax.fori_loop(0, length // chunk, cut, 0)
        total_ref[...] = jnp.zeros_like(total_ref)

    def blocks_at(block, blocks):
        at = pl.ds(pl.multiple_of(block * LANES, LANES), blocks * LANES)
        return dot3((xh[:, at], xl[:, at]), (wh_ref[at, :], wl_ref[at, :]))

    for i in range(TOGETHER):
        start, end = edge_ref[step * TOGETHER + i], edge_ref[step * TOGETHER + i + 1]
        odd = (end - start) % 2

        @pl.when(odd == 1)
        def _():
            acc[i] = blocks_at(end - 1, 1)

        @pl.when(odd == 0)
        def _():
            acc[i] = blocks_at(end - 2, 2)

        def two(n, carry):
            acc[i] += blocks_at(start + 2 * n, 2)
            return carry

        lax.fori_loop(0, (end - start - 1) // 2, two, 0)

    for u in range(pieces * cols // LANES):
        at = tile(u)
        cos, sin = tw_ref[0, at, :], tw_ref[1, at, :]
        sum_r, sum_i = total_ref[0, at, :], total_ref[1, at, :]
        for i in range(TOGETHER):
            re, im = acc[i, at, :times], acc[i, at, times:]
            vr, vi = re * cos - im * sin, re * sin + im * cos
            level_ref[i, 0, at, :] = vr
            level_ref[i, 1, at, :] = vi
            sum_r, sum_i = sum_r + vr, sum_i + vi
        total_ref[0, at, :] = sum_r
        total_ref[1, at, :] = sum_i


def bins_first(half, banks, place, edges, own, rest, table, twist, after):
    cols, length = rest[0].shape
    rows, times = twist.shape[1:]
    smem = pl.BlockSpec(memory_space=pltpu.SMEM)
    fixed = lambda shape: pl.BlockSpec(shape, lambda i: (0,) * len(shape))
    return pl.pallas_call(
        functools.partial(bins_first_kernel, len(own), banks),
        grid=(BINS // TOGETHER,),
        in_specs=[smem, smem]
        + [pl.BlockSpec((cols, 2 * N1 - length), lambda i: (half, 0))] * len(own)
        + [fixed((cols, length))] * len(rest)
        + [fixed((2 * N1, 2 * times))] * 2
        + [fixed((2, rows, times))]
        + [ANY] * len(after),
        out_specs=[
            pl.BlockSpec((TOGETHER, 2, rows, times), lambda i: (i, 0, 0, 0)),
            fixed((2, rows, times)),
        ],
        out_shape=[
            jax.ShapeDtypeStruct((BINS, 2, rows, times), F32),
            jax.ShapeDtypeStruct((2, rows, times), F32),
        ],
        scratch_shapes=[
            pltpu.VMEM((rows, 2 * N1), BF16),
            pltpu.VMEM((rows, 2 * N1), BF16),
            pltpu.VMEM((TOGETHER, rows, 2 * times), F32),
        ],
        compiler_params=pltpu.CompilerParams(vmem_limit_bytes=VMEM_LIMIT),
        cost_estimate=COST,
        name="bins_first",
    )(place, edges, *own, *rest, *table, twist, *after)


def bins_second_kernel(halves, which_ref, scale_ref, gain_ref, share_ref, *refs):
    level_refs, total_refs = refs[:halves], refs[halves : 2 * halves]
    w2h_ref, w2l_ref, out_ref, snr_ref, chi, hold = refs[2 * halves :]
    times = out_ref.shape[0]
    part_rows = LANES // halves
    step = pl.program_id(0)

    @pl.when(step == 0)
    def _():
        chi[...] = jnp.zeros_like(chi)

    def rows_of(get, u):
        at = slice(u * part_rows, (u + 1) * part_rows)
        return jnp.concatenate([get(h, at) for h in range(halves)], axis=0)

    def keep(a, re, im):
        chi[a] += re * re + im * im

    for i in range(TOGETHER):
        gain, share = gain_ref[step * TOGETHER + i], share_ref[step * TOGETHER + i]

        def deviation(p):
            return lambda h, at: (
                level_refs[h][i, p, at, :] * gain - total_refs[h][p, at, :] * share
            )

        x = [tuple(rows_of(deviation(p), u) for p in range(2)) for u in range(FOUR)]
        second_points(x, w2h_ref, w2l_ref, keep)

    @pl.when(step == BINS // TOGETHER - 1)
    def _():
        scale = scale_ref[which_ref[0]]

        def whole(p):
            return lambda h, at: total_refs[h][p, at, :] * scale

        def put(a, re, im):
            for p, value in enumerate((re, im)):
                for g in range(times // LANES):
                    hold[p, g, pl.ds(a, LANES, stride=FOUR), :] = value[:, tile(g)]

        y = [tuple(rows_of(whole(p), u) for p in range(2)) for u in range(FOUR)]
        second_points(y, w2h_ref, w2l_ref, put)
        for g in range(times // LANES):
            for a in range(FOUR):
                hold[2, g, pl.ds(a, LANES, stride=FOUR), :] = chi[a, :, tile(g)]
            for p in range(2):
                snr_ref[0, 0, p, tile(g), :] = hold[p, g].T
            out_ref[tile(g), :] = hold[2, g].T


def bins_second(which, scale, gain, share, levels, totals, second, tmpls, dets):
    _, _, rows, times = levels[0].shape
    halves = len(levels)
    smem = pl.BlockSpec(memory_space=pltpu.SMEM)
    fixed = lambda shape: pl.BlockSpec(shape, lambda i, w: (0,) * len(shape))
    return pl.pallas_call(
        functools.partial(bins_second_kernel, halves),
        grid_spec=pltpu.PrefetchScalarGridSpec(
            num_scalar_prefetch=1,
            grid=(BINS // TOGETHER,),
            in_specs=[smem, smem, smem]
            + [pl.BlockSpec((TOGETHER, 2, rows, times), lambda i, w: (i, 0, 0, 0))] * halves
            + [fixed((2, rows, times))] * halves
            + [fixed((FOUR * 2 * LANES, 2 * LANES))] * 2,
            out_specs=[
                fixed((times, N2)),
                pl.BlockSpec((1, 1, 2, times, N2), lambda i, w: (w[0], w[1], 0, 0, 0)),
            ],
            scratch_shapes=[
                pltpu.VMEM((FOUR, LANES, times), F32),
                pltpu.VMEM((3, times // LANES, N2, LANES), F32),
            ],
        ),
        out_shape=[
            jax.ShapeDtypeStruct((times, N2), F32),
            jax.ShapeDtypeStruct((tmpls, dets, 2, times, N2), F32),
        ],
        compiler_params=pltpu.CompilerParams(vmem_limit_bytes=VMEM_LIMIT),
        cost_estimate=COST,
        name="bins_second",
    )(which, scale, gain, share, *levels, *totals, *second)


def handed_on(arrays, after):
    count = len(arrays)
    return pl.pallas_call(
        lambda *refs: None,
        in_specs=[ANY] * (count + len(after)),
        out_specs=[ANY] * count,
        out_shape=[jax.ShapeDtypeStruct(x.shape, x.dtype) for x in arrays],
        input_output_aliases={i: i for i in range(count)},
        compiler_params=pltpu.CompilerParams(vmem_limit_bytes=VMEM_LIMIT),
        cost_estimate=COST,
        name="handed_on",
    )(*arrays, *after)


def swap(x, freq, k):
    return lax.ppermute(x, "freq", [(i, i ^ k) for i in range(freq)])


def far_pieces(own, freq):
    return [own] + [swap(own, freq, k) for k in range(2, freq, 2)]


def near_pieces(far, freq):
    return [x for even in far for x in (even, swap(even, freq, 1))]


def per_device(strain, templates, coinc_tmpl, coinc_det, bin_edges):
    freq, banks = lax.axis_size("freq"), lax.axis_size("bank")
    place = lax.axis_index("freq").astype(jnp.int32)
    bank = lax.axis_index("bank").astype(jnp.int32)
    tmpls, _, cols, _ = templates.shape
    slots, dets = coinc_tmpl.shape[0], strain.shape[0]
    times = N1 // freq
    part = cols // HALVES

    slices = [strain[:, :, h * part : (h + 1) * part] for h in range(HALVES)]
    strains = [lax.all_gather(x, "bank", axis=0, tiled=False) for x in slices]
    first = tuple(jnp.asarray(t) for t in first_table())
    second = tuple(jnp.asarray(t) for t in second_table(cols, HALVES))
    stage = jnp.asarray(stage_table())

    column = place * cols + jnp.arange(cols, dtype=jnp.int32)
    lane = jnp.arange(N1, dtype=jnp.int32)
    time_of_lane = lane // LANES + COARSE * (lane % LANES)
    twist = jnp.stack(phase(column[:, None] * time_of_lane[None, :], N1 * N2))
    own_time = place * times + jnp.arange(times, dtype=jnp.int32)
    table = bank_table(own_time)
    own_twist = []
    for h in range(HALVES):
        rows = jnp.arange(freq * part, dtype=jnp.int32)
        rows = rows // part * cols + h * part + rows % part
        own_twist.append(jnp.stack(phase(rows[:, None] * own_time[None, :], N1 * N2)))

    which = [jnp.stack([coinc_tmpl[j], coinc_det[j], bank]) for j in range(slots)]
    series = jnp.arange(tmpls * dets - 1, dtype=jnp.int32)
    series = series + (series >= which[0][0] * dets + which[0][1])
    info = jnp.stack([series // dets, series % dets], axis=1).reshape(-1)
    info = jnp.concatenate([place.reshape(1), info])
    ends = jnp.zeros((1,), jnp.int32), jnp.full((1,), NBLK, jnp.int32)
    edges = [
        jnp.concatenate([ends[0], bin_edges[coinc_tmpl[j]], ends[1]]) for j in range(slots)
    ]
    here = jnp.stack([place, bank])

    power = (templates[:, 0] ** 2 + templates[:, 1] ** 2).sum(axis=1)
    power = power.reshape(tmpls, NBLK, BLOCK).sum(axis=2)
    own = [entry_product((0,), banks, 0, w, templates, strain[None], slices) for w in which]
    wide = own[0].shape[1]
    power = jnp.pad(power.reshape(1, -1), ((0, 7), (0, wide - tmpls * NBLK)))
    own[0] = jnp.concatenate([own[0], power], axis=0)
    own = [near_pieces(far_pieces(x, freq), freq) for x in own]
    gathered = [x for entry in own for x in entry[1:]]

    block_power = sum(x[cols, : tmpls * NBLK] for x in own[0]).reshape(tmpls, NBLK)
    sigma_sq = block_power.sum(axis=1)
    inv_sigma = lax.rsqrt(sigma_sq)
    bin_of = jnp.sum(
        jnp.arange(NBLK, dtype=jnp.int32)[None, :, None] >= bin_edges[:, None, :], axis=2
    )
    inside = bin_of[:, None, :] == jnp.arange(BINS, dtype=jnp.int32)[None, :, None]
    weights = jnp.where(inside, block_power[:, None, :], 0.0).sum(axis=2) / sigma_sq[:, None]
    gains = [inv_sigma[coinc_tmpl[j]] * lax.rsqrt(weights[coinc_tmpl[j]]) for j in range(slots)]
    shares = [gains[j] * weights[coinc_tmpl[j]] for j in range(slots)]
    which, inv_sigma, gains, shares, twist, info, edges, here, table, own_twist = (
        lax.optimization_barrier(
            (which, inv_sigma, gains, shares, twist, info, edges, here, table, own_twist)
        )
    )

    def exchange(x):
        got = lax.all_to_all(
            x.reshape(freq, -1, LANES), "freq", split_axis=0, concat_axis=0, tiled=True
        )
        return got.reshape(x.shape)

    early = range((tmpls * dets + 1) // 2)
    late = range(len(early), tmpls * dets - 1)
    parts, halves, last = [], [], []
    later = tuple(range(1, banks))
    for h in range(HALVES):
        after = [x[0] for x in halves[-1]] if halves else gathered
        half = [entry_product(later, banks, h, w, templates, strains[h], after) for w in which]
        far = [far_pieces(x, freq) for x in half]
        fixed = info, templates, strains[h], first, stage, twist
        sent, token = first_section(freq, h, early, 0, len(early), *fixed, [], half)
        *last, token2 = first_section(
            freq, h, late, h * len(late), HALVES * len(late), *fixed, last, half
        )
        far = [x[:1] + list(handed_on(x[1:], [token, token2] + parts)) for x in far]
        rest = [near_pieces(x, freq) for x in far]
        (ready,) = handed_on([sent], [x for entry in rest for x in entry[1:]])
        parts.append(exchange(ready))
        halves.append(
            [
                bins_first(
                    h, banks, here, edges[j], own[j], rest[j], table, own_twist[h], [ready]
                )
                for j in range(slots)
            ]
        )
    last = exchange(handed_on(last, [parts[-1]] + [x[1] for x in halves[-1]])[0])

    chi, snr = [], None
    for j in range(slots):
        levels, totals = zip(*[x[j] for x in halves])
        one, series_of = bins_second(
            which[j], inv_sigma, gains[j], shares[j], levels, totals, second, tmpls, dets
        )
        chi.append(one)
        snr = series_of if snr is None else snr
    parts = [(x, 0) for x in parts]
    snr = second_section(freq, early, info, inv_sigma, parts, second, snr, chi)
    parts = [(last, h * len(late)) for h in range(HALVES)]
    snr = second_section(freq, late, info, inv_sigma, parts, second, snr, [])
    return (snr, jnp.stack(chi))


def solution(mesh):
    placed = (
        P(None, None, "freq", "bank"),
        P("bank", None, "freq", None),
        P("bank"),
        P("bank"),
        P("bank", None),
    )
    return jax.shard_map(
        per_device,
        mesh=mesh,
        in_specs=placed,
        out_specs=(P("bank", None, None, "freq", None), P("bank", "freq", None)),
        check_vma=False,
    )
```

```python
import functools

import jax
import jax.numpy as jnp
import ml_dtypes
import numpy as np
from jax import lax
from jax.experimental import pallas as pl
from jax.experimental.pallas import tpu as pltpu
from jax.sharding import PartitionSpec as P

N1 = 2048
N2 = 512
NBLK = 32
BLOCK = N1 // NBLK
BINS = 16
LANES = 128
COARSE = N1 // LANES
FOUR = N2 // LANES
F32 = jnp.float32
BF16 = jnp.bfloat16
MIB = 1 << 20
VMEM_LIMIT = 56 * MIB
ANY = pl.BlockSpec(memory_space=pl.ANY)
COST = pl.CostEstimate(flops=MIB, bytes_accessed=MIB, transcendentals=0)


def split_table(table):
    high = table.astype(ml_dtypes.bfloat16)
    low = (table - high.astype(np.float64)).astype(ml_dtypes.bfloat16)
    return high, low


def first_table():
    angle = 2 * np.pi * (np.outer(np.arange(LANES), np.arange(LANES)) % LANES) / LANES
    cos, sin = np.cos(angle), np.sin(angle)
    return split_table(np.block([[cos, sin], [-sin, cos]]))


def stage_table():
    angle = 2 * np.pi * np.outer(np.arange(COARSE), np.arange(LANES)) / N1
    return np.concatenate([np.cos(angle), np.sin(angle)]).astype(np.float32)


def second_table(cols, halves):
    order = np.arange(LANES).reshape(LANES // cols, halves, cols // halves)
    order = order.transpose(1, 0, 2).reshape(-1)
    blocks = []
    for a in range(FOUR):
        n2 = a + FOUR * np.arange(LANES)
        angle = 2 * np.pi * (np.outer(n2, order) % N2) / N2
        cos, sin = np.cos(angle), np.sin(angle)
        blocks.append(np.block([[cos, -sin], [sin, cos]]))
    return split_table(np.concatenate(blocks))


def split(x):
    high = x.astype(BF16)
    return high, (x - high.astype(F32)).astype(BF16)


def phase(index, length):
    angle = (index % length).astype(F32) * (2.0 * np.pi / length)
    return jnp.cos(angle), jnp.sin(angle)


def times_i(z):
    return (-z[1], z[0])


def plus(x, y):
    return (x[0] + y[0], x[1] + y[1])


def minus(x, y):
    return (x[0] - y[0], x[1] - y[1])


def dft4(x):
    s0, s1 = plus(x[0], x[2]), minus(x[0], x[2])
    s2, s3 = plus(x[1], x[3]), times_i(minus(x[1], x[3]))
    return [plus(s0, s2), plus(s1, s3), minus(s0, s2), minus(s1, s3)]


def turn(z, step):
    step %= 16
    if step == 0:
        return z
    if step == 4:
        return times_i(z)
    if step == 8:
        return (-z[0], -z[1])
    half = float(np.sqrt(0.5))
    if step == 2:
        return ((z[0] - z[1]) * half, (z[0] + z[1]) * half)
    if step == 6:
        return ((z[0] + z[1]) * -half, (z[0] - z[1]) * half)
    cos, sin = float(np.cos(np.pi * step / 8)), float(np.sin(np.pi * step / 8))
    return (z[0] * cos - z[1] * sin, z[0] * sin + z[1] * cos)


def dft16(x):
    columns = [dft4([x[4 * u1 + u0] for u1 in range(4)]) for u0 in range(4)]
    out = [None] * 16
    for a0 in range(4):
        ys = dft4([turn(columns[u0][a0], u0 * a0) for u0 in range(4)])
        for a1 in range(4):
            out[a0 + 4 * a1] = ys[a1]
    return out


def dot3(left, right):
    (lh, ll), (rh, rl) = left, right
    return jnp.dot(
        jnp.concatenate([lh, lh, ll], axis=1),
        jnp.concatenate([rh, rl, rh], axis=0),
        preferred_element_type=F32,
    )


def products(tmpl, strain_ref, where, rows=slice(None)):
    per_piece = COARSE // strain_ref.shape[0]
    for u in range(COARSE):
        off = u % per_piece
        there = slice(off * LANES, (off + 1) * LANES)
        hr, hi = tmpl(0, u), tmpl(1, u)
        sr = strain_ref[(u // per_piece,) + where + (0, rows, there)]
        si = strain_ref[(u // per_piece,) + where + (1, rows, there)]
        yield u, hr * sr + hi * si, hr * si - hi * sr


def tile(u):
    return slice(u * LANES, (u + 1) * LANES)


def first_kernel(
    freq, info_ref, tmpl_ref, strain_ref, wh_ref, wl_ref, stage_ref, tw_ref, *refs
):
    out_ref, token_ref, gh, gl, z = refs[-5:]
    token_ref[...] = jnp.zeros_like(token_ref)
    rows = tmpl_ref.shape[2]
    for r in range(0, rows, ROWS):
        at = slice(r, r + ROWS)
        got = products(lambda p, u: tmpl_ref[0, p, at, tile(u)], strain_ref, (0,), at)
        y = dft16([(re, im) for _, re, im in got])
        for a in range(COARSE):
            cos, sin = stage_ref[a : a + 1, :], stage_ref[COARSE + a : COARSE + a + 1, :]
            yr, yi = y[a]
            to = slice(a * rows + r, a * rows + r + ROWS)
            gh[to, :LANES], gl[to, :LANES] = split(yr * cos - yi * sin)
            gh[to, LANES:], gl[to, LANES:] = split(yr * sin + yi * cos)
    z[...] = dot3((gh[...], gl[...]), (wh_ref[...], wl_ref[...]))
    width = LANES // freq
    slot = lax.broadcasted_iota(jnp.int32, (ROWS, LANES), 1) // width
    for group in range(COARSE // freq):
        for r in range(0, rows, ROWS):
            at = slice(r, r + ROWS)
            turned = []
            for i in range(freq):
                a = group * freq + i
                to = slice(a * rows + r, a * rows + r + ROWS)
                zr, zi = z[to, :LANES], z[to, LANES:]
                cos, sin = tw_ref[0, at, tile(a)], tw_ref[1, at, tile(a)]
                pair = (zr * cos - zi * sin, zr * sin + zi * cos)
                if i:
                    pair = tuple(pltpu.roll(v, i * width, 1) for v in pair)
                turned.append(pair)
            for q in range(freq):
                for p in range(2):
                    value = turned[(0 - q) % freq][p]
                    for s in range(1, freq):
                        value = jnp.where(slot == s, turned[(s - q) % freq][p], value)
                    out_ref[q, 0, p, group, at] = value


ROWS = 16
LOTS = 2
TOGETHER = 2


def first_section(freq, start, info, templates, strain, first, stage, twist, earlier, after):
    tmpls, _, cols, _ = templates.shape
    pieces, dets, _, rows, piece_len = strain.shape
    block, series = start // rows, tmpls * dets - 1
    groups = COARSE // freq
    table = pl.BlockSpec((2 * LANES, 2 * LANES), lambda i, n: (0, 0))
    out = (freq, series, 2, groups, cols, LANES)
    return pl.pallas_call(
        functools.partial(first_kernel, freq),
        grid_spec=pltpu.PrefetchScalarGridSpec(
            num_scalar_prefetch=1,
            grid=(series,),
            in_specs=[
                pl.BlockSpec(
                    (1, 2, rows, N1), lambda i, n: (n[1 + 2 * (i)], 0, block, 0)
                ),
                pl.BlockSpec(
                    (pieces, 1, 2, rows, piece_len), lambda i, n: (0, n[2 + 2 * (i)], 0, 0, 0)
                ),
                table,
                table,
                pl.BlockSpec((2 * COARSE, LANES), lambda i, n: (0, 0)),
                pl.BlockSpec((2, rows, N1), lambda i, n: (0, block, 0)),
            ]
            + [ANY] * (len(earlier) + len(after)),
            out_specs=[
                pl.BlockSpec(
                    (freq, 1, 2, groups, rows, LANES), lambda i, n: (0, i, 0, 0, block, 0)
                ),
                pl.BlockSpec((8, LANES), lambda i, n: (0, 0)),
            ],
            scratch_shapes=[
                pltpu.VMEM((COARSE * rows, 2 * LANES), BF16),
                pltpu.VMEM((COARSE * rows, 2 * LANES), BF16),
                pltpu.VMEM((COARSE * rows, 2 * LANES), F32),
            ],
        ),
        out_shape=[
            jax.ShapeDtypeStruct(out, F32),
            jax.ShapeDtypeStruct((8, LANES), F32),
        ],
        input_output_aliases={7: 0} if earlier else {},
        compiler_params=pltpu.CompilerParams(vmem_limit_bytes=VMEM_LIMIT),
        cost_estimate=pl.CostEstimate(
            flops=60 * series * rows * N1 * LANES, bytes_accessed=16 * MIB, transcendentals=0
        ),
        name="first_section",
    )(info, templates, strain, first[0], first[1], stage, twist, *earlier, *after)


def entry_kernel(steps, banks, which_ref, tmpl_ref, strain_ref, *refs):
    out_ref = refs[-1]
    length = N1 // banks
    first_half = lax.broadcasted_iota(jnp.int32, (ROWS, LANES), 1) < BLOCK
    for n, k in enumerate(steps):
        part = lax.rem(which_ref[2] + k, banks)
        for u in range(length // LANES):
            lane = pl.ds(pl.multiple_of(part * length + u * LANES, LANES), LANES)
            hr, hi = tmpl_ref[0, 0, :, lane], tmpl_ref[0, 1, :, lane]
            piece = 0 if strain_ref.shape[0] == 1 else part
            sr, si = strain_ref[piece, 0, 0, :, tile(u)], strain_ref[piece, 0, 1, :, tile(u)]
            re, im = hr * sr + hi * si, hr * si - hi * sr
            to = 2 * (n * length // LANES + u)
            out_ref[:, tile(to)] = jnp.where(first_half, re, pltpu.roll(im, BLOCK, 1))
            out_ref[:, tile(to + 1)] = jnp.where(first_half, pltpu.roll(re, BLOCK, 1), im)


def entry_product(steps, banks, start, which, templates, strain, after):
    pieces, _, _, cols, length = strain.shape
    first = start // ROWS
    return pl.pallas_call(
        functools.partial(entry_kernel, steps, banks),
        grid_spec=pltpu.PrefetchScalarGridSpec(
            num_scalar_prefetch=1,
            grid=(cols // ROWS,),
            in_specs=[
                pl.BlockSpec((1, 2, ROWS, N1), lambda c, w: (w[0], 0, first + c, 0)),
                pl.BlockSpec((pieces, 1, 2, ROWS, length), lambda c, w: (0, w[1], 0, c, 0)),
            ]
            + [ANY] * len(after),
            out_specs=pl.BlockSpec((ROWS, 2 * length * len(steps)), lambda c, w: (c, 0)),
        ),
        out_shape=jax.ShapeDtypeStruct((cols, 2 * length * len(steps)), F32),
        compiler_params=pltpu.CompilerParams(vmem_limit_bytes=VMEM_LIMIT),
        cost_estimate=COST,
        name="entry_product",
    )(which, templates, strain, *after)


def second_points(x, w2h_ref, w2l_ref, use):
    for a, (yr, yi) in enumerate(dft4(x)):
        y = jnp.concatenate([yr, yi], axis=0)
        at = slice(a * 2 * LANES, (a + 1) * 2 * LANES)
        z = dot3((w2h_ref[at, :], w2l_ref[at, :]), split(y))
        use(a, z[:LANES], z[LANES:])


def second_kernel(freq, halves, info_ref, scale_ref, *refs):
    part_refs, (w2h_ref, w2l_ref) = refs[:halves], refs[halves : halves + 2]
    out_ref, hold, order = refs[-3:]
    place = info_ref[0]
    groups, cols = part_refs[0].shape[3:5]
    per = LANES // (halves * cols)
    width = LANES // freq
    scale = scale_ref[info_ref[1 + 2 * pl.program_id(0)]]

    def rows_of(p, u):
        tiles = [
            jnp.concatenate(
                [ref[u * per + f, 0, p, g] for ref in part_refs for f in range(per)],
                axis=0,
            )
            for g in range(groups)
        ]
        return jnp.concatenate(tiles, axis=1)

    x = [(rows_of(0, u), rows_of(1, u)) for u in range(FOUR)]

    def keep(a, re, im):
        for p, value in enumerate((re, im)):
            for g in range(groups):
                hold[p, g, pl.ds(a, LANES, stride=FOUR), :] = value[:, tile(g)] * scale

    second_points(x, w2h_ref, w2l_ref, keep)
    for p in range(2):
        for g in range(groups):
            turned = hold[p, g].T
            for s in range(freq):
                a = g * freq + lax.rem(s - place + freq, freq)
                for j in range(FOUR):
                    order[p, j, pl.ds(a, width, stride=COARSE), :] = turned[
                        s * width : (s + 1) * width, tile(j)
                    ]
        for j in range(FOUR):
            out_ref[0, 0, p, :, tile(j)] = order[p, j]


def second_section(freq, info, scale, parts, second, snr, after):
    _, series, _, groups, cols, _ = parts[0].shape
    halves = len(parts)
    times = groups * LANES
    smem = pl.BlockSpec(memory_space=pltpu.SMEM)
    table = pl.BlockSpec((FOUR * 2 * LANES, 2 * LANES), lambda i, n: (0, 0))


    part = pl.BlockSpec(
        (freq, 1, 2, groups, cols, LANES), lambda i, n: (0, i, 0, 0, 0, 0)
    )
    return pl.pallas_call(
        functools.partial(second_kernel, freq, halves),
        grid_spec=pltpu.PrefetchScalarGridSpec(
            num_scalar_prefetch=1,
            grid=(series,),
            in_specs=[smem] + [part] * halves + [table, table, ANY] + [ANY] * len(after),
            out_specs=pl.BlockSpec(
                (1, 1, 2, times, N2), lambda i, n: (n[1 + 2 * i], n[2 + 2 * i], 0, 0, 0)
            ),
            scratch_shapes=[
                pltpu.VMEM((2, groups, N2, LANES), F32),
                pltpu.VMEM((2, FOUR, times, LANES), F32),
            ],
        ),
        out_shape=jax.ShapeDtypeStruct(snr.shape, F32),
        input_output_aliases={4 + halves: 0},
        compiler_params=pltpu.CompilerParams(vmem_limit_bytes=VMEM_LIMIT),
        cost_estimate=COST,
        name="second_section",
    )(info, scale, *parts, *second, snr, *after)


BLOCKS = 4


def bank_kernel(block_ref, inner_ref, high_ref, low_ref):
    times = block_ref.shape[-1]
    rc, rs = inner_ref[0], inner_ref[1]
    for b in range(BLOCKS):
        bc, bs = block_ref[b, 0:1, :], block_ref[b, 1:2, :]
        cos, sin = split(bc * rc - bs * rs), split(bc * rs + bs * rc)
        top = slice(2 * b * BLOCK, (2 * b + 1) * BLOCK)
        low = slice((2 * b + 1) * BLOCK, (2 * b + 2) * BLOCK)
        for ref, c, s in zip((high_ref, low_ref), cos, sin):
            ref[top, :times] = c
            ref[top, times:] = s
            ref[low, :times] = -s
            ref[low, times:] = c


def bank_table(own_time):
    times = own_time.shape[0]
    block = jnp.arange(NBLK, dtype=jnp.int32)[:, None] * own_time[None, :]
    block = jnp.stack(phase(block, NBLK), axis=1)
    inner = jnp.arange(BLOCK, dtype=jnp.int32)[:, None] * own_time[None, :]
    inner = jnp.stack(phase(inner, N1))
    return pl.pallas_call(
        bank_kernel,
        grid=(NBLK // BLOCKS,),
        in_specs=[
            pl.BlockSpec((BLOCKS, 2, times), lambda b: (b, 0, 0)),
            pl.BlockSpec((2, BLOCK, times), lambda b: (0, 0, 0)),
        ],
        out_specs=[pl.BlockSpec((BLOCKS * 2 * BLOCK, 2 * times), lambda b: (b, 0))] * 2,
        out_shape=[jax.ShapeDtypeStruct((2 * N1, 2 * times), BF16)] * 2,
        compiler_params=pltpu.CompilerParams(vmem_limit_bytes=VMEM_LIMIT),
        cost_estimate=COST,
        name="bank_table",
    )(block, inner)


def bins_first_kernel(pieces, banks, place_ref, edge_ref, *refs):
    lots = LOTS
    own_refs, rest_refs = refs[:pieces], refs[pieces : (1 + lots) * pieces]
    wh_ref, wl_ref, tw_ref = refs[(1 + lots) * pieces :][:3]
    level_ref, total_ref, xh, xl, acc = refs[-5:]
    times = total_ref.shape[-1]
    cols = total_ref.shape[1] // pieces
    length = 2 * N1 // banks
    chunk = FOUR * LANES
    step = pl.program_id(0)

    def put(ref, row, lane, to):
        def cut(i, carry):
            at = pl.ds(pl.multiple_of(lane + i * chunk, chunk), chunk)
            there = pl.ds(pl.multiple_of(to + i * chunk, chunk), chunk)
            xh[row, there], xl[row, there] = split(ref[:, at])
            return carry

        lax.fori_loop(0, length // chunk, cut, 0)

    @pl.when(step == 0)
    def _():
        for k in range(pieces):
            base = (place_ref[0] ^ k) * cols
            row = pl.ds(pl.multiple_of(base, ROWS), cols)
            put(own_refs[k], row, 0, place_ref[1] * length)
            for n in range(1, banks):
                start = 0
                for lot in range(lots):
                    ref = rest_refs[lot * pieces + k]
                    rows = ref.shape[0]
                    row = pl.ds(pl.multiple_of(base + start, ROWS), rows)
                    put(ref, row, (n - 1) * length, lax.rem(place_ref[1] + n, banks) * length)
                    start += rows
        total_ref[...] = jnp.zeros_like(total_ref)

    def blocks_at(block, blocks):
        at = pl.ds(pl.multiple_of(block * LANES, LANES), blocks * LANES)
        return dot3((xh[:, at], xl[:, at]), (wh_ref[at, :], wl_ref[at, :]))

    for i in range(TOGETHER):
        start, end = edge_ref[step * TOGETHER + i], edge_ref[step * TOGETHER + i + 1]
        odd = (end - start) % 2

        @pl.when(odd == 1)
        def _():
            acc[i] = blocks_at(end - 1, 1)

        @pl.when(odd == 0)
        def _():
            acc[i] = blocks_at(end - 2, 2)

        def two(n, carry):
            acc[i] += blocks_at(start + 2 * n, 2)
            return carry

        lax.fori_loop(0, (end - start - 1) // 2, two, 0)

    for u in range(FOUR):
        at = tile(u)
        cos, sin = tw_ref[0, at, :], tw_ref[1, at, :]
        sum_r, sum_i = total_ref[0, at, :], total_ref[1, at, :]
        for i in range(TOGETHER):
            re, im = acc[i, at, :times], acc[i, at, times:]
            vr, vi = re * cos - im * sin, re * sin + im * cos
            level_ref[i, 0, at, :] = vr
            level_ref[i, 1, at, :] = vi
            sum_r, sum_i = sum_r + vr, sum_i + vi
        total_ref[0, at, :] = sum_r
        total_ref[1, at, :] = sum_i


def bins_first(banks, place, edges, own, rest, table, twist, after):
    rows, times = twist.shape[1:]
    smem = pl.BlockSpec(memory_space=pltpu.SMEM)
    once = pl.Buffered(1)

    def fixed(shape):
        return pl.BlockSpec(shape, lambda i: (0,) * len(shape), pipeline_mode=once)

    rest = [x for lot in rest for x in lot]
    cols = rows // len(own)
    return pl.pallas_call(
        functools.partial(bins_first_kernel, len(own), banks),
        grid=(BINS // TOGETHER,),
        in_specs=[smem, smem]
        + [fixed((cols, x.shape[1])) for x in own]
        + [fixed(x.shape) for x in rest]
        + [fixed((2 * N1, 2 * times))] * 2
        + [fixed((2, rows, times))]
        + [ANY] * len(after),
        out_specs=[
            pl.BlockSpec((TOGETHER, 2, rows, times), lambda i: (i, 0, 0, 0)),
            pl.BlockSpec((2, rows, times), lambda i: (0, 0, 0)),
        ],
        out_shape=[
            jax.ShapeDtypeStruct((BINS, 2, rows, times), F32),
            jax.ShapeDtypeStruct((2, rows, times), F32),
        ],
        scratch_shapes=[
            pltpu.VMEM((rows, 2 * N1), BF16),
            pltpu.VMEM((rows, 2 * N1), BF16),
            pltpu.VMEM((TOGETHER, rows, 2 * times), F32),
        ],
        compiler_params=pltpu.CompilerParams(vmem_limit_bytes=VMEM_LIMIT),
        cost_estimate=COST,
        name="bins_first",
    )(place, edges, *own, *rest, *table, twist, *after)


def bins_second_kernel(halves, which_ref, scale_ref, gain_ref, share_ref, *refs):
    level_refs, total_refs = refs[:halves], refs[halves : 2 * halves]
    w2h_ref, w2l_ref, out_ref, snr_ref, chi, hold = refs[2 * halves :]
    times = out_ref.shape[0]
    part_rows = LANES // halves
    step = pl.program_id(0)

    @pl.when(step == 0)
    def _():
        chi[...] = jnp.zeros_like(chi)

    def rows_of(get, u):
        at = slice(u * part_rows, (u + 1) * part_rows)
        return jnp.concatenate([get(h, at) for h in range(halves)], axis=0)

    def keep(a, re, im):
        chi[a] += re * re + im * im

    for i in range(TOGETHER):
        gain, share = gain_ref[step * TOGETHER + i], share_ref[step * TOGETHER + i]

        def deviation(p):
            return lambda h, at: (
                level_refs[h][i, p, at, :] * gain - total_refs[h][p, at, :] * share
            )

        x = [tuple(rows_of(deviation(p), u) for p in range(2)) for u in range(FOUR)]
        second_points(x, w2h_ref, w2l_ref, keep)

    @pl.when(step == BINS // TOGETHER - 1)
    def _():
        scale = scale_ref[which_ref[0]]

        def whole(p):
            return lambda h, at: total_refs[h][p, at, :] * scale

        def put(a, re, im):
            for p, value in enumerate((re, im)):
                for g in range(times // LANES):
                    hold[p, g, pl.ds(a, LANES, stride=FOUR), :] = value[:, tile(g)]

        y = [tuple(rows_of(whole(p), u) for p in range(2)) for u in range(FOUR)]
        second_points(y, w2h_ref, w2l_ref, put)
        for g in range(times // LANES):
            for a in range(FOUR):
                hold[2, g, pl.ds(a, LANES, stride=FOUR), :] = chi[a, :, tile(g)]
            for p in range(2):
                snr_ref[0, 0, p, tile(g), :] = hold[p, g].T
            out_ref[tile(g), :] = hold[2, g].T


def bins_second(which, scale, gain, share, levels, totals, second, tmpls, dets):
    _, _, rows, times = levels[0].shape
    halves = len(levels)
    smem = pl.BlockSpec(memory_space=pltpu.SMEM)
    fixed = lambda shape: pl.BlockSpec(shape, lambda i, w: (0,) * len(shape))
    return pl.pallas_call(
        functools.partial(bins_second_kernel, halves),
        grid_spec=pltpu.PrefetchScalarGridSpec(
            num_scalar_prefetch=1,
            grid=(BINS // TOGETHER,),
            in_specs=[smem, smem, smem]
            + [pl.BlockSpec((TOGETHER, 2, rows, times), lambda i, w: (i, 0, 0, 0))] * halves
            + [fixed((2, rows, times))] * halves
            + [fixed((FOUR * 2 * LANES, 2 * LANES))] * 2,
            out_specs=[
                fixed((times, N2)),
                pl.BlockSpec((1, 1, 2, times, N2), lambda i, w: (w[0], w[1], 0, 0, 0)),
            ],
            scratch_shapes=[
                pltpu.VMEM((FOUR, LANES, times), F32),
                pltpu.VMEM((3, times // LANES, N2, LANES), F32),
            ],
        ),
        out_shape=[
            jax.ShapeDtypeStruct((times, N2), F32),
            jax.ShapeDtypeStruct((tmpls, dets, 2, times, N2), F32),
        ],
        compiler_params=pltpu.CompilerParams(vmem_limit_bytes=VMEM_LIMIT),
        cost_estimate=COST,
        name="bins_second",
    )(which, scale, gain, share, *levels, *totals, *second)


def handed_on(arrays, after):
    count = len(arrays)
    return pl.pallas_call(
        lambda *refs: None,
        in_specs=[ANY] * (count + len(after)),
        out_specs=[ANY] * count,
        out_shape=[jax.ShapeDtypeStruct(x.shape, x.dtype) for x in arrays],
        input_output_aliases={i: i for i in range(count)},
        compiler_params=pltpu.CompilerParams(vmem_limit_bytes=VMEM_LIMIT),
        cost_estimate=COST,
        name="handed_on",
    )(*arrays, *after)


def swap(x, freq, k):
    return lax.ppermute(x, "freq", [(i, i ^ k) for i in range(freq)])


def far_pieces(own, freq):
    return [own] + [swap(own, freq, k) for k in range(2, freq, 2)]


def near_pieces(far, freq):
    return [x for even in far for x in (even, swap(even, freq, 1))]


def per_device(strain, templates, coinc_tmpl, coinc_det, bin_edges):
    freq, banks = lax.axis_size("freq"), lax.axis_size("bank")
    place = lax.axis_index("freq").astype(jnp.int32)
    bank = lax.axis_index("bank").astype(jnp.int32)
    tmpls, _, cols, _ = templates.shape
    slots, dets = coinc_tmpl.shape[0], strain.shape[0]
    times = N1 // freq

    starts = (0, cols - ROWS, cols)
    slices = [strain[:, :, starts[h] : starts[h + 1]] for h in range(LOTS)]
    strains = [lax.all_gather(x, "bank", axis=0, tiled=False) for x in slices]
    first = tuple(jnp.asarray(t) for t in first_table())
    second = tuple(jnp.asarray(t) for t in second_table(cols, 1))
    stage = jnp.asarray(stage_table())

    column = place * cols + jnp.arange(cols, dtype=jnp.int32)
    lane = jnp.arange(N1, dtype=jnp.int32)
    time_of_lane = lane // LANES + COARSE * (lane % LANES)
    twist = jnp.stack(phase(column[:, None] * time_of_lane[None, :], N1 * N2))
    own_time = place * times + jnp.arange(times, dtype=jnp.int32)
    table = bank_table(own_time)
    all_columns = jnp.arange(N2, dtype=jnp.int32)
    own_twist = jnp.stack(phase(all_columns[:, None] * own_time[None, :], N1 * N2))

    which = [jnp.stack([coinc_tmpl[j], coinc_det[j], bank]) for j in range(slots)]
    series = jnp.arange(tmpls * dets - 1, dtype=jnp.int32)
    series = series + (series >= which[0][0] * dets + which[0][1])
    info = jnp.stack([series // dets, series % dets], axis=1).reshape(-1)
    info = jnp.concatenate([place.reshape(1), info])
    ends = jnp.zeros((1,), jnp.int32), jnp.full((1,), NBLK, jnp.int32)
    edges = [
        jnp.concatenate([ends[0], bin_edges[coinc_tmpl[j]], ends[1]]) for j in range(slots)
    ]
    here = jnp.stack([place, bank])

    power = (templates[:, 0] ** 2 + templates[:, 1] ** 2).sum(axis=1)
    power = power.reshape(tmpls, NBLK, BLOCK).sum(axis=2)
    own = [entry_product((0,), banks, 0, w, templates, strain[None], slices) for w in which]
    wide = own[0].shape[1]
    power = jnp.pad(power.reshape(1, -1), ((0, 7), (0, wide - tmpls * NBLK)))
    own[0] = jnp.concatenate([own[0], power], axis=0)
    own = [near_pieces(far_pieces(x, freq), freq) for x in own]
    gathered = [x for entry in own for x in entry[1:]]

    block_power = sum(x[cols, : tmpls * NBLK] for x in own[0]).reshape(tmpls, NBLK)
    sigma_sq = block_power.sum(axis=1)
    inv_sigma = lax.rsqrt(sigma_sq)
    bin_of = jnp.sum(
        jnp.arange(NBLK, dtype=jnp.int32)[None, :, None] >= bin_edges[:, None, :], axis=2
    )
    inside = bin_of[:, None, :] == jnp.arange(BINS, dtype=jnp.int32)[None, :, None]
    weights = jnp.where(inside, block_power[:, None, :], 0.0).sum(axis=2) / sigma_sq[:, None]
    gains = [inv_sigma[coinc_tmpl[j]] * lax.rsqrt(weights[coinc_tmpl[j]]) for j in range(slots)]
    shares = [gains[j] * weights[coinc_tmpl[j]] for j in range(slots)]
    which, inv_sigma, gains, shares, twist, info, edges, here, table, own_twist = (
        lax.optimization_barrier(
            (which, inv_sigma, gains, shares, twist, info, edges, here, table, own_twist)
        )
    )

    rest, sent = [], []
    later = tuple(range(1, banks))
    for h in range(LOTS):
        lot = [
            entry_product(later, banks, starts[h], w, templates, strains[h], gathered)
            for w in which
        ]
        far = [far_pieces(x, freq) for x in lot]
        *sent, token = first_section(
            freq, starts[h], info, templates, strains[h], first, stage, twist, sent, lot
        )
        far = [x[:1] + list(handed_on(x[1:], [token])) for x in far]
        rest.append([near_pieces(x, freq) for x in far])
        gathered = [x for entry in rest[-1] for x in entry[1:]]
    (ready,) = handed_on(sent, gathered)
    got = lax.all_to_all(
        ready.reshape(freq, -1, LANES), "freq", split_axis=0, concat_axis=0, tiled=True
    )
    got = got.reshape(ready.shape)

    chi, snr = [], None
    for j in range(slots):
        entry = [x[j] for x in rest]
        levels, total = bins_first(
            banks, here, edges[j], own[j], entry, table, own_twist, [ready]
        )
        one, series_of = bins_second(
            which[j], inv_sigma, gains[j], shares[j], [levels], [total], second, tmpls, dets
        )
        chi.append(one)
        snr = series_of if snr is None else snr
    snr = second_section(freq, info, inv_sigma, [got], second, snr, chi)
    return (snr, jnp.stack(chi))


def solution(mesh):
    placed = (
        P(None, None, "freq", "bank"),
        P("bank", None, "freq", None),
        P("bank"),
        P("bank"),
        P("bank", None),
    )
    return jax.shard_map(
        per_device,
        mesh=mesh,
        in_specs=placed,
        out_specs=(P("bank", None, None, "freq", None), P("bank", "freq", None)),
        check_vma=False,
    )
```

```python
import functools

import jax
import jax.numpy as jnp
import ml_dtypes
import numpy as np
from jax import lax
from jax.experimental import pallas as pl
from jax.experimental.pallas import tpu as pltpu
from jax.sharding import PartitionSpec as P

N1 = 2048
N2 = 512
NBLK = 32
BLOCK = N1 // NBLK
BINS = 16
LANES = 128
COARSE = N1 // LANES
FOUR = N2 // LANES
F32 = jnp.float32
BF16 = jnp.bfloat16
MIB = 1 << 20
VMEM_LIMIT = 56 * MIB
ANY = pl.BlockSpec(memory_space=pl.ANY)
COST = pl.CostEstimate(flops=MIB, bytes_accessed=MIB, transcendentals=0)


def split_table(table):
    high = table.astype(ml_dtypes.bfloat16)
    low = (table - high.astype(np.float64)).astype(ml_dtypes.bfloat16)
    return high, low


def first_table():
    angle = 2 * np.pi * (np.outer(np.arange(LANES), np.arange(LANES)) % LANES) / LANES
    cos, sin = np.cos(angle), np.sin(angle)
    return split_table(np.block([[cos, sin], [-sin, cos]]))


def stage_table():
    angle = 2 * np.pi * np.outer(np.arange(COARSE), np.arange(LANES)) / N1
    return np.concatenate([np.cos(angle), np.sin(angle)]).astype(np.float32)


def second_table(cols, halves):
    order = np.arange(LANES).reshape(LANES // cols, halves, cols // halves)
    order = order.transpose(1, 0, 2).reshape(-1)
    blocks = []
    for a in range(FOUR):
        n2 = a + FOUR * np.arange(LANES)
        angle = 2 * np.pi * (np.outer(n2, order) % N2) / N2
        cos, sin = np.cos(angle), np.sin(angle)
        blocks.append(np.block([[cos, -sin], [sin, cos]]))
    return split_table(np.concatenate(blocks))


def split(x):
    high = x.astype(BF16)
    return high, (x - high.astype(F32)).astype(BF16)


def phase(index, length):
    angle = (index % length).astype(F32) * (2.0 * np.pi / length)
    return jnp.cos(angle), jnp.sin(angle)


def times_i(z):
    return (-z[1], z[0])


def plus(x, y):
    return (x[0] + y[0], x[1] + y[1])


def minus(x, y):
    return (x[0] - y[0], x[1] - y[1])


def dft4(x):
    s0, s1 = plus(x[0], x[2]), minus(x[0], x[2])
    s2, s3 = plus(x[1], x[3]), times_i(minus(x[1], x[3]))
    return [plus(s0, s2), plus(s1, s3), minus(s0, s2), minus(s1, s3)]


def turn(z, step):
    step %= 16
    if step == 0:
        return z
    if step == 4:
        return times_i(z)
    if step == 8:
        return (-z[0], -z[1])
    half = float(np.sqrt(0.5))
    if step == 2:
        return ((z[0] - z[1]) * half, (z[0] + z[1]) * half)
    if step == 6:
        return ((z[0] + z[1]) * -half, (z[0] - z[1]) * half)
    cos, sin = float(np.cos(np.pi * step / 8)), float(np.sin(np.pi * step / 8))
    return (z[0] * cos - z[1] * sin, z[0] * sin + z[1] * cos)


def dft16(x):
    columns = [dft4([x[4 * u1 + u0] for u1 in range(4)]) for u0 in range(4)]
    out = [None] * 16
    for a0 in range(4):
        ys = dft4([turn(columns[u0][a0], u0 * a0) for u0 in range(4)])
        for a1 in range(4):
            out[a0 + 4 * a1] = ys[a1]
    return out


def dot3(left, right):
    (lh, ll), (rh, rl) = left, right
    return jnp.dot(
        jnp.concatenate([lh, lh, ll], axis=1),
        jnp.concatenate([rh, rl, rh], axis=0),
        preferred_element_type=F32,
    )


def products(tmpl, strain_ref, where, rows=slice(None)):
    per_piece = COARSE // strain_ref.shape[0]
    for u in range(COARSE):
        off = u % per_piece
        there = slice(off * LANES, (off + 1) * LANES)
        hr, hi = tmpl(0, u), tmpl(1, u)
        sr = strain_ref[(u // per_piece,) + where + (0, rows, there)]
        si = strain_ref[(u // per_piece,) + where + (1, rows, there)]
        yield u, hr * sr + hi * si, hr * si - hi * sr


def tile(u):
    return slice(u * LANES, (u + 1) * LANES)


def first_kernel(
    freq, info_ref, tmpl_ref, strain_ref, wh_ref, wl_ref, stage_ref, tw_ref, *refs
):
    out_ref, token_ref, gh, gl, z = refs[-5:]
    token_ref[...] = jnp.zeros_like(token_ref)
    rows = tmpl_ref.shape[2]
    for r in range(0, rows, ROWS):
        at = slice(r, r + ROWS)
        got = products(lambda p, u: tmpl_ref[0, p, at, tile(u)], strain_ref, (0,), at)
        y = dft16([(re, im) for _, re, im in got])
        for a in range(COARSE):
            cos, sin = stage_ref[a : a + 1, :], stage_ref[COARSE + a : COARSE + a + 1, :]
            yr, yi = y[a]
            to = slice(a * rows + r, a * rows + r + ROWS)
            gh[to, :LANES], gl[to, :LANES] = split(yr * cos - yi * sin)
            gh[to, LANES:], gl[to, LANES:] = split(yr * sin + yi * cos)
    z[...] = dot3((gh[...], gl[...]), (wh_ref[...], wl_ref[...]))
    width = LANES // freq
    slot = lax.broadcasted_iota(jnp.int32, (ROWS, LANES), 1) // width
    for group in range(COARSE // freq):
        for r in range(0, rows, ROWS):
            at = slice(r, r + ROWS)
            turned = []
            for i in range(freq):
                a = group * freq + i
                to = slice(a * rows + r, a * rows + r + ROWS)
                zr, zi = z[to, :LANES], z[to, LANES:]
                cos, sin = tw_ref[0, at, tile(a)], tw_ref[1, at, tile(a)]
                pair = (zr * cos - zi * sin, zr * sin + zi * cos)
                if i:
                    pair = tuple(pltpu.roll(v, i * width, 1) for v in pair)
                turned.append(pair)
            for q in range(freq):
                for p in range(2):
                    value = turned[(0 - q) % freq][p]
                    for s in range(1, freq):
                        value = jnp.where(slot == s, turned[(s - q) % freq][p], value)
                    out_ref[q, 0, p, group, at] = value


ROWS = 16
HALVES = 2
TOGETHER = 2


def first_section(freq, half, info, templates, strain, first, stage, twist, after):
    tmpls = templates.shape[0]
    pieces, dets, _, rows, piece_len = strain.shape
    series = tmpls * dets - 1
    groups = COARSE // freq
    table = pl.BlockSpec((2 * LANES, 2 * LANES), lambda i, n: (0, 0))
    out = (freq, series, 2, groups, rows, LANES)
    return pl.pallas_call(
        functools.partial(first_kernel, freq),
        grid_spec=pltpu.PrefetchScalarGridSpec(
            num_scalar_prefetch=1,
            grid=(series,),
            in_specs=[
                pl.BlockSpec(
                    (1, 2, rows, N1), lambda i, n: (n[1 + 2 * i], 0, half, 0)
                ),
                pl.BlockSpec(
                    (pieces, 1, 2, rows, piece_len), lambda i, n: (0, n[2 + 2 * i], 0, 0, 0)
                ),
                table,
                table,
                pl.BlockSpec((2 * COARSE, LANES), lambda i, n: (0, 0)),
                pl.BlockSpec((2, rows, N1), lambda i, n: (0, half, 0)),
            ]
            + [ANY] * len(after),
            out_specs=[
                pl.BlockSpec(
                    (freq, 1, 2, groups, rows, LANES), lambda i, n: (0, i, 0, 0, 0, 0)
                ),
                pl.BlockSpec((8, LANES), lambda i, n: (0, 0)),
            ],
            scratch_shapes=[
                pltpu.VMEM((COARSE * rows, 2 * LANES), BF16),
                pltpu.VMEM((COARSE * rows, 2 * LANES), BF16),
                pltpu.VMEM((COARSE * rows, 2 * LANES), F32),
            ],
        ),
        out_shape=[
            jax.ShapeDtypeStruct(out, F32),
            jax.ShapeDtypeStruct((8, LANES), F32),
        ],
        compiler_params=pltpu.CompilerParams(vmem_limit_bytes=VMEM_LIMIT),
        cost_estimate=pl.CostEstimate(
            flops=60 * series * rows * N1 * LANES, bytes_accessed=16 * MIB, transcendentals=0
        ),
        name="first_section",
    )(info, templates, strain, first[0], first[1], stage, twist, *after)


def entry_kernel(steps, banks, which_ref, tmpl_ref, strain_ref, *refs):
    out_ref = refs[-1]
    length = N1 // banks
    first_half = lax.broadcasted_iota(jnp.int32, (ROWS, LANES), 1) < BLOCK
    for n, k in enumerate(steps):
        part = lax.rem(which_ref[2] + k, banks)
        for u in range(length // LANES):
            lane = pl.ds(pl.multiple_of(part * length + u * LANES, LANES), LANES)
            hr, hi = tmpl_ref[0, 0, :, lane], tmpl_ref[0, 1, :, lane]
            piece = 0 if strain_ref.shape[0] == 1 else part
            sr, si = strain_ref[piece, 0, 0, :, tile(u)], strain_ref[piece, 0, 1, :, tile(u)]
            re, im = hr * sr + hi * si, hr * si - hi * sr
            to = 2 * (n * length // LANES + u)
            out_ref[:, tile(to)] = jnp.where(first_half, re, pltpu.roll(im, BLOCK, 1))
            out_ref[:, tile(to + 1)] = jnp.where(first_half, pltpu.roll(re, BLOCK, 1), im)


def entry_product(steps, banks, half, which, templates, strain, after):
    pieces, _, _, cols, length = strain.shape
    first = half * cols // ROWS
    return pl.pallas_call(
        functools.partial(entry_kernel, steps, banks),
        grid_spec=pltpu.PrefetchScalarGridSpec(
            num_scalar_prefetch=1,
            grid=(cols // ROWS,),
            in_specs=[
                pl.BlockSpec((1, 2, ROWS, N1), lambda c, w: (w[0], 0, first + c, 0)),
                pl.BlockSpec((pieces, 1, 2, ROWS, length), lambda c, w: (0, w[1], 0, c, 0)),
            ]
            + [ANY] * len(after),
            out_specs=pl.BlockSpec((ROWS, 2 * length * len(steps)), lambda c, w: (c, 0)),
        ),
        out_shape=jax.ShapeDtypeStruct((cols, 2 * length * len(steps)), F32),
        compiler_params=pltpu.CompilerParams(vmem_limit_bytes=VMEM_LIMIT),
        cost_estimate=COST,
        name="entry_product",
    )(which, templates, strain, *after)


def second_points(x, w2h_ref, w2l_ref, use):
    for a, (yr, yi) in enumerate(dft4(x)):
        y = jnp.concatenate([yr, yi], axis=0)
        at = slice(a * 2 * LANES, (a + 1) * 2 * LANES)
        z = dot3((w2h_ref[at, :], w2l_ref[at, :]), split(y))
        use(a, z[:LANES], z[LANES:])


def second_kernel(freq, halves, info_ref, scale_ref, *refs):
    part_refs, (w2h_ref, w2l_ref) = refs[:halves], refs[halves : halves + 2]
    out_ref, hold, order = refs[-3:]
    place = info_ref[0]
    groups, cols = part_refs[0].shape[3:5]
    per = LANES // (halves * cols)
    width = LANES // freq
    scale = scale_ref[info_ref[1 + 2 * pl.program_id(0)]]

    def rows_of(p, u):
        tiles = [
            jnp.concatenate(
                [ref[u * per + f, 0, p, g] for ref in part_refs for f in range(per)],
                axis=0,
            )
            for g in range(groups)
        ]
        return jnp.concatenate(tiles, axis=1)

    x = [(rows_of(0, u), rows_of(1, u)) for u in range(FOUR)]

    def keep(a, re, im):
        for p, value in enumerate((re, im)):
            for g in range(groups):
                hold[p, g, pl.ds(a, LANES, stride=FOUR), :] = value[:, tile(g)] * scale

    second_points(x, w2h_ref, w2l_ref, keep)
    for p in range(2):
        for g in range(groups):
            turned = hold[p, g].T
            for s in range(freq):
                a = g * freq + lax.rem(s - place + freq, freq)
                for j in range(FOUR):
                    order[p, j, pl.ds(a, width, stride=COARSE), :] = turned[
                        s * width : (s + 1) * width, tile(j)
                    ]
        for j in range(FOUR):
            out_ref[0, 0, p, :, tile(j)] = order[p, j]


def second_section(freq, info, scale, parts, second, snr, after):
    _, series, _, groups, cols, _ = parts[0].shape
    halves = len(parts)
    times = groups * LANES
    smem = pl.BlockSpec(memory_space=pltpu.SMEM)
    table = pl.BlockSpec((FOUR * 2 * LANES, 2 * LANES), lambda i, n: (0, 0))
    part = pl.BlockSpec(
        (freq, 1, 2, groups, cols, LANES), lambda i, n: (0, i, 0, 0, 0, 0)
    )
    return pl.pallas_call(
        functools.partial(second_kernel, freq, halves),
        grid_spec=pltpu.PrefetchScalarGridSpec(
            num_scalar_prefetch=1,
            grid=(series,),
            in_specs=[smem] + [part] * halves + [table, table, ANY] + [ANY] * len(after),
            out_specs=pl.BlockSpec(
                (1, 1, 2, times, N2), lambda i, n: (n[1 + 2 * i], n[2 + 2 * i], 0, 0, 0)
            ),
            scratch_shapes=[
                pltpu.VMEM((2, groups, N2, LANES), F32),
                pltpu.VMEM((2, FOUR, times, LANES), F32),
            ],
        ),
        out_shape=jax.ShapeDtypeStruct(snr.shape, F32),
        input_output_aliases={4 + halves: 0},
        compiler_params=pltpu.CompilerParams(vmem_limit_bytes=VMEM_LIMIT),
        cost_estimate=COST,
        name="second_section",
    )(info, scale, *parts, *second, snr, *after)


BLOCKS = 4


def bank_kernel(block_ref, inner_ref, high_ref, low_ref):
    times = block_ref.shape[-1]
    rc, rs = inner_ref[0], inner_ref[1]
    for b in range(BLOCKS):
        bc, bs = block_ref[b, 0:1, :], block_ref[b, 1:2, :]
        cos, sin = split(bc * rc - bs * rs), split(bc * rs + bs * rc)
        top = slice(2 * b * BLOCK, (2 * b + 1) * BLOCK)
        low = slice((2 * b + 1) * BLOCK, (2 * b + 2) * BLOCK)
        for ref, c, s in zip((high_ref, low_ref), cos, sin):
            ref[top, :times] = c
            ref[top, times:] = s
            ref[low, :times] = -s
            ref[low, times:] = c


def bank_table(own_time):
    times = own_time.shape[0]
    block = jnp.arange(NBLK, dtype=jnp.int32)[:, None] * own_time[None, :]
    block = jnp.stack(phase(block, NBLK), axis=1)
    inner = jnp.arange(BLOCK, dtype=jnp.int32)[:, None] * own_time[None, :]
    inner = jnp.stack(phase(inner, N1))
    return pl.pallas_call(
        bank_kernel,
        grid=(NBLK // BLOCKS,),
        in_specs=[
            pl.BlockSpec((BLOCKS, 2, times), lambda b: (b, 0, 0)),
            pl.BlockSpec((2, BLOCK, times), lambda b: (0, 0, 0)),
        ],
        out_specs=[pl.BlockSpec((BLOCKS * 2 * BLOCK, 2 * times), lambda b: (b, 0))] * 2,
        out_shape=[jax.ShapeDtypeStruct((2 * N1, 2 * times), BF16)] * 2,
        compiler_params=pltpu.CompilerParams(vmem_limit_bytes=VMEM_LIMIT),
        cost_estimate=COST,
        name="bank_table",
    )(block, inner)


def bins_first_kernel(pieces, banks, place_ref, edge_ref, *refs):
    own_refs, rest_refs = refs[:pieces], refs[pieces : 2 * pieces]
    table_refs, tw_ref = refs[2 * pieces : 2 * pieces + 2], refs[2 * pieces + 2]
    level_ref, total_ref, xh, xl, acc, wh_ref, wl_ref, sems = refs[-8:]
    times = total_ref.shape[-1]
    cols = own_refs[0].shape[0]
    length = 2 * N1 // banks
    chunk = FOUR * LANES
    step = pl.program_id(0)

    @pl.when(step == 0)
    def _():
        copies = [
            pltpu.make_async_copy(source, target, sems.at[i])
            for i, (source, target) in enumerate(zip(table_refs, (wh_ref, wl_ref)))
        ]
        for copy in copies:
            copy.start()
        for k in range(pieces):
            row = pl.ds(pl.multiple_of((place_ref[0] ^ k) * cols, cols), cols)
            for n in range(banks):
                ref = rest_refs[k] if n else own_refs[k]
                start = lax.rem(place_ref[1] + n, banks) * length

                def cut(i, carry):
                    lane = max(n - 1, 0) * length + i * chunk
                    x = ref[:, pl.ds(pl.multiple_of(lane, chunk), chunk)]
                    to = pl.ds(pl.multiple_of(start + i * chunk, chunk), chunk)
                    xh[row, to], xl[row, to] = split(x)
                    return carry

                lax.fori_loop(0, length // chunk, cut, 0)
        total_ref[...] = jnp.zeros_like(total_ref)
        for copy in copies:
            copy.wait()

    def blocks_at(block, blocks):
        at = pl.ds(pl.multiple_of(block * LANES, LANES), blocks * LANES)
        return dot3((xh[:, at], xl[:, at]), (wh_ref[at, :], wl_ref[at, :]))

    for i in range(TOGETHER):
        start, end = edge_ref[step * TOGETHER + i], edge_ref[step * TOGETHER + i + 1]
        odd = (end - start) % 2

        @pl.when(odd == 1)
        def _():
            acc[i] = blocks_at(end - 1, 1)

        @pl.when(odd == 0)
        def _():
            acc[i] = blocks_at(end - 2, 2)

        def two(n, carry):
            acc[i] += blocks_at(start + 2 * n, 2)
            return carry

        lax.fori_loop(0, (end - start - 1) // 2, two, 0)

    for u in range(pieces * cols // LANES):
        at = tile(u)
        cos, sin = tw_ref[0, at, :], tw_ref[1, at, :]
        sum_r, sum_i = total_ref[0, at, :], total_ref[1, at, :]
        for i in range(TOGETHER):
            re, im = acc[i, at, :times], acc[i, at, times:]
            vr, vi = re * cos - im * sin, re * sin + im * cos
            level_ref[i, 0, at, :] = vr
            level_ref[i, 1, at, :] = vi
            sum_r, sum_i = sum_r + vr, sum_i + vi
        total_ref[0, at, :] = sum_r
        total_ref[1, at, :] = sum_i


def bins_first(half, banks, place, edges, own, rest, table, twist, after):
    cols, length = rest[0].shape
    rows, times = twist.shape[1:]
    smem = pl.BlockSpec(memory_space=pltpu.SMEM)
    fixed = lambda shape: pl.BlockSpec(shape, lambda i: (0,) * len(shape))
    return pl.pallas_call(
        functools.partial(bins_first_kernel, len(own), banks),
        grid=(BINS // TOGETHER,),
        in_specs=[smem, smem]
        + [pl.BlockSpec((cols, 2 * N1 - length), lambda i: (half, 0))] * len(own)
        + [fixed((cols, length))] * len(rest)
        + [ANY] * 2
        + [fixed((2, rows, times))]
        + [ANY] * len(after),
        out_specs=[
            pl.BlockSpec((TOGETHER, 2, rows, times), lambda i: (i, 0, 0, 0)),
            fixed((2, rows, times)),
        ],
        out_shape=[
            jax.ShapeDtypeStruct((BINS, 2, rows, times), F32),
            jax.ShapeDtypeStruct((2, rows, times), F32),
        ],
        scratch_shapes=[
            pltpu.VMEM((rows, 2 * N1), BF16),
            pltpu.VMEM((rows, 2 * N1), BF16),
            pltpu.VMEM((TOGETHER, rows, 2 * times), F32),
            pltpu.VMEM((2 * N1, 2 * times), BF16),
            pltpu.VMEM((2 * N1, 2 * times), BF16),
            pltpu.SemaphoreType.DMA((2,)),
        ],
        compiler_params=pltpu.CompilerParams(vmem_limit_bytes=VMEM_LIMIT),
        cost_estimate=COST,
        name="bins_first",
    )(place, edges, *own, *rest, *table, twist, *after)


def bins_second_kernel(halves, which_ref, scale_ref, gain_ref, share_ref, *refs):
    level_refs, total_refs = refs[:halves], refs[halves : 2 * halves]
    w2h_ref, w2l_ref, out_ref, snr_ref, chi, hold = refs[2 * halves :]
    times = out_ref.shape[0]
    part_rows = LANES // halves
    step = pl.program_id(0)

    @pl.when(step == 0)
    def _():
        chi[...] = jnp.zeros_like(chi)

    def rows_of(get, u):
        at = slice(u * part_rows, (u + 1) * part_rows)
        return jnp.concatenate([get(h, at) for h in range(halves)], axis=0)

    def keep(a, re, im):
        chi[a] += re * re + im * im

    for i in range(TOGETHER):
        gain, share = gain_ref[step * TOGETHER + i], share_ref[step * TOGETHER + i]

        def deviation(p):
            return lambda h, at: (
                level_refs[h][i, p, at, :] * gain - total_refs[h][p, at, :] * share
            )

        x = [tuple(rows_of(deviation(p), u) for p in range(2)) for u in range(FOUR)]
        second_points(x, w2h_ref, w2l_ref, keep)

    @pl.when(step == BINS // TOGETHER - 1)
    def _():
        scale = scale_ref[which_ref[0]]

        def whole(p):
            return lambda h, at: total_refs[h][p, at, :] * scale

        def put(a, re, im):
            for p, value in enumerate((re, im)):
                for g in range(times // LANES):
                    hold[p, g, pl.ds(a, LANES, stride=FOUR), :] = value[:, tile(g)]

        y = [tuple(rows_of(whole(p), u) for p in range(2)) for u in range(FOUR)]
        second_points(y, w2h_ref, w2l_ref, put)
        for g in range(times // LANES):
            for a in range(FOUR):
                hold[2, g, pl.ds(a, LANES, stride=FOUR), :] = chi[a, :, tile(g)]
            for p in range(2):
                snr_ref[0, 0, p, tile(g), :] = hold[p, g].T
            out_ref[tile(g), :] = hold[2, g].T


def bins_second(which, scale, gain, share, levels, totals, second, tmpls, dets):
    _, _, rows, times = levels[0].shape
    halves = len(levels)
    smem = pl.BlockSpec(memory_space=pltpu.SMEM)
    fixed = lambda shape: pl.BlockSpec(shape, lambda i, w: (0,) * len(shape))
    return pl.pallas_call(
        functools.partial(bins_second_kernel, halves),
        grid_spec=pltpu.PrefetchScalarGridSpec(
            num_scalar_prefetch=1,
            grid=(BINS // TOGETHER,),
            in_specs=[smem, smem, smem]
            + [pl.BlockSpec((TOGETHER, 2, rows, times), lambda i, w: (i, 0, 0, 0))] * halves
            + [fixed((2, rows, times))] * halves
            + [fixed((FOUR * 2 * LANES, 2 * LANES))] * 2,
            out_specs=[
                fixed((times, N2)),
                pl.BlockSpec((1, 1, 2, times, N2), lambda i, w: (w[0], w[1], 0, 0, 0)),
            ],
            scratch_shapes=[
                pltpu.VMEM((FOUR, LANES, times), F32),
                pltpu.VMEM((3, times // LANES, N2, LANES), F32),
            ],
        ),
        out_shape=[
            jax.ShapeDtypeStruct((times, N2), F32),
            jax.ShapeDtypeStruct((tmpls, dets, 2, times, N2), F32),
        ],
        compiler_params=pltpu.CompilerParams(vmem_limit_bytes=VMEM_LIMIT),
        cost_estimate=COST,
        name="bins_second",
    )(which, scale, gain, share, *levels, *totals, *second)


def handed_on(arrays, after):
    count = len(arrays)
    return pl.pallas_call(
        lambda *refs: None,
        in_specs=[ANY] * (count + len(after)),
        out_specs=[ANY] * count,
        out_shape=[jax.ShapeDtypeStruct(x.shape, x.dtype) for x in arrays],
        input_output_aliases={i: i for i in range(count)},
        compiler_params=pltpu.CompilerParams(vmem_limit_bytes=VMEM_LIMIT),
        cost_estimate=COST,
        name="handed_on",
    )(*arrays, *after)


def swap(x, freq, k):
    return lax.ppermute(x, "freq", [(i, i ^ k) for i in range(freq)])


def far_pieces(own, freq):
    return [own] + [swap(own, freq, k) for k in range(2, freq, 2)]


def near_pieces(far, freq):
    return [x for even in far for x in (even, swap(even, freq, 1))]


def per_device(strain, templates, coinc_tmpl, coinc_det, bin_edges):
    freq, banks = lax.axis_size("freq"), lax.axis_size("bank")
    place = lax.axis_index("freq").astype(jnp.int32)
    bank = lax.axis_index("bank").astype(jnp.int32)
    tmpls, _, cols, _ = templates.shape
    slots, dets = coinc_tmpl.shape[0], strain.shape[0]
    times = N1 // freq
    part = cols // HALVES

    slices = [strain[:, :, h * part : (h + 1) * part] for h in range(HALVES)]
    strains = [lax.all_gather(x, "bank", axis=0, tiled=False) for x in slices]
    first = tuple(jnp.asarray(t) for t in first_table())
    second = tuple(jnp.asarray(t) for t in second_table(cols, HALVES))
    stage = jnp.asarray(stage_table())

    column = place * cols + jnp.arange(cols, dtype=jnp.int32)
    lane = jnp.arange(N1, dtype=jnp.int32)
    time_of_lane = lane // LANES + COARSE * (lane % LANES)
    twist = jnp.stack(phase(column[:, None] * time_of_lane[None, :], N1 * N2))
    own_time = place * times + jnp.arange(times, dtype=jnp.int32)
    table = bank_table(own_time)
    own_twist = []
    for h in range(HALVES):
        rows = jnp.arange(freq * part, dtype=jnp.int32)
        rows = rows // part * cols + h * part + rows % part
        own_twist.append(jnp.stack(phase(rows[:, None] * own_time[None, :], N1 * N2)))

    which = [jnp.stack([coinc_tmpl[j], coinc_det[j], bank]) for j in range(slots)]
    series = jnp.arange(tmpls * dets - 1, dtype=jnp.int32)
    series = series + (series >= which[0][0] * dets + which[0][1])
    info = jnp.stack([series // dets, series % dets], axis=1).reshape(-1)
    info = jnp.concatenate([place.reshape(1), info])
    ends = jnp.zeros((1,), jnp.int32), jnp.full((1,), NBLK, jnp.int32)
    edges = [
        jnp.concatenate([ends[0], bin_edges[coinc_tmpl[j]], ends[1]]) for j in range(slots)
    ]
    here = jnp.stack([place, bank])

    power = (templates[:, 0] ** 2 + templates[:, 1] ** 2).sum(axis=1)
    power = power.reshape(tmpls, NBLK, BLOCK).sum(axis=2)
    own = [entry_product((0,), banks, 0, w, templates, strain[None], slices) for w in which]
    wide = own[0].shape[1]
    power = jnp.pad(power.reshape(1, -1), ((0, 7), (0, wide - tmpls * NBLK)))
    own[0] = jnp.concatenate([own[0], power], axis=0)
    own = [near_pieces(far_pieces(x, freq), freq) for x in own]
    gathered = [x for entry in own for x in entry[1:]]

    block_power = sum(x[cols, : tmpls * NBLK] for x in own[0]).reshape(tmpls, NBLK)
    sigma_sq = block_power.sum(axis=1)
    inv_sigma = lax.rsqrt(sigma_sq)
    bin_of = jnp.sum(
        jnp.arange(NBLK, dtype=jnp.int32)[None, :, None] >= bin_edges[:, None, :], axis=2
    )
    inside = bin_of[:, None, :] == jnp.arange(BINS, dtype=jnp.int32)[None, :, None]
    weights = jnp.where(inside, block_power[:, None, :], 0.0).sum(axis=2) / sigma_sq[:, None]
    gains = [inv_sigma[coinc_tmpl[j]] * lax.rsqrt(weights[coinc_tmpl[j]]) for j in range(slots)]
    shares = [gains[j] * weights[coinc_tmpl[j]] for j in range(slots)]
    which, inv_sigma, gains, shares, twist, info, edges, here, table, own_twist = (
        lax.optimization_barrier(
            (which, inv_sigma, gains, shares, twist, info, edges, here, table, own_twist)
        )
    )

    parts, halves = [], []
    later = tuple(range(1, banks))
    for h in range(HALVES):
        after = [x[0] for x in halves[-1]] if halves else gathered
        half = [entry_product(later, banks, h, w, templates, strains[h], after) for w in which]
        far = [far_pieces(x, freq) for x in half]
        sent, token = first_section(
            freq, h, info, templates, strains[h], first, stage, twist, half
        )
        far = [x[:1] + list(handed_on(x[1:], [token] + parts)) for x in far]
        rest = [near_pieces(x, freq) for x in far]
        (ready,) = handed_on([sent], [x for entry in rest for x in entry[1:]])
        got = lax.all_to_all(
            ready.reshape(freq, -1, LANES), "freq", split_axis=0, concat_axis=0, tiled=True
        )
        parts.append(got.reshape(ready.shape))
        halves.append(
            [
                bins_first(
                    h, banks, here, edges[j], own[j], rest[j], table, own_twist[h], [ready]
                )
                for j in range(slots)
            ]
        )

    chi, snr = [], None
    for j in range(slots):
        levels, totals = zip(*[x[j] for x in halves])
        one, series_of = bins_second(
            which[j], inv_sigma, gains[j], shares[j], levels, totals, second, tmpls, dets
        )
        chi.append(one)
        snr = series_of if snr is None else snr
    snr = second_section(freq, info, inv_sigma, parts, second, snr, chi)
    return (snr, jnp.stack(chi))


def solution(mesh):
    placed = (
        P(None, None, "freq", "bank"),
        P("bank", None, "freq", None),
        P("bank"),
        P("bank"),
        P("bank", None),
    )
    return jax.shard_map(
        per_device,
        mesh=mesh,
        in_specs=placed,
        out_specs=(P("bank", None, None, "freq", None), P("bank", "freq", None)),
        check_vma=False,
    )
```

```python
import functools

import jax
import jax.numpy as jnp
import ml_dtypes
import numpy as np
from jax import lax
from jax.experimental import pallas as pl
from jax.experimental.pallas import tpu as pltpu
from jax.sharding import PartitionSpec as P

N1 = 2048
N2 = 512
NBLK = 32
BLOCK = N1 // NBLK
BINS = 16
LANES = 128
COARSE = N1 // LANES
FOUR = N2 // LANES
F32 = jnp.float32
BF16 = jnp.bfloat16
MIB = 1 << 20
VMEM_LIMIT = 56 * MIB
ANY = pl.BlockSpec(memory_space=pl.ANY)
COST = pl.CostEstimate(flops=MIB, bytes_accessed=MIB, transcendentals=0)


def split_table(table):
    high = table.astype(ml_dtypes.bfloat16)
    low = (table - high.astype(np.float64)).astype(ml_dtypes.bfloat16)
    return high, low


def first_table():
    angle = 2 * np.pi * (np.outer(np.arange(LANES), np.arange(LANES)) % LANES) / LANES
    cos, sin = np.cos(angle), np.sin(angle)
    return split_table(np.block([[cos, sin], [-sin, cos]]))


def stage_table():
    angle = 2 * np.pi * np.outer(np.arange(COARSE), np.arange(LANES)) / N1
    return np.concatenate([np.cos(angle), np.sin(angle)]).astype(np.float32)


def second_table(cols, halves):
    order = np.arange(LANES).reshape(LANES // cols, halves, cols // halves)
    order = order.transpose(1, 0, 2).reshape(-1)
    blocks = []
    for a in range(FOUR):
        n2 = a + FOUR * np.arange(LANES)
        angle = 2 * np.pi * (np.outer(n2, order) % N2) / N2
        cos, sin = np.cos(angle), np.sin(angle)
        blocks.append(np.block([[cos, -sin], [sin, cos]]))
    return np.concatenate([part for block in blocks for part in split_table(block)])


def split(x):
    high = x.astype(BF16)
    return high, (x - high.astype(F32)).astype(BF16)


def phase(index, length):
    angle = (index % length).astype(F32) * (2.0 * np.pi / length)
    return jnp.cos(angle), jnp.sin(angle)


def times_i(z):
    return (-z[1], z[0])


def plus(x, y):
    return (x[0] + y[0], x[1] + y[1])


def minus(x, y):
    return (x[0] - y[0], x[1] - y[1])


def dft4(x):
    s0, s1 = plus(x[0], x[2]), minus(x[0], x[2])
    s2, s3 = plus(x[1], x[3]), times_i(minus(x[1], x[3]))
    return [plus(s0, s2), plus(s1, s3), minus(s0, s2), minus(s1, s3)]


def turn(z, step):
    step %= 16
    if step == 0:
        return z
    if step == 4:
        return times_i(z)
    if step == 8:
        return (-z[0], -z[1])
    half = float(np.sqrt(0.5))
    if step == 2:
        return ((z[0] - z[1]) * half, (z[0] + z[1]) * half)
    if step == 6:
        return ((z[0] + z[1]) * -half, (z[0] - z[1]) * half)
    cos, sin = float(np.cos(np.pi * step / 8)), float(np.sin(np.pi * step / 8))
    return (z[0] * cos - z[1] * sin, z[0] * sin + z[1] * cos)


def dft16(x):
    columns = [dft4([x[4 * u1 + u0] for u1 in range(4)]) for u0 in range(4)]
    out = [None] * 16
    for a0 in range(4):
        ys = dft4([turn(columns[u0][a0], u0 * a0) for u0 in range(4)])
        for a1 in range(4):
            out[a0 + 4 * a1] = ys[a1]
    return out


def dot3(left, right):
    (lh, ll), (rh, rl) = left, right
    return jnp.dot(
        jnp.concatenate([lh, lh, ll], axis=1),
        jnp.concatenate([rh, rl, rh], axis=0),
        preferred_element_type=F32,
    )


def rows_dot3(left, right):
    half = left.shape[0] // 2
    high, low = right
    both = jnp.dot(left, high, preferred_element_type=F32)
    cross = jnp.dot(left[:half], low, preferred_element_type=F32)
    return both[:half] + (both[half:] + cross)


def products(tmpl, strain_ref, where, rows=slice(None)):
    per_piece = COARSE // strain_ref.shape[0]
    for u in range(COARSE):
        off = u % per_piece
        there = slice(off * LANES, (off + 1) * LANES)
        hr, hi = tmpl(0, u), tmpl(1, u)
        sr = strain_ref[(u // per_piece,) + where + (0, rows, there)]
        si = strain_ref[(u // per_piece,) + where + (1, rows, there)]
        yield u, hr * sr + hi * si, hr * si - hi * sr


def tile(u):
    return slice(u * LANES, (u + 1) * LANES)


def first_kernel(
    freq, info_ref, tmpl_ref, strain_ref, wh_ref, wl_ref, stage_ref, tw_ref, *refs
):
    out_ref, token_ref, gh, gl, z = refs[-5:]
    token_ref[...] = jnp.zeros_like(token_ref)
    rows = tmpl_ref.shape[2]
    for r in range(0, rows, ROWS):
        at = slice(r, r + ROWS)
        got = products(lambda p, u: tmpl_ref[0, p, at, tile(u)], strain_ref, (0,), at)
        y = dft16([(re, im) for _, re, im in got])
        for a in range(COARSE):
            cos, sin = stage_ref[a : a + 1, :], stage_ref[COARSE + a : COARSE + a + 1, :]
            yr, yi = y[a]
            to = slice(a * rows + r, a * rows + r + ROWS)
            gh[to, :LANES], gl[to, :LANES] = split(yr * cos - yi * sin)
            gh[to, LANES:], gl[to, LANES:] = split(yr * sin + yi * cos)
    z[...] = dot3((gh[...], gl[...]), (wh_ref[...], wl_ref[...]))
    width = LANES // freq
    slot = lax.broadcasted_iota(jnp.int32, (ROWS, LANES), 1) // width
    for group in range(COARSE // freq):
        for r in range(0, rows, ROWS):
            at = slice(r, r + ROWS)
            turned = []
            for i in range(freq):
                a = group * freq + i
                to = slice(a * rows + r, a * rows + r + ROWS)
                zr, zi = z[to, :LANES], z[to, LANES:]
                cos, sin = tw_ref[0, at, tile(a)], tw_ref[1, at, tile(a)]
                pair = (zr * cos - zi * sin, zr * sin + zi * cos)
                if i:
                    pair = tuple(pltpu.roll(v, i * width, 1) for v in pair)
                turned.append(pair)
            for q in range(freq):
                for p in range(2):
                    value = turned[(0 - q) % freq][p]
                    for s in range(1, freq):
                        value = jnp.where(slot == s, turned[(s - q) % freq][p], value)
                    out_ref[q, 0, p, group, at] = value


ROWS = 16
HALVES = 2
TOGETHER = 2


def first_section(freq, half, info, templates, strain, first, stage, twist, after):
    tmpls = templates.shape[0]
    pieces, dets, _, rows, piece_len = strain.shape
    series = tmpls * dets - 1
    groups = COARSE // freq
    table = pl.BlockSpec((2 * LANES, 2 * LANES), lambda i, n: (0, 0))
    out = (freq, series, 2, groups, rows, LANES)
    return pl.pallas_call(
        functools.partial(first_kernel, freq),
        grid_spec=pltpu.PrefetchScalarGridSpec(
            num_scalar_prefetch=1,
            grid=(series,),
            in_specs=[
                pl.BlockSpec(
                    (1, 2, rows, N1), lambda i, n: (n[1 + 2 * i], 0, half, 0)
                ),
                pl.BlockSpec(
                    (pieces, 1, 2, rows, piece_len), lambda i, n: (0, n[2 + 2 * i], 0, 0, 0)
                ),
                table,
                table,
                pl.BlockSpec((2 * COARSE, LANES), lambda i, n: (0, 0)),
                pl.BlockSpec((2, rows, N1), lambda i, n: (0, half, 0)),
            ]
            + [ANY] * len(after),
            out_specs=[
                pl.BlockSpec(
                    (freq, 1, 2, groups, rows, LANES), lambda i, n: (0, i, 0, 0, 0, 0)
                ),
                pl.BlockSpec((8, LANES), lambda i, n: (0, 0)),
            ],
            scratch_shapes=[
                pltpu.VMEM((COARSE * rows, 2 * LANES), BF16),
                pltpu.VMEM((COARSE * rows, 2 * LANES), BF16),
                pltpu.VMEM((COARSE * rows, 2 * LANES), F32),
            ],
        ),
        out_shape=[
            jax.ShapeDtypeStruct(out, F32),
            jax.ShapeDtypeStruct((8, LANES), F32),
        ],
        compiler_params=pltpu.CompilerParams(vmem_limit_bytes=VMEM_LIMIT),
        cost_estimate=pl.CostEstimate(
            flops=60 * series * rows * N1 * LANES, bytes_accessed=16 * MIB, transcendentals=0
        ),
        name="first_section",
    )(info, templates, strain, first[0], first[1], stage, twist, *after)


def entry_kernel(steps, banks, which_ref, tmpl_ref, strain_ref, *refs):
    out_ref = refs[-1]
    length = N1 // banks
    first_half = lax.broadcasted_iota(jnp.int32, (ROWS, LANES), 1) < BLOCK
    for n, k in enumerate(steps):
        part = lax.rem(which_ref[2] + k, banks)
        for u in range(length // LANES):
            lane = pl.ds(pl.multiple_of(part * length + u * LANES, LANES), LANES)
            hr, hi = tmpl_ref[0, 0, :, lane], tmpl_ref[0, 1, :, lane]
            piece = 0 if strain_ref.shape[0] == 1 else part
            sr, si = strain_ref[piece, 0, 0, :, tile(u)], strain_ref[piece, 0, 1, :, tile(u)]
            re, im = hr * sr + hi * si, hr * si - hi * sr
            to = 2 * (n * length // LANES + u)
            out_ref[:, tile(to)] = jnp.where(first_half, re, pltpu.roll(im, BLOCK, 1))
            out_ref[:, tile(to + 1)] = jnp.where(first_half, pltpu.roll(re, BLOCK, 1), im)


def entry_product(steps, banks, half, which, templates, strain, after):
    pieces, _, _, cols, length = strain.shape
    first = half * cols // ROWS
    return pl.pallas_call(
        functools.partial(entry_kernel, steps, banks),
        grid_spec=pltpu.PrefetchScalarGridSpec(
            num_scalar_prefetch=1,
            grid=(cols // ROWS,),
            in_specs=[
                pl.BlockSpec((1, 2, ROWS, N1), lambda c, w: (w[0], 0, first + c, 0)),
                pl.BlockSpec((pieces, 1, 2, ROWS, length), lambda c, w: (0, w[1], 0, c, 0)),
            ]
            + [ANY] * len(after),
            out_specs=pl.BlockSpec((ROWS, 2 * length * len(steps)), lambda c, w: (c, 0)),
        ),
        out_shape=jax.ShapeDtypeStruct((cols, 2 * length * len(steps)), F32),
        compiler_params=pltpu.CompilerParams(vmem_limit_bytes=VMEM_LIMIT),
        cost_estimate=COST,
        name="entry_product",
    )(which, templates, strain, *after)


def second_points(x, w2_ref, use):
    for a, (yr, yi) in enumerate(dft4(x)):
        y = jnp.concatenate([yr, yi], axis=0)
        table = w2_ref[a * 4 * LANES : (a + 1) * 4 * LANES, :]
        z = rows_dot3(table, split(y))
        use(a, z[:LANES], z[LANES:])


def second_kernel(freq, halves, info_ref, scale_ref, *refs):
    part_refs, w2_ref = refs[:halves], refs[halves]
    out_ref, hold, order = refs[-3:]
    place = info_ref[0]
    groups, cols = part_refs[0].shape[3:5]
    per = LANES // (halves * cols)
    width = LANES // freq
    scale = scale_ref[info_ref[1 + 2 * pl.program_id(0)]]

    def rows_of(p, u):
        tiles = [
            jnp.concatenate(
                [ref[u * per + f, 0, p, g] for ref in part_refs for f in range(per)],
                axis=0,
            )
            for g in range(groups)
        ]
        return jnp.concatenate(tiles, axis=1)

    x = [(rows_of(0, u), rows_of(1, u)) for u in range(FOUR)]

    def keep(a, re, im):
        for p, value in enumerate((re, im)):
            for g in range(groups):
                hold[p, g, pl.ds(a, LANES, stride=FOUR), :] = value[:, tile(g)] * scale

    second_points(x, w2_ref, keep)
    for p in range(2):
        for g in range(groups):
            turned = hold[p, g].T
            for s in range(freq):
                a = g * freq + lax.rem(s - place + freq, freq)
                for j in range(FOUR):
                    order[p, j, pl.ds(a, width, stride=COARSE), :] = turned[
                        s * width : (s + 1) * width, tile(j)
                    ]
        for j in range(FOUR):
            out_ref[0, 0, p, :, tile(j)] = order[p, j]


def second_section(freq, info, scale, parts, second, snr, after):
    _, series, _, groups, cols, _ = parts[0].shape
    halves = len(parts)
    times = groups * LANES
    smem = pl.BlockSpec(memory_space=pltpu.SMEM)
    table = pl.BlockSpec((FOUR * 4 * LANES, 2 * LANES), lambda i, n: (0, 0))
    part = pl.BlockSpec(
        (freq, 1, 2, groups, cols, LANES), lambda i, n: (0, i, 0, 0, 0, 0)
    )
    return pl.pallas_call(
        functools.partial(second_kernel, freq, halves),
        grid_spec=pltpu.PrefetchScalarGridSpec(
            num_scalar_prefetch=1,
            grid=(series,),
            in_specs=[smem] + [part] * halves + [table, ANY] + [ANY] * len(after),
            out_specs=pl.BlockSpec(
                (1, 1, 2, times, N2), lambda i, n: (n[1 + 2 * i], n[2 + 2 * i], 0, 0, 0)
            ),
            scratch_shapes=[
                pltpu.VMEM((2, groups, N2, LANES), F32),
                pltpu.VMEM((2, FOUR, times, LANES), F32),
            ],
        ),
        out_shape=jax.ShapeDtypeStruct(snr.shape, F32),
        input_output_aliases={3 + halves: 0},
        compiler_params=pltpu.CompilerParams(vmem_limit_bytes=VMEM_LIMIT),
        cost_estimate=COST,
        name="second_section",
    )(info, scale, *parts, second, snr, *after)


BLOCKS = 4


def bank_kernel(block_ref, inner_ref, high_ref, low_ref):
    times = block_ref.shape[-1]
    rc, rs = inner_ref[0], inner_ref[1]
    for b in range(BLOCKS):
        bc, bs = block_ref[b, 0:1, :], block_ref[b, 1:2, :]
        cos, sin = split(bc * rc - bs * rs), split(bc * rs + bs * rc)
        top = slice(2 * b * BLOCK, (2 * b + 1) * BLOCK)
        low = slice((2 * b + 1) * BLOCK, (2 * b + 2) * BLOCK)
        for ref, c, s in zip((high_ref, low_ref), cos, sin):
            ref[top, :times] = c
            ref[top, times:] = s
            ref[low, :times] = -s
            ref[low, times:] = c


def bank_table(own_time):
    times = own_time.shape[0]
    block = jnp.arange(NBLK, dtype=jnp.int32)[:, None] * own_time[None, :]
    block = jnp.stack(phase(block, NBLK), axis=1)
    inner = jnp.arange(BLOCK, dtype=jnp.int32)[:, None] * own_time[None, :]
    inner = jnp.stack(phase(inner, N1))
    return pl.pallas_call(
        bank_kernel,
        grid=(NBLK // BLOCKS,),
        in_specs=[
            pl.BlockSpec((BLOCKS, 2, times), lambda b: (b, 0, 0)),
            pl.BlockSpec((2, BLOCK, times), lambda b: (0, 0, 0)),
        ],
        out_specs=[pl.BlockSpec((BLOCKS * 2 * BLOCK, 2 * times), lambda b: (b, 0))] * 2,
        out_shape=[jax.ShapeDtypeStruct((2 * N1, 2 * times), BF16)] * 2,
        compiler_params=pltpu.CompilerParams(vmem_limit_bytes=VMEM_LIMIT),
        cost_estimate=COST,
        name="bank_table",
    )(block, inner)


def bins_first_kernel(pieces, banks, place_ref, edge_ref, *refs):
    own_refs, rest_refs = refs[:pieces], refs[pieces : 2 * pieces]
    wh_ref, wl_ref, tw_ref = refs[2 * pieces : 2 * pieces + 3]
    level_ref, total_ref, x, acc = refs[-4:]
    times = total_ref.shape[-1]
    cols = own_refs[0].shape[0]
    length = 2 * N1 // banks
    chunk = FOUR * LANES
    step = pl.program_id(0)

    @pl.when(step == 0)
    def _():
        for k in range(pieces):
            row = pl.multiple_of((place_ref[0] ^ k) * cols, cols)
            low = pl.multiple_of(row + pieces * cols, cols)
            for n in range(banks):
                ref = rest_refs[k] if n else own_refs[k]
                start = lax.rem(place_ref[1] + n, banks) * length

                def cut(i, carry):
                    lane = max(n - 1, 0) * length + i * chunk
                    part = split(ref[:, pl.ds(pl.multiple_of(lane, chunk), chunk)])
                    to = pl.ds(pl.multiple_of(start + i * chunk, chunk), chunk)
                    x[pl.ds(row, cols), to], x[pl.ds(low, cols), to] = part
                    return carry

                lax.fori_loop(0, length // chunk, cut, 0)
        total_ref[...] = jnp.zeros_like(total_ref)

    def blocks_at(block, blocks):
        at = pl.ds(pl.multiple_of(block * LANES, LANES), blocks * LANES)
        return rows_dot3(x[:, at], (wh_ref[at, :], wl_ref[at, :]))

    for i in range(TOGETHER):
        start, end = edge_ref[step * TOGETHER + i], edge_ref[step * TOGETHER + i + 1]
        odd = (end - start) % 2

        @pl.when(odd == 1)
        def _():
            acc[i] = blocks_at(end - 1, 1)

        @pl.when(odd == 0)
        def _():
            acc[i] = blocks_at(end - 2, 2)

        def two(n, carry):
            acc[i] += blocks_at(start + 2 * n, 2)
            return carry

        lax.fori_loop(0, (end - start - 1) // 2, two, 0)

    for u in range(pieces * cols // LANES):
        at = tile(u)
        cos, sin = tw_ref[0, at, :], tw_ref[1, at, :]
        sum_r, sum_i = total_ref[0, at, :], total_ref[1, at, :]
        for i in range(TOGETHER):
            re, im = acc[i, at, :times], acc[i, at, times:]
            vr, vi = re * cos - im * sin, re * sin + im * cos
            level_ref[i, 0, at, :] = vr
            level_ref[i, 1, at, :] = vi
            sum_r, sum_i = sum_r + vr, sum_i + vi
        total_ref[0, at, :] = sum_r
        total_ref[1, at, :] = sum_i


def bins_first(half, banks, place, edges, own, rest, table, twist, after):
    cols, length = rest[0].shape
    rows, times = twist.shape[1:]
    smem = pl.BlockSpec(memory_space=pltpu.SMEM)
    fixed = lambda shape: pl.BlockSpec(shape, lambda i: (0,) * len(shape))
    return pl.pallas_call(
        functools.partial(bins_first_kernel, len(own), banks),
        grid=(BINS // TOGETHER,),
        in_specs=[smem, smem]
        + [pl.BlockSpec((cols, 2 * N1 - length), lambda i: (half, 0))] * len(own)
        + [fixed((cols, length))] * len(rest)
        + [fixed((2 * N1, 2 * times))] * 2
        + [fixed((2, rows, times))]
        + [ANY] * len(after),
        out_specs=[
            pl.BlockSpec((TOGETHER, 2, rows, times), lambda i: (i, 0, 0, 0)),
            fixed((2, rows, times)),
        ],
        out_shape=[
            jax.ShapeDtypeStruct((BINS, 2, rows, times), F32),
            jax.ShapeDtypeStruct((2, rows, times), F32),
        ],
        scratch_shapes=[
            pltpu.VMEM((2 * rows, 2 * N1), BF16),
            pltpu.VMEM((TOGETHER, rows, 2 * times), F32),
        ],
        compiler_params=pltpu.CompilerParams(vmem_limit_bytes=VMEM_LIMIT),
        cost_estimate=COST,
        name="bins_first",
    )(place, edges, *own, *rest, *table, twist, *after)


def bins_second_kernel(halves, which_ref, scale_ref, gain_ref, share_ref, *refs):
    level_refs, total_refs = refs[:halves], refs[halves : 2 * halves]
    w2_ref, out_ref, snr_ref, chi, hold = refs[2 * halves :]
    times = out_ref.shape[0]
    part_rows = LANES // halves
    step = pl.program_id(0)

    @pl.when(step == 0)
    def _():
        chi[...] = jnp.zeros_like(chi)

    def rows_of(get, u):
        at = slice(u * part_rows, (u + 1) * part_rows)
        return jnp.concatenate([get(h, at) for h in range(halves)], axis=0)

    def keep(a, re, im):
        chi[a] += re * re + im * im

    for i in range(TOGETHER):
        gain, share = gain_ref[step * TOGETHER + i], share_ref[step * TOGETHER + i]

        def deviation(p):
            return lambda h, at: (
                level_refs[h][i, p, at, :] * gain - total_refs[h][p, at, :] * share
            )

        x = [tuple(rows_of(deviation(p), u) for p in range(2)) for u in range(FOUR)]
        second_points(x, w2_ref, keep)

    @pl.when(step == BINS // TOGETHER - 1)
    def _():
        scale = scale_ref[which_ref[0]]

        def whole(p):
            return lambda h, at: total_refs[h][p, at, :] * scale

        def put(a, re, im):
            for p, value in enumerate((re, im)):
                for g in range(times // LANES):
                    hold[p, g, pl.ds(a, LANES, stride=FOUR), :] = value[:, tile(g)]

        y = [tuple(rows_of(whole(p), u) for p in range(2)) for u in range(FOUR)]
        second_points(y, w2_ref, put)
        for g in range(times // LANES):
            for a in range(FOUR):
                hold[2, g, pl.ds(a, LANES, stride=FOUR), :] = chi[a, :, tile(g)]
            for p in range(2):
                snr_ref[0, 0, p, tile(g), :] = hold[p, g].T
            out_ref[tile(g), :] = hold[2, g].T


def bins_second(which, scale, gain, share, levels, totals, second, tmpls, dets):
    _, _, rows, times = levels[0].shape
    halves = len(levels)
    smem = pl.BlockSpec(memory_space=pltpu.SMEM)
    fixed = lambda shape: pl.BlockSpec(shape, lambda i, w: (0,) * len(shape))
    return pl.pallas_call(
        functools.partial(bins_second_kernel, halves),
        grid_spec=pltpu.PrefetchScalarGridSpec(
            num_scalar_prefetch=1,
            grid=(BINS // TOGETHER,),
            in_specs=[smem, smem, smem]
            + [pl.BlockSpec((TOGETHER, 2, rows, times), lambda i, w: (i, 0, 0, 0))] * halves
            + [fixed((2, rows, times))] * halves
            + [fixed((FOUR * 4 * LANES, 2 * LANES))],
            out_specs=[
                fixed((times, N2)),
                pl.BlockSpec((1, 1, 2, times, N2), lambda i, w: (w[0], w[1], 0, 0, 0)),
            ],
            scratch_shapes=[
                pltpu.VMEM((FOUR, LANES, times), F32),
                pltpu.VMEM((3, times // LANES, N2, LANES), F32),
            ],
        ),
        out_shape=[
            jax.ShapeDtypeStruct((times, N2), F32),
            jax.ShapeDtypeStruct((tmpls, dets, 2, times, N2), F32),
        ],
        compiler_params=pltpu.CompilerParams(vmem_limit_bytes=VMEM_LIMIT),
        cost_estimate=COST,
        name="bins_second",
    )(which, scale, gain, share, *levels, *totals, second)


def handed_on(arrays, after):
    count = len(arrays)
    return pl.pallas_call(
        lambda *refs: None,
        in_specs=[ANY] * (count + len(after)),
        out_specs=[ANY] * count,
        out_shape=[jax.ShapeDtypeStruct(x.shape, x.dtype) for x in arrays],
        input_output_aliases={i: i for i in range(count)},
        compiler_params=pltpu.CompilerParams(vmem_limit_bytes=VMEM_LIMIT),
        cost_estimate=COST,
        name="handed_on",
    )(*arrays, *after)


def swap(x, freq, k):
    return lax.ppermute(x, "freq", [(i, i ^ k) for i in range(freq)])


def far_pieces(own, freq):
    return [own] + [swap(own, freq, k) for k in range(2, freq, 2)]


def near_pieces(far, freq):
    return [x for even in far for x in (even, swap(even, freq, 1))]


def per_device(strain, templates, coinc_tmpl, coinc_det, bin_edges):
    freq, banks = lax.axis_size("freq"), lax.axis_size("bank")
    place = lax.axis_index("freq").astype(jnp.int32)
    bank = lax.axis_index("bank").astype(jnp.int32)
    tmpls, _, cols, _ = templates.shape
    slots, dets = coinc_tmpl.shape[0], strain.shape[0]
    times = N1 // freq
    part = cols // HALVES

    slices = [strain[:, :, h * part : (h + 1) * part] for h in range(HALVES)]
    strains = [lax.all_gather(x, "bank", axis=0, tiled=False) for x in slices]
    first = tuple(jnp.asarray(t) for t in first_table())
    second = jnp.asarray(second_table(cols, HALVES))
    stage = jnp.asarray(stage_table())

    column = place * cols + jnp.arange(cols, dtype=jnp.int32)
    lane = jnp.arange(N1, dtype=jnp.int32)
    time_of_lane = lane // LANES + COARSE * (lane % LANES)
    twist = jnp.stack(phase(column[:, None] * time_of_lane[None, :], N1 * N2))
    own_time = place * times + jnp.arange(times, dtype=jnp.int32)
    table = bank_table(own_time)
    own_twist = []
    for h in range(HALVES):
        rows = jnp.arange(freq * part, dtype=jnp.int32)
        rows = rows // part * cols + h * part + rows % part
        own_twist.append(jnp.stack(phase(rows[:, None] * own_time[None, :], N1 * N2)))

    which = [jnp.stack([coinc_tmpl[j], coinc_det[j], bank]) for j in range(slots)]
    series = jnp.arange(tmpls * dets - 1, dtype=jnp.int32)
    series = series + (series >= which[0][0] * dets + which[0][1])
    info = jnp.stack([series // dets, series % dets], axis=1).reshape(-1)
    info = jnp.concatenate([place.reshape(1), info])
    ends = jnp.zeros((1,), jnp.int32), jnp.full((1,), NBLK, jnp.int32)
    edges = [
        jnp.concatenate([ends[0], bin_edges[coinc_tmpl[j]], ends[1]]) for j in range(slots)
    ]
    here = jnp.stack([place, bank])

    power = (templates[:, 0] ** 2 + templates[:, 1] ** 2).sum(axis=1)
    power = power.reshape(tmpls, NBLK, BLOCK).sum(axis=2)
    own = [entry_product((0,), banks, 0, w, templates, strain[None], slices) for w in which]
    wide = own[0].shape[1]
    power = jnp.pad(power.reshape(1, -1), ((0, 7), (0, wide - tmpls * NBLK)))
    own[0] = jnp.concatenate([own[0], power], axis=0)
    own = [near_pieces(far_pieces(x, freq), freq) for x in own]
    gathered = [x for entry in own for x in entry[1:]]

    block_power = sum(x[cols, : tmpls * NBLK] for x in own[0]).reshape(tmpls, NBLK)
    sigma_sq = block_power.sum(axis=1)
    inv_sigma = lax.rsqrt(sigma_sq)
    bin_of = jnp.sum(
        jnp.arange(NBLK, dtype=jnp.int32)[None, :, None] >= bin_edges[:, None, :], axis=2
    )
    inside = bin_of[:, None, :] == jnp.arange(BINS, dtype=jnp.int32)[None, :, None]
    weights = jnp.where(inside, block_power[:, None, :], 0.0).sum(axis=2) / sigma_sq[:, None]
    gains = [inv_sigma[coinc_tmpl[j]] * lax.rsqrt(weights[coinc_tmpl[j]]) for j in range(slots)]
    shares = [gains[j] * weights[coinc_tmpl[j]] for j in range(slots)]
    which, inv_sigma, gains, shares, twist, info, edges, here, table, own_twist = (
        lax.optimization_barrier(
            (which, inv_sigma, gains, shares, twist, info, edges, here, table, own_twist)
        )
    )

    parts, halves = [], []
    later = tuple(range(1, banks))
    for h in range(HALVES):
        after = [x[0] for x in halves[-1]] if halves else gathered
        half = [entry_product(later, banks, h, w, templates, strains[h], after) for w in which]
        far = [far_pieces(x, freq) for x in half]
        sent, token = first_section(
            freq, h, info, templates, strains[h], first, stage, twist, half
        )
        far = [x[:1] + list(handed_on(x[1:], [token] + parts)) for x in far]
        rest = [near_pieces(x, freq) for x in far]
        (ready,) = handed_on([sent], [x for entry in rest for x in entry[1:]])
        got = lax.all_to_all(
            ready.reshape(freq, -1, LANES), "freq", split_axis=0, concat_axis=0, tiled=True
        )
        parts.append(got.reshape(ready.shape))
        halves.append(
            [
                bins_first(
                    h, banks, here, edges[j], own[j], rest[j], table, own_twist[h], [ready]
                )
                for j in range(slots)
            ]
        )

    chi, snr = [], None
    for j in range(slots):
        levels, totals = zip(*[x[j] for x in halves])
        one, series_of = bins_second(
            which[j], inv_sigma, gains[j], shares[j], levels, totals, second, tmpls, dets
        )
        chi.append(one)
        snr = series_of if snr is None else snr
    snr = second_section(freq, info, inv_sigma, parts, second, snr, chi)
    return (snr, jnp.stack(chi))


def solution(mesh):
    placed = (
        P(None, None, "freq", "bank"),
        P("bank", None, "freq", None),
        P("bank"),
        P("bank"),
        P("bank", None),
    )
    return jax.shard_map(
        per_device,
        mesh=mesh,
        in_specs=placed,
        out_specs=(P("bank", None, None, "freq", None), P("bank", "freq", None)),
        check_vma=False,
    )
```

```python
import functools

import jax
import jax.numpy as jnp
import ml_dtypes
import numpy as np
from jax import lax
from jax.experimental import pallas as pl
from jax.experimental.pallas import tpu as pltpu
from jax.sharding import PartitionSpec as P

N1 = 2048
N2 = 512
NBLK = 32
BLOCK = N1 // NBLK
BINS = 16
LANES = 128
COARSE = N1 // LANES
FOUR = N2 // LANES
F32 = jnp.float32
BF16 = jnp.bfloat16
MIB = 1 << 20
VMEM_LIMIT = 56 * MIB
ANY = pl.BlockSpec(memory_space=pl.ANY)
COST = pl.CostEstimate(flops=MIB, bytes_accessed=MIB, transcendentals=0)


def split_table(table):
    high = table.astype(ml_dtypes.bfloat16)
    low = (table - high.astype(np.float64)).astype(ml_dtypes.bfloat16)
    return high, low


def first_table():
    angle = 2 * np.pi * (np.outer(np.arange(LANES), np.arange(LANES)) % LANES) / LANES
    cos, sin = np.cos(angle), np.sin(angle)
    return split_table(np.block([[cos, sin], [-sin, cos]]))


def stage_table():
    angle = 2 * np.pi * np.outer(np.arange(COARSE), np.arange(LANES)) / N1
    return np.concatenate([np.cos(angle), np.sin(angle)]).astype(np.float32)


def second_table(cols, halves):
    order = np.arange(LANES).reshape(LANES // cols, halves, cols // halves)
    order = order.transpose(1, 0, 2).reshape(-1)
    blocks = []
    for a in range(FOUR):
        n2 = a + FOUR * np.arange(LANES)
        angle = 2 * np.pi * (np.outer(n2, order) % N2) / N2
        cos, sin = np.cos(angle), np.sin(angle)
        blocks.append(np.block([[cos, -sin], [sin, cos]]))
    return np.concatenate([part for block in blocks for part in split_table(block)])


def split(x):
    high = x.astype(BF16)
    return high, (x - high.astype(F32)).astype(BF16)


def phase(index, length):
    angle = (index % length).astype(F32) * (2.0 * np.pi / length)
    return jnp.cos(angle), jnp.sin(angle)


def times_i(z):
    return (-z[1], z[0])


def plus(x, y):
    return (x[0] + y[0], x[1] + y[1])


def minus(x, y):
    return (x[0] - y[0], x[1] - y[1])


def dft4(x):
    s0, s1 = plus(x[0], x[2]), minus(x[0], x[2])
    s2, s3 = plus(x[1], x[3]), times_i(minus(x[1], x[3]))
    return [plus(s0, s2), plus(s1, s3), minus(s0, s2), minus(s1, s3)]


def turn(z, step):
    step %= 16
    if step == 0:
        return z
    if step == 4:
        return times_i(z)
    if step == 8:
        return (-z[0], -z[1])
    half = float(np.sqrt(0.5))
    if step == 2:
        return ((z[0] - z[1]) * half, (z[0] + z[1]) * half)
    if step == 6:
        return ((z[0] + z[1]) * -half, (z[0] - z[1]) * half)
    cos, sin = float(np.cos(np.pi * step / 8)), float(np.sin(np.pi * step / 8))
    return (z[0] * cos - z[1] * sin, z[0] * sin + z[1] * cos)


def dft16(x):
    columns = [dft4([x[4 * u1 + u0] for u1 in range(4)]) for u0 in range(4)]
    out = [None] * 16
    for a0 in range(4):
        ys = dft4([turn(columns[u0][a0], u0 * a0) for u0 in range(4)])
        for a1 in range(4):
            out[a0 + 4 * a1] = ys[a1]
    return out


def dot3(left, right):
    (lh, ll), (rh, rl) = left, right
    return jnp.dot(
        jnp.concatenate([lh, lh, ll], axis=1),
        jnp.concatenate([rh, rl, rh], axis=0),
        preferred_element_type=F32,
    )


def rows_dot3(left, right):
    half = left.shape[0] // 2
    high, low = right
    both = jnp.dot(left, high, preferred_element_type=F32)
    cross = jnp.dot(left[:half], low, preferred_element_type=F32)
    return both[:half] + (both[half:] + cross)


def products(tmpl, strain_ref, where, rows=slice(None)):
    per_piece = COARSE // strain_ref.shape[0]
    for u in range(COARSE):
        off = u % per_piece
        there = slice(off * LANES, (off + 1) * LANES)
        hr, hi = tmpl(0, u), tmpl(1, u)
        sr = strain_ref[(u // per_piece,) + where + (0, rows, there)]
        si = strain_ref[(u // per_piece,) + where + (1, rows, there)]
        yield u, hr * sr + hi * si, hr * si - hi * sr


def tile(u):
    return slice(u * LANES, (u + 1) * LANES)


def first_kernel(
    freq, info_ref, tmpl_ref, strain_ref, wh_ref, wl_ref, stage_ref, tw_ref, *refs
):
    out_ref, token_ref, gh, gl, z = refs[-5:]
    token_ref[...] = jnp.zeros_like(token_ref)
    rows = tmpl_ref.shape[2]
    for r in range(0, rows, ROWS):
        at = slice(r, r + ROWS)
        got = products(lambda p, u: tmpl_ref[0, p, at, tile(u)], strain_ref, (0,), at)
        y = dft16([(re, im) for _, re, im in got])
        for a in range(COARSE):
            cos, sin = stage_ref[a : a + 1, :], stage_ref[COARSE + a : COARSE + a + 1, :]
            yr, yi = y[a]
            to = slice(a * rows + r, a * rows + r + ROWS)
            gh[to, :LANES], gl[to, :LANES] = split(yr * cos - yi * sin)
            gh[to, LANES:], gl[to, LANES:] = split(yr * sin + yi * cos)
    z[...] = dot3((gh[...], gl[...]), (wh_ref[...], wl_ref[...]))
    width = LANES // freq
    slot = lax.broadcasted_iota(jnp.int32, (ROWS, LANES), 1) // width
    for group in range(COARSE // freq):
        for r in range(0, rows, ROWS):
            at = slice(r, r + ROWS)
            turned = []
            for i in range(freq):
                a = group * freq + i
                to = slice(a * rows + r, a * rows + r + ROWS)
                zr, zi = z[to, :LANES], z[to, LANES:]
                cos, sin = tw_ref[0, at, tile(a)], tw_ref[1, at, tile(a)]
                pair = (zr * cos - zi * sin, zr * sin + zi * cos)
                if i:
                    pair = tuple(pltpu.roll(v, i * width, 1) for v in pair)
                turned.append(pair)
            for q in range(freq):
                for p in range(2):
                    value = turned[(0 - q) % freq][p]
                    for s in range(1, freq):
                        value = jnp.where(slot == s, turned[(s - q) % freq][p], value)
                    out_ref[q, 0, p, group, at] = value


ROWS = 16
HALVES = 2
TOGETHER = 2


def first_section(freq, half, info, templates, strain, first, stage, twist, after):
    tmpls = templates.shape[0]
    pieces, dets, _, rows, piece_len = strain.shape
    series = tmpls * dets - 1
    groups = COARSE // freq
    table = pl.BlockSpec((2 * LANES, 2 * LANES), lambda i, n: (0, 0))
    out = (freq, series, 2, groups, rows, LANES)
    return pl.pallas_call(
        functools.partial(first_kernel, freq),
        grid_spec=pltpu.PrefetchScalarGridSpec(
            num_scalar_prefetch=1,
            grid=(series,),
            in_specs=[
                pl.BlockSpec(
                    (1, 2, rows, N1), lambda i, n: (n[1 + 2 * i], 0, half, 0)
                ),
                pl.BlockSpec(
                    (pieces, 1, 2, rows, piece_len), lambda i, n: (0, n[2 + 2 * i], 0, 0, 0)
                ),
                table,
                table,
                pl.BlockSpec((2 * COARSE, LANES), lambda i, n: (0, 0)),
                pl.BlockSpec((2, rows, N1), lambda i, n: (0, half, 0)),
            ]
            + [ANY] * len(after),
            out_specs=[
                pl.BlockSpec(
                    (freq, 1, 2, groups, rows, LANES), lambda i, n: (0, i, 0, 0, 0, 0)
                ),
                pl.BlockSpec((8, LANES), lambda i, n: (0, 0)),
            ],
            scratch_shapes=[
                pltpu.VMEM((COARSE * rows, 2 * LANES), BF16),
                pltpu.VMEM((COARSE * rows, 2 * LANES), BF16),
                pltpu.VMEM((COARSE * rows, 2 * LANES), F32),
            ],
        ),
        out_shape=[
            jax.ShapeDtypeStruct(out, F32),
            jax.ShapeDtypeStruct((8, LANES), F32),
        ],
        compiler_params=pltpu.CompilerParams(vmem_limit_bytes=VMEM_LIMIT),
        cost_estimate=pl.CostEstimate(
            flops=60 * series * rows * N1 * LANES, bytes_accessed=16 * MIB, transcendentals=0
        ),
        name="first_section",
    )(info, templates, strain, first[0], first[1], stage, twist, *after)


def entry_kernel(steps, banks, which_ref, tmpl_ref, strain_ref, *refs):
    out_ref = refs[-1]
    length = N1 // banks
    first_half = lax.broadcasted_iota(jnp.int32, (ROWS, LANES), 1) < BLOCK
    for n, k in enumerate(steps):
        part = lax.rem(which_ref[2] + k, banks)
        for u in range(length // LANES):
            lane = pl.ds(pl.multiple_of(part * length + u * LANES, LANES), LANES)
            hr, hi = tmpl_ref[0, 0, :, lane], tmpl_ref[0, 1, :, lane]
            piece = 0 if strain_ref.shape[0] == 1 else part
            sr, si = strain_ref[piece, 0, 0, :, tile(u)], strain_ref[piece, 0, 1, :, tile(u)]
            re, im = hr * sr + hi * si, hr * si - hi * sr
            to = 2 * (n * length // LANES + u)
            out_ref[:, tile(to)] = jnp.where(first_half, re, pltpu.roll(im, BLOCK, 1))
            out_ref[:, tile(to + 1)] = jnp.where(first_half, pltpu.roll(re, BLOCK, 1), im)


def entry_product(steps, banks, half, which, templates, strain, after):
    pieces, _, _, cols, length = strain.shape
    first = half * cols // ROWS
    return pl.pallas_call(
        functools.partial(entry_kernel, steps, banks),
        grid_spec=pltpu.PrefetchScalarGridSpec(
            num_scalar_prefetch=1,
            grid=(cols // ROWS,),
            in_specs=[
                pl.BlockSpec((1, 2, ROWS, N1), lambda c, w: (w[0], 0, first + c, 0)),
                pl.BlockSpec((pieces, 1, 2, ROWS, length), lambda c, w: (0, w[1], 0, c, 0)),
            ]
            + [ANY] * len(after),
            out_specs=pl.BlockSpec((ROWS, 2 * length * len(steps)), lambda c, w: (c, 0)),
        ),
        out_shape=jax.ShapeDtypeStruct((cols, 2 * length * len(steps)), F32),
        compiler_params=pltpu.CompilerParams(vmem_limit_bytes=VMEM_LIMIT),
        cost_estimate=COST,
        name="entry_product",
    )(which, templates, strain, *after)


def second_points(get, w2_ref, y_ref, use):
    for r in range(0, LANES, ROWS):
        for g in range(y_ref.shape[-1] // LANES):
            x = [(get(0, u, r, g), get(1, u, r, g)) for u in range(FOUR)]
            for a, y in enumerate(dft4(x)):
                for p in range(2):
                    at = slice(p * LANES + r, p * LANES + r + ROWS)
                    y_ref[a, 0, at, tile(g)], y_ref[a, 1, at, tile(g)] = split(y[p])
    for a in range(FOUR):
        table = w2_ref[a * 4 * LANES : (a + 1) * 4 * LANES, :]
        z = rows_dot3(table, (y_ref[a, 0], y_ref[a, 1]))
        use(a, z[:LANES], z[LANES:])


def second_kernel(freq, halves, info_ref, scale_ref, *refs):
    part_refs, w2_ref = refs[:halves], refs[halves]
    out_ref, hold, order, y_ref = refs[-4:]
    place = info_ref[0]
    groups, cols = part_refs[0].shape[3:5]
    per = LANES // (halves * cols)
    width = LANES // freq
    scale = scale_ref[info_ref[1 + 2 * pl.program_id(0)]]

    def get(p, u, r, g):
        half, row = divmod(r, per * cols)
        device, row = divmod(row, cols)
        return part_refs[half][u * per + device, 0, p, g, row : row + ROWS, :]

    def keep(a, re, im):
        for p, value in enumerate((re, im)):
            for g in range(groups):
                hold[p, g, pl.ds(a, LANES, stride=FOUR), :] = value[:, tile(g)] * scale

    second_points(get, w2_ref, y_ref, keep)
    for p in range(2):
        for g in range(groups):
            turned = hold[p, g].T
            for s in range(freq):
                a = g * freq + lax.rem(s - place + freq, freq)
                for j in range(FOUR):
                    order[p, j, pl.ds(a, width, stride=COARSE), :] = turned[
                        s * width : (s + 1) * width, tile(j)
                    ]
        for j in range(FOUR):
            out_ref[0, 0, p, :, tile(j)] = order[p, j]


def second_section(freq, info, scale, parts, second, snr, after):
    _, series, _, groups, cols, _ = parts[0].shape
    halves = len(parts)
    times = groups * LANES
    smem = pl.BlockSpec(memory_space=pltpu.SMEM)
    table = pl.BlockSpec((FOUR * 4 * LANES, 2 * LANES), lambda i, n: (0, 0))
    part = pl.BlockSpec(
        (freq, 1, 2, groups, cols, LANES), lambda i, n: (0, i, 0, 0, 0, 0)
    )
    return pl.pallas_call(
        functools.partial(second_kernel, freq, halves),
        grid_spec=pltpu.PrefetchScalarGridSpec(
            num_scalar_prefetch=1,
            grid=(series,),
            in_specs=[smem] + [part] * halves + [table, ANY] + [ANY] * len(after),
            out_specs=pl.BlockSpec(
                (1, 1, 2, times, N2), lambda i, n: (n[1 + 2 * i], n[2 + 2 * i], 0, 0, 0)
            ),
            scratch_shapes=[
                pltpu.VMEM((2, groups, N2, LANES), F32),
                pltpu.VMEM((2, FOUR, times, LANES), F32),
                pltpu.VMEM((FOUR, 2, 2 * LANES, times), BF16),
            ],
        ),
        out_shape=jax.ShapeDtypeStruct(snr.shape, F32),
        input_output_aliases={3 + halves: 0},
        compiler_params=pltpu.CompilerParams(vmem_limit_bytes=VMEM_LIMIT),
        cost_estimate=COST,
        name="second_section",
    )(info, scale, *parts, second, snr, *after)


BLOCKS = 4


def bank_kernel(block_ref, inner_ref, high_ref, low_ref):
    times = block_ref.shape[-1]
    rc, rs = inner_ref[0], inner_ref[1]
    for b in range(BLOCKS):
        bc, bs = block_ref[b, 0:1, :], block_ref[b, 1:2, :]
        cos, sin = split(bc * rc - bs * rs), split(bc * rs + bs * rc)
        top = slice(2 * b * BLOCK, (2 * b + 1) * BLOCK)
        low = slice((2 * b + 1) * BLOCK, (2 * b + 2) * BLOCK)
        for ref, c, s in zip((high_ref, low_ref), cos, sin):
            ref[top, :times] = c
            ref[top, times:] = s
            ref[low, :times] = -s
            ref[low, times:] = c


def bank_table(own_time):
    times = own_time.shape[0]
    block = jnp.arange(NBLK, dtype=jnp.int32)[:, None] * own_time[None, :]
    block = jnp.stack(phase(block, NBLK), axis=1)
    inner = jnp.arange(BLOCK, dtype=jnp.int32)[:, None] * own_time[None, :]
    inner = jnp.stack(phase(inner, N1))
    return pl.pallas_call(
        bank_kernel,
        grid=(NBLK // BLOCKS,),
        in_specs=[
            pl.BlockSpec((BLOCKS, 2, times), lambda b: (b, 0, 0)),
            pl.BlockSpec((2, BLOCK, times), lambda b: (0, 0, 0)),
        ],
        out_specs=[pl.BlockSpec((BLOCKS * 2 * BLOCK, 2 * times), lambda b: (b, 0))] * 2,
        out_shape=[jax.ShapeDtypeStruct((2 * N1, 2 * times), BF16)] * 2,
        compiler_params=pltpu.CompilerParams(vmem_limit_bytes=VMEM_LIMIT),
        cost_estimate=COST,
        name="bank_table",
    )(block, inner)


def bins_first_kernel(pieces, banks, place_ref, edge_ref, *refs):
    own_refs, rest_refs = refs[:pieces], refs[pieces : 2 * pieces]
    wh_ref, wl_ref, tw_ref = refs[2 * pieces : 2 * pieces + 3]
    level_ref, total_ref, x, acc = refs[-4:]
    times = total_ref.shape[-1]
    cols = own_refs[0].shape[0]
    length = 2 * N1 // banks
    chunk = FOUR * LANES
    step = pl.program_id(0)

    @pl.when(step == 0)
    def _():
        for k in range(pieces):
            row = pl.multiple_of((place_ref[0] ^ k) * cols, cols)
            low = pl.multiple_of(row + pieces * cols, cols)
            for n in range(banks):
                ref = rest_refs[k] if n else own_refs[k]
                start = lax.rem(place_ref[1] + n, banks) * length

                def cut(i, carry):
                    lane = max(n - 1, 0) * length + i * chunk
                    part = split(ref[:, pl.ds(pl.multiple_of(lane, chunk), chunk)])
                    to = pl.ds(pl.multiple_of(start + i * chunk, chunk), chunk)
                    x[pl.ds(row, cols), to], x[pl.ds(low, cols), to] = part
                    return carry

                lax.fori_loop(0, length // chunk, cut, 0)
        total_ref[...] = jnp.zeros_like(total_ref)

    def blocks_at(block, blocks):
        at = pl.ds(pl.multiple_of(block * LANES, LANES), blocks * LANES)
        return rows_dot3(x[:, at], (wh_ref[at, :], wl_ref[at, :]))

    for i in range(TOGETHER):
        start, end = edge_ref[step * TOGETHER + i], edge_ref[step * TOGETHER + i + 1]
        odd = (end - start) % 2

        @pl.when(odd == 1)
        def _():
            acc[i] = blocks_at(end - 1, 1)

        @pl.when(odd == 0)
        def _():
            acc[i] = blocks_at(end - 2, 2)

        def two(n, carry):
            acc[i] += blocks_at(start + 2 * n, 2)
            return carry

        lax.fori_loop(0, (end - start - 1) // 2, two, 0)

    for r in range(0, pieces * cols, ROWS):
        at = slice(r, r + ROWS)
        for g in range(times // LANES):
            cos, sin = tw_ref[0, at, tile(g)], tw_ref[1, at, tile(g)]
            sum_r, sum_i = total_ref[0, at, tile(g)], total_ref[1, at, tile(g)]
            for i in range(TOGETHER):
                re, im = acc[i, at, tile(g)], acc[i, at, tile(times // LANES + g)]
                vr, vi = re * cos - im * sin, re * sin + im * cos
                level_ref[i, 0, at, tile(g)] = vr
                level_ref[i, 1, at, tile(g)] = vi
                sum_r, sum_i = sum_r + vr, sum_i + vi
            total_ref[0, at, tile(g)] = sum_r
            total_ref[1, at, tile(g)] = sum_i


def bins_first(half, banks, place, edges, own, rest, table, twist, after):
    cols, length = rest[0].shape
    rows, times = twist.shape[1:]
    smem = pl.BlockSpec(memory_space=pltpu.SMEM)
    fixed = lambda shape: pl.BlockSpec(shape, lambda i: (0,) * len(shape))
    return pl.pallas_call(
        functools.partial(bins_first_kernel, len(own), banks),
        grid=(BINS // TOGETHER,),
        in_specs=[smem, smem]
        + [pl.BlockSpec((cols, 2 * N1 - length), lambda i: (half, 0))] * len(own)
        + [fixed((cols, length))] * len(rest)
        + [fixed((2 * N1, 2 * times))] * 2
        + [fixed((2, rows, times))]
        + [ANY] * len(after),
        out_specs=[
            pl.BlockSpec((TOGETHER, 2, rows, times), lambda i: (i, 0, 0, 0)),
            fixed((2, rows, times)),
        ],
        out_shape=[
            jax.ShapeDtypeStruct((BINS, 2, rows, times), F32),
            jax.ShapeDtypeStruct((2, rows, times), F32),
        ],
        scratch_shapes=[
            pltpu.VMEM((2 * rows, 2 * N1), BF16),
            pltpu.VMEM((TOGETHER, rows, 2 * times), F32),
        ],
        compiler_params=pltpu.CompilerParams(vmem_limit_bytes=VMEM_LIMIT),
        cost_estimate=COST,
        name="bins_first",
    )(place, edges, *own, *rest, *table, twist, *after)


def bins_second_kernel(halves, which_ref, scale_ref, gain_ref, share_ref, *refs):
    level_refs, total_refs = refs[:halves], refs[halves : 2 * halves]
    w2_ref, out_ref, snr_ref, chi, hold, y_ref = refs[2 * halves :]
    times = out_ref.shape[0]
    part_rows = LANES // halves
    step = pl.program_id(0)

    @pl.when(step == 0)
    def _():
        chi[...] = jnp.zeros_like(chi)

    def place_of(u, r):
        half, row = divmod(r, part_rows)
        row += u * part_rows
        return half, slice(row, row + ROWS)

    def keep(a, re, im):
        chi[a] += re * re + im * im

    for i in range(TOGETHER):
        gain, share = gain_ref[step * TOGETHER + i], share_ref[step * TOGETHER + i]

        def deviation(p, u, r, g):
            h, at = place_of(u, r)
            whole = total_refs[h][p, at, tile(g)]
            return level_refs[h][i, p, at, tile(g)] * gain - whole * share

        second_points(deviation, w2_ref, y_ref.at[i], keep)

    @pl.when(step == BINS // TOGETHER - 1)
    def _():
        scale = scale_ref[which_ref[0]]

        def whole(p, u, r, g):
            h, at = place_of(u, r)
            return total_refs[h][p, at, tile(g)] * scale

        def put(a, re, im):
            for p, value in enumerate((re, im)):
                for g in range(times // LANES):
                    hold[p, g, pl.ds(a, LANES, stride=FOUR), :] = value[:, tile(g)]

        second_points(whole, w2_ref, y_ref.at[0], put)
        for g in range(times // LANES):
            for a in range(FOUR):
                hold[2, g, pl.ds(a, LANES, stride=FOUR), :] = chi[a, :, tile(g)]
            for p in range(2):
                snr_ref[0, 0, p, tile(g), :] = hold[p, g].T
            out_ref[tile(g), :] = hold[2, g].T


def bins_second(which, scale, gain, share, levels, totals, second, tmpls, dets):
    _, _, rows, times = levels[0].shape
    halves = len(levels)
    smem = pl.BlockSpec(memory_space=pltpu.SMEM)
    fixed = lambda shape: pl.BlockSpec(shape, lambda i, w: (0,) * len(shape))
    return pl.pallas_call(
        functools.partial(bins_second_kernel, halves),
        grid_spec=pltpu.PrefetchScalarGridSpec(
            num_scalar_prefetch=1,
            grid=(BINS // TOGETHER,),
            in_specs=[smem, smem, smem]
            + [pl.BlockSpec((TOGETHER, 2, rows, times), lambda i, w: (i, 0, 0, 0))] * halves
            + [fixed((2, rows, times))] * halves
            + [fixed((FOUR * 4 * LANES, 2 * LANES))],
            out_specs=[
                fixed((times, N2)),
                pl.BlockSpec((1, 1, 2, times, N2), lambda i, w: (w[0], w[1], 0, 0, 0)),
            ],
            scratch_shapes=[
                pltpu.VMEM((FOUR, LANES, times), F32),
                pltpu.VMEM((3, times // LANES, N2, LANES), F32),
                pltpu.VMEM((TOGETHER, FOUR, 2, 2 * LANES, times), BF16),
            ],
        ),
        out_shape=[
            jax.ShapeDtypeStruct((times, N2), F32),
            jax.ShapeDtypeStruct((tmpls, dets, 2, times, N2), F32),
        ],
        compiler_params=pltpu.CompilerParams(vmem_limit_bytes=VMEM_LIMIT),
        cost_estimate=COST,
        name="bins_second",
    )(which, scale, gain, share, *levels, *totals, second)


def handed_on(arrays, after):
    count = len(arrays)
    return pl.pallas_call(
        lambda *refs: None,
        in_specs=[ANY] * (count + len(after)),
        out_specs=[ANY] * count,
        out_shape=[jax.ShapeDtypeStruct(x.shape, x.dtype) for x in arrays],
        input_output_aliases={i: i for i in range(count)},
        compiler_params=pltpu.CompilerParams(vmem_limit_bytes=VMEM_LIMIT),
        cost_estimate=COST,
        name="handed_on",
    )(*arrays, *after)


def swap(x, freq, k):
    return lax.ppermute(x, "freq", [(i, i ^ k) for i in range(freq)])


def far_pieces(own, freq):
    return [own] + [swap(own, freq, k) for k in range(2, freq, 2)]


def near_pieces(far, freq):
    return [x for even in far for x in (even, swap(even, freq, 1))]


def per_device(strain, templates, coinc_tmpl, coinc_det, bin_edges):
    freq, banks = lax.axis_size("freq"), lax.axis_size("bank")
    place = lax.axis_index("freq").astype(jnp.int32)
    bank = lax.axis_index("bank").astype(jnp.int32)
    tmpls, _, cols, _ = templates.shape
    slots, dets = coinc_tmpl.shape[0], strain.shape[0]
    times = N1 // freq
    part = cols // HALVES

    slices = [strain[:, :, h * part : (h + 1) * part] for h in range(HALVES)]
    strains = [lax.all_gather(x, "bank", axis=0, tiled=False) for x in slices]
    first = tuple(jnp.asarray(t) for t in first_table())
    second = jnp.asarray(second_table(cols, HALVES))
    stage = jnp.asarray(stage_table())

    column = place * cols + jnp.arange(cols, dtype=jnp.int32)
    lane = jnp.arange(N1, dtype=jnp.int32)
    time_of_lane = lane // LANES + COARSE * (lane % LANES)
    twist = jnp.stack(phase(column[:, None] * time_of_lane[None, :], N1 * N2))
    own_time = place * times + jnp.arange(times, dtype=jnp.int32)
    table = bank_table(own_time)
    own_twist = []
    for h in range(HALVES):
        rows = jnp.arange(freq * part, dtype=jnp.int32)
        rows = rows // part * cols + h * part + rows % part
        own_twist.append(jnp.stack(phase(rows[:, None] * own_time[None, :], N1 * N2)))

    which = [jnp.stack([coinc_tmpl[j], coinc_det[j], bank]) for j in range(slots)]
    series = jnp.arange(tmpls * dets - 1, dtype=jnp.int32)
    series = series + (series >= which[0][0] * dets + which[0][1])
    info = jnp.stack([series // dets, series % dets], axis=1).reshape(-1)
    info = jnp.concatenate([place.reshape(1), info])
    ends = jnp.zeros((1,), jnp.int32), jnp.full((1,), NBLK, jnp.int32)
    edges = [
        jnp.concatenate([ends[0], bin_edges[coinc_tmpl[j]], ends[1]]) for j in range(slots)
    ]
    here = jnp.stack([place, bank])

    power = (templates[:, 0] ** 2 + templates[:, 1] ** 2).sum(axis=1)
    power = power.reshape(tmpls, NBLK, BLOCK).sum(axis=2)
    own = [entry_product((0,), banks, 0, w, templates, strain[None], slices) for w in which]
    wide = own[0].shape[1]
    power = jnp.pad(power.reshape(1, -1), ((0, 7), (0, wide - tmpls * NBLK)))
    own[0] = jnp.concatenate([own[0], power], axis=0)
    own = [near_pieces(far_pieces(x, freq), freq) for x in own]
    gathered = [x for entry in own for x in entry[1:]]

    block_power = sum(x[cols, : tmpls * NBLK] for x in own[0]).reshape(tmpls, NBLK)
    sigma_sq = block_power.sum(axis=1)
    inv_sigma = lax.rsqrt(sigma_sq)
    bin_of = jnp.sum(
        jnp.arange(NBLK, dtype=jnp.int32)[None, :, None] >= bin_edges[:, None, :], axis=2
    )
    inside = bin_of[:, None, :] == jnp.arange(BINS, dtype=jnp.int32)[None, :, None]
    weights = jnp.where(inside, block_power[:, None, :], 0.0).sum(axis=2) / sigma_sq[:, None]
    gains = [inv_sigma[coinc_tmpl[j]] * lax.rsqrt(weights[coinc_tmpl[j]]) for j in range(slots)]
    shares = [gains[j] * weights[coinc_tmpl[j]] for j in range(slots)]
    which, inv_sigma, gains, shares, twist, info, edges, here, table, own_twist = (
        lax.optimization_barrier(
            (which, inv_sigma, gains, shares, twist, info, edges, here, table, own_twist)
        )
    )

    parts, halves = [], []
    later = tuple(range(1, banks))
    for h in range(HALVES):
        after = [x[0] for x in halves[-1]] if halves else gathered
        half = [entry_product(later, banks, h, w, templates, strains[h], after) for w in which]
        far = [far_pieces(x, freq) for x in half]
        sent, token = first_section(
            freq, h, info, templates, strains[h], first, stage, twist, half
        )
        far = [x[:1] + list(handed_on(x[1:], [token] + parts)) for x in far]
        rest = [near_pieces(x, freq) for x in far]
        (ready,) = handed_on([sent], [x for entry in rest for x in entry[1:]])
        got = lax.all_to_all(
            ready.reshape(freq, -1, LANES), "freq", split_axis=0, concat_axis=0, tiled=True
        )
        parts.append(got.reshape(ready.shape))
        halves.append(
            [
                bins_first(
                    h, banks, here, edges[j], own[j], rest[j], table, own_twist[h], [ready]
                )
                for j in range(slots)
            ]
        )

    chi, snr = [], None
    for j in range(slots):
        levels, totals = zip(*[x[j] for x in halves])
        one, series_of = bins_second(
            which[j], inv_sigma, gains[j], shares[j], levels, totals, second, tmpls, dets
        )
        chi.append(one)
        snr = series_of if snr is None else snr
    snr = second_section(freq, info, inv_sigma, parts, second, snr, chi)
    return (snr, jnp.stack(chi))


def solution(mesh):
    placed = (
        P(None, None, "freq", "bank"),
        P("bank", None, "freq", None),
        P("bank"),
        P("bank"),
        P("bank", None),
    )
    return jax.shard_map(
        per_device,
        mesh=mesh,
        in_specs=placed,
        out_specs=(P("bank", None, None, "freq", None), P("bank", "freq", None)),
        check_vma=False,
    )
```

```python
import functools

import jax
import jax.numpy as jnp
import ml_dtypes
import numpy as np
from jax import lax
from jax.experimental import pallas as pl
from jax.experimental.pallas import tpu as pltpu
from jax.sharding import PartitionSpec as P

N1 = 2048
N2 = 512
NBLK = 32
BLOCK = N1 // NBLK
BINS = 16
LANES = 128
COARSE = N1 // LANES
FOUR = N2 // LANES
F32 = jnp.float32
BF16 = jnp.bfloat16
MIB = 1 << 20
VMEM_LIMIT = 56 * MIB
ANY = pl.BlockSpec(memory_space=pl.ANY)
COST = pl.CostEstimate(flops=MIB, bytes_accessed=MIB, transcendentals=0)


def split_table(table):
    high = table.astype(ml_dtypes.bfloat16)
    low = (table - high.astype(np.float64)).astype(ml_dtypes.bfloat16)
    return high, low


def first_table():
    angle = 2 * np.pi * (np.outer(np.arange(LANES), np.arange(LANES)) % LANES) / LANES
    cos, sin = np.cos(angle), np.sin(angle)
    return split_table(np.block([[cos, sin], [-sin, cos]]))


def stage_table():
    angle = 2 * np.pi * np.outer(np.arange(COARSE), np.arange(LANES)) / N1
    return np.concatenate([np.cos(angle), np.sin(angle)]).astype(np.float32)


def second_table(cols, halves):
    order = np.arange(LANES).reshape(LANES // cols, halves, cols // halves)
    order = order.transpose(1, 0, 2).reshape(-1)
    blocks = []
    for a in range(FOUR):
        n2 = a + FOUR * np.arange(LANES)
        angle = 2 * np.pi * (np.outer(n2, order) % N2) / N2
        cos, sin = np.cos(angle), np.sin(angle)
        blocks.append(np.block([[cos, -sin], [sin, cos]]))
    return np.concatenate([part for block in blocks for part in split_table(block)])


def split(x):
    high = x.astype(BF16)
    return high, (x - high.astype(F32)).astype(BF16)


def phase(index, length):
    angle = (index % length).astype(F32) * (2.0 * np.pi / length)
    return jnp.cos(angle), jnp.sin(angle)


def times_i(z):
    return (-z[1], z[0])


def plus(x, y):
    return (x[0] + y[0], x[1] + y[1])


def minus(x, y):
    return (x[0] - y[0], x[1] - y[1])


def dft4(x):
    s0, s1 = plus(x[0], x[2]), minus(x[0], x[2])
    s2, s3 = plus(x[1], x[3]), times_i(minus(x[1], x[3]))
    return [plus(s0, s2), plus(s1, s3), minus(s0, s2), minus(s1, s3)]


def turn(z, step):
    step %= 16
    if step == 0:
        return z
    if step == 4:
        return times_i(z)
    if step == 8:
        return (-z[0], -z[1])
    half = float(np.sqrt(0.5))
    if step == 2:
        return ((z[0] - z[1]) * half, (z[0] + z[1]) * half)
    if step == 6:
        return ((z[0] + z[1]) * -half, (z[0] - z[1]) * half)
    cos, sin = float(np.cos(np.pi * step / 8)), float(np.sin(np.pi * step / 8))
    return (z[0] * cos - z[1] * sin, z[0] * sin + z[1] * cos)


def dft16(x):
    columns = [dft4([x[4 * u1 + u0] for u1 in range(4)]) for u0 in range(4)]
    out = [None] * 16
    for a0 in range(4):
        ys = dft4([turn(columns[u0][a0], u0 * a0) for u0 in range(4)])
        for a1 in range(4):
            out[a0 + 4 * a1] = ys[a1]
    return out


def dot3(left, right):
    (lh, ll), (rh, rl) = left, right
    return jnp.dot(
        jnp.concatenate([lh, lh, ll], axis=1),
        jnp.concatenate([rh, rl, rh], axis=0),
        preferred_element_type=F32,
    )


def rows_dot3(left, right):
    half = left.shape[0] // 2
    high, low = right
    both = jnp.dot(left, high, preferred_element_type=F32)
    cross = jnp.dot(left[:half], low, preferred_element_type=F32)
    return both[:half] + (both[half:] + cross)


def products(tmpl, strain_ref, where, rows=slice(None)):
    per_piece = COARSE // strain_ref.shape[0]
    for u in range(COARSE):
        off = u % per_piece
        there = slice(off * LANES, (off + 1) * LANES)
        hr, hi = tmpl(0, u), tmpl(1, u)
        sr = strain_ref[(u // per_piece,) + where + (0, rows, there)]
        si = strain_ref[(u // per_piece,) + where + (1, rows, there)]
        yield u, hr * sr + hi * si, hr * si - hi * sr


def tile(u):
    return slice(u * LANES, (u + 1) * LANES)


def first_kernel(
    freq, info_ref, tmpl_ref, strain_ref, wh_ref, wl_ref, stage_ref, tw_ref, *refs
):
    out_ref, token_ref, gh, gl, z = refs[-5:]
    token_ref[...] = jnp.zeros_like(token_ref)
    rows = tmpl_ref.shape[2]
    for r in range(0, rows, ROWS):
        at = slice(r, r + ROWS)
        got = products(lambda p, u: tmpl_ref[0, p, at, tile(u)], strain_ref, (0,), at)
        y = dft16([(re, im) for _, re, im in got])
        for a in range(COARSE):
            cos, sin = stage_ref[a : a + 1, :], stage_ref[COARSE + a : COARSE + a + 1, :]
            yr, yi = y[a]
            to = slice(a * rows + r, a * rows + r + ROWS)
            gh[to, :LANES], gl[to, :LANES] = split(yr * cos - yi * sin)
            gh[to, LANES:], gl[to, LANES:] = split(yr * sin + yi * cos)
    z[...] = dot3((gh[...], gl[...]), (wh_ref[...], wl_ref[...]))
    width = LANES // freq
    slot = lax.broadcasted_iota(jnp.int32, (ROWS, LANES), 1) // width
    for group in range(COARSE // freq):
        for r in range(0, rows, ROWS):
            at = slice(r, r + ROWS)
            turned = []
            for i in range(freq):
                a = group * freq + i
                to = slice(a * rows + r, a * rows + r + ROWS)
                zr, zi = z[to, :LANES], z[to, LANES:]
                cos, sin = tw_ref[0, at, tile(a)], tw_ref[1, at, tile(a)]
                pair = (zr * cos - zi * sin, zr * sin + zi * cos)
                if i:
                    pair = tuple(pltpu.roll(v, i * width, 1) for v in pair)
                turned.append(pair)
            for q in range(freq):
                for p in range(2):
                    value = turned[(0 - q) % freq][p]
                    for s in range(1, freq):
                        value = jnp.where(slot == s, turned[(s - q) % freq][p], value)
                    out_ref[q, 0, p, group, at] = value


ROWS = 16
HALVES = 2
TOGETHER = 2


def first_section(freq, half, info, templates, strain, first, stage, twist, after):
    tmpls = templates.shape[0]
    pieces, dets, _, rows, piece_len = strain.shape
    series = tmpls * dets - 1
    groups = COARSE // freq
    table = pl.BlockSpec((2 * LANES, 2 * LANES), lambda i, n: (0, 0))
    out = (freq, series, 2, groups, rows, LANES)
    return pl.pallas_call(
        functools.partial(first_kernel, freq),
        grid_spec=pltpu.PrefetchScalarGridSpec(
            num_scalar_prefetch=1,
            grid=(series,),
            in_specs=[
                pl.BlockSpec(
                    (1, 2, rows, N1), lambda i, n: (n[1 + 2 * i], 0, half, 0)
                ),
                pl.BlockSpec(
                    (pieces, 1, 2, rows, piece_len), lambda i, n: (0, n[2 + 2 * i], 0, 0, 0)
                ),
                table,
                table,
                pl.BlockSpec((2 * COARSE, LANES), lambda i, n: (0, 0)),
                pl.BlockSpec((2, rows, N1), lambda i, n: (0, half, 0)),
            ]
            + [ANY] * len(after),
            out_specs=[
                pl.BlockSpec(
                    (freq, 1, 2, groups, rows, LANES), lambda i, n: (0, i, 0, 0, 0, 0)
                ),
                pl.BlockSpec((8, LANES), lambda i, n: (0, 0)),
            ],
            scratch_shapes=[
                pltpu.VMEM((COARSE * rows, 2 * LANES), BF16),
                pltpu.VMEM((COARSE * rows, 2 * LANES), BF16),
                pltpu.VMEM((COARSE * rows, 2 * LANES), F32),
            ],
        ),
        out_shape=[
            jax.ShapeDtypeStruct(out, F32),
            jax.ShapeDtypeStruct((8, LANES), F32),
        ],
        compiler_params=pltpu.CompilerParams(vmem_limit_bytes=VMEM_LIMIT),
        cost_estimate=pl.CostEstimate(
            flops=60 * series * rows * N1 * LANES, bytes_accessed=16 * MIB, transcendentals=0
        ),
        name="first_section",
    )(info, templates, strain, first[0], first[1], stage, twist, *after)


def entry_kernel(steps, banks, which_ref, tmpl_ref, strain_ref, *refs):
    out_ref = refs[-1]
    length = N1 // banks
    first_half = lax.broadcasted_iota(jnp.int32, (ROWS, LANES), 1) < BLOCK
    for n, k in enumerate(steps):
        part = lax.rem(which_ref[2] + k, banks)
        for u in range(length // LANES):
            lane = pl.ds(pl.multiple_of(part * length + u * LANES, LANES), LANES)
            hr, hi = tmpl_ref[0, 0, :, lane], tmpl_ref[0, 1, :, lane]
            piece = 0 if strain_ref.shape[0] == 1 else part
            sr, si = strain_ref[piece, 0, 0, :, tile(u)], strain_ref[piece, 0, 1, :, tile(u)]
            re, im = hr * sr + hi * si, hr * si - hi * sr
            to = 2 * (n * length // LANES + u)
            out_ref[:, tile(to)] = jnp.where(first_half, re, pltpu.roll(im, BLOCK, 1))
            out_ref[:, tile(to + 1)] = jnp.where(first_half, pltpu.roll(re, BLOCK, 1), im)


def entry_product(steps, banks, half, which, templates, strain, after):
    pieces, _, _, cols, length = strain.shape
    first = half * cols // ROWS
    return pl.pallas_call(
        functools.partial(entry_kernel, steps, banks),
        grid_spec=pltpu.PrefetchScalarGridSpec(
            num_scalar_prefetch=1,
            grid=(cols // ROWS,),
            in_specs=[
                pl.BlockSpec((1, 2, ROWS, N1), lambda c, w: (w[0], 0, first + c, 0)),
                pl.BlockSpec((pieces, 1, 2, ROWS, length), lambda c, w: (0, w[1], 0, c, 0)),
            ]
            + [ANY] * len(after),
            out_specs=pl.BlockSpec((ROWS, 2 * length * len(steps)), lambda c, w: (c, 0)),
        ),
        out_shape=jax.ShapeDtypeStruct((cols, 2 * length * len(steps)), F32),
        compiler_params=pltpu.CompilerParams(vmem_limit_bytes=VMEM_LIMIT),
        cost_estimate=COST,
        name="entry_product",
    )(which, templates, strain, *after)


def second_points(x, w2_ref, use):
    for a, (yr, yi) in enumerate(dft4(x)):
        y = jnp.concatenate([yr, yi], axis=0)
        table = w2_ref[a * 4 * LANES : (a + 1) * 4 * LANES, :]
        z = rows_dot3(table, split(y))
        use(a, z[:LANES], z[LANES:])


def second_kernel(freq, halves, info_ref, scale_ref, *refs):
    part_refs, w2_ref = refs[:halves], refs[halves]
    out_ref, hold, order = refs[-3:]
    place = info_ref[0]
    groups, cols = part_refs[0].shape[3:5]
    per = LANES // (halves * cols)
    width = LANES // freq
    scale = scale_ref[info_ref[1 + 2 * pl.program_id(0)]]

    def rows_of(p, u):
        tiles = [
            jnp.concatenate(
                [ref[u * per + f, 0, p, g] for ref in part_refs for f in range(per)],
                axis=0,
            )
            for g in range(groups)
        ]
        return jnp.concatenate(tiles, axis=1)

    x = [(rows_of(0, u), rows_of(1, u)) for u in range(FOUR)]

    def keep(a, re, im):
        for p, value in enumerate((re, im)):
            for g in range(groups):
                hold[p, g, pl.ds(a, LANES, stride=FOUR), :] = value[:, tile(g)] * scale

    second_points(x, w2_ref, keep)
    for p in range(2):
        for g in range(groups):
            turned = hold[p, g].T
            for s in range(freq):
                a = g * freq + lax.rem(s - place + freq, freq)
                for j in range(FOUR):
                    order[p, j, pl.ds(a, width, stride=COARSE), :] = turned[
                        s * width : (s + 1) * width, tile(j)
                    ]
        for j in range(FOUR):
            out_ref[0, 0, p, :, tile(j)] = order[p, j]


def second_section(freq, info, scale, parts, second, snr, after):
    _, series, _, groups, cols, _ = parts[0].shape
    halves = len(parts)
    times = groups * LANES
    smem = pl.BlockSpec(memory_space=pltpu.SMEM)
    table = pl.BlockSpec((FOUR * 4 * LANES, 2 * LANES), lambda i, n: (0, 0))
    part = pl.BlockSpec(
        (freq, 1, 2, groups, cols, LANES), lambda i, n: (0, i, 0, 0, 0, 0)
    )
    return pl.pallas_call(
        functools.partial(second_kernel, freq, halves),
        grid_spec=pltpu.PrefetchScalarGridSpec(
            num_scalar_prefetch=1,
            grid=(series,),
            in_specs=[smem] + [part] * halves + [table, ANY] + [ANY] * len(after),
            out_specs=pl.BlockSpec(
                (1, 1, 2, times, N2), lambda i, n: (n[1 + 2 * i], n[2 + 2 * i], 0, 0, 0)
            ),
            scratch_shapes=[
                pltpu.VMEM((2, groups, N2, LANES), F32),
                pltpu.VMEM((2, FOUR, times, LANES), F32),
            ],
        ),
        out_shape=jax.ShapeDtypeStruct(snr.shape, F32),
        input_output_aliases={3 + halves: 0},
        compiler_params=pltpu.CompilerParams(vmem_limit_bytes=VMEM_LIMIT),
        cost_estimate=COST,
        name="second_section",
    )(info, scale, *parts, second, snr, *after)


BLOCKS = 4


def bank_kernel(block_ref, inner_ref, high_ref, low_ref):
    times = block_ref.shape[-1]
    rc, rs = inner_ref[0], inner_ref[1]
    for b in range(BLOCKS):
        bc, bs = block_ref[b, 0:1, :], block_ref[b, 1:2, :]
        cos, sin = split(bc * rc - bs * rs), split(bc * rs + bs * rc)
        top = slice(2 * b * BLOCK, (2 * b + 1) * BLOCK)
        low = slice((2 * b + 1) * BLOCK, (2 * b + 2) * BLOCK)
        for ref, c, s in zip((high_ref, low_ref), cos, sin):
            ref[top, :times] = c
            ref[top, times:] = s
            ref[low, :times] = -s
            ref[low, times:] = c


def bank_table(own_time):
    times = own_time.shape[0]
    block = jnp.arange(NBLK, dtype=jnp.int32)[:, None] * own_time[None, :]
    block = jnp.stack(phase(block, NBLK), axis=1)
    inner = jnp.arange(BLOCK, dtype=jnp.int32)[:, None] * own_time[None, :]
    inner = jnp.stack(phase(inner, N1))
    return pl.pallas_call(
        bank_kernel,
        grid=(NBLK // BLOCKS,),
        in_specs=[
            pl.BlockSpec((BLOCKS, 2, times), lambda b: (b, 0, 0)),
            pl.BlockSpec((2, BLOCK, times), lambda b: (0, 0, 0)),
        ],
        out_specs=[pl.BlockSpec((BLOCKS * 2 * BLOCK, 2 * times), lambda b: (b, 0))] * 2,
        out_shape=[jax.ShapeDtypeStruct((2 * N1, 2 * times), BF16)] * 2,
        compiler_params=pltpu.CompilerParams(vmem_limit_bytes=VMEM_LIMIT),
        cost_estimate=COST,
        name="bank_table",
    )(block, inner)


def bins_first_kernel(pieces, banks, place_ref, edge_ref, *refs):
    own_refs, rest_refs = refs[:pieces], refs[pieces : 2 * pieces]
    wh_ref, wl_ref, tw_ref = refs[2 * pieces : 2 * pieces + 3]
    level_ref, total_ref, x, acc = refs[-4:]
    times = total_ref.shape[-1]
    cols = own_refs[0].shape[0]
    length = 2 * N1 // banks
    chunk = FOUR * LANES
    step = pl.program_id(0)

    @pl.when(step == 0)
    def _():
        for k in range(pieces):
            row = pl.multiple_of((place_ref[0] ^ k) * cols, cols)
            low = pl.multiple_of(row + pieces * cols, cols)
            for n in range(banks):
                ref = rest_refs[k] if n else own_refs[k]
                start = lax.rem(place_ref[1] + n, banks) * length

                def cut(i, carry):
                    lane = max(n - 1, 0) * length + i * chunk
                    part = split(ref[:, pl.ds(pl.multiple_of(lane, chunk), chunk)])
                    to = pl.ds(pl.multiple_of(start + i * chunk, chunk), chunk)
                    x[pl.ds(row, cols), to], x[pl.ds(low, cols), to] = part
                    return carry

                lax.fori_loop(0, length // chunk, cut, 0)
        total_ref[...] = jnp.zeros_like(total_ref)

    def blocks_at(block, blocks):
        at = pl.ds(pl.multiple_of(block * LANES, LANES), blocks * LANES)
        return rows_dot3(x[:, at], (wh_ref[at, :], wl_ref[at, :]))

    for i in range(TOGETHER):
        start, end = edge_ref[step * TOGETHER + i], edge_ref[step * TOGETHER + i + 1]
        odd = (end - start) % 2

        @pl.when(odd == 1)
        def _():
            acc[i] = blocks_at(end - 1, 1)

        @pl.when(odd == 0)
        def _():
            acc[i] = blocks_at(end - 2, 2)

        def two(n, carry):
            acc[i] += blocks_at(start + 2 * n, 2)
            return carry

        lax.fori_loop(0, (end - start - 1) // 2, two, 0)

    for u in range(pieces * cols // LANES):
        at = tile(u)
        cos, sin = tw_ref[0, at, :], tw_ref[1, at, :]
        sum_r, sum_i = total_ref[0, at, :], total_ref[1, at, :]
        for i in range(TOGETHER):
            re, im = acc[i, at, :times], acc[i, at, times:]
            vr, vi = re * cos - im * sin, re * sin + im * cos
            level_ref[i, 0, at, :] = vr
            level_ref[i, 1, at, :] = vi
            sum_r, sum_i = sum_r + vr, sum_i + vi
        total_ref[0, at, :] = sum_r
        total_ref[1, at, :] = sum_i


def bins_first(half, banks, place, edges, own, rest, table, twist, after):
    cols, length = rest[0].shape
    rows, times = twist.shape[1:]
    smem = pl.BlockSpec(memory_space=pltpu.SMEM)
    fixed = lambda shape: pl.BlockSpec(shape, lambda i: (0,) * len(shape))
    return pl.pallas_call(
        functools.partial(bins_first_kernel, len(own), banks),
        grid=(BINS // TOGETHER,),
        in_specs=[smem, smem]
        + [pl.BlockSpec((cols, 2 * N1 - length), lambda i: (half, 0))] * len(own)
        + [fixed((cols, length))] * len(rest)
        + [fixed((2 * N1, 2 * times))] * 2
        + [fixed((2, rows, times))]
        + [ANY] * len(after),
        out_specs=[
            pl.BlockSpec((TOGETHER, 2, rows, times), lambda i: (i, 0, 0, 0)),
            fixed((2, rows, times)),
        ],
        out_shape=[
            jax.ShapeDtypeStruct((BINS, 2, rows, times), F32),
            jax.ShapeDtypeStruct((2, rows, times), F32),
        ],
        scratch_shapes=[
            pltpu.VMEM((2 * rows, 2 * N1), BF16),
            pltpu.VMEM((TOGETHER, rows, 2 * times), F32),
        ],
        compiler_params=pltpu.CompilerParams(vmem_limit_bytes=VMEM_LIMIT),
        cost_estimate=COST,
        name="bins_first",
    )(place, edges, *own, *rest, *table, twist, *after)


def bins_second_kernel(halves, which_ref, scale_ref, gain_ref, share_ref, *refs):
    level_refs, total_refs = refs[:halves], refs[halves : 2 * halves]
    w2_ref, out_ref, snr_ref, chi, hold = refs[2 * halves :]
    times = out_ref.shape[0]
    part_rows = LANES // halves
    step = pl.program_id(0)

    @pl.when(step == 0)
    def _():
        chi[...] = jnp.zeros_like(chi)

    def rows_of(get, u):
        at = slice(u * part_rows, (u + 1) * part_rows)
        return jnp.concatenate([get(h, at) for h in range(halves)], axis=0)

    def keep(a, re, im):
        chi[a] += re * re + im * im

    for i in range(TOGETHER):
        gain, share = gain_ref[step * TOGETHER + i], share_ref[step * TOGETHER + i]

        def deviation(p):
            return lambda h, at: (
                level_refs[h][i, p, at, :] * gain - total_refs[h][p, at, :] * share
            )

        x = [tuple(rows_of(deviation(p), u) for p in range(2)) for u in range(FOUR)]
        second_points(x, w2_ref, keep)

    @pl.when(step == BINS // TOGETHER - 1)
    def _():
        scale = scale_ref[which_ref[0]]

        def whole(p):
            return lambda h, at: total_refs[h][p, at, :] * scale

        def put(a, re, im):
            for p, value in enumerate((re, im)):
                for g in range(times // LANES):
                    hold[p, g, pl.ds(a, LANES, stride=FOUR), :] = value[:, tile(g)]

        y = [tuple(rows_of(whole(p), u) for p in range(2)) for u in range(FOUR)]
        second_points(y, w2_ref, put)
        for g in range(times // LANES):
            for a in range(FOUR):
                hold[2, g, pl.ds(a, LANES, stride=FOUR), :] = chi[a, :, tile(g)]
            for p in range(2):
                snr_ref[0, 0, p, tile(g), :] = hold[p, g].T
            out_ref[tile(g), :] = hold[2, g].T


def bins_second(which, scale, gain, share, levels, totals, second, tmpls, dets):
    _, _, rows, times = levels[0].shape
    halves = len(levels)
    smem = pl.BlockSpec(memory_space=pltpu.SMEM)
    fixed = lambda shape: pl.BlockSpec(shape, lambda i, w: (0,) * len(shape))
    return pl.pallas_call(
        functools.partial(bins_second_kernel, halves),
        grid_spec=pltpu.PrefetchScalarGridSpec(
            num_scalar_prefetch=1,
            grid=(BINS // TOGETHER,),
            in_specs=[smem, smem, smem]
            + [pl.BlockSpec((TOGETHER, 2, rows, times), lambda i, w: (i, 0, 0, 0))] * halves
            + [fixed((2, rows, times))] * halves
            + [fixed((FOUR * 4 * LANES, 2 * LANES))],
            out_specs=[
                fixed((times, N2)),
                pl.BlockSpec((1, 1, 2, times, N2), lambda i, w: (w[0], w[1], 0, 0, 0)),
            ],
            scratch_shapes=[
                pltpu.VMEM((FOUR, LANES, times), F32),
                pltpu.VMEM((3, times // LANES, N2, LANES), F32),
            ],
        ),
        out_shape=[
            jax.ShapeDtypeStruct((times, N2), F32),
            jax.ShapeDtypeStruct((tmpls, dets, 2, times, N2), F32),
        ],
        compiler_params=pltpu.CompilerParams(vmem_limit_bytes=VMEM_LIMIT),
        cost_estimate=COST,
        name="bins_second",
    )(which, scale, gain, share, *levels, *totals, second)


def handed_on(arrays, after):
    count = len(arrays)
    return pl.pallas_call(
        lambda *refs: None,
        in_specs=[ANY] * (count + len(after)),
        out_specs=[ANY] * count,
        out_shape=[jax.ShapeDtypeStruct(x.shape, x.dtype) for x in arrays],
        input_output_aliases={i: i for i in range(count)},
        compiler_params=pltpu.CompilerParams(vmem_limit_bytes=VMEM_LIMIT),
        cost_estimate=COST,
        name="handed_on",
    )(*arrays, *after)


def swap(x, freq, k):
    return lax.ppermute(x, "freq", [(i, i ^ k) for i in range(freq)])


def far_pieces(own, freq):
    return [own] + [swap(own, freq, k) for k in range(2, freq, 2)]


def near_pieces(far, freq):
    return [x for even in far for x in (even, swap(even, freq, 1))]


def per_device(strain, templates, coinc_tmpl, coinc_det, bin_edges):
    freq, banks = lax.axis_size("freq"), lax.axis_size("bank")
    place = lax.axis_index("freq").astype(jnp.int32)
    bank = lax.axis_index("bank").astype(jnp.int32)
    tmpls, _, cols, _ = templates.shape
    slots, dets = coinc_tmpl.shape[0], strain.shape[0]
    times = N1 // freq
    part = cols // HALVES

    slices = [strain[:, :, h * part : (h + 1) * part] for h in range(HALVES)]
    strains = [lax.all_gather(x, "bank", axis=0, tiled=False) for x in slices]
    first = tuple(jnp.asarray(t) for t in first_table())
    second = jnp.asarray(second_table(cols, HALVES))
    stage = jnp.asarray(stage_table())

    column = place * cols + jnp.arange(cols, dtype=jnp.int32)
    lane = jnp.arange(N1, dtype=jnp.int32)
    time_of_lane = lane // LANES + COARSE * (lane % LANES)
    twist = jnp.stack(phase(column[:, None] * time_of_lane[None, :], N1 * N2))
    own_time = place * times + jnp.arange(times, dtype=jnp.int32)
    table = bank_table(own_time)
    own_twist = []
    for h in range(HALVES):
        rows = jnp.arange(freq * part, dtype=jnp.int32)
        rows = rows // part * cols + h * part + rows % part
        own_twist.append(jnp.stack(phase(rows[:, None] * own_time[None, :], N1 * N2)))

    which = [jnp.stack([coinc_tmpl[j], coinc_det[j], bank]) for j in range(slots)]
    series = jnp.arange(tmpls * dets - 1, dtype=jnp.int32)
    series = series + (series >= which[0][0] * dets + which[0][1])
    info = jnp.stack([series // dets, series % dets], axis=1).reshape(-1)
    info = jnp.concatenate([place.reshape(1), info])
    ends = jnp.zeros((1,), jnp.int32), jnp.full((1,), NBLK, jnp.int32)
    edges = [
        jnp.concatenate([ends[0], bin_edges[coinc_tmpl[j]], ends[1]]) for j in range(slots)
    ]
    here = jnp.stack([place, bank])

    power = (templates[:, 0] ** 2 + templates[:, 1] ** 2).sum(axis=1)
    power = power.reshape(tmpls, NBLK, BLOCK).sum(axis=2)
    own = [entry_product((0,), banks, 0, w, templates, strain[None], slices) for w in which]
    wide = own[0].shape[1]
    power = jnp.pad(power.reshape(1, -1), ((0, 7), (0, wide - tmpls * NBLK)))
    own[0] = jnp.concatenate([own[0], power], axis=0)
    own = [near_pieces(far_pieces(x, freq), freq) for x in own]
    gathered = [x for entry in own for x in entry[1:]]

    block_power = sum(x[cols, : tmpls * NBLK] for x in own[0]).reshape(tmpls, NBLK)
    sigma_sq = block_power.sum(axis=1)
    inv_sigma = lax.rsqrt(sigma_sq)
    bin_of = jnp.sum(
        jnp.arange(NBLK, dtype=jnp.int32)[None, :, None] >= bin_edges[:, None, :], axis=2
    )
    inside = bin_of[:, None, :] == jnp.arange(BINS, dtype=jnp.int32)[None, :, None]
    weights = jnp.where(inside, block_power[:, None, :], 0.0).sum(axis=2) / sigma_sq[:, None]
    gains = [inv_sigma[coinc_tmpl[j]] * lax.rsqrt(weights[coinc_tmpl[j]]) for j in range(slots)]
    shares = [gains[j] * weights[coinc_tmpl[j]] for j in range(slots)]
    which, inv_sigma, gains, shares, twist, info, edges, here, table, own_twist = (
        lax.optimization_barrier(
            (which, inv_sigma, gains, shares, twist, info, edges, here, table, own_twist)
        )
    )

    def exchange(x):
        got = lax.all_to_all(
            x.reshape(freq, -1, LANES), "freq", split_axis=0, concat_axis=0, tiled=True
        )
        return got.reshape(x.shape)

    def bins_of(h, rest, after):
        return [
            bins_first(h, banks, here, edges[j], own[j], rest[j], table, own_twist[h], after)
            for j in range(slots)
        ]

    parts, halves, rest, after = [], [], [], gathered
    later = tuple(range(1, banks))
    for h in range(HALVES):
        half = [entry_product(later, banks, h, w, templates, strains[h], after) for w in which]
        far = [far_pieces(x, freq) for x in half]
        sent, token = first_section(
            freq, h, info, templates, strains[h], first, stage, twist, half
        )
        if h:
            halves.append(bins_of(h - 1, rest, [token]))
        done = [token] + parts + [x[1] for one in halves for x in one]
        far = [x[:1] + list(handed_on(x[1:], done)) for x in far]
        rest = [near_pieces(x, freq) for x in far]
        if h == HALVES - 1:
            (sent,) = handed_on([sent], [x for entry in rest for x in entry[1:]])
        parts.append(exchange(sent))
        after = [token]
    halves.append(bins_of(HALVES - 1, rest, [sent]))

    chi, snr = [], None
    for j in range(slots):
        levels, totals = zip(*[x[j] for x in halves])
        one, series_of = bins_second(
            which[j], inv_sigma, gains[j], shares[j], levels, totals, second, tmpls, dets
        )
        chi.append(one)
        snr = series_of if snr is None else snr
    snr = second_section(freq, info, inv_sigma, parts, second, snr, chi)
    return (snr, jnp.stack(chi))


def solution(mesh):
    placed = (
        P(None, None, "freq", "bank"),
        P("bank", None, "freq", None),
        P("bank"),
        P("bank"),
        P("bank", None),
    )
    return jax.shard_map(
        per_device,
        mesh=mesh,
        in_specs=placed,
        out_specs=(P("bank", None, None, "freq", None), P("bank", "freq", None)),
        check_vma=False,
    )
```

```python
import functools

import jax
import jax.numpy as jnp
import ml_dtypes
import numpy as np
from jax import lax
from jax.experimental import pallas as pl
from jax.experimental.pallas import tpu as pltpu
from jax.sharding import PartitionSpec as P

N1 = 2048
N2 = 512
NBLK = 32
BLOCK = N1 // NBLK
BINS = 16
LANES = 128
COARSE = N1 // LANES
FOUR = N2 // LANES
F32 = jnp.float32
BF16 = jnp.bfloat16
MIB = 1 << 20
VMEM_LIMIT = 56 * MIB
ANY = pl.BlockSpec(memory_space=pl.ANY)
COST = pl.CostEstimate(flops=MIB, bytes_accessed=MIB, transcendentals=0)


def split_table(table):
    high = table.astype(ml_dtypes.bfloat16)
    low = (table - high.astype(np.float64)).astype(ml_dtypes.bfloat16)
    return high, low


def first_table():
    angle = 2 * np.pi * (np.outer(np.arange(LANES), np.arange(LANES)) % LANES) / LANES
    cos, sin = np.cos(angle), np.sin(angle)
    return split_table(np.block([[cos, sin], [-sin, cos]]))


def stage_table():
    angle = 2 * np.pi * np.outer(np.arange(COARSE), np.arange(LANES)) / N1
    return np.concatenate([np.cos(angle), np.sin(angle)]).astype(np.float32)


def second_table(cols, halves):
    order = np.arange(LANES).reshape(LANES // cols, halves, cols // halves)
    order = order.transpose(1, 0, 2).reshape(-1)
    blocks = []
    for a in range(FOUR):
        n2 = a + FOUR * np.arange(LANES)
        angle = 2 * np.pi * (np.outer(n2, order) % N2) / N2
        cos, sin = np.cos(angle), np.sin(angle)
        blocks.append(np.block([[cos, -sin], [sin, cos]]))
    return np.concatenate([part for block in blocks for part in split_table(block)])


def split(x):
    high = x.astype(BF16)
    return high, (x - high.astype(F32)).astype(BF16)


def phase(index, length):
    angle = (index % length).astype(F32) * (2.0 * np.pi / length)
    return jnp.cos(angle), jnp.sin(angle)


def times_i(z):
    return (-z[1], z[0])


def plus(x, y):
    return (x[0] + y[0], x[1] + y[1])


def minus(x, y):
    return (x[0] - y[0], x[1] - y[1])


def dft4(x):
    s0, s1 = plus(x[0], x[2]), minus(x[0], x[2])
    s2, s3 = plus(x[1], x[3]), times_i(minus(x[1], x[3]))
    return [plus(s0, s2), plus(s1, s3), minus(s0, s2), minus(s1, s3)]


def turn(z, step):
    step %= 16
    if step == 0:
        return z
    if step == 4:
        return times_i(z)
    if step == 8:
        return (-z[0], -z[1])
    half = float(np.sqrt(0.5))
    if step == 2:
        return ((z[0] - z[1]) * half, (z[0] + z[1]) * half)
    if step == 6:
        return ((z[0] + z[1]) * -half, (z[0] - z[1]) * half)
    cos, sin = float(np.cos(np.pi * step / 8)), float(np.sin(np.pi * step / 8))
    return (z[0] * cos - z[1] * sin, z[0] * sin + z[1] * cos)


def dft16(x):
    columns = [dft4([x[4 * u1 + u0] for u1 in range(4)]) for u0 in range(4)]
    out = [None] * 16
    for a0 in range(4):
        ys = dft4([turn(columns[u0][a0], u0 * a0) for u0 in range(4)])
        for a1 in range(4):
            out[a0 + 4 * a1] = ys[a1]
    return out


def dot3(left, right):
    (lh, ll), (rh, rl) = left, right
    return jnp.dot(
        jnp.concatenate([lh, lh, ll], axis=1),
        jnp.concatenate([rh, rl, rh], axis=0),
        preferred_element_type=F32,
    )


def rows_dot3(left, right):
    half = left.shape[0] // 2
    high, low = right
    both = jnp.dot(left, high, preferred_element_type=F32)
    cross = jnp.dot(left[:half], low, preferred_element_type=F32)
    return both[:half] + (both[half:] + cross)


def products(tmpl, strain_ref, where, rows=slice(None)):
    per_piece = COARSE // strain_ref.shape[0]
    for u in range(COARSE):
        off = u % per_piece
        there = slice(off * LANES, (off + 1) * LANES)
        hr, hi = tmpl(0, u), tmpl(1, u)
        sr = strain_ref[(u // per_piece,) + where + (0, rows, there)]
        si = strain_ref[(u // per_piece,) + where + (1, rows, there)]
        yield u, hr * sr + hi * si, hr * si - hi * sr


def tile(u):
    return slice(u * LANES, (u + 1) * LANES)


def first_kernel(
    freq, info_ref, tmpl_ref, strain_ref, wh_ref, wl_ref, stage_ref, tw_ref, *refs
):
    out_ref, token_ref, gh, gl, z = refs[-5:]
    token_ref[...] = jnp.zeros_like(token_ref)
    rows = tmpl_ref.shape[2]
    for r in range(0, rows, ROWS):
        at = slice(r, r + ROWS)
        got = products(lambda p, u: tmpl_ref[0, p, at, tile(u)], strain_ref, (0,), at)
        y = dft16([(re, im) for _, re, im in got])
        for a in range(COARSE):
            cos, sin = stage_ref[a : a + 1, :], stage_ref[COARSE + a : COARSE + a + 1, :]
            yr, yi = y[a]
            to = slice(a * rows + r, a * rows + r + ROWS)
            gh[to, :LANES], gl[to, :LANES] = split(yr * cos - yi * sin)
            gh[to, LANES:], gl[to, LANES:] = split(yr * sin + yi * cos)
    z[...] = dot3((gh[...], gl[...]), (wh_ref[...], wl_ref[...]))
    width = LANES // freq
    slot = lax.broadcasted_iota(jnp.int32, (ROWS, LANES), 1) // width
    for group in range(COARSE // freq):
        for r in range(0, rows, ROWS):
            at = slice(r, r + ROWS)
            turned = []
            for i in range(freq):
                a = group * freq + i
                to = slice(a * rows + r, a * rows + r + ROWS)
                zr, zi = z[to, :LANES], z[to, LANES:]
                cos, sin = tw_ref[0, at, tile(a)], tw_ref[1, at, tile(a)]
                pair = (zr * cos - zi * sin, zr * sin + zi * cos)
                if i:
                    pair = tuple(pltpu.roll(v, i * width, 1) for v in pair)
                turned.append(pair)
            for q in range(freq):
                for p in range(2):
                    value = turned[(0 - q) % freq][p]
                    for s in range(1, freq):
                        value = jnp.where(slot == s, turned[(s - q) % freq][p], value)
                    out_ref[q, 0, p, group, at] = value


ROWS = 16
HALVES = 2
TOGETHER = 2


def first_section(freq, half, info, templates, strain, first, stage, twist, after):
    tmpls = templates.shape[0]
    pieces, dets, _, rows, piece_len = strain.shape
    series = tmpls * dets - 1
    groups = COARSE // freq
    table = pl.BlockSpec((2 * LANES, 2 * LANES), lambda i, n: (0, 0))
    out = (freq, series, 2, groups, rows, LANES)
    return pl.pallas_call(
        functools.partial(first_kernel, freq),
        grid_spec=pltpu.PrefetchScalarGridSpec(
            num_scalar_prefetch=1,
            grid=(series,),
            in_specs=[
                pl.BlockSpec(
                    (1, 2, rows, N1), lambda i, n: (n[1 + 2 * i], 0, half, 0)
                ),
                pl.BlockSpec(
                    (pieces, 1, 2, rows, piece_len), lambda i, n: (0, n[2 + 2 * i], 0, 0, 0)
                ),
                table,
                table,
                pl.BlockSpec((2 * COARSE, LANES), lambda i, n: (0, 0)),
                pl.BlockSpec((2, rows, N1), lambda i, n: (0, half, 0)),
            ]
            + [ANY] * len(after),
            out_specs=[
                pl.BlockSpec(
                    (freq, 1, 2, groups, rows, LANES), lambda i, n: (0, i, 0, 0, 0, 0)
                ),
                pl.BlockSpec((8, LANES), lambda i, n: (0, 0)),
            ],
            scratch_shapes=[
                pltpu.VMEM((COARSE * rows, 2 * LANES), BF16),
                pltpu.VMEM((COARSE * rows, 2 * LANES), BF16),
                pltpu.VMEM((COARSE * rows, 2 * LANES), F32),
            ],
        ),
        out_shape=[
            jax.ShapeDtypeStruct(out, F32),
            jax.ShapeDtypeStruct((8, LANES), F32),
        ],
        compiler_params=pltpu.CompilerParams(vmem_limit_bytes=VMEM_LIMIT),
        cost_estimate=pl.CostEstimate(
            flops=60 * series * rows * N1 * LANES, bytes_accessed=16 * MIB, transcendentals=0
        ),
        name="first_section",
    )(info, templates, strain, first[0], first[1], stage, twist, *after)


def entry_kernel(steps, banks, which_ref, tmpl_ref, strain_ref, *refs):
    out_ref = refs[-1]
    length = N1 // banks
    first_half = lax.broadcasted_iota(jnp.int32, (ROWS, LANES), 1) < BLOCK
    for n, k in enumerate(steps):
        part = lax.rem(which_ref[2] + k, banks)
        for u in range(length // LANES):
            lane = pl.ds(pl.multiple_of(part * length + u * LANES, LANES), LANES)
            hr, hi = tmpl_ref[0, 0, :, lane], tmpl_ref[0, 1, :, lane]
            piece = 0 if strain_ref.shape[0] == 1 else part
            sr, si = strain_ref[piece, 0, 0, :, tile(u)], strain_ref[piece, 0, 1, :, tile(u)]
            re, im = hr * sr + hi * si, hr * si - hi * sr
            to = 2 * (n * length // LANES + u)
            out_ref[:, tile(to)] = jnp.where(first_half, re, pltpu.roll(im, BLOCK, 1))
            out_ref[:, tile(to + 1)] = jnp.where(first_half, pltpu.roll(re, BLOCK, 1), im)


def entry_product(steps, banks, half, which, templates, strain, after):
    pieces, _, _, cols, length = strain.shape
    first = half * cols // ROWS
    return pl.pallas_call(
        functools.partial(entry_kernel, steps, banks),
        grid_spec=pltpu.PrefetchScalarGridSpec(
            num_scalar_prefetch=1,
            grid=(cols // ROWS,),
            in_specs=[
                pl.BlockSpec((1, 2, ROWS, N1), lambda c, w: (w[0], 0, first + c, 0)),
                pl.BlockSpec((pieces, 1, 2, ROWS, length), lambda c, w: (0, w[1], 0, c, 0)),
            ]
            + [ANY] * len(after),
            out_specs=pl.BlockSpec((ROWS, 2 * length * len(steps)), lambda c, w: (c, 0)),
        ),
        out_shape=jax.ShapeDtypeStruct((cols, 2 * length * len(steps)), F32),
        compiler_params=pltpu.CompilerParams(vmem_limit_bytes=VMEM_LIMIT),
        cost_estimate=COST,
        name="entry_product",
    )(which, templates, strain, *after)


def second_points(x, w2_ref, use):
    for a, (yr, yi) in enumerate(dft4(x)):
        y = jnp.concatenate([yr, yi], axis=0)
        table = w2_ref[a * 4 * LANES : (a + 1) * 4 * LANES, :]
        z = rows_dot3(table, split(y))
        use(a, z[:LANES], z[LANES:])


def second_kernel(freq, halves, info_ref, scale_ref, *refs):
    part_refs, w2_ref = refs[:halves], refs[halves]
    out_ref, hold, order = refs[-3:]
    place = info_ref[0]
    groups, cols = part_refs[0].shape[3:5]
    per = LANES // (halves * cols)
    width = LANES // freq
    scale = scale_ref[info_ref[1 + 2 * pl.program_id(0)]]

    def rows_of(p, u):
        tiles = [
            jnp.concatenate(
                [ref[u * per + f, 0, p, g] for ref in part_refs for f in range(per)],
                axis=0,
            )
            for g in range(groups)
        ]
        return jnp.concatenate(tiles, axis=1)

    x = [(rows_of(0, u), rows_of(1, u)) for u in range(FOUR)]

    def keep(a, re, im):
        for p, value in enumerate((re, im)):
            for g in range(groups):
                hold[p, g, pl.ds(a, LANES, stride=FOUR), :] = value[:, tile(g)] * scale

    second_points(x, w2_ref, keep)
    for p in range(2):
        for g in range(groups):
            turned = hold[p, g].T
            for s in range(freq):
                a = g * freq + lax.rem(s - place + freq, freq)
                for j in range(FOUR):
                    order[p, j, pl.ds(a, width, stride=COARSE), :] = turned[
                        s * width : (s + 1) * width, tile(j)
                    ]
        for j in range(FOUR):
            out_ref[0, 0, p, :, tile(j)] = order[p, j]


def second_section(freq, info, scale, parts, second, snr, after):
    _, series, _, groups, cols, _ = parts[0].shape
    halves = len(parts)
    times = groups * LANES
    smem = pl.BlockSpec(memory_space=pltpu.SMEM)
    table = pl.BlockSpec((FOUR * 4 * LANES, 2 * LANES), lambda i, n: (0, 0))
    part = pl.BlockSpec(
        (freq, 1, 2, groups, cols, LANES), lambda i, n: (0, i, 0, 0, 0, 0)
    )
    return pl.pallas_call(
        functools.partial(second_kernel, freq, halves),
        grid_spec=pltpu.PrefetchScalarGridSpec(
            num_scalar_prefetch=1,
            grid=(series,),
            in_specs=[smem] + [part] * halves + [table, ANY] + [ANY] * len(after),
            out_specs=pl.BlockSpec(
                (1, 1, 2, times, N2), lambda i, n: (n[1 + 2 * i], n[2 + 2 * i], 0, 0, 0)
            ),
            scratch_shapes=[
                pltpu.VMEM((2, groups, N2, LANES), F32),
                pltpu.VMEM((2, FOUR, times, LANES), F32),
            ],
        ),
        out_shape=jax.ShapeDtypeStruct(snr.shape, F32),
        input_output_aliases={3 + halves: 0},
        compiler_params=pltpu.CompilerParams(vmem_limit_bytes=VMEM_LIMIT),
        cost_estimate=COST,
        name="second_section",
    )(info, scale, *parts, second, snr, *after)


BLOCKS = 4


def bank_kernel(block_ref, inner_ref, high_ref, low_ref):
    times = block_ref.shape[-1]
    rc, rs = inner_ref[0], inner_ref[1]
    for b in range(BLOCKS):
        bc, bs = block_ref[b, 0:1, :], block_ref[b, 1:2, :]
        cos, sin = split(bc * rc - bs * rs), split(bc * rs + bs * rc)
        top = slice(2 * b * BLOCK, (2 * b + 1) * BLOCK)
        low = slice((2 * b + 1) * BLOCK, (2 * b + 2) * BLOCK)
        for ref, c, s in zip((high_ref, low_ref), cos, sin):
            ref[top, :times] = c
            ref[top, times:] = s
            ref[low, :times] = -s
            ref[low, times:] = c


def bank_table(own_time):
    times = own_time.shape[0]
    block = jnp.arange(NBLK, dtype=jnp.int32)[:, None] * own_time[None, :]
    block = jnp.stack(phase(block, NBLK), axis=1)
    inner = jnp.arange(BLOCK, dtype=jnp.int32)[:, None] * own_time[None, :]
    inner = jnp.stack(phase(inner, N1))
    return pl.pallas_call(
        bank_kernel,
        grid=(NBLK // BLOCKS,),
        in_specs=[
            pl.BlockSpec((BLOCKS, 2, times), lambda b: (b, 0, 0)),
            pl.BlockSpec((2, BLOCK, times), lambda b: (0, 0, 0)),
        ],
        out_specs=[pl.BlockSpec((BLOCKS * 2 * BLOCK, 2 * times), lambda b: (b, 0))] * 2,
        out_shape=[jax.ShapeDtypeStruct((2 * N1, 2 * times), BF16)] * 2,
        compiler_params=pltpu.CompilerParams(vmem_limit_bytes=VMEM_LIMIT),
        cost_estimate=COST,
        name="bank_table",
    )(block, inner)


def bins_first_kernel(pieces, banks, place_ref, edge_ref, *refs):
    own_refs, rest_refs = refs[:pieces], refs[pieces : 2 * pieces]
    wh_ref, wl_ref, tw_ref = refs[2 * pieces : 2 * pieces + 3]
    level_ref, total_ref, x, acc = refs[-4:]
    times = total_ref.shape[-1]
    cols = own_refs[0].shape[0]
    length = 2 * N1 // banks
    chunk = FOUR * LANES
    step = pl.program_id(0)

    @pl.when(step == 0)
    def _():
        for k in range(pieces):
            row = pl.multiple_of((place_ref[0] ^ k) * cols, cols)
            low = pl.multiple_of(row + pieces * cols, cols)
            for n in range(banks):
                ref = rest_refs[k] if n else own_refs[k]
                start = lax.rem(place_ref[1] + n, banks) * length

                def cut(i, carry):
                    lane = max(n - 1, 0) * length + i * chunk
                    part = split(ref[:, pl.ds(pl.multiple_of(lane, chunk), chunk)])
                    to = pl.ds(pl.multiple_of(start + i * chunk, chunk), chunk)
                    x[pl.ds(row, cols), to], x[pl.ds(low, cols), to] = part
                    return carry

                lax.fori_loop(0, length // chunk, cut, 0)
        total_ref[...] = jnp.zeros_like(total_ref)

    def blocks_at(block, blocks):
        at = pl.ds(pl.multiple_of(block * LANES, LANES), blocks * LANES)
        return rows_dot3(x[:, at], (wh_ref[at, :], wl_ref[at, :]))

    for i in range(TOGETHER):
        start, end = edge_ref[step * TOGETHER + i], edge_ref[step * TOGETHER + i + 1]
        odd = (end - start) % 2

        @pl.when(odd == 1)
        def _():
            acc[i] = blocks_at(end - 1, 1)

        @pl.when(odd == 0)
        def _():
            acc[i] = blocks_at(end - 2, 2)

        def two(n, carry):
            acc[i] += blocks_at(start + 2 * n, 2)
            return carry

        lax.fori_loop(0, (end - start - 1) // 2, two, 0)

    for u in range(pieces * cols // LANES):
        at = tile(u)
        cos, sin = tw_ref[0, at, :], tw_ref[1, at, :]
        sum_r, sum_i = total_ref[0, at, :], total_ref[1, at, :]
        for i in range(TOGETHER):
            re, im = acc[i, at, :times], acc[i, at, times:]
            vr, vi = re * cos - im * sin, re * sin + im * cos
            level_ref[i, 0, at, :] = vr
            level_ref[i, 1, at, :] = vi
            sum_r, sum_i = sum_r + vr, sum_i + vi
        total_ref[0, at, :] = sum_r
        total_ref[1, at, :] = sum_i


def bins_first(half, banks, place, edges, own, rest, table, twist, after):
    cols, length = rest[0].shape
    rows, times = twist.shape[1:]
    smem = pl.BlockSpec(memory_space=pltpu.SMEM)
    fixed = lambda shape: pl.BlockSpec(shape, lambda i: (0,) * len(shape))
    return pl.pallas_call(
        functools.partial(bins_first_kernel, len(own), banks),
        grid=(BINS // TOGETHER,),
        in_specs=[smem, smem]
        + [pl.BlockSpec((cols, 2 * N1 - length), lambda i: (half, 0))] * len(own)
        + [fixed((cols, length))] * len(rest)
        + [fixed((2 * N1, 2 * times))] * 2
        + [fixed((2, rows, times))]
        + [ANY] * len(after),
        out_specs=[
            pl.BlockSpec((TOGETHER, 2, rows, times), lambda i: (i, 0, 0, 0)),
            fixed((2, rows, times)),
        ],
        out_shape=[
            jax.ShapeDtypeStruct((BINS, 2, rows, times), F32),
            jax.ShapeDtypeStruct((2, rows, times), F32),
        ],
        scratch_shapes=[
            pltpu.VMEM((2 * rows, 2 * N1), BF16),
            pltpu.VMEM((TOGETHER, rows, 2 * times), F32),
        ],
        compiler_params=pltpu.CompilerParams(vmem_limit_bytes=VMEM_LIMIT),
        cost_estimate=COST,
        name="bins_first",
    )(place, edges, *own, *rest, *table, twist, *after)


def bins_second_kernel(halves, which_ref, scale_ref, gain_ref, share_ref, *refs):
    level_refs, total_refs = refs[:halves], refs[halves : 2 * halves]
    w2_ref, out_ref, snr_ref, chi, hold = refs[2 * halves :]
    times = out_ref.shape[0]
    part_rows = LANES // halves
    step = pl.program_id(0)

    @pl.when(step == 0)
    def _():
        chi[...] = jnp.zeros_like(chi)

    def rows_of(get, u):
        at = slice(u * part_rows, (u + 1) * part_rows)
        return jnp.concatenate([get(h, at) for h in range(halves)], axis=0)

    def keep(a, re, im):
        chi[a] += re * re + im * im

    for i in range(TOGETHER):
        gain, share = gain_ref[step * TOGETHER + i], share_ref[step * TOGETHER + i]

        def deviation(p):
            return lambda h, at: (
                level_refs[h][i, p, at, :] * gain - total_refs[h][p, at, :] * share
            )

        x = [tuple(rows_of(deviation(p), u) for p in range(2)) for u in range(FOUR)]
        second_points(x, w2_ref, keep)

    @pl.when(step == BINS // TOGETHER - 1)
    def _():
        scale = scale_ref[which_ref[0]]

        def whole(p):
            return lambda h, at: total_refs[h][p, at, :] * scale

        def put(a, re, im):
            for p, value in enumerate((re, im)):
                for g in range(times // LANES):
                    hold[p, g, pl.ds(a, LANES, stride=FOUR), :] = value[:, tile(g)]

        y = [tuple(rows_of(whole(p), u) for p in range(2)) for u in range(FOUR)]
        second_points(y, w2_ref, put)
        for g in range(times // LANES):
            for a in range(FOUR):
                hold[2, g, pl.ds(a, LANES, stride=FOUR), :] = chi[a, :, tile(g)]
            for p in range(2):
                snr_ref[0, 0, p, tile(g), :] = hold[p, g].T
            out_ref[tile(g), :] = hold[2, g].T


def bins_second(which, scale, gain, share, levels, totals, second, tmpls, dets):
    _, _, rows, times = levels[0].shape
    halves = len(levels)
    smem = pl.BlockSpec(memory_space=pltpu.SMEM)
    fixed = lambda shape: pl.BlockSpec(shape, lambda i, w: (0,) * len(shape))
    return pl.pallas_call(
        functools.partial(bins_second_kernel, halves),
        grid_spec=pltpu.PrefetchScalarGridSpec(
            num_scalar_prefetch=1,
            grid=(BINS // TOGETHER,),
            in_specs=[smem, smem, smem]
            + [pl.BlockSpec((TOGETHER, 2, rows, times), lambda i, w: (i, 0, 0, 0))] * halves
            + [fixed((2, rows, times))] * halves
            + [fixed((FOUR * 4 * LANES, 2 * LANES))],
            out_specs=[
                fixed((times, N2)),
                pl.BlockSpec((1, 1, 2, times, N2), lambda i, w: (w[0], w[1], 0, 0, 0)),
            ],
            scratch_shapes=[
                pltpu.VMEM((FOUR, LANES, times), F32),
                pltpu.VMEM((3, times // LANES, N2, LANES), F32),
            ],
        ),
        out_shape=[
            jax.ShapeDtypeStruct((times, N2), F32),
            jax.ShapeDtypeStruct((tmpls, dets, 2, times, N2), F32),
        ],
        compiler_params=pltpu.CompilerParams(vmem_limit_bytes=VMEM_LIMIT),
        cost_estimate=COST,
        name="bins_second",
    )(which, scale, gain, share, *levels, *totals, second)


def handed_on(arrays, after):
    count = len(arrays)
    return pl.pallas_call(
        lambda *refs: None,
        in_specs=[ANY] * (count + len(after)),
        out_specs=[ANY] * count,
        out_shape=[jax.ShapeDtypeStruct(x.shape, x.dtype) for x in arrays],
        input_output_aliases={i: i for i in range(count)},
        compiler_params=pltpu.CompilerParams(vmem_limit_bytes=VMEM_LIMIT),
        cost_estimate=COST,
        name="handed_on",
    )(*arrays, *after)


def swap(x, freq, k):
    return lax.ppermute(x, "freq", [(i, i ^ k) for i in range(freq)])


def far_pieces(own, freq):
    return [own] + [swap(own, freq, k) for k in range(2, freq, 2)]


def near_pieces(far, freq):
    return [x for even in far for x in (even, swap(even, freq, 1))]


def per_device(strain, templates, coinc_tmpl, coinc_det, bin_edges):
    freq, banks = lax.axis_size("freq"), lax.axis_size("bank")
    place = lax.axis_index("freq").astype(jnp.int32)
    bank = lax.axis_index("bank").astype(jnp.int32)
    tmpls, _, cols, _ = templates.shape
    slots, dets = coinc_tmpl.shape[0], strain.shape[0]
    times = N1 // freq
    part = cols // HALVES

    slices = [strain[:, :, h * part : (h + 1) * part] for h in range(HALVES)]
    strains = [lax.all_gather(x, "bank", axis=0, tiled=False) for x in slices]
    first = tuple(jnp.asarray(t) for t in first_table())
    second = jnp.asarray(second_table(cols, HALVES))
    stage = jnp.asarray(stage_table())

    column = place * cols + jnp.arange(cols, dtype=jnp.int32)
    lane = jnp.arange(N1, dtype=jnp.int32)
    time_of_lane = lane // LANES + COARSE * (lane % LANES)
    twist = jnp.stack(phase(column[:, None] * time_of_lane[None, :], N1 * N2))
    own_time = place * times + jnp.arange(times, dtype=jnp.int32)
    table = bank_table(own_time)
    own_twist = []
    for h in range(HALVES):
        rows = jnp.arange(freq * part, dtype=jnp.int32)
        rows = rows // part * cols + h * part + rows % part
        own_twist.append(jnp.stack(phase(rows[:, None] * own_time[None, :], N1 * N2)))

    which = [jnp.stack([coinc_tmpl[j], coinc_det[j], bank]) for j in range(slots)]
    series = jnp.arange(tmpls * dets - 1, dtype=jnp.int32)
    series = series + (series >= which[0][0] * dets + which[0][1])
    info = jnp.stack([series // dets, series % dets], axis=1).reshape(-1)
    info = jnp.concatenate([place.reshape(1), info])
    ends = jnp.zeros((1,), jnp.int32), jnp.full((1,), NBLK, jnp.int32)
    edges = [
        jnp.concatenate([ends[0], bin_edges[coinc_tmpl[j]], ends[1]]) for j in range(slots)
    ]
    here = jnp.stack([place, bank])

    power = (templates[:, 0] ** 2 + templates[:, 1] ** 2).sum(axis=1)
    power = power.reshape(tmpls, NBLK, BLOCK).sum(axis=2)
    own = [entry_product((0,), banks, 0, w, templates, strain[None], slices) for w in which]
    wide = own[0].shape[1]
    power = jnp.pad(power.reshape(1, -1), ((0, 7), (0, wide - tmpls * NBLK)))
    own[0] = jnp.concatenate([own[0], power], axis=0)
    own = [near_pieces(far_pieces(x, freq), freq) for x in own]
    gathered = [x for entry in own for x in entry[1:]]

    block_power = sum(x[cols, : tmpls * NBLK] for x in own[0]).reshape(tmpls, NBLK)
    sigma_sq = block_power.sum(axis=1)
    inv_sigma = lax.rsqrt(sigma_sq)
    bin_of = jnp.sum(
        jnp.arange(NBLK, dtype=jnp.int32)[None, :, None] >= bin_edges[:, None, :], axis=2
    )
    inside = bin_of[:, None, :] == jnp.arange(BINS, dtype=jnp.int32)[None, :, None]
    weights = jnp.where(inside, block_power[:, None, :], 0.0).sum(axis=2) / sigma_sq[:, None]
    gains = [inv_sigma[coinc_tmpl[j]] * lax.rsqrt(weights[coinc_tmpl[j]]) for j in range(slots)]
    shares = [gains[j] * weights[coinc_tmpl[j]] for j in range(slots)]
    which, inv_sigma, gains, shares, twist, info, edges, here, table, own_twist = (
        lax.optimization_barrier(
            (which, inv_sigma, gains, shares, twist, info, edges, here, table, own_twist)
        )
    )

    def exchange(x):
        got = lax.all_to_all(
            x.reshape(freq, -1, LANES), "freq", split_axis=0, concat_axis=0, tiled=True
        )
        return got.reshape(x.shape)

    def bins_of(h, rest, after):
        return [
            bins_first(h, banks, here, edges[j], own[j], rest[j], table, own_twist[h], after)
            for j in range(slots)
        ]

    parts, halves, rest, after = [], [], [], gathered
    later = tuple(range(1, banks))
    for h in range(HALVES):
        half = [entry_product(later, banks, h, w, templates, strains[h], after) for w in which]
        far = [far_pieces(x, freq) for x in half]
        sent, token = first_section(
            freq, h, info, templates, strains[h], first, stage, twist, half
        )
        if h < HALVES - 1:
            (sent,) = handed_on([sent], [x[-1] for x in far])
        if h:
            halves.append(bins_of(h - 1, rest, [token]))
        done = [token] + parts + [x[1] for one in halves for x in one]
        far = [x[:1] + list(handed_on(x[1:], done)) for x in far]
        rest = [near_pieces(x, freq) for x in far]
        if h == HALVES - 1:
            (sent,) = handed_on([sent], [x for entry in rest for x in entry[1:]])
        parts.append(exchange(sent))
        after = [token]
    halves.append(bins_of(HALVES - 1, rest, [sent]))

    chi, snr = [], None
    for j in range(slots):
        levels, totals = zip(*[x[j] for x in halves])
        one, series_of = bins_second(
            which[j], inv_sigma, gains[j], shares[j], levels, totals, second, tmpls, dets
        )
        chi.append(one)
        snr = series_of if snr is None else snr
    snr = second_section(freq, info, inv_sigma, parts, second, snr, chi)
    return (snr, jnp.stack(chi))


def solution(mesh):
    placed = (
        P(None, None, "freq", "bank"),
        P("bank", None, "freq", None),
        P("bank"),
        P("bank"),
        P("bank", None),
    )
    return jax.shard_map(
        per_device,
        mesh=mesh,
        in_specs=placed,
        out_specs=(P("bank", None, None, "freq", None), P("bank", "freq", None)),
        check_vma=False,
    )
```

```python
import functools

import jax
import jax.numpy as jnp
import ml_dtypes
import numpy as np
from jax import lax
from jax.experimental import pallas as pl
from jax.experimental.pallas import tpu as pltpu
from jax.sharding import PartitionSpec as P

N1 = 2048
N2 = 512
NBLK = 32
BLOCK = N1 // NBLK
BINS = 16
LANES = 128
COARSE = N1 // LANES
FOUR = N2 // LANES
F32 = jnp.float32
BF16 = jnp.bfloat16
MIB = 1 << 20
VMEM_LIMIT = 56 * MIB
ANY = pl.BlockSpec(memory_space=pl.ANY)
COST = pl.CostEstimate(flops=MIB, bytes_accessed=MIB, transcendentals=0)


def split_table(table):
    high = table.astype(ml_dtypes.bfloat16)
    low = (table - high.astype(np.float64)).astype(ml_dtypes.bfloat16)
    return high, low


def first_table():
    angle = 2 * np.pi * (np.outer(np.arange(LANES), np.arange(LANES)) % LANES) / LANES
    cos, sin = np.cos(angle), np.sin(angle)
    return split_table(np.block([[cos, sin], [-sin, cos]]))


def stage_table():
    angle = 2 * np.pi * np.outer(np.arange(COARSE), np.arange(LANES)) / N1
    return np.concatenate([np.cos(angle), np.sin(angle)]).astype(np.float32)


def second_table(cols, halves):
    order = np.arange(LANES).reshape(LANES // cols, halves, cols // halves)
    order = order.transpose(1, 0, 2).reshape(-1)
    blocks = []
    for a in range(FOUR):
        n2 = a + FOUR * np.arange(LANES)
        angle = 2 * np.pi * (np.outer(n2, order) % N2) / N2
        cos, sin = np.cos(angle), np.sin(angle)
        blocks.append(np.block([[cos, -sin], [sin, cos]]))
    return np.concatenate([part for block in blocks for part in split_table(block)])


def split(x):
    high = x.astype(BF16)
    return high, (x - high.astype(F32)).astype(BF16)


def phase(index, length):
    angle = (index % length).astype(F32) * (2.0 * np.pi / length)
    return jnp.cos(angle), jnp.sin(angle)


def times_i(z):
    return (-z[1], z[0])


def plus(x, y):
    return (x[0] + y[0], x[1] + y[1])


def minus(x, y):
    return (x[0] - y[0], x[1] - y[1])


def dft4(x):
    s0, s1 = plus(x[0], x[2]), minus(x[0], x[2])
    s2, s3 = plus(x[1], x[3]), times_i(minus(x[1], x[3]))
    return [plus(s0, s2), plus(s1, s3), minus(s0, s2), minus(s1, s3)]


def turn(z, step):
    step %= 16
    if step == 0:
        return z
    if step == 4:
        return times_i(z)
    if step == 8:
        return (-z[0], -z[1])
    half = float(np.sqrt(0.5))
    if step == 2:
        return ((z[0] - z[1]) * half, (z[0] + z[1]) * half)
    if step == 6:
        return ((z[0] + z[1]) * -half, (z[0] - z[1]) * half)
    cos, sin = float(np.cos(np.pi * step / 8)), float(np.sin(np.pi * step / 8))
    return (z[0] * cos - z[1] * sin, z[0] * sin + z[1] * cos)


def dft16(x):
    columns = [dft4([x[4 * u1 + u0] for u1 in range(4)]) for u0 in range(4)]
    out = [None] * 16
    for a0 in range(4):
        ys = dft4([turn(columns[u0][a0], u0 * a0) for u0 in range(4)])
        for a1 in range(4):
            out[a0 + 4 * a1] = ys[a1]
    return out


def dot3(left, right):
    (lh, ll), (rh, rl) = left, right
    return jnp.dot(
        jnp.concatenate([lh, lh, ll], axis=1),
        jnp.concatenate([rh, rl, rh], axis=0),
        preferred_element_type=F32,
    )


def rows_dot3(left, right):
    half = left.shape[0] // 2
    high, low = right
    both = jnp.dot(left, high, preferred_element_type=F32)
    cross = jnp.dot(left[:half], low, preferred_element_type=F32)
    return both[:half] + (both[half:] + cross)


def products(tmpl, strain_ref, where, rows=slice(None)):
    per_piece = COARSE // strain_ref.shape[0]
    for u in range(COARSE):
        off = u % per_piece
        there = slice(off * LANES, (off + 1) * LANES)
        hr, hi = tmpl(0, u), tmpl(1, u)
        sr = strain_ref[(u // per_piece,) + where + (0, rows, there)]
        si = strain_ref[(u // per_piece,) + where + (1, rows, there)]
        yield u, hr * sr + hi * si, hr * si - hi * sr


def tile(u):
    return slice(u * LANES, (u + 1) * LANES)


def first_kernel(
    freq, info_ref, tmpl_ref, strain_ref, wh_ref, wl_ref, stage_ref, tw_ref, *refs
):
    out_ref, token_ref, gh, gl, z = refs[-5:]
    token_ref[...] = jnp.zeros_like(token_ref)
    rows = tmpl_ref.shape[2]
    for r in range(0, rows, ROWS):
        at = slice(r, r + ROWS)
        got = products(lambda p, u: tmpl_ref[0, p, at, tile(u)], strain_ref, (0,), at)
        y = dft16([(re, im) for _, re, im in got])
        for a in range(COARSE):
            cos, sin = stage_ref[a : a + 1, :], stage_ref[COARSE + a : COARSE + a + 1, :]
            yr, yi = y[a]
            to = slice(a * rows + r, a * rows + r + ROWS)
            gh[to, :LANES], gl[to, :LANES] = split(yr * cos - yi * sin)
            gh[to, LANES:], gl[to, LANES:] = split(yr * sin + yi * cos)
    z[...] = dot3((gh[...], gl[...]), (wh_ref[...], wl_ref[...]))
    width = LANES // freq
    slot = lax.broadcasted_iota(jnp.int32, (ROWS, LANES), 1) // width
    for group in range(COARSE // freq):
        for r in range(0, rows, ROWS):
            at = slice(r, r + ROWS)
            turned = []
            for i in range(freq):
                a = group * freq + i
                to = slice(a * rows + r, a * rows + r + ROWS)
                zr, zi = z[to, :LANES], z[to, LANES:]
                cos, sin = tw_ref[0, at, tile(a)], tw_ref[1, at, tile(a)]
                pair = (zr * cos - zi * sin, zr * sin + zi * cos)
                if i:
                    pair = tuple(pltpu.roll(v, i * width, 1) for v in pair)
                turned.append(pair)
            for q in range(freq):
                for p in range(2):
                    value = turned[(0 - q) % freq][p]
                    for s in range(1, freq):
                        value = jnp.where(slot == s, turned[(s - q) % freq][p], value)
                    out_ref[q, 0, p, group, at] = value


ROWS = 16
HALVES = 2
TOGETHER = 2


def first_section(freq, half, info, templates, strain, first, stage, twist, after):
    tmpls = templates.shape[0]
    pieces, dets, _, rows, piece_len = strain.shape
    series = tmpls * dets - 1
    groups = COARSE // freq
    table = pl.BlockSpec((2 * LANES, 2 * LANES), lambda i, n: (0, 0))
    out = (freq, series, 2, groups, rows, LANES)
    return pl.pallas_call(
        functools.partial(first_kernel, freq),
        grid_spec=pltpu.PrefetchScalarGridSpec(
            num_scalar_prefetch=1,
            grid=(series,),
            in_specs=[
                pl.BlockSpec(
                    (1, 2, rows, N1), lambda i, n: (n[1 + 2 * i], 0, half, 0)
                ),
                pl.BlockSpec(
                    (pieces, 1, 2, rows, piece_len), lambda i, n: (0, n[2 + 2 * i], 0, 0, 0)
                ),
                table,
                table,
                pl.BlockSpec((2 * COARSE, LANES), lambda i, n: (0, 0)),
                pl.BlockSpec((2, rows, N1), lambda i, n: (0, half, 0)),
            ]
            + [ANY] * len(after),
            out_specs=[
                pl.BlockSpec(
                    (freq, 1, 2, groups, rows, LANES), lambda i, n: (0, i, 0, 0, 0, 0)
                ),
                pl.BlockSpec((8, LANES), lambda i, n: (0, 0)),
            ],
            scratch_shapes=[
                pltpu.VMEM((COARSE * rows, 2 * LANES), BF16),
                pltpu.VMEM((COARSE * rows, 2 * LANES), BF16),
                pltpu.VMEM((COARSE * rows, 2 * LANES), F32),
            ],
        ),
        out_shape=[
            jax.ShapeDtypeStruct(out, F32),
            jax.ShapeDtypeStruct((8, LANES), F32),
        ],
        compiler_params=pltpu.CompilerParams(vmem_limit_bytes=VMEM_LIMIT),
        cost_estimate=pl.CostEstimate(
            flops=60 * series * rows * N1 * LANES, bytes_accessed=16 * MIB, transcendentals=0
        ),
        name="first_section",
    )(info, templates, strain, first[0], first[1], stage, twist, *after)


def entry_kernel(steps, banks, which_ref, tmpl_ref, strain_ref, *refs):
    out_ref = refs[-1]
    length = N1 // banks
    first_half = lax.broadcasted_iota(jnp.int32, (ROWS, LANES), 1) < BLOCK
    for n, k in enumerate(steps):
        part = lax.rem(which_ref[2] + k, banks)
        for u in range(length // LANES):
            lane = pl.ds(pl.multiple_of(part * length + u * LANES, LANES), LANES)
            hr, hi = tmpl_ref[0, 0, :, lane], tmpl_ref[0, 1, :, lane]
            piece = 0 if strain_ref.shape[0] == 1 else part
            sr, si = strain_ref[piece, 0, 0, :, tile(u)], strain_ref[piece, 0, 1, :, tile(u)]
            re, im = hr * sr + hi * si, hr * si - hi * sr
            to = 2 * (n * length // LANES + u)
            out_ref[:, tile(to)] = jnp.where(first_half, re, pltpu.roll(im, BLOCK, 1))
            out_ref[:, tile(to + 1)] = jnp.where(first_half, pltpu.roll(re, BLOCK, 1), im)


def entry_product(steps, banks, half, which, templates, strain, after):
    pieces, _, _, cols, length = strain.shape
    first = half * cols // ROWS
    return pl.pallas_call(
        functools.partial(entry_kernel, steps, banks),
        grid_spec=pltpu.PrefetchScalarGridSpec(
            num_scalar_prefetch=1,
            grid=(cols // ROWS,),
            in_specs=[
                pl.BlockSpec((1, 2, ROWS, N1), lambda c, w: (w[0], 0, first + c, 0)),
                pl.BlockSpec((pieces, 1, 2, ROWS, length), lambda c, w: (0, w[1], 0, c, 0)),
            ]
            + [ANY] * len(after),
            out_specs=pl.BlockSpec((ROWS, 2 * length * len(steps)), lambda c, w: (c, 0)),
        ),
        out_shape=jax.ShapeDtypeStruct((cols, 2 * length * len(steps)), F32),
        compiler_params=pltpu.CompilerParams(vmem_limit_bytes=VMEM_LIMIT),
        cost_estimate=COST,
        name="entry_product",
    )(which, templates, strain, *after)


def second_points(x, w2_ref, use):
    for a, (yr, yi) in enumerate(dft4(x)):
        y = jnp.concatenate([yr, yi], axis=0)
        table = w2_ref[a * 4 * LANES : (a + 1) * 4 * LANES, :]
        z = rows_dot3(table, split(y))
        use(a, z[:LANES], z[LANES:])


def second_kernel(freq, halves, info_ref, scale_ref, *refs):
    part_refs, w2_ref = refs[:halves], refs[halves]
    out_ref, hold, order = refs[-3:]
    place = info_ref[0]
    groups, cols = part_refs[0].shape[3:5]
    per = LANES // (halves * cols)
    width = LANES // freq
    scale = scale_ref[info_ref[1 + 2 * pl.program_id(0)]]

    def rows_of(p, u):
        tiles = [
            jnp.concatenate(
                [ref[u * per + f, 0, p, g] for ref in part_refs for f in range(per)],
                axis=0,
            )
            for g in range(groups)
        ]
        return jnp.concatenate(tiles, axis=1)

    x = [(rows_of(0, u), rows_of(1, u)) for u in range(FOUR)]

    def keep(a, re, im):
        for p, value in enumerate((re, im)):
            for g in range(groups):
                hold[p, g, pl.ds(a, LANES, stride=FOUR), :] = value[:, tile(g)] * scale

    second_points(x, w2_ref, keep)
    for p in range(2):
        for g in range(groups):
            turned = hold[p, g].T
            for s in range(freq):
                a = g * freq + lax.rem(s - place + freq, freq)
                for j in range(FOUR):
                    order[p, j, pl.ds(a, width, stride=COARSE), :] = turned[
                        s * width : (s + 1) * width, tile(j)
                    ]
        for j in range(FOUR):
            out_ref[0, 0, p, :, tile(j)] = order[p, j]


def second_section(freq, info, scale, parts, second, snr, after):
    _, series, _, groups, cols, _ = parts[0].shape
    halves = len(parts)
    times = groups * LANES
    smem = pl.BlockSpec(memory_space=pltpu.SMEM)
    table = pl.BlockSpec((FOUR * 4 * LANES, 2 * LANES), lambda i, n: (0, 0))
    part = pl.BlockSpec(
        (freq, 1, 2, groups, cols, LANES), lambda i, n: (0, i, 0, 0, 0, 0)
    )
    return pl.pallas_call(
        functools.partial(second_kernel, freq, halves),
        grid_spec=pltpu.PrefetchScalarGridSpec(
            num_scalar_prefetch=1,
            grid=(series,),
            in_specs=[smem] + [part] * halves + [table, ANY] + [ANY] * len(after),
            out_specs=pl.BlockSpec(
                (1, 1, 2, times, N2), lambda i, n: (n[1 + 2 * i], n[2 + 2 * i], 0, 0, 0)
            ),
            scratch_shapes=[
                pltpu.VMEM((2, groups, N2, LANES), F32),
                pltpu.VMEM((2, FOUR, times, LANES), F32),
            ],
        ),
        out_shape=jax.ShapeDtypeStruct(snr.shape, F32),
        input_output_aliases={3 + halves: 0},
        compiler_params=pltpu.CompilerParams(vmem_limit_bytes=VMEM_LIMIT),
        cost_estimate=COST,
        name="second_section",
    )(info, scale, *parts, second, snr, *after)


BLOCKS = 4


def bank_kernel(block_ref, inner_ref, high_ref, low_ref):
    times = block_ref.shape[-1]
    rc, rs = inner_ref[0], inner_ref[1]
    for b in range(BLOCKS):
        bc, bs = block_ref[b, 0:1, :], block_ref[b, 1:2, :]
        cos, sin = split(bc * rc - bs * rs), split(bc * rs + bs * rc)
        top = slice(2 * b * BLOCK, (2 * b + 1) * BLOCK)
        low = slice((2 * b + 1) * BLOCK, (2 * b + 2) * BLOCK)
        for ref, c, s in zip((high_ref, low_ref), cos, sin):
            ref[top, :times] = c
            ref[top, times:] = s
            ref[low, :times] = -s
            ref[low, times:] = c


def bank_table(own_time):
    times = own_time.shape[0]
    block = jnp.arange(NBLK, dtype=jnp.int32)[:, None] * own_time[None, :]
    block = jnp.stack(phase(block, NBLK), axis=1)
    inner = jnp.arange(BLOCK, dtype=jnp.int32)[:, None] * own_time[None, :]
    inner = jnp.stack(phase(inner, N1))
    return pl.pallas_call(
        bank_kernel,
        grid=(NBLK // BLOCKS,),
        in_specs=[
            pl.BlockSpec((BLOCKS, 2, times), lambda b: (b, 0, 0)),
            pl.BlockSpec((2, BLOCK, times), lambda b: (0, 0, 0)),
        ],
        out_specs=[pl.BlockSpec((BLOCKS * 2 * BLOCK, 2 * times), lambda b: (b, 0))] * 2,
        out_shape=[jax.ShapeDtypeStruct((2 * N1, 2 * times), BF16)] * 2,
        compiler_params=pltpu.CompilerParams(vmem_limit_bytes=VMEM_LIMIT),
        cost_estimate=COST,
        name="bank_table",
    )(block, inner)


def bins_first_kernel(pieces, banks, place_ref, edge_ref, *refs):
    own_refs, rest_refs = refs[:pieces], refs[pieces : 2 * pieces]
    wh_ref, wl_ref, tw_ref = refs[2 * pieces : 2 * pieces + 3]
    level_ref, total_ref, x, acc = refs[-4:]
    times = total_ref.shape[-1]
    cols = own_refs[0].shape[0]
    length = 2 * N1 // banks
    chunk = FOUR * LANES
    step = pl.program_id(0)

    @pl.when(step == 0)
    def _():
        for k in range(pieces):
            row = pl.multiple_of((place_ref[0] ^ k) * cols, cols)
            low = pl.multiple_of(row + pieces * cols, cols)
            for n in range(banks):
                ref = rest_refs[k] if n else own_refs[k]
                start = lax.rem(place_ref[1] + n, banks) * length

                def cut(i, carry):
                    lane = max(n - 1, 0) * length + i * chunk
                    part = split(ref[:, pl.ds(pl.multiple_of(lane, chunk), chunk)])
                    to = pl.ds(pl.multiple_of(start + i * chunk, chunk), chunk)
                    x[pl.ds(row, cols), to], x[pl.ds(low, cols), to] = part
                    return carry

                lax.fori_loop(0, length // chunk, cut, 0)
        total_ref[...] = jnp.zeros_like(total_ref)

    def blocks_at(block, blocks):
        at = pl.ds(pl.multiple_of(block * LANES, LANES), blocks * LANES)
        return rows_dot3(x[:, at], (wh_ref[at, :], wl_ref[at, :]))

    for i in range(TOGETHER):
        start, end = edge_ref[step * TOGETHER + i], edge_ref[step * TOGETHER + i + 1]
        odd = (end - start) % 2

        @pl.when(odd == 1)
        def _():
            acc[i] = blocks_at(end - 1, 1)

        @pl.when(odd == 0)
        def _():
            acc[i] = blocks_at(end - 2, 2)

        def two(n, carry):
            acc[i] += blocks_at(start + 2 * n, 2)
            return carry

        lax.fori_loop(0, (end - start - 1) // 2, two, 0)

    for u in range(pieces * cols // LANES):
        at = tile(u)
        cos, sin = tw_ref[0, at, :], tw_ref[1, at, :]
        sum_r, sum_i = total_ref[0, at, :], total_ref[1, at, :]
        for i in range(TOGETHER):
            re, im = acc[i, at, :times], acc[i, at, times:]
            vr, vi = re * cos - im * sin, re * sin + im * cos
            level_ref[i, 0, at, :] = vr
            level_ref[i, 1, at, :] = vi
            sum_r, sum_i = sum_r + vr, sum_i + vi
        total_ref[0, at, :] = sum_r
        total_ref[1, at, :] = sum_i


def bins_first(half, banks, place, edges, own, rest, table, twist, after):
    cols, length = rest[0].shape
    rows, times = twist.shape[1:]
    smem = pl.BlockSpec(memory_space=pltpu.SMEM)
    fixed = lambda shape: pl.BlockSpec(shape, lambda i: (0,) * len(shape))
    return pl.pallas_call(
        functools.partial(bins_first_kernel, len(own), banks),
        grid=(BINS // TOGETHER,),
        in_specs=[smem, smem]
        + [pl.BlockSpec((cols, 2 * N1 - length), lambda i: (half, 0))] * len(own)
        + [fixed((cols, length))] * len(rest)
        + [fixed((2 * N1, 2 * times))] * 2
        + [fixed((2, rows, times))]
        + [ANY] * len(after),
        out_specs=[
            pl.BlockSpec((TOGETHER, 2, rows, times), lambda i: (i, 0, 0, 0)),
            fixed((2, rows, times)),
        ],
        out_shape=[
            jax.ShapeDtypeStruct((BINS, 2, rows, times), F32),
            jax.ShapeDtypeStruct((2, rows, times), F32),
        ],
        scratch_shapes=[
            pltpu.VMEM((2 * rows, 2 * N1), BF16),
            pltpu.VMEM((TOGETHER, rows, 2 * times), F32),
        ],
        compiler_params=pltpu.CompilerParams(vmem_limit_bytes=VMEM_LIMIT),
        cost_estimate=COST,
        name="bins_first",
    )(place, edges, *own, *rest, *table, twist, *after)


def bins_second_kernel(halves, which_ref, scale_ref, gain_ref, share_ref, *refs):
    level_refs, total_refs = refs[:halves], refs[halves : 2 * halves]
    w2_ref, out_ref, snr_ref, chi, hold = refs[2 * halves :]
    times = out_ref.shape[0]
    part_rows = LANES // halves
    step = pl.program_id(0)

    @pl.when(step == 0)
    def _():
        chi[...] = jnp.zeros_like(chi)

    def rows_of(get, u):
        at = slice(u * part_rows, (u + 1) * part_rows)
        return jnp.concatenate([get(h, at) for h in range(halves)], axis=0)

    def keep(a, re, im):
        chi[a] += re * re + im * im

    for i in range(TOGETHER):
        gain, share = gain_ref[step * TOGETHER + i], share_ref[step * TOGETHER + i]

        def deviation(p):
            return lambda h, at: (
                level_refs[h][i, p, at, :] * gain - total_refs[h][p, at, :] * share
            )

        x = [tuple(rows_of(deviation(p), u) for p in range(2)) for u in range(FOUR)]
        second_points(x, w2_ref, keep)

    @pl.when(step == BINS // TOGETHER - 1)
    def _():
        scale = scale_ref[which_ref[0]]

        def whole(p):
            return lambda h, at: total_refs[h][p, at, :] * scale

        def put(a, re, im):
            for p, value in enumerate((re, im)):
                for g in range(times // LANES):
                    hold[p, g, pl.ds(a, LANES, stride=FOUR), :] = value[:, tile(g)]

        y = [tuple(rows_of(whole(p), u) for p in range(2)) for u in range(FOUR)]
        second_points(y, w2_ref, put)
        for g in range(times // LANES):
            for a in range(FOUR):
                hold[2, g, pl.ds(a, LANES, stride=FOUR), :] = chi[a, :, tile(g)]
            for p in range(2):
                snr_ref[0, 0, p, tile(g), :] = hold[p, g].T
            out_ref[tile(g), :] = hold[2, g].T


def bins_second(which, scale, gain, share, levels, totals, second, tmpls, dets):
    _, _, rows, times = levels[0].shape
    halves = len(levels)
    smem = pl.BlockSpec(memory_space=pltpu.SMEM)
    fixed = lambda shape: pl.BlockSpec(shape, lambda i, w: (0,) * len(shape))
    return pl.pallas_call(
        functools.partial(bins_second_kernel, halves),
        grid_spec=pltpu.PrefetchScalarGridSpec(
            num_scalar_prefetch=1,
            grid=(BINS // TOGETHER,),
            in_specs=[smem, smem, smem]
            + [pl.BlockSpec((TOGETHER, 2, rows, times), lambda i, w: (i, 0, 0, 0))] * halves
            + [fixed((2, rows, times))] * halves
            + [fixed((FOUR * 4 * LANES, 2 * LANES))],
            out_specs=[
                fixed((times, N2)),
                pl.BlockSpec((1, 1, 2, times, N2), lambda i, w: (w[0], w[1], 0, 0, 0)),
            ],
            scratch_shapes=[
                pltpu.VMEM((FOUR, LANES, times), F32),
                pltpu.VMEM((3, times // LANES, N2, LANES), F32),
            ],
        ),
        out_shape=[
            jax.ShapeDtypeStruct((times, N2), F32),
            jax.ShapeDtypeStruct((tmpls, dets, 2, times, N2), F32),
        ],
        compiler_params=pltpu.CompilerParams(vmem_limit_bytes=VMEM_LIMIT),
        cost_estimate=COST,
        name="bins_second",
    )(which, scale, gain, share, *levels, *totals, second)


def handed_on(arrays, after):
    count = len(arrays)
    return pl.pallas_call(
        lambda *refs: None,
        in_specs=[ANY] * (count + len(after)),
        out_specs=[ANY] * count,
        out_shape=[jax.ShapeDtypeStruct(x.shape, x.dtype) for x in arrays],
        input_output_aliases={i: i for i in range(count)},
        compiler_params=pltpu.CompilerParams(vmem_limit_bytes=VMEM_LIMIT),
        cost_estimate=COST,
        name="handed_on",
    )(*arrays, *after)


def swap(x, freq, k):
    return lax.ppermute(x, "freq", [(i, i ^ k) for i in range(freq)])


def far_pieces(own, freq):
    return [own] + [swap(own, freq, k) for k in range(2, freq, 2)]


def near_pieces(far, freq):
    return [x for even in far for x in (even, swap(even, freq, 1))]


def per_device(strain, templates, coinc_tmpl, coinc_det, bin_edges):
    freq, banks = lax.axis_size("freq"), lax.axis_size("bank")
    place = lax.axis_index("freq").astype(jnp.int32)
    bank = lax.axis_index("bank").astype(jnp.int32)
    tmpls, _, cols, _ = templates.shape
    slots, dets = coinc_tmpl.shape[0], strain.shape[0]
    times = N1 // freq
    part = cols // HALVES

    slices = [strain[:, :, h * part : (h + 1) * part] for h in range(HALVES)]
    strains = [lax.all_gather(x, "bank", axis=0, tiled=False) for x in slices]
    first = tuple(jnp.asarray(t) for t in first_table())
    second = jnp.asarray(second_table(cols, HALVES))
    stage = jnp.asarray(stage_table())

    column = place * cols + jnp.arange(cols, dtype=jnp.int32)
    lane = jnp.arange(N1, dtype=jnp.int32)
    time_of_lane = lane // LANES + COARSE * (lane % LANES)
    twist = jnp.stack(phase(column[:, None] * time_of_lane[None, :], N1 * N2))
    own_time = place * times + jnp.arange(times, dtype=jnp.int32)
    table = bank_table(own_time)
    own_twist = []
    for h in range(HALVES):
        rows = jnp.arange(freq * part, dtype=jnp.int32)
        rows = rows // part * cols + h * part + rows % part
        own_twist.append(jnp.stack(phase(rows[:, None] * own_time[None, :], N1 * N2)))

    which = [jnp.stack([coinc_tmpl[j], coinc_det[j], bank]) for j in range(slots)]
    series = jnp.arange(tmpls * dets - 1, dtype=jnp.int32)
    series = series + (series >= which[0][0] * dets + which[0][1])
    info = jnp.stack([series // dets, series % dets], axis=1).reshape(-1)
    info = jnp.concatenate([place.reshape(1), info])
    ends = jnp.zeros((1,), jnp.int32), jnp.full((1,), NBLK, jnp.int32)
    edges = [
        jnp.concatenate([ends[0], bin_edges[coinc_tmpl[j]], ends[1]]) for j in range(slots)
    ]
    here = jnp.stack([place, bank])

    power = (templates[:, 0] ** 2 + templates[:, 1] ** 2).sum(axis=1)
    power = power.reshape(tmpls, NBLK, BLOCK).sum(axis=2)
    own = [entry_product((0,), banks, 0, w, templates, strain[None], slices) for w in which]
    wide = own[0].shape[1]
    power = jnp.pad(power.reshape(1, -1), ((0, 7), (0, wide - tmpls * NBLK)))
    own[0] = jnp.concatenate([own[0], power], axis=0)
    own = [near_pieces(far_pieces(x, freq), freq) for x in own]
    gathered = [x for entry in own for x in entry[1:]]

    block_power = sum(x[cols, : tmpls * NBLK] for x in own[0]).reshape(tmpls, NBLK)
    sigma_sq = block_power.sum(axis=1)
    inv_sigma = lax.rsqrt(sigma_sq)
    bin_of = jnp.sum(
        jnp.arange(NBLK, dtype=jnp.int32)[None, :, None] >= bin_edges[:, None, :], axis=2
    )
    inside = bin_of[:, None, :] == jnp.arange(BINS, dtype=jnp.int32)[None, :, None]
    weights = jnp.where(inside, block_power[:, None, :], 0.0).sum(axis=2) / sigma_sq[:, None]
    gains = [inv_sigma[coinc_tmpl[j]] * lax.rsqrt(weights[coinc_tmpl[j]]) for j in range(slots)]
    shares = [gains[j] * weights[coinc_tmpl[j]] for j in range(slots)]
    which, inv_sigma, gains, shares, twist, info, edges, here, table, own_twist = (
        lax.optimization_barrier(
            (which, inv_sigma, gains, shares, twist, info, edges, here, table, own_twist)
        )
    )

    def exchange(x):
        got = lax.all_to_all(
            x.reshape(freq, -1, LANES), "freq", split_axis=0, concat_axis=0, tiled=True
        )
        return got.reshape(x.shape)

    def bins_of(h, rest, after):
        return [
            bins_first(h, banks, here, edges[j], own[j], rest[j], table, own_twist[h], after)
            for j in range(slots)
        ]

    parts, halves, rest, after = [], [], [], gathered
    later = tuple(range(1, banks))
    for h in range(HALVES):
        half = [entry_product(later, banks, h, w, templates, strains[h], after) for w in which]
        far = [far_pieces(x, freq) for x in half]
        sent, token = first_section(
            freq, h, info, templates, strains[h], first, stage, twist, half
        )
        if h < HALVES - 1:
            (sent,) = handed_on([sent], [piece for x in far for piece in x[1:]])
        if h:
            halves.append(bins_of(h - 1, rest, [token]))
        done = [token] + parts + [x[1] for one in halves for x in one]
        far = [x[:1] + list(handed_on(x[1:], done)) for x in far]
        rest = [near_pieces(x, freq) for x in far]
        if h == HALVES - 1:
            (sent,) = handed_on([sent], [x for entry in rest for x in entry[1:]])
        parts.append(exchange(sent))
        after = [token]
    halves.append(bins_of(HALVES - 1, rest, [sent]))

    chi, snr = [], None
    for j in range(slots):
        levels, totals = zip(*[x[j] for x in halves])
        one, series_of = bins_second(
            which[j], inv_sigma, gains[j], shares[j], levels, totals, second, tmpls, dets
        )
        chi.append(one)
        snr = series_of if snr is None else snr
    snr = second_section(freq, info, inv_sigma, parts, second, snr, chi)
    return (snr, jnp.stack(chi))


def solution(mesh):
    placed = (
        P(None, None, "freq", "bank"),
        P("bank", None, "freq", None),
        P("bank"),
        P("bank"),
        P("bank", None),
    )
    return jax.shard_map(
        per_device,
        mesh=mesh,
        in_specs=placed,
        out_specs=(P("bank", None, None, "freq", None), P("bank", "freq", None)),
        check_vma=False,
    )
```

```python
import functools

import jax
import jax.numpy as jnp
import ml_dtypes
import numpy as np
from jax import lax
from jax.experimental import pallas as pl
from jax.experimental.pallas import tpu as pltpu
from jax.sharding import PartitionSpec as P

N1 = 2048
N2 = 512
NBLK = 32
BLOCK = N1 // NBLK
BINS = 16
LANES = 128
COARSE = N1 // LANES
FOUR = N2 // LANES
F32 = jnp.float32
BF16 = jnp.bfloat16
MIB = 1 << 20
VMEM_LIMIT = 56 * MIB
ANY = pl.BlockSpec(memory_space=pl.ANY)
COST = pl.CostEstimate(flops=MIB, bytes_accessed=MIB, transcendentals=0)


def split_table(table):
    high = table.astype(ml_dtypes.bfloat16)
    low = (table - high.astype(np.float64)).astype(ml_dtypes.bfloat16)
    return high, low


def first_table():
    angle = 2 * np.pi * (np.outer(np.arange(LANES), np.arange(LANES)) % LANES) / LANES
    cos, sin = np.cos(angle), np.sin(angle)
    return split_table(np.block([[cos, sin], [-sin, cos]]))


def stage_table():
    angle = 2 * np.pi * np.outer(np.arange(COARSE), np.arange(LANES)) / N1
    return np.concatenate([np.cos(angle), np.sin(angle)]).astype(np.float32)


def second_table(cols, halves):
    order = np.arange(LANES).reshape(LANES // cols, halves, cols // halves)
    order = order.transpose(1, 0, 2).reshape(-1)
    blocks = []
    for a in range(FOUR):
        n2 = a + FOUR * np.arange(LANES)
        angle = 2 * np.pi * (np.outer(n2, order) % N2) / N2
        cos, sin = np.cos(angle), np.sin(angle)
        blocks.append(np.block([[cos, -sin], [sin, cos]]))
    return np.concatenate([part for block in blocks for part in split_table(block)])


def split(x):
    high = x.astype(BF16)
    return high, (x - high.astype(F32)).astype(BF16)


def phase(index, length):
    angle = (index % length).astype(F32) * (2.0 * np.pi / length)
    return jnp.cos(angle), jnp.sin(angle)


def times_i(z):
    return (-z[1], z[0])


def plus(x, y):
    return (x[0] + y[0], x[1] + y[1])


def minus(x, y):
    return (x[0] - y[0], x[1] - y[1])


def dft4(x):
    s0, s1 = plus(x[0], x[2]), minus(x[0], x[2])
    s2, s3 = plus(x[1], x[3]), times_i(minus(x[1], x[3]))
    return [plus(s0, s2), plus(s1, s3), minus(s0, s2), minus(s1, s3)]


def turn(z, step):
    step %= 16
    if step == 0:
        return z
    if step == 4:
        return times_i(z)
    if step == 8:
        return (-z[0], -z[1])
    half = float(np.sqrt(0.5))
    if step == 2:
        return ((z[0] - z[1]) * half, (z[0] + z[1]) * half)
    if step == 6:
        return ((z[0] + z[1]) * -half, (z[0] - z[1]) * half)
    cos, sin = float(np.cos(np.pi * step / 8)), float(np.sin(np.pi * step / 8))
    return (z[0] * cos - z[1] * sin, z[0] * sin + z[1] * cos)


def dft16(x):
    columns = [dft4([x[4 * u1 + u0] for u1 in range(4)]) for u0 in range(4)]
    out = [None] * 16
    for a0 in range(4):
        ys = dft4([turn(columns[u0][a0], u0 * a0) for u0 in range(4)])
        for a1 in range(4):
            out[a0 + 4 * a1] = ys[a1]
    return out


def dot3(left, right):
    (lh, ll), (rh, rl) = left, right
    return jnp.dot(
        jnp.concatenate([lh, lh, ll], axis=1),
        jnp.concatenate([rh, rl, rh], axis=0),
        preferred_element_type=F32,
    )


def rows_dot3(left, right):
    half = left.shape[0] // 2
    high, low = right
    both = jnp.dot(left, high, preferred_element_type=F32)
    cross = jnp.dot(left[:half], low, preferred_element_type=F32)
    return both[:half] + (both[half:] + cross)


def products(tmpl, strain_ref, where, rows=slice(None)):
    per_piece = COARSE // strain_ref.shape[0]
    for u in range(COARSE):
        off = u % per_piece
        there = slice(off * LANES, (off + 1) * LANES)
        hr, hi = tmpl(0, u), tmpl(1, u)
        sr = strain_ref[(u // per_piece,) + where + (0, rows, there)]
        si = strain_ref[(u // per_piece,) + where + (1, rows, there)]
        yield u, hr * sr + hi * si, hr * si - hi * sr


def tile(u):
    return slice(u * LANES, (u + 1) * LANES)


def first_kernel(
    freq, info_ref, tmpl_ref, strain_ref, wh_ref, wl_ref, stage_ref, tw_ref, *refs
):
    out_ref, token_ref, gh, gl, z = refs[-5:]
    token_ref[...] = jnp.zeros_like(token_ref)
    rows = tmpl_ref.shape[2]
    for r in range(0, rows, ROWS):
        at = slice(r, r + ROWS)
        got = products(lambda p, u: tmpl_ref[0, p, at, tile(u)], strain_ref, (0,), at)
        y = dft16([(re, im) for _, re, im in got])
        for a in range(COARSE):
            cos, sin = stage_ref[a : a + 1, :], stage_ref[COARSE + a : COARSE + a + 1, :]
            yr, yi = y[a]
            to = slice(a * rows + r, a * rows + r + ROWS)
            gh[to, :LANES], gl[to, :LANES] = split(yr * cos - yi * sin)
            gh[to, LANES:], gl[to, LANES:] = split(yr * sin + yi * cos)
    z[...] = dot3((gh[...], gl[...]), (wh_ref[...], wl_ref[...]))
    width = LANES // freq
    slot = lax.broadcasted_iota(jnp.int32, (ROWS, LANES), 1) // width
    for group in range(COARSE // freq):
        for r in range(0, rows, ROWS):
            at = slice(r, r + ROWS)
            turned = []
            for i in range(freq):
                a = group * freq + i
                to = slice(a * rows + r, a * rows + r + ROWS)
                zr, zi = z[to, :LANES], z[to, LANES:]
                cos, sin = tw_ref[0, at, tile(a)], tw_ref[1, at, tile(a)]
                pair = (zr * cos - zi * sin, zr * sin + zi * cos)
                if i:
                    pair = tuple(pltpu.roll(v, i * width, 1) for v in pair)
                turned.append(pair)
            for q in range(freq):
                for p in range(2):
                    value = turned[(0 - q) % freq][p]
                    for s in range(1, freq):
                        value = jnp.where(slot == s, turned[(s - q) % freq][p], value)
                    out_ref[q, 0, p, group, at] = value


ROWS = 16
HALVES = 2
TOGETHER = 2


def first_section(freq, half, info, templates, strain, first, stage, twist, after):
    tmpls = templates.shape[0]
    pieces, dets, _, rows, piece_len = strain.shape
    series = tmpls * dets - 1
    groups = COARSE // freq
    table = pl.BlockSpec((2 * LANES, 2 * LANES), lambda i, n: (0, 0))
    out = (freq, series, 2, groups, rows, LANES)
    return pl.pallas_call(
        functools.partial(first_kernel, freq),
        grid_spec=pltpu.PrefetchScalarGridSpec(
            num_scalar_prefetch=1,
            grid=(series,),
            in_specs=[
                pl.BlockSpec(
                    (1, 2, rows, N1), lambda i, n: (n[1 + 2 * i], 0, half, 0)
                ),
                pl.BlockSpec(
                    (pieces, 1, 2, rows, piece_len), lambda i, n: (0, n[2 + 2 * i], 0, 0, 0)
                ),
                table,
                table,
                pl.BlockSpec((2 * COARSE, LANES), lambda i, n: (0, 0)),
                pl.BlockSpec((2, rows, N1), lambda i, n: (0, half, 0)),
            ]
            + [ANY] * len(after),
            out_specs=[
                pl.BlockSpec(
                    (freq, 1, 2, groups, rows, LANES), lambda i, n: (0, i, 0, 0, 0, 0)
                ),
                pl.BlockSpec((8, LANES), lambda i, n: (0, 0)),
            ],
            scratch_shapes=[
                pltpu.VMEM((COARSE * rows, 2 * LANES), BF16),
                pltpu.VMEM((COARSE * rows, 2 * LANES), BF16),
                pltpu.VMEM((COARSE * rows, 2 * LANES), F32),
            ],
        ),
        out_shape=[
            jax.ShapeDtypeStruct(out, F32),
            jax.ShapeDtypeStruct((8, LANES), F32),
        ],
        compiler_params=pltpu.CompilerParams(vmem_limit_bytes=VMEM_LIMIT),
        cost_estimate=pl.CostEstimate(
            flops=60 * series * rows * N1 * LANES, bytes_accessed=16 * MIB, transcendentals=0
        ),
        name="first_section",
    )(info, templates, strain, first[0], first[1], stage, twist, *after)


def entry_kernel(steps, banks, which_ref, tmpl_ref, strain_ref, *refs):
    out_ref = refs[-1]
    length = N1 // banks
    first_half = lax.broadcasted_iota(jnp.int32, (ROWS, LANES), 1) < BLOCK
    for n, k in enumerate(steps):
        part = lax.rem(which_ref[2] + k, banks)
        for u in range(length // LANES):
            lane = pl.ds(pl.multiple_of(part * length + u * LANES, LANES), LANES)
            hr, hi = tmpl_ref[0, 0, :, lane], tmpl_ref[0, 1, :, lane]
            piece = 0 if strain_ref.shape[0] == 1 else part
            sr, si = strain_ref[piece, 0, 0, :, tile(u)], strain_ref[piece, 0, 1, :, tile(u)]
            re, im = hr * sr + hi * si, hr * si - hi * sr
            to = 2 * (n * length // LANES + u)
            out_ref[:, tile(to)] = jnp.where(first_half, re, pltpu.roll(im, BLOCK, 1))
            out_ref[:, tile(to + 1)] = jnp.where(first_half, pltpu.roll(re, BLOCK, 1), im)


def entry_product(steps, banks, half, which, templates, strain, after):
    pieces, _, _, cols, length = strain.shape
    first = half * cols // ROWS
    return pl.pallas_call(
        functools.partial(entry_kernel, steps, banks),
        grid_spec=pltpu.PrefetchScalarGridSpec(
            num_scalar_prefetch=1,
            grid=(cols // ROWS,),
            in_specs=[
                pl.BlockSpec((1, 2, ROWS, N1), lambda c, w: (w[0], 0, first + c, 0)),
                pl.BlockSpec((pieces, 1, 2, ROWS, length), lambda c, w: (0, w[1], 0, c, 0)),
            ]
            + [ANY] * len(after),
            out_specs=pl.BlockSpec((ROWS, 2 * length * len(steps)), lambda c, w: (c, 0)),
        ),
        out_shape=jax.ShapeDtypeStruct((cols, 2 * length * len(steps)), F32),
        compiler_params=pltpu.CompilerParams(vmem_limit_bytes=VMEM_LIMIT),
        cost_estimate=COST,
        name="entry_product",
    )(which, templates, strain, *after)


def second_points(x, w2_ref, use):
    for a, (yr, yi) in enumerate(dft4(x)):
        y = jnp.concatenate([yr, yi], axis=0)
        table = w2_ref[a * 4 * LANES : (a + 1) * 4 * LANES, :]
        z = rows_dot3(table, split(y))
        use(a, z[:LANES], z[LANES:])


def second_kernel(freq, halves, info_ref, scale_ref, *refs):
    part_refs, w2_ref = refs[:halves], refs[halves]
    out_ref, hold, order = refs[-3:]
    place = info_ref[0]
    groups, cols = part_refs[0].shape[3:5]
    per = LANES // (halves * cols)
    width = LANES // freq
    scale = scale_ref[info_ref[1 + 2 * pl.program_id(0)]]

    def rows_of(p, u):
        tiles = [
            jnp.concatenate(
                [ref[u * per + f, 0, p, g] for ref in part_refs for f in range(per)],
                axis=0,
            )
            for g in range(groups)
        ]
        return jnp.concatenate(tiles, axis=1)

    x = [(rows_of(0, u), rows_of(1, u)) for u in range(FOUR)]

    def keep(a, re, im):
        for p, value in enumerate((re, im)):
            for g in range(groups):
                hold[p, g, pl.ds(a, LANES, stride=FOUR), :] = value[:, tile(g)] * scale

    second_points(x, w2_ref, keep)
    for p in range(2):
        for g in range(groups):
            turned = hold[p, g].T
            for s in range(freq):
                a = g * freq + lax.rem(s - place + freq, freq)
                for j in range(FOUR):
                    order[p, j, pl.ds(a, width, stride=COARSE), :] = turned[
                        s * width : (s + 1) * width, tile(j)
                    ]
        for j in range(FOUR):
            out_ref[0, 0, p, :, tile(j)] = order[p, j]


def second_section(freq, info, scale, parts, second, snr, after):
    _, series, _, groups, cols, _ = parts[0].shape
    halves = len(parts)
    times = groups * LANES
    smem = pl.BlockSpec(memory_space=pltpu.SMEM)
    table = pl.BlockSpec((FOUR * 4 * LANES, 2 * LANES), lambda i, n: (0, 0))
    part = pl.BlockSpec(
        (freq, 1, 2, groups, cols, LANES), lambda i, n: (0, i, 0, 0, 0, 0)
    )
    return pl.pallas_call(
        functools.partial(second_kernel, freq, halves),
        grid_spec=pltpu.PrefetchScalarGridSpec(
            num_scalar_prefetch=1,
            grid=(series,),
            in_specs=[smem] + [part] * halves + [table, ANY] + [ANY] * len(after),
            out_specs=pl.BlockSpec(
                (1, 1, 2, times, N2), lambda i, n: (n[1 + 2 * i], n[2 + 2 * i], 0, 0, 0)
            ),
            scratch_shapes=[
                pltpu.VMEM((2, groups, N2, LANES), F32),
                pltpu.VMEM((2, FOUR, times, LANES), F32),
            ],
        ),
        out_shape=jax.ShapeDtypeStruct(snr.shape, F32),
        input_output_aliases={3 + halves: 0},
        compiler_params=pltpu.CompilerParams(vmem_limit_bytes=24 * MIB),
        cost_estimate=COST,
        name="second_section",
    )(info, scale, *parts, second, snr, *after)


BLOCKS = 4


def bank_kernel(block_ref, inner_ref, high_ref, low_ref):
    times = block_ref.shape[-1]
    rc, rs = inner_ref[0], inner_ref[1]
    for b in range(BLOCKS):
        bc, bs = block_ref[b, 0:1, :], block_ref[b, 1:2, :]
        cos, sin = split(bc * rc - bs * rs), split(bc * rs + bs * rc)
        top = slice(2 * b * BLOCK, (2 * b + 1) * BLOCK)
        low = slice((2 * b + 1) * BLOCK, (2 * b + 2) * BLOCK)
        for ref, c, s in zip((high_ref, low_ref), cos, sin):
            ref[top, :times] = c
            ref[top, times:] = s
            ref[low, :times] = -s
            ref[low, times:] = c


def bank_table(own_time):
    times = own_time.shape[0]
    block = jnp.arange(NBLK, dtype=jnp.int32)[:, None] * own_time[None, :]
    block = jnp.stack(phase(block, NBLK), axis=1)
    inner = jnp.arange(BLOCK, dtype=jnp.int32)[:, None] * own_time[None, :]
    inner = jnp.stack(phase(inner, N1))
    return pl.pallas_call(
        bank_kernel,
        grid=(NBLK // BLOCKS,),
        in_specs=[
            pl.BlockSpec((BLOCKS, 2, times), lambda b: (b, 0, 0)),
            pl.BlockSpec((2, BLOCK, times), lambda b: (0, 0, 0)),
        ],
        out_specs=[pl.BlockSpec((BLOCKS * 2 * BLOCK, 2 * times), lambda b: (b, 0))] * 2,
        out_shape=[jax.ShapeDtypeStruct((2 * N1, 2 * times), BF16)] * 2,
        compiler_params=pltpu.CompilerParams(vmem_limit_bytes=VMEM_LIMIT),
        cost_estimate=COST,
        name="bank_table",
    )(block, inner)


def bins_first_kernel(pieces, banks, place_ref, edge_ref, *refs):
    own_refs, rest_refs = refs[:pieces], refs[pieces : 2 * pieces]
    wh_ref, wl_ref, tw_ref = refs[2 * pieces : 2 * pieces + 3]
    level_ref, total_ref, x, acc = refs[-4:]
    times = total_ref.shape[-1]
    cols = own_refs[0].shape[0]
    length = 2 * N1 // banks
    chunk = FOUR * LANES
    step = pl.program_id(0)

    @pl.when(step == 0)
    def _():
        for k in range(pieces):
            row = pl.multiple_of((place_ref[0] ^ k) * cols, cols)
            low = pl.multiple_of(row + pieces * cols, cols)
            for n in range(banks):
                ref = rest_refs[k] if n else own_refs[k]
                start = lax.rem(place_ref[1] + n, banks) * length

                def cut(i, carry):
                    lane = max(n - 1, 0) * length + i * chunk
                    part = split(ref[:, pl.ds(pl.multiple_of(lane, chunk), chunk)])
                    to = pl.ds(pl.multiple_of(start + i * chunk, chunk), chunk)
                    x[pl.ds(row, cols), to], x[pl.ds(low, cols), to] = part
                    return carry

                lax.fori_loop(0, length // chunk, cut, 0)
        total_ref[...] = jnp.zeros_like(total_ref)

    def blocks_at(block, blocks):
        at = pl.ds(pl.multiple_of(block * LANES, LANES), blocks * LANES)
        return rows_dot3(x[:, at], (wh_ref[at, :], wl_ref[at, :]))

    for i in range(TOGETHER):
        start, end = edge_ref[step * TOGETHER + i], edge_ref[step * TOGETHER + i + 1]
        odd = (end - start) % 2

        @pl.when(odd == 1)
        def _():
            acc[i] = blocks_at(end - 1, 1)

        @pl.when(odd == 0)
        def _():
            acc[i] = blocks_at(end - 2, 2)

        def two(n, carry):
            acc[i] += blocks_at(start + 2 * n, 2)
            return carry

        lax.fori_loop(0, (end - start - 1) // 2, two, 0)

    for u in range(pieces * cols // LANES):
        at = tile(u)
        cos, sin = tw_ref[0, at, :], tw_ref[1, at, :]
        sum_r, sum_i = total_ref[0, at, :], total_ref[1, at, :]
        for i in range(TOGETHER):
            re, im = acc[i, at, :times], acc[i, at, times:]
            vr, vi = re * cos - im * sin, re * sin + im * cos
            level_ref[i, 0, at, :] = vr
            level_ref[i, 1, at, :] = vi
            sum_r, sum_i = sum_r + vr, sum_i + vi
        total_ref[0, at, :] = sum_r
        total_ref[1, at, :] = sum_i


def bins_first(half, banks, place, edges, own, rest, table, twist, after):
    cols, length = rest[0].shape
    rows, times = twist.shape[1:]
    smem = pl.BlockSpec(memory_space=pltpu.SMEM)
    fixed = lambda shape: pl.BlockSpec(shape, lambda i: (0,) * len(shape))
    return pl.pallas_call(
        functools.partial(bins_first_kernel, len(own), banks),
        grid=(BINS // TOGETHER,),
        in_specs=[smem, smem]
        + [pl.BlockSpec((cols, 2 * N1 - length), lambda i: (half, 0))] * len(own)
        + [fixed((cols, length))] * len(rest)
        + [fixed((2 * N1, 2 * times))] * 2
        + [fixed((2, rows, times))]
        + [ANY] * len(after),
        out_specs=[
            pl.BlockSpec((TOGETHER, 2, rows, times), lambda i: (i, 0, 0, 0)),
            fixed((2, rows, times)),
        ],
        out_shape=[
            jax.ShapeDtypeStruct((BINS, 2, rows, times), F32),
            jax.ShapeDtypeStruct((2, rows, times), F32),
        ],
        scratch_shapes=[
            pltpu.VMEM((2 * rows, 2 * N1), BF16),
            pltpu.VMEM((TOGETHER, rows, 2 * times), F32),
        ],
        compiler_params=pltpu.CompilerParams(vmem_limit_bytes=VMEM_LIMIT),
        cost_estimate=COST,
        name="bins_first",
    )(place, edges, *own, *rest, *table, twist, *after)


def bins_second_kernel(halves, which_ref, scale_ref, gain_ref, share_ref, *refs):
    level_refs, total_refs = refs[:halves], refs[halves : 2 * halves]
    w2_ref, out_ref, snr_ref, chi, hold = refs[2 * halves :]
    times = out_ref.shape[0]
    part_rows = LANES // halves
    step = pl.program_id(0)

    @pl.when(step == 0)
    def _():
        chi[...] = jnp.zeros_like(chi)

    def rows_of(get, u):
        at = slice(u * part_rows, (u + 1) * part_rows)
        return jnp.concatenate([get(h, at) for h in range(halves)], axis=0)

    def keep(a, re, im):
        chi[a] += re * re + im * im

    for i in range(TOGETHER):
        gain, share = gain_ref[step * TOGETHER + i], share_ref[step * TOGETHER + i]

        def deviation(p):
            return lambda h, at: (
                level_refs[h][i, p, at, :] * gain - total_refs[h][p, at, :] * share
            )

        x = [tuple(rows_of(deviation(p), u) for p in range(2)) for u in range(FOUR)]
        second_points(x, w2_ref, keep)

    @pl.when(step == BINS // TOGETHER - 1)
    def _():
        scale = scale_ref[which_ref[0]]

        def whole(p):
            return lambda h, at: total_refs[h][p, at, :] * scale

        def put(a, re, im):
            for p, value in enumerate((re, im)):
                for g in range(times // LANES):
                    hold[p, g, pl.ds(a, LANES, stride=FOUR), :] = value[:, tile(g)]

        y = [tuple(rows_of(whole(p), u) for p in range(2)) for u in range(FOUR)]
        second_points(y, w2_ref, put)
        for g in range(times // LANES):
            for a in range(FOUR):
                hold[2, g, pl.ds(a, LANES, stride=FOUR), :] = chi[a, :, tile(g)]
            for p in range(2):
                snr_ref[0, 0, p, tile(g), :] = hold[p, g].T
            out_ref[tile(g), :] = hold[2, g].T


def bins_second(which, scale, gain, share, levels, totals, second, tmpls, dets):
    _, _, rows, times = levels[0].shape
    halves = len(levels)
    smem = pl.BlockSpec(memory_space=pltpu.SMEM)
    fixed = lambda shape: pl.BlockSpec(shape, lambda i, w: (0,) * len(shape))
    return pl.pallas_call(
        functools.partial(bins_second_kernel, halves),
        grid_spec=pltpu.PrefetchScalarGridSpec(
            num_scalar_prefetch=1,
            grid=(BINS // TOGETHER,),
            in_specs=[smem, smem, smem]
            + [pl.BlockSpec((TOGETHER, 2, rows, times), lambda i, w: (i, 0, 0, 0))] * halves
            + [fixed((2, rows, times))] * halves
            + [fixed((FOUR * 4 * LANES, 2 * LANES))],
            out_specs=[
                fixed((times, N2)),
                pl.BlockSpec((1, 1, 2, times, N2), lambda i, w: (w[0], w[1], 0, 0, 0)),
            ],
            scratch_shapes=[
                pltpu.VMEM((FOUR, LANES, times), F32),
                pltpu.VMEM((3, times // LANES, N2, LANES), F32),
            ],
        ),
        out_shape=[
            jax.ShapeDtypeStruct((times, N2), F32),
            jax.ShapeDtypeStruct((tmpls, dets, 2, times, N2), F32),
        ],
        compiler_params=pltpu.CompilerParams(vmem_limit_bytes=VMEM_LIMIT),
        cost_estimate=COST,
        name="bins_second",
    )(which, scale, gain, share, *levels, *totals, second)


def handed_on(arrays, after):
    count = len(arrays)
    return pl.pallas_call(
        lambda *refs: None,
        in_specs=[ANY] * (count + len(after)),
        out_specs=[ANY] * count,
        out_shape=[jax.ShapeDtypeStruct(x.shape, x.dtype) for x in arrays],
        input_output_aliases={i: i for i in range(count)},
        compiler_params=pltpu.CompilerParams(vmem_limit_bytes=VMEM_LIMIT),
        cost_estimate=COST,
        name="handed_on",
    )(*arrays, *after)


def swap(x, freq, k):
    return lax.ppermute(x, "freq", [(i, i ^ k) for i in range(freq)])


def far_pieces(own, freq):
    return [own] + [swap(own, freq, k) for k in range(2, freq, 2)]


def near_pieces(far, freq):
    return [x for even in far for x in (even, swap(even, freq, 1))]


def per_device(strain, templates, coinc_tmpl, coinc_det, bin_edges):
    freq, banks = lax.axis_size("freq"), lax.axis_size("bank")
    place = lax.axis_index("freq").astype(jnp.int32)
    bank = lax.axis_index("bank").astype(jnp.int32)
    tmpls, _, cols, _ = templates.shape
    slots, dets = coinc_tmpl.shape[0], strain.shape[0]
    times = N1 // freq
    part = cols // HALVES

    slices = [strain[:, :, h * part : (h + 1) * part] for h in range(HALVES)]
    strains = [lax.all_gather(x, "bank", axis=0, tiled=False) for x in slices]
    first = tuple(jnp.asarray(t) for t in first_table())
    second = jnp.asarray(second_table(cols, HALVES))
    stage = jnp.asarray(stage_table())

    column = place * cols + jnp.arange(cols, dtype=jnp.int32)
    lane = jnp.arange(N1, dtype=jnp.int32)
    time_of_lane = lane // LANES + COARSE * (lane % LANES)
    twist = jnp.stack(phase(column[:, None] * time_of_lane[None, :], N1 * N2))
    own_time = place * times + jnp.arange(times, dtype=jnp.int32)
    table = bank_table(own_time)
    own_twist = []
    for h in range(HALVES):
        rows = jnp.arange(freq * part, dtype=jnp.int32)
        rows = rows // part * cols + h * part + rows % part
        own_twist.append(jnp.stack(phase(rows[:, None] * own_time[None, :], N1 * N2)))

    which = [jnp.stack([coinc_tmpl[j], coinc_det[j], bank]) for j in range(slots)]
    series = jnp.arange(tmpls * dets - 1, dtype=jnp.int32)
    series = series + (series >= which[0][0] * dets + which[0][1])
    info = jnp.stack([series // dets, series % dets], axis=1).reshape(-1)
    info = jnp.concatenate([place.reshape(1), info])
    ends = jnp.zeros((1,), jnp.int32), jnp.full((1,), NBLK, jnp.int32)
    edges = [
        jnp.concatenate([ends[0], bin_edges[coinc_tmpl[j]], ends[1]]) for j in range(slots)
    ]
    here = jnp.stack([place, bank])

    power = (templates[:, 0] ** 2 + templates[:, 1] ** 2).sum(axis=1)
    power = power.reshape(tmpls, NBLK, BLOCK).sum(axis=2)
    own = [entry_product((0,), banks, 0, w, templates, strain[None], slices) for w in which]
    wide = own[0].shape[1]
    power = jnp.pad(power.reshape(1, -1), ((0, 7), (0, wide - tmpls * NBLK)))
    own[0] = jnp.concatenate([own[0], power], axis=0)
    own = [near_pieces(far_pieces(x, freq), freq) for x in own]
    gathered = [x for entry in own for x in entry[1:]]

    block_power = sum(x[cols, : tmpls * NBLK] for x in own[0]).reshape(tmpls, NBLK)
    sigma_sq = block_power.sum(axis=1)
    inv_sigma = lax.rsqrt(sigma_sq)
    bin_of = jnp.sum(
        jnp.arange(NBLK, dtype=jnp.int32)[None, :, None] >= bin_edges[:, None, :], axis=2
    )
    inside = bin_of[:, None, :] == jnp.arange(BINS, dtype=jnp.int32)[None, :, None]
    weights = jnp.where(inside, block_power[:, None, :], 0.0).sum(axis=2) / sigma_sq[:, None]
    gains = [inv_sigma[coinc_tmpl[j]] * lax.rsqrt(weights[coinc_tmpl[j]]) for j in range(slots)]
    shares = [gains[j] * weights[coinc_tmpl[j]] for j in range(slots)]
    which, inv_sigma, gains, shares, twist, info, edges, here, table, own_twist = (
        lax.optimization_barrier(
            (which, inv_sigma, gains, shares, twist, info, edges, here, table, own_twist)
        )
    )

    def exchange(x):
        got = lax.all_to_all(
            x.reshape(freq, -1, LANES), "freq", split_axis=0, concat_axis=0, tiled=True
        )
        return got.reshape(x.shape)

    def bins_of(h, rest, after):
        return [
            bins_first(h, banks, here, edges[j], own[j], rest[j], table, own_twist[h], after)
            for j in range(slots)
        ]

    parts, halves, rest, after = [], [], [], gathered
    later = tuple(range(1, banks))
    for h in range(HALVES):
        half = [entry_product(later, banks, h, w, templates, strains[h], after) for w in which]
        far = [far_pieces(x, freq) for x in half]
        sent, token = first_section(
            freq, h, info, templates, strains[h], first, stage, twist, half
        )
        if h < HALVES - 1:
            (sent,) = handed_on([sent], [piece for x in far for piece in x[1:]])
        if h:
            halves.append(bins_of(h - 1, rest, [token]))
        done = [token] + parts + [x[1] for one in halves for x in one]
        far = [x[:1] + list(handed_on(x[1:], done)) for x in far]
        rest = [near_pieces(x, freq) for x in far]
        if h == HALVES - 1:
            (sent,) = handed_on([sent], [x for entry in rest for x in entry[1:]])
        parts.append(exchange(sent))
        after = [token]
    halves.append(bins_of(HALVES - 1, rest, [sent]))

    chi, snr = [], None
    for j in range(slots):
        levels, totals = zip(*[x[j] for x in halves])
        one, series_of = bins_second(
            which[j], inv_sigma, gains[j], shares[j], levels, totals, second, tmpls, dets
        )
        chi.append(one)
        snr = series_of if snr is None else snr
    snr = second_section(freq, info, inv_sigma, parts, second, snr, chi)
    return (snr, jnp.stack(chi))


def solution(mesh):
    placed = (
        P(None, None, "freq", "bank"),
        P("bank", None, "freq", None),
        P("bank"),
        P("bank"),
        P("bank", None),
    )
    return jax.shard_map(
        per_device,
        mesh=mesh,
        in_specs=placed,
        out_specs=(P("bank", None, None, "freq", None), P("bank", "freq", None)),
        check_vma=False,
    )
```
